32 devices in a mesh: group: 2 (over y), inst: 4 (over x, core), tp: 4 (over z).
Axes of the slice: x: 2, y: 2, z: 4, core: 2. Of those that a mesh axis runs over, the one named last changes fastest.
Arguments:
- mig_hidden: bfloat16 [8, 64, 2, 5120], P(('group', 'inst'), None, None, 'tp'), parts along dimension 0, may hold values from -6 to 6
- mig_dest: int32 [8, 2], P('group'), parts along dimension 0, may hold values from 0 to 3, as said below
- mig_count: int32 [8, 2], P('group'), parts along dimension 0, may hold values from 48 to 64
- attn_gain: bfloat16 [5120], P('tp'), may hold values from 0.099609375 to 1.8984375
- kv_weight: bfloat16 [5120, 2048], P('tp'), may hold values from -0.078125 to 0.078125
- k_gain: bfloat16 [128], replicated, may hold values from 0.099609375 to 1.8984375
- query: bfloat16 [8, 5, 8192], P(('group', 'inst')), parts along dimension 0, may hold values from -113.137085 to 113.137085
- new_kv: bfloat16 [8, 5, 2048], P(('group', 'inst')), parts along dimension 0, may hold values from -5 to 5
- k_cache: bfloat16 [8, 3, 4096, 1024], P(('group', 'inst'), None, 'tp'), parts along dimension 0, may hold values from -4 to 4
- v_cache: bfloat16 [8, 3, 4096, 1024], P(('group', 'inst'), None, 'tp'), parts along dimension 0, may hold values from -5 to 5
- lengths: int32 [8, 3], P(('group', 'inst')), parts along dimension 0, may hold values from 256 to 4096
Outputs:
- attn_out: bfloat16 [8, 5, 8192], P(('group', 'inst'), None, 'tp'), parts along dimension 0
The draws below stay inside these ranges and needn't reach their ends.
There are 2 independent parts, one for each index of `group`. The reference program is written for one: setup_inputs(seed, part) draws one part's arguments, and reference() takes and returns one part's arrays. A program takes and returns all parts, laid end to end along the dimension named above; an argument that names none is the same for every part. Nothing has to cross between parts.
Inputs may be any that keep to these rules, and one draw needn't show every extreme that they name: `mig_dest`: each instance receives exactly 2 requests, never its own, and each instance sends its 2 requests to different instances.
All inputs are finite; a program needn't handle non-finite values.
Results may differ from the reference program's by a relative error of at most 0.02.
Values may be sent and summed in bfloat16 or wider, within the bound.
No kernel may reach another device: no remote copies, remote signals or barrier semaphores. Data moves between devices by JAX's collectives and lax.ppermute only.
A program may use at most 64 MiB of HBM per device.

```python
import jax
import jax.numpy as jnp
from jax import lax

D = 5120
H = 64
KVH = 8
HD = 128
REQ = 2
RES = 3
CAP = 64
CTX = 4096
NR = 5
N_INST = 4


def draw_mig_dest(key, part):
    key = jax.random.fold_in(key, 11)
    order = jax.random.permutation(jax.random.fold_in(key, 1), N_INST)
    offsets = jax.random.permutation(jax.random.fold_in(key, 2), N_INST - 1)[:REQ] + 1
    place = jnp.argsort(order, stable=True)
    return order[(place[:, None] + offsets[None, :]) % N_INST].astype(jnp.int32)


def draw_mig_count(key, part):
    key = jax.random.fold_in(key, 12)
    counts = jax.random.randint(jax.random.fold_in(key, 1), (N_INST, REQ), CAP - CAP // 4, CAP + 1)
    return counts.at[0, 0].set(CAP).astype(jnp.int32)


def draw_lengths(key, part):
    key = jax.random.fold_in(key, 13)
    shifts = jax.random.randint(jax.random.fold_in(key, 1), (N_INST, RES), 0, 4)
    base = jnp.right_shift(jnp.full((N_INST, RES), CTX, jnp.int32), shifts)
    cut = jax.random.randint(jax.random.fold_in(key, 2), (N_INST, RES), 0, jnp.maximum(base // 2, 1))
    return (base - cut).at[0, 0].set(CTX).astype(jnp.int32)


def draw_k_cache(key, part):
    key = jax.random.fold_in(key, 14)
    cache = jnp.clip(jax.random.normal(key, (N_INST, RES, CTX, KVH * HD), jnp.float32), -4.0, 4.0)
    return cache.astype(jnp.bfloat16)


def draw_query(key, part):
    key = jax.random.fold_in(key, 15)
    rows = jnp.clip(jax.random.normal(key, (N_INST, RES + REQ, H * HD), jnp.float32), -4.5, 4.5)
    return rows.astype(jnp.bfloat16)


def level_of(stream_key, dims, split, low, top_value):
    loudness = 1.0
    for axis_at, parts in split:
        heights = jax.random.uniform(jax.random.fold_in(jax.random.fold_in(stream_key, 6), axis_at), (parts,), jnp.float32, low / len(split), top_value / len(split))
        loudness = loudness * jnp.repeat(jnp.exp(heights), dims[axis_at] // parts).reshape((-1,) + (1,) * (len(dims) - 1 - axis_at))
    return loudness


def centred(rng, shape, spread, most, pieces=(), held_as=jnp.bfloat16):
    entries = jax.random.normal(rng, shape, jnp.float32) * spread
    if len(pieces) > 0:
        entries = level_of(rng, shape, pieces, -0.22, 0.18) * entries
    return jnp.clip(entries, min=-most, max=most).astype(held_as)


def setup_inputs(seed: int = 0, part: int = 0) -> dict:
    key_of = jax.random.split(jax.random.key(seed), 12)
    part_splits = jax.random.split(jax.random.fold_in(key_of[11], part), 12)
    return {
        "mig_hidden": centred(part_splits[0], (N_INST, CAP, REQ, D), 1.0, 6.0, ((0, 4), (3, 4))),
        "mig_dest": draw_mig_dest(jax.random.fold_in(jax.random.fold_in(key_of[11], part), 71), part),
        "mig_count": draw_mig_count(jax.random.fold_in(jax.random.fold_in(key_of[11], part), 71), part),
        "attn_gain": jnp.clip(1.0 + 0.18 * jax.random.normal(key_of[3], (D,), jnp.float32), 0.099609375, 1.8984375).astype(jnp.bfloat16),
        "kv_weight": centred(key_of[4], (D, 2 * KVH * HD), D ** -0.5, 0.078125, ((0, 4),)),
        "k_gain": jnp.clip(1.0 + 0.18 * jax.random.normal(key_of[5], (HD,), jnp.float32), 0.099609375, 1.8984375).astype(jnp.bfloat16),
        "query": draw_query(jax.random.fold_in(jax.random.fold_in(key_of[11], part), 71), part),
        "new_kv": centred(part_splits[7], (N_INST, NR, 2 * KVH * HD), 1.0, 5.0, ((0, 4),)),
        "k_cache": draw_k_cache(jax.random.fold_in(jax.random.fold_in(key_of[11], part), 71), part),
        "v_cache": centred(part_splits[9], (N_INST, RES, CTX, KVH * HD), 1.0, 5.0, ((0, 4), (2, 4))),
        "lengths": draw_lengths(jax.random.fold_in(jax.random.fold_in(key_of[11], part), 71), part),
    }


EPS = 1e-06
THETA = 1000000.0

def rotate(keys, positions):
    half = keys.shape[-1] // 2
    freq = THETA ** (-jnp.arange(half, dtype=jnp.float32) * 2.0 / keys.shape[-1])
    angle = positions[..., None] * freq
    first = keys[..., :half]
    second = keys[..., half:]
    cosine = jnp.cos(angle)
    sine = jnp.sin(angle)
    return jnp.concatenate([first * cosine - second * sine, second * cosine + first * sine], axis=-1)

def attend(query_row, cache_keys, cache_values, valid, own):
    group = H // KVH
    heads_q = query_row.astype(jnp.float32).reshape(KVH, group, HD)
    heads_k = cache_keys.astype(jnp.float32).reshape(-1, KVH, HD)
    heads_v = cache_values.astype(jnp.float32).reshape(-1, KVH, HD)
    scores = jnp.einsum('gqd,pgd->gqp', heads_q, heads_k) / jnp.sqrt(jnp.float32(HD))
    scores = jnp.where(valid[None, None, :], scores, -jnp.inf)
    own_key = own[:KVH * HD].astype(jnp.float32).reshape(KVH, HD)
    own_value = own[KVH * HD:].astype(jnp.float32).reshape(KVH, HD)
    own_score = jnp.einsum('gqd,gd->gq', heads_q, own_key) / jnp.sqrt(jnp.float32(HD))
    top = jnp.maximum(lax.optimization_barrier(jnp.max(scores, axis=-1)), own_score)
    weights = jnp.exp(scores - top[..., None])
    own_weight = jnp.exp(own_score - top)
    denom = lax.optimization_barrier(jnp.sum(weights, axis=-1)) + own_weight
    numer = jnp.einsum('gqp,pgd->gqd', weights.astype(jnp.bfloat16).astype(jnp.float32), heads_v)
    numer = numer + own_weight.astype(jnp.bfloat16).astype(jnp.float32)[..., None] * own_value[:, None, :]
    return (numer / denom[..., None]).astype(jnp.bfloat16).reshape(H * HD)

def reference(mig_hidden, mig_dest, mig_count, attn_gain, kv_weight, k_gain, query, new_kv, k_cache, v_cache, lengths):
    wide = mig_hidden.astype(jnp.float32)
    scale = lax.rsqrt(lax.optimization_barrier(jnp.mean(wide * wide, axis=-1, keepdims=True)) + EPS)
    normed = (wide * scale * attn_gain.astype(jnp.float32)).astype(jnp.bfloat16)
    kv = jnp.dot(normed.reshape(-1, D), kv_weight, preferred_element_type=jnp.float32)
    kv = kv.reshape(N_INST, CAP, REQ, 2 * KVH * HD)
    keys = kv[..., :KVH * HD].reshape(N_INST, CAP, REQ, KVH, HD)
    keys = keys * lax.rsqrt(lax.optimization_barrier(jnp.mean(keys * keys, axis=-1, keepdims=True)) + EPS) * k_gain.astype(jnp.float32)
    slots = jnp.arange(CAP).astype(jnp.float32)
    keys = rotate(keys, slots[None, :, None, None])
    keys = keys.reshape(N_INST, CAP, REQ, KVH * HD).astype(jnp.bfloat16)
    values = kv[..., KVH * HD:].astype(jnp.bfloat16)
    results = []
    for dest in range(N_INST):
        match = mig_dest == dest
        sources = jnp.nonzero(jnp.any(match, axis=1), size=REQ)[0].astype(jnp.int32)
        which = jnp.argmax(match, axis=1).astype(jnp.int32)[sources]
        moved_keys = keys[sources, :, which]
        moved_values = values[sources, :, which]
        counts = mig_count[sources, which]
        for item in range(RES + REQ):
            if item < RES:
                valid = jnp.arange(CTX) < lengths[dest, item]
                row = attend(query[dest, item], k_cache[dest, item], v_cache[dest, item], valid, new_kv[dest, item])
            else:
                valid = jnp.arange(CAP) < counts[item - RES]
                row = attend(query[dest, item], moved_keys[item - RES], moved_values[item - RES], valid, new_kv[dest, item])
            results.append(row)
    return jnp.stack(results).reshape(N_INST, RES + REQ, H * HD)
```

```python
import functools

import jax
import jax.numpy as jnp
import numpy as np
from jax import lax
from jax.experimental import pallas as pl
from jax.experimental.pallas import tpu as pltpu
from jax.sharding import PartitionSpec as P

EPS = 1e-06
THETA = 1000000.0
ABSENT = -1e30
F32 = jnp.float32
BF16 = jnp.bfloat16
VMEM_LIMIT = 56 * 1024 * 1024

VMEM = pl.BlockSpec(memory_space=pltpu.VMEM)
SMEM = pl.BlockSpec(memory_space=pltpu.SMEM)
ANYWHERE = pl.BlockSpec(memory_space=pl.ANY)


def iota(shape, dim):
    return lax.broadcasted_iota(jnp.int32, shape, dim)


def column_to_row(column, period):
    n = column.shape[0]
    spread = jnp.where(iota((n, 128), 0) % period == iota((n, 128), 1), column, 0.0)
    return jnp.sum(spread.reshape(n // period, period, 128), axis=1)


def row_to_column(row, n):
    return jnp.sum(
        jnp.where(iota((n, 128), 0) == iota((n, 128), 1), row, 0.0), axis=1, keepdims=True
    )


def split_bf16(x):
    high = x.astype(BF16)
    return high, (x - high.astype(F32)).astype(BF16)


def project_kernel(ranks, rank_ref, x_ref, gain_ref, wk_ref, wv_ref, *rest):
    outs, sq_ref, xg_ref = rest[:ranks], rest[ranks], rest[ranks + 1]
    step = pl.program_id(0)
    slots, requests, _ = x_ref.shape

    @pl.when(step == 0)
    def _():
        gain = gain_ref[...].astype(F32)
        for r in range(requests):
            x = x_ref[:, r, :].astype(F32)
            xg_ref[r * slots : (r + 1) * slots, :] = (x * gain).astype(BF16)
            sq_ref[r : r + 1, :] = column_to_row(jnp.sum(x * x, axis=1, keepdims=True), slots)

    width = wk_ref.shape[1]
    keys = jnp.dot(xg_ref[...], wk_ref[...], preferred_element_type=F32).astype(BF16)
    values = jnp.dot(xg_ref[...], wv_ref[...], preferred_element_type=F32).astype(BF16)
    for j in range(ranks):

        @pl.when(step == j)
        def _():
            outs[j][:, :width] = keys
            outs[j][:, width:] = values


def project(rank, x, gain, weight, ranks, heads_mine, group, kv_mine):
    slots, requests, feats = x.shape
    width = weight.shape[1] // 2
    kv_heads = width // 128
    piece = kv_mine * 128

    def column(j, rank_ref):
        return lax.rem(rank_ref[0] + j, ranks) * heads_mine // group // kv_mine

    spec = pltpu.PrefetchScalarGridSpec(
        num_scalar_prefetch=1,
        grid=(ranks,),
        in_specs=[
            pl.BlockSpec((slots, requests, feats), lambda j, s: (0, 0, 0)),
            pl.BlockSpec((1, feats), lambda j, s: (0, 0)),
            pl.BlockSpec((feats, piece), lambda j, s: (0, column(j, s))),
            pl.BlockSpec((feats, piece), lambda j, s: (0, kv_heads // kv_mine + column(j, s))),
        ],
        out_specs=[pl.BlockSpec((requests * slots, 2 * piece), lambda j, s: (0, 0))] * ranks
        + [pl.BlockSpec((requests, 128), lambda j, s: (0, 0))],
        scratch_shapes=[pltpu.VMEM((requests * slots, feats), BF16)],
    )
    outs = pl.pallas_call(
        functools.partial(project_kernel, ranks),
        grid_spec=spec,
        out_shape=[jax.ShapeDtypeStruct((requests * slots, 2 * piece), BF16)] * ranks
        + [jax.ShapeDtypeStruct((requests, 128), F32)],
        compiler_params=pltpu.CompilerParams(vmem_limit_bytes=VMEM_LIMIT),
        cost_estimate=pl.CostEstimate(
            flops=2 * requests * slots * feats * 2 * width,
            bytes_accessed=2 * feats * 2 * width,
            transcendentals=0,
        ),
        name="project",
    )(rank, x, gain, weight, weight)
    return outs[:ranks], outs[ranks]


def resident_kernel(ranks, rank_ref, len_ref, q_ref, sq_ref, k_hbm, v_hbm, *rest):
    outs = rest[:ranks]
    k_buf, v_buf, o_all, m_all, l_all, sems = rest[ranks:]
    residents, positions, width = k_buf.shape
    copies = []
    for r in range(residents):
        copies.append(
            (
                pltpu.make_async_copy(k_hbm.at[r], k_buf.at[r], sems.at[0, r]),
                pltpu.make_async_copy(v_hbm.at[r], v_buf.at[r], sems.at[1, r]),
            )
        )
    for pair in copies:
        for copy in pair:
            copy.start()
    heads = q_ref.shape[1]
    kv_heads = width // 128
    group = heads // kv_heads
    pair_rows = 2 * group
    heads_mine = heads // ranks
    rank = rank_ref[0]
    top_half = iota((pair_rows, 128), 0) < group
    scale = F32(1.0) / jnp.sqrt(F32(128.0))
    for r in range(residents):
        copies[r][0].wait()
        valid = rank * positions + iota((pair_rows, positions), 1) < len_ref[0, r]
        weights = []
        for p in range(kv_heads // 2):
            rows = slice(p * pair_rows, (p + 1) * pair_rows)
            q = q_ref[r, rows, :]
            zero = jnp.zeros_like(q)
            lhs = jnp.concatenate(
                [jnp.where(top_half, q, zero), jnp.where(top_half, zero, q)], axis=1
            )
            scores = lax.dot_general(
                lhs,
                k_buf[r, :, p * 256 : (p + 1) * 256],
                (((1,), (1,)), ((), ())),
                preferred_element_type=F32,
            )
            scores = jnp.where(valid, scores * scale, ABSENT)
            peak = jnp.max(scores, axis=1, keepdims=True).astype(BF16).astype(F32)
            weight = jnp.where(valid, jnp.exp(scores - peak), 0.0)
            m_all[r, rows, :] = peak
            l_all[r, rows, :] = jnp.sum(weight, axis=1, keepdims=True)
            weights.append(weight.astype(BF16))
        copies[r][1].wait()
        for p in range(kv_heads // 2):
            rows = slice(p * pair_rows, (p + 1) * pair_rows)
            both = jnp.dot(
                weights[p], v_buf[r, :, p * 256 : (p + 1) * 256], preferred_element_type=F32
            )
            o_all[r, rows, :] = jnp.where(top_half, both[:, :128], both[:, 128:])
    stats = []
    for r in range(residents):
        peak = column_to_row(m_all[r], heads_mine)
        high, low = split_bf16(column_to_row(l_all[r], heads_mine))
        stats.append((peak, high.astype(F32), low.astype(F32)))
    for t in range(ranks):
        for r in range(residents):
            for i in range(3):
                o_all[residents + i, t * residents + r : t * residents + r + 1, :] = stats[r][i][
                    t : t + 1
                ]
    sq_high, sq_low = split_bf16(sq_ref[...])
    requests = sq_ref.shape[0]
    for j in range(ranks):
        target = lax.rem(rank + j, ranks)
        parts = [
            o_all[r, pl.ds(target * heads_mine, heads_mine), :] for r in range(residents)
        ] + [
            o_all[residents + i, pl.ds(target * residents, residents), :] for i in range(3)
        ]
        parts += [sq_high.astype(F32), sq_low.astype(F32)]
        filled = residents * (heads_mine + 3) + 2 * requests
        rest_rows = outs[j].shape[0] - filled
        if rest_rows:
            parts.append(jnp.zeros((rest_rows, 128), F32))
        outs[j][...] = jnp.concatenate(parts, axis=0).astype(BF16)


def attend_resident(rank, lengths, queries, squares, k_cache, v_cache, ranks):
    residents, positions, width = k_cache.shape
    heads = queries.shape[1]
    heads_mine = heads // ranks
    requests = squares.shape[0]
    rows = -(-(residents * (heads_mine + 3) + 2 * requests) // 16) * 16
    return pl.pallas_call(
        functools.partial(resident_kernel, ranks),
        in_specs=[SMEM, SMEM, VMEM, VMEM, ANYWHERE, ANYWHERE],
        out_specs=[VMEM] * ranks,
        out_shape=[jax.ShapeDtypeStruct((rows, 128), BF16)] * ranks,
        scratch_shapes=[
            pltpu.VMEM((residents, positions, width), BF16),
            pltpu.VMEM((residents, positions, width), BF16),
            pltpu.VMEM((residents + 3, heads, 128), F32),
            pltpu.VMEM((residents, heads, 1), F32),
            pltpu.VMEM((residents, heads, 1), F32),
            pltpu.SemaphoreType.DMA((2, residents)),
        ],
        compiler_params=pltpu.CompilerParams(vmem_limit_bytes=VMEM_LIMIT),
        cost_estimate=pl.CostEstimate(
            flops=4 * residents * heads * positions * 128,
            bytes_accessed=4 * residents * positions * width,
            transcendentals=residents * heads * positions,
        ),
        name="attend_resident",
    )(rank, lengths, queries, squares, k_cache, v_cache)


def expand(own, rows):
    per = rows // own.shape[0]
    which = iota((rows, 128), 0) // per
    out = jnp.broadcast_to(own[0:1], (rows, 128))
    for h in range(1, own.shape[0]):
        out = jnp.where(which == h, own[h : h + 1], out)
    return out


def moved_kernel(
    insts, ranks, features, at_sq, here_ref, dest_ref, count_ref, gain_ref, cos_ref, sin_ref, *rest
):
    pieces, rest = rest[:ranks], rest[ranks:]
    payloads, rest = rest[:ranks], rest[ranks:]
    asks, rest = rest[: insts - 1], rest[insts - 1 :]
    out_ref, ask_ref, line_ref = rest
    here = here_ref[0]
    requests = dest_ref.shape[1]
    slots = pieces[0].shape[0] // requests
    piece = pieces[0].shape[1] // 2
    kv_mine = piece // 128
    heads_mine = line_ref.shape[1] // 128
    which = iota((heads_mine, 128), 0) // (heads_mine // kv_mine)
    which_slots = iota((heads_mine, slots), 0) // (heads_mine // kv_mine)
    lane = iota((heads_mine, slots), 1)
    scale = F32(1.0) / jnp.sqrt(F32(128.0))
    gain = gain_ref[...].astype(F32)
    squares = None
    for t in range(ranks):
        high = payloads[t][at_sq : at_sq + requests, :].astype(F32)
        low = payloads[t][at_sq + requests : at_sq + 2 * requests, :].astype(F32)
        squares = high + low if squares is None else squares + high + low
    for r in range(requests):
        dest = dest_ref[here, r]
        count = count_ref[here, r]
        place = jnp.int32(0)
        for s in range(insts):
            for c in range(requests):
                place += jnp.where((dest_ref[s, c] == dest) & (here > s), 1, 0).astype(jnp.int32)
        shift = lax.rem(here - dest + insts, insts)
        for j in range(1, insts):

            @pl.when(shift == j)
            def _():
                ask_ref[...] = asks[j - 1][place]

        ask = ask_ref[...]
        q = ask[:heads_mine]
        own_k = expand(ask[heads_mine : heads_mine + kv_mine].astype(F32), heads_mine)
        own_v = expand(ask[heads_mine + kv_mine : heads_mine + 2 * kv_mine].astype(F32), heads_mine)
        rows = slice(r * slots, (r + 1) * slots)
        kv = pieces[0][rows, :].astype(F32)
        for t in range(1, ranks):
            kv = kv + pieces[t][rows, :].astype(F32)
        kv = kv * lax.rsqrt(row_to_column(squares[r : r + 1], slots) / features + EPS)
        scores = None
        values = []
        for h in range(kv_mine):
            key = kv[:, h * 128 : (h + 1) * 128]
            key = key * lax.rsqrt(jnp.mean(key * key, axis=1, keepdims=True) + EPS) * gain
            key = key * cos_ref[...] + pltpu.roll(key, 64, 1) * sin_ref[...]
            part = lax.dot_general(
                q, key.astype(BF16), (((1,), (1,)), ((), ())), preferred_element_type=F32
            )
            scores = part if scores is None else jnp.where(which_slots == h, part, scores)
            values.append(kv[:, piece + h * 128 : piece + (h + 1) * 128].astype(BF16))
        valid = lane < count
        scores = jnp.where(valid, scores * scale, ABSENT)
        own_score = jnp.sum(q.astype(F32) * own_k, axis=1, keepdims=True) * scale
        top = jnp.maximum(jnp.max(scores, axis=1, keepdims=True), own_score)
        weights = jnp.where(valid, jnp.exp(scores - top), 0.0)
        own_weight = jnp.exp(own_score - top)
        total = jnp.sum(weights, axis=1, keepdims=True) + own_weight
        weights = weights.astype(BF16)
        summed = None
        for h in range(kv_mine):
            part = jnp.dot(weights, values[h], preferred_element_type=F32)
            summed = part if summed is None else jnp.where(which == h, part, summed)
        summed = summed + own_weight.astype(BF16).astype(F32) * own_v
        result = summed / total
        for h in range(heads_mine):
            line_ref[r : r + 1, h * 128 : (h + 1) * 128] = result[h : h + 1, :]
    out_ref[...] = line_ref[...].astype(BF16)


def attend_moved(here, dest, count, k_gain, cos, sin, pieces, payloads, asks, heads_mine, at_sq, features):
    requests = dest.shape[1]
    insts, ranks = len(asks) + 1, len(pieces)
    return pl.pallas_call(
        functools.partial(moved_kernel, insts, ranks, features, at_sq),
        in_specs=[SMEM] * 3 + [VMEM] * (3 + 2 * ranks + insts - 1),
        out_specs=VMEM,
        out_shape=jax.ShapeDtypeStruct((requests, heads_mine * 128), BF16),
        scratch_shapes=[
            pltpu.VMEM(asks[0].shape[1:], BF16),
            pltpu.VMEM((requests, heads_mine * 128), F32),
        ],
        compiler_params=pltpu.CompilerParams(vmem_limit_bytes=VMEM_LIMIT),
        name="attend_moved",
    )(here, dest, count, k_gain, cos, sin, *pieces, *payloads, *asks)


def combine_kernel(ranks, residents, ask_ref, *rest):
    payloads = rest[:ranks]
    out_ref, line_ref = rest[ranks:]
    heads_mine = line_ref.shape[1] // 128
    kv_mine = (ask_ref.shape[1] - heads_mine) // 2
    scale = F32(1.0) / jnp.sqrt(F32(128.0))
    at = residents * heads_mine
    for r in range(residents):
        q = ask_ref[r, :heads_mine, :].astype(F32)
        own_k = expand(ask_ref[r, heads_mine : heads_mine + kv_mine, :].astype(F32), heads_mine)
        own_v = expand(
            ask_ref[r, heads_mine + kv_mine : heads_mine + 2 * kv_mine, :].astype(F32), heads_mine
        )
        own_score = jnp.sum(q * own_k, axis=1, keepdims=True) * scale
        peaks, totals = [], []
        for t in range(ranks):
            stat = payloads[t][at : at + 3 * residents, :].astype(F32)
            peaks.append(row_to_column(stat[r : r + 1], heads_mine))
            total = stat[residents + r : residents + r + 1]
            total = total + stat[2 * residents + r : 2 * residents + r + 1]
            totals.append(row_to_column(total, heads_mine))
        top = own_score
        for t in range(ranks):
            top = jnp.maximum(top, peaks[t])
        own_weight = jnp.exp(own_score - top)
        denom = own_weight
        numer = own_weight.astype(BF16).astype(F32) * own_v
        for t in range(ranks):
            keep = jnp.exp(peaks[t] - top)
            denom = denom + keep * totals[t]
            numer = numer + keep * payloads[t][r * heads_mine : (r + 1) * heads_mine, :].astype(F32)
        result = numer / denom
        for h in range(heads_mine):
            line_ref[r : r + 1, h * 128 : (h + 1) * 128] = result[h : h + 1, :]
    out_ref[...] = line_ref[...].astype(BF16)


def combine_resident(asks, payloads, residents, heads_mine):
    return pl.pallas_call(
        functools.partial(combine_kernel, len(payloads), residents),
        in_specs=[VMEM] * (1 + len(payloads)),
        out_specs=VMEM,
        out_shape=jax.ShapeDtypeStruct((residents, heads_mine * 128), BF16),
        scratch_shapes=[pltpu.VMEM((residents, heads_mine * 128), F32)],
        compiler_params=pltpu.CompilerParams(vmem_limit_bytes=VMEM_LIMIT),
        name="combine_resident",
    )(asks, *payloads)


def finish_kernel(insts, here_ref, dest_ref, kept_ref, *rest):
    moved = rest[: insts - 1]
    out_ref, line_ref = rest[insts - 1 :]
    residents = kept_ref.shape[0]
    requests = dest_ref.shape[1]
    here = here_ref[0]
    line_ref[:residents, :] = kept_ref[...].astype(F32)
    place = jnp.int32(residents)
    for s in range(insts):
        for c in range(requests):
            mine = dest_ref[s, c] == here
            shift = lax.rem(here - s + insts, insts)
            for j in range(1, insts):

                @pl.when(mine & (shift == j))
                def _():
                    line_ref[pl.ds(place, 1), :] = moved[j - 1][c : c + 1, :].astype(F32)

            place += jnp.where(mine, 1, 0).astype(jnp.int32)
    out_ref[...] = line_ref[...].astype(BF16)


def finish(here, dest, kept, moved):
    residents, width = kept.shape
    rows = residents + dest.shape[1]
    return pl.pallas_call(
        functools.partial(finish_kernel, len(moved) + 1),
        in_specs=[SMEM, SMEM, VMEM] + [VMEM] * len(moved),
        out_specs=VMEM,
        out_shape=jax.ShapeDtypeStruct((rows, width), BF16),
        scratch_shapes=[pltpu.VMEM((rows, width), F32)],
        compiler_params=pltpu.CompilerParams(vmem_limit_bytes=VMEM_LIMIT),
        name="finish",
    )(here, dest, kept, *moved)


def shifted(x, axis, j, n):
    return lax.ppermute(x, axis, [(i, (i + j) % n) for i in range(n)])


def rotation(slots, head_size):
    half = head_size // 2
    freq = THETA ** (-np.arange(half) * 2.0 / head_size)
    angle = np.arange(slots)[:, None] * freq[None, :]
    cos, sin = np.cos(angle), np.sin(angle)
    return (
        np.concatenate([cos, cos], axis=1).astype(np.float32),
        np.concatenate([-sin, sin], axis=1).astype(np.float32),
    )


def per_device(
    mig_hidden,
    mig_dest,
    mig_count,
    attn_gain,
    kv_weight,
    k_gain,
    query,
    new_kv,
    k_cache,
    v_cache,
    lengths,
):
    insts = lax.axis_size("inst")
    ranks = lax.axis_size("tp")
    here = lax.axis_index("inst").astype(jnp.int32).reshape(1)
    rank = lax.axis_index("tp").astype(jnp.int32).reshape(1)
    head_size = k_gain.shape[0]
    slots, requests, feats = mig_hidden.shape[1:]
    residents = k_cache.shape[1]
    decoded = query.shape[1]
    heads = query.shape[2] // head_size
    kv_heads = kv_weight.shape[1] // 2 // head_size
    heads_mine = heads // ranks
    group = heads // kv_heads
    kv_mine = max(1, heads_mine // group)

    queries = query[0].reshape(decoded, heads, head_size)
    own = new_kv[0].reshape(decoded, 2, kv_heads, head_size)
    my_queries = lax.dynamic_slice_in_dim(queries, rank[0] * heads_mine, heads_mine, 1)
    my_own = lax.dynamic_slice_in_dim(own, rank[0] * heads_mine // group, kv_mine, 2)
    asks = jnp.concatenate(
        [my_queries, my_own.reshape(decoded, 2 * kv_mine, head_size)], axis=1
    )
    asked = [shifted(asks[residents:], "inst", j, insts) for j in range(1, insts)]

    pieces, squares = project(
        rank, mig_hidden[0], attn_gain.reshape(1, feats), kv_weight, ranks, heads_mine, group, kv_mine
    )
    pieces = [pieces[0]] + [shifted(pieces[j], "tp", j, ranks) for j in range(1, ranks)]
    payloads = attend_resident(rank, lengths, queries, squares, k_cache[0], v_cache[0], ranks)
    payloads = [payloads[0]] + [shifted(payloads[j], "tp", j, ranks) for j in range(1, ranks)]
    kept = combine_resident(asks, payloads, residents, heads_mine)
    cos, sin = rotation(slots, head_size)
    moved = attend_moved(
        here,
        mig_dest,
        mig_count,
        k_gain.reshape(1, head_size),
        cos,
        sin,
        pieces,
        payloads,
        asked,
        heads_mine,
        residents * (heads_mine + 3),
        feats * ranks,
    )
    moved = [shifted(moved, "inst", j, insts) for j in range(1, insts)]
    return finish(here, mig_dest, kept, moved)[None]


def solution(mesh):
    placed = (
        P(("group", "inst"), None, None, "tp"),
        P("group", None),
        P("group", None),
        P("tp"),
        P("tp", None),
        P(),
        P(("group", "inst"), None, None),
        P(("group", "inst"), None, None),
        P(("group", "inst"), None, "tp", None),
        P(("group", "inst"), None, "tp", None),
        P(("group", "inst"), None),
    )
    return jax.shard_map(
        per_device,
        mesh=mesh,
        in_specs=placed,
        out_specs=P(("group", "inst"), None, "tp"),
        check_vma=False,
    )
```

```python
import functools

import jax
import jax.numpy as jnp
import numpy as np
from jax import lax
from jax.experimental import pallas as pl
from jax.experimental.pallas import tpu as pltpu
from jax.sharding import PartitionSpec as P

EPS = 1e-06
THETA = 1000000.0
ABSENT = -1e30
F32 = jnp.float32
BF16 = jnp.bfloat16
MIB = 1024 * 1024

VMEM = pl.BlockSpec(memory_space=pltpu.VMEM)
SMEM = pl.BlockSpec(memory_space=pltpu.SMEM)
HBM = pl.BlockSpec(memory_space=pltpu.HBM)


def iota(shape, dim):
    return lax.broadcasted_iota(jnp.int32, shape, dim)


def column_to_row(column, period):
    n = column.shape[0]
    spread = jnp.where(iota((n, 128), 0) % period == iota((n, 128), 1), column, 0.0)
    return jnp.sum(spread.reshape(n // period, period, 128), axis=1)


def row_to_column(row, n):
    return jnp.sum(
        jnp.where(iota((n, 128), 0) == iota((n, 128), 1), row, 0.0), axis=1, keepdims=True
    )


def split_bf16(x):
    high = x.astype(BF16)
    return high, (x - high.astype(F32)).astype(BF16)


def project_kernel(ranks, group, rank_ref, gain_ref, x_hbm, w_hbm, *rest):
    outs, sq_ref = rest[:ranks], rest[ranks]
    x_ref, w_ref, xg_ref, x_sem, w_sems = rest[ranks + 1 :]
    slots, requests, feats = x_ref.shape
    piece = w_ref.shape[2] // 2
    kv_width = w_hbm.shape[1] // 2
    heads_mine = kv_width // 128 * group // ranks
    rank = rank_ref[0]
    x_copy = pltpu.make_async_copy(x_hbm, x_ref, x_sem)
    x_copy.start()
    copies = []
    for j in range(ranks):
        first = lax.rem(rank + j, ranks) * heads_mine // group * 128
        first = pl.multiple_of(first, 128)
        pair = (
            pltpu.make_async_copy(
                w_hbm.at[:, pl.ds(first, piece)], w_ref.at[j, :, :piece], w_sems.at[0, j]
            ),
            pltpu.make_async_copy(
                w_hbm.at[:, pl.ds(kv_width + first, piece)], w_ref.at[j, :, piece:], w_sems.at[1, j]
            ),
        )
        copies.append(pair)
        for copy in pair:
            copy.start()
    x_copy.wait()
    rows = slots * requests
    squares = jnp.zeros((rows, 128), F32)
    for c in range(0, feats, 128):
        width = min(128, feats - c)
        x = x_ref[:, :, c : c + width].astype(F32).reshape(rows, width)
        gain = gain_ref[c : c + width].astype(F32).reshape(1, width)
        xg_ref[:, c : c + width] = (x * gain).astype(BF16)
        x = x * x
        if width < 128:
            x = jnp.concatenate([x, jnp.zeros((rows, 128 - width), F32)], axis=1)
        squares = squares + x
    sq_ref[...] = column_to_row(jnp.sum(squares, axis=1, keepdims=True), 128)
    for j in range(ranks):
        for copy in copies[j]:
            copy.wait()
        outs[j][...] = jnp.dot(xg_ref[...], w_ref[j], preferred_element_type=F32).astype(BF16)


def project(rank, x, gain, weight, ranks, group, kv_mine):
    slots, requests, feats = x.shape
    rows = slots * requests
    piece = kv_mine * 128
    outs = pl.pallas_call(
        functools.partial(project_kernel, ranks, group),
        in_specs=[SMEM, VMEM, HBM, HBM],
        out_specs=[VMEM] * (ranks + 1),
        out_shape=[jax.ShapeDtypeStruct((rows, 2 * piece), BF16)] * ranks
        + [jax.ShapeDtypeStruct((rows // 128, 128), F32)],
        scratch_shapes=[
            pltpu.VMEM((slots, requests, feats), BF16),
            pltpu.VMEM((ranks, feats, 2 * piece), BF16),
            pltpu.VMEM((rows, feats), BF16),
            pltpu.SemaphoreType.DMA,
            pltpu.SemaphoreType.DMA((2, ranks)),
        ],
        compiler_params=pltpu.CompilerParams(vmem_limit_bytes=16 * MIB),
        cost_estimate=pl.CostEstimate(
            flops=4 * rows * feats * piece * ranks,
            bytes_accessed=4 * feats * piece * ranks,
            transcendentals=0,
        ),
        name="project",
    )(rank, gain, x, weight)
    return outs[:ranks], outs[ranks]


def resident_kernel(ranks, rank_ref, len_ref, q_ref, sq_ref, k_hbm, v_hbm, *rest):
    outs = rest[:ranks]
    k_buf, v_buf, o_all, s_all, sems = rest[ranks:]
    residents, positions, width = k_buf.shape
    copies = []
    for r in range(residents):
        copies.append(
            (
                pltpu.make_async_copy(k_hbm.at[r], k_buf.at[r], sems.at[0, r]),
                pltpu.make_async_copy(v_hbm.at[r], v_buf.at[r], sems.at[1, r]),
            )
        )
    for pair in copies:
        for copy in pair:
            copy.start()
    heads = q_ref.shape[1]
    kv_heads = width // 128
    group = heads // kv_heads
    pair_rows = 2 * group
    heads_mine = heads // ranks
    rank = rank_ref[0]
    top_half = iota((pair_rows, 128), 0) < group
    own_block = iota((heads, width), 0) // group == iota((heads, width), 1) // 128
    scale = F32(1.0) / jnp.sqrt(F32(128.0))
    for r in range(residents):
        wide = jnp.concatenate([q_ref[r]] * kv_heads, axis=1)
        wide = jnp.where(own_block, wide, jnp.zeros_like(wide))
        if heads < 128:
            wide = jnp.concatenate([wide, jnp.zeros((128 - heads, width), BF16)], axis=0)
        copies[r][0].wait()
        scores = lax.dot_general(
            k_buf[r], wide, (((1,), (1,)), ((), ())), preferred_element_type=F32
        )
        scores = jnp.transpose(scores)[:heads]
        valid = rank * positions + iota((heads, positions), 1) < len_ref[0, r]
        scores = jnp.where(valid, scores * scale, ABSENT)
        peak = jnp.max(scores, axis=1, keepdims=True).astype(BF16).astype(F32)
        weights = jnp.where(valid, jnp.exp(scores - peak), 0.0)
        high, low = split_bf16(jnp.sum(weights, axis=1, keepdims=True))
        s_all[r, 0] = column_to_row(peak, heads_mine)
        s_all[r, 1] = column_to_row(high.astype(F32), heads_mine)
        s_all[r, 2] = column_to_row(low.astype(F32), heads_mine)
        weights = weights.astype(BF16)
        copies[r][1].wait()
        for p in range(kv_heads // 2):
            rows = slice(p * pair_rows, (p + 1) * pair_rows)
            both = jnp.dot(
                weights[rows], v_buf[r, :, p * 256 : (p + 1) * 256], preferred_element_type=F32
            )
            o_all[r, rows, :] = jnp.where(top_half, both[:, :128], both[:, 128:])
    sq_high, sq_low = split_bf16(sq_ref[...])
    sq_rows = sq_ref.shape[0]
    filled = residents * (heads_mine + 3) + 2 * sq_rows
    for j in range(ranks):
        target = lax.rem(rank + j, ranks)
        first = pl.multiple_of(target * heads_mine, heads_mine)
        parts = [o_all[r, pl.ds(first, heads_mine), :] for r in range(residents)]
        parts += [s_all[r, i, pl.ds(target, 1), :] for i in range(3) for r in range(residents)]
        parts += [sq_high.astype(F32), sq_low.astype(F32)]
        if outs[j].shape[0] > filled:
            parts.append(jnp.zeros((outs[j].shape[0] - filled, 128), F32))
        outs[j][...] = jnp.concatenate(parts, axis=0).astype(BF16)


def attend_resident(rank, lengths, queries, squares, k_cache, v_cache, ranks):
    residents, positions, width = k_cache.shape
    heads = queries.shape[1]
    heads_mine = heads // ranks
    rows = -(-(residents * (heads_mine + 3) + 2 * squares.shape[0]) // 16) * 16
    return pl.pallas_call(
        functools.partial(resident_kernel, ranks),
        in_specs=[SMEM, SMEM, VMEM, VMEM, HBM, HBM],
        out_specs=[VMEM] * ranks,
        out_shape=[jax.ShapeDtypeStruct((rows, 128), BF16)] * ranks,
        scratch_shapes=[
            pltpu.VMEM((residents, positions, width), BF16),
            pltpu.VMEM((residents, positions, width), BF16),
            pltpu.VMEM((residents, heads, 128), F32),
            pltpu.VMEM((residents, 3, ranks, 128), F32),
            pltpu.SemaphoreType.DMA((2, residents)),
        ],
        compiler_params=pltpu.CompilerParams(vmem_limit_bytes=32 * MIB),
        cost_estimate=pl.CostEstimate(
            flops=4 * residents * heads * positions * 128,
            bytes_accessed=4 * residents * positions * width,
            transcendentals=residents * heads * positions,
        ),
        name="attend_resident",
    )(rank, lengths, queries, squares, k_cache, v_cache)


def expand(own, rows):
    per = rows // own.shape[0]
    which = iota((rows, 128), 0) // per
    out = jnp.broadcast_to(own[0:1], (rows, 128))
    for h in range(1, own.shape[0]):
        out = jnp.where(which == h, own[h : h + 1], out)
    return out


def moved_kernel(
    insts, ranks, features, at_sq, here_ref, dest_ref, count_ref, gain_ref, cos_ref, sin_ref, *rest
):
    pieces, rest = rest[:ranks], rest[ranks:]
    payloads, rest = rest[:ranks], rest[ranks:]
    asks, rest = rest[: insts - 1], rest[insts - 1 :]
    out_ref, q_ref, own_ref, line_ref = rest
    here = here_ref[0]
    requests = dest_ref.shape[0]
    tokens = pieces[0].shape[0]
    piece = pieces[0].shape[1] // 2
    kv_mine = piece // 128
    heads_mine = line_ref.shape[1] // 128
    rows = requests * heads_mine
    scale = F32(1.0) / jnp.sqrt(F32(128.0))
    gain = gain_ref[...].astype(F32)

    row_request = iota((rows, tokens), 0) // heads_mine
    limit = jnp.zeros((rows, tokens), jnp.int32)
    for r in range(requests):
        dest = dest_ref[r, here]
        limit = jnp.where(row_request == r, count_ref[r, here], limit)
        place = jnp.int32(0)
        for s in range(insts):
            for c in range(requests):
                place += jnp.where((dest_ref[c, s] == dest) & (here > s), 1, 0).astype(jnp.int32)
        shift = lax.rem(here - dest + insts, insts)
        for j in range(1, insts):

            @pl.when(shift == j)
            def _():
                ask = asks[j - 1][place].astype(F32)
                at = slice(r * heads_mine, (r + 1) * heads_mine)
                q_ref[at, :] = ask[:heads_mine]
                own_ref[0, at, :] = expand(ask[heads_mine : heads_mine + kv_mine], heads_mine)
                own_ref[1, at, :] = expand(
                    ask[heads_mine + kv_mine : heads_mine + 2 * kv_mine], heads_mine
                )

    squares = None
    blocks = tokens // 128
    for t in range(ranks):
        both = payloads[t][at_sq : at_sq + 2 * blocks, :].astype(F32)
        both = both[:blocks] + both[blocks:]
        squares = both if squares is None else squares + both
    squares = jnp.concatenate(
        [row_to_column(squares[b : b + 1], 128) for b in range(blocks)], axis=0
    )
    kv = pieces[0][...].astype(F32)
    for t in range(1, ranks):
        kv = kv + pieces[t][...].astype(F32)
    kv = kv * lax.rsqrt(squares / features + EPS)

    q = q_ref[...]
    q16 = q.astype(BF16)
    which = iota((rows, tokens), 0) % heads_mine // (heads_mine // kv_mine)
    scores = None
    for h in range(kv_mine):
        key = kv[:, h * 128 : (h + 1) * 128]
        key = key * lax.rsqrt(jnp.mean(key * key, axis=1, keepdims=True) + EPS) * gain
        key = key * cos_ref[...] + pltpu.roll(key, 64, 1) * sin_ref[...]
        part = lax.dot_general(
            q16, key.astype(BF16), (((1,), (1,)), ((), ())), preferred_element_type=F32
        )
        scores = part if scores is None else jnp.where(which == h, part, scores)
    token = iota((rows, tokens), 1)
    valid = (token % requests == row_request) & (token // requests < limit)
    scores = jnp.where(valid, scores * scale, ABSENT)
    own_score = jnp.sum(q * own_ref[0], axis=1, keepdims=True) * scale
    top = jnp.maximum(jnp.max(scores, axis=1, keepdims=True), own_score)
    weights = jnp.where(valid, jnp.exp(scores - top), 0.0)
    own_weight = jnp.exp(own_score - top)
    total = jnp.sum(weights, axis=1, keepdims=True) + own_weight
    weights = weights.astype(BF16)
    summed = None
    for h in range(kv_mine):
        value = kv[:, piece + h * 128 : piece + (h + 1) * 128].astype(BF16)
        part = jnp.dot(weights, value, preferred_element_type=F32)
        summed = part if summed is None else jnp.where(which[:, :128] == h, part, summed)
    summed = summed + own_weight.astype(BF16).astype(F32) * own_ref[1]
    result = summed / total
    for r in range(requests):
        for h in range(heads_mine):
            at = r * heads_mine + h
            line_ref[r : r + 1, h * 128 : (h + 1) * 128] = result[at : at + 1, :]
    out_ref[...] = line_ref[...].astype(BF16)


def attend_moved(here, dest, count, k_gain, cos, sin, pieces, payloads, asks, heads_mine, at_sq, features):
    requests = dest.shape[0]
    insts, ranks = len(asks) + 1, len(pieces)
    rows = requests * heads_mine
    return pl.pallas_call(
        functools.partial(moved_kernel, insts, ranks, features, at_sq),
        in_specs=[SMEM] * 3 + [VMEM] * (3 + 2 * ranks + insts - 1),
        out_specs=VMEM,
        out_shape=jax.ShapeDtypeStruct((requests, heads_mine * 128), BF16),
        scratch_shapes=[
            pltpu.VMEM((rows, 128), F32),
            pltpu.VMEM((2, rows, 128), F32),
            pltpu.VMEM((requests, heads_mine * 128), F32),
        ],
        compiler_params=pltpu.CompilerParams(vmem_limit_bytes=16 * MIB),
        name="attend_moved",
    )(here, dest, count, k_gain, cos, sin, *pieces, *payloads, *asks)


def combine_kernel(ranks, residents, ask_ref, *rest):
    payloads = rest[:ranks]
    out_ref, line_ref = rest[ranks:]
    heads_mine = line_ref.shape[1] // 128
    kv_mine = (ask_ref.shape[1] - heads_mine) // 2
    scale = F32(1.0) / jnp.sqrt(F32(128.0))
    at = residents * heads_mine
    for r in range(residents):
        q = ask_ref[r, :heads_mine, :].astype(F32)
        own_k = expand(ask_ref[r, heads_mine : heads_mine + kv_mine, :].astype(F32), heads_mine)
        own_v = expand(
            ask_ref[r, heads_mine + kv_mine : heads_mine + 2 * kv_mine, :].astype(F32), heads_mine
        )
        own_score = jnp.sum(q * own_k, axis=1, keepdims=True) * scale
        peaks, totals = [], []
        for t in range(ranks):
            stat = payloads[t][at : at + 3 * residents, :].astype(F32)
            peaks.append(row_to_column(stat[r : r + 1], heads_mine))
            total = stat[residents + r : residents + r + 1]
            total = total + stat[2 * residents + r : 2 * residents + r + 1]
            totals.append(row_to_column(total, heads_mine))
        top = own_score
        for t in range(ranks):
            top = jnp.maximum(top, peaks[t])
        own_weight = jnp.exp(own_score - top)
        denom = own_weight
        numer = own_weight.astype(BF16).astype(F32) * own_v
        for t in range(ranks):
            keep = jnp.exp(peaks[t] - top)
            denom = denom + keep * totals[t]
            numer = numer + keep * payloads[t][r * heads_mine : (r + 1) * heads_mine, :].astype(F32)
        result = numer / denom
        for h in range(heads_mine):
            line_ref[r : r + 1, h * 128 : (h + 1) * 128] = result[h : h + 1, :]
    out_ref[...] = line_ref[...].astype(BF16)


def combine_resident(asks, payloads, residents, heads_mine):
    return pl.pallas_call(
        functools.partial(combine_kernel, len(payloads), residents),
        in_specs=[VMEM] * (1 + len(payloads)),
        out_specs=VMEM,
        out_shape=jax.ShapeDtypeStruct((residents, heads_mine * 128), BF16),
        scratch_shapes=[pltpu.VMEM((residents, heads_mine * 128), F32)],
        compiler_params=pltpu.CompilerParams(vmem_limit_bytes=8 * MIB),
        name="combine_resident",
    )(asks, *payloads)


def finish_kernel(insts, here_ref, dest_ref, kept_ref, *rest):
    moved = rest[: insts - 1]
    out_ref, line_ref = rest[insts - 1 :]
    residents = kept_ref.shape[0]
    requests = dest_ref.shape[0]
    here = here_ref[0]
    line_ref[:residents, :] = kept_ref[...].astype(F32)
    place = jnp.int32(residents)
    for s in range(insts):
        for c in range(requests):
            mine = dest_ref[c, s] == here
            shift = lax.rem(here - s + insts, insts)
            for j in range(1, insts):

                @pl.when(mine & (shift == j))
                def _():
                    line_ref[pl.ds(place, 1), :] = moved[j - 1][c : c + 1, :].astype(F32)

            place += jnp.where(mine, 1, 0).astype(jnp.int32)
    out_ref[...] = line_ref[...].astype(BF16)


def finish(here, dest, kept, moved):
    residents, width = kept.shape
    rows = residents + dest.shape[0]
    return pl.pallas_call(
        functools.partial(finish_kernel, len(moved) + 1),
        in_specs=[SMEM, SMEM, VMEM] + [VMEM] * len(moved),
        out_specs=VMEM,
        out_shape=jax.ShapeDtypeStruct((rows, width), BF16),
        scratch_shapes=[pltpu.VMEM((rows, width), F32)],
        compiler_params=pltpu.CompilerParams(vmem_limit_bytes=8 * MIB),
        name="finish",
    )(here, dest, kept, *moved)


def shifted(x, axis, j, n):
    return lax.ppermute(x, axis, [(i, (i + j) % n) for i in range(n)])


def rotation(slots, requests, head_size):
    half = head_size // 2
    freq = THETA ** (-np.arange(half) * 2.0 / head_size)
    angle = np.repeat(np.arange(slots), requests)[:, None] * freq[None, :]
    cos, sin = np.cos(angle), np.sin(angle)
    return (
        np.concatenate([cos, cos], axis=1).astype(np.float32),
        np.concatenate([-sin, sin], axis=1).astype(np.float32),
    )


def per_device(
    mig_hidden,
    mig_dest,
    mig_count,
    attn_gain,
    kv_weight,
    k_gain,
    query,
    new_kv,
    k_cache,
    v_cache,
    lengths,
):
    insts = lax.axis_size("inst")
    ranks = lax.axis_size("tp")
    here = lax.axis_index("inst").astype(jnp.int32).reshape(1)
    rank = lax.axis_index("tp").astype(jnp.int32).reshape(1)
    head_size = k_gain.shape[0]
    slots, requests, feats = mig_hidden.shape[1:]
    residents = k_cache.shape[1]
    decoded = query.shape[1]
    heads = query.shape[2] // head_size
    kv_heads = kv_weight.shape[1] // 2 // head_size
    heads_mine = heads // ranks
    group = heads // kv_heads
    kv_mine = max(1, heads_mine // group)

    queries = query[0].reshape(decoded, heads, head_size)
    own = new_kv[0].reshape(decoded, 2, kv_heads, head_size)
    my_queries = lax.dynamic_slice_in_dim(queries, rank[0] * heads_mine, heads_mine, 1)
    my_own = lax.dynamic_slice_in_dim(own, rank[0] * heads_mine // group, kv_mine, 2)
    asks = jnp.concatenate(
        [my_queries, my_own.reshape(decoded, 2 * kv_mine, head_size)], axis=1
    )
    asked = [shifted(asks[residents:], "inst", j, insts) for j in range(1, insts)]

    pieces, squares = project(
        rank, mig_hidden[0], attn_gain, kv_weight, ranks, group, kv_mine
    )
    pieces = [pieces[0]] + [shifted(pieces[j], "tp", j, ranks) for j in range(1, ranks)]
    payloads = attend_resident(rank, lengths, queries, squares, k_cache[0], v_cache[0], ranks)
    payloads = [payloads[0]] + [shifted(payloads[j], "tp", j, ranks) for j in range(1, ranks)]
    kept = combine_resident(asks, payloads, residents, heads_mine)
    dest, count = mig_dest.T, mig_count.T
    cos, sin = rotation(slots, requests, head_size)
    moved = attend_moved(
        here,
        dest,
        count,
        k_gain.reshape(1, head_size),
        cos,
        sin,
        pieces,
        payloads,
        asked,
        heads_mine,
        residents * (heads_mine + 3),
        feats * ranks,
    )
    moved = [shifted(moved, "inst", j, insts) for j in range(1, insts)]
    return finish(here, dest, kept, moved)[None]


def solution(mesh):
    placed = (
        P(("group", "inst"), None, None, "tp"),
        P("group", None),
        P("group", None),
        P("tp"),
        P("tp", None),
        P(),
        P(("group", "inst"), None, None),
        P(("group", "inst"), None, None),
        P(("group", "inst"), None, "tp", None),
        P(("group", "inst"), None, "tp", None),
        P(("group", "inst"), None),
    )
    return jax.shard_map(
        per_device,
        mesh=mesh,
        in_specs=placed,
        out_specs=P(("group", "inst"), None, "tp"),
        check_vma=False,
    )
```

```python
import functools

import jax
import jax.numpy as jnp
import numpy as np
from jax import lax
from jax.experimental import pallas as pl
from jax.experimental.pallas import tpu as pltpu
from jax.sharding import PartitionSpec as P

EPS = 1e-06
THETA = 1000000.0
ABSENT = -1e30
F32 = jnp.float32
BF16 = jnp.bfloat16
MIB = 1024 * 1024

VMEM = pl.BlockSpec(memory_space=pltpu.VMEM)
SMEM = pl.BlockSpec(memory_space=pltpu.SMEM)
HBM = pl.BlockSpec(memory_space=pltpu.HBM)


def iota(shape, dim):
    return lax.broadcasted_iota(jnp.int32, shape, dim)


def column_to_row(column, period):
    n = column.shape[0]
    spread = jnp.where(iota((n, 128), 0) % period == iota((n, 128), 1), column, 0.0)
    return jnp.sum(spread.reshape(n // period, period, 128), axis=1)


def row_to_column(row, n):
    return jnp.sum(
        jnp.where(iota((n, 128), 0) == iota((n, 128), 1), row, 0.0), axis=1, keepdims=True
    )


def split_bf16(x):
    high = x.astype(BF16)
    return high, (x - high.astype(F32)).astype(BF16)


def project_kernel(ranks, group, gain_hbm, x_hbm, w_hbm, *rest):
    outs, sq_ref = rest[:ranks], rest[ranks]
    gain_ref, x_ref, w_ref, xg_ref, in_sems, w_sems = rest[ranks + 1 :]
    slots, requests, feats = x_ref.shape
    piece = w_ref.shape[2] // 2
    kv_width = w_hbm.shape[1] // 2
    heads_mine = kv_width // 128 * group // ranks
    rank = lax.axis_index("tp")
    gain_copy = pltpu.make_async_copy(gain_hbm, gain_ref, in_sems.at[0])
    gain_copy.start()
    x_copy = pltpu.make_async_copy(x_hbm, x_ref, in_sems.at[1])
    x_copy.start()
    copies = []
    for j in range(ranks):
        first = lax.rem(rank + j, ranks) * heads_mine // group * 128
        first = pl.multiple_of(first, 128)
        pair = (
            pltpu.make_async_copy(
                w_hbm.at[:, pl.ds(first, piece)], w_ref.at[j, :, :piece], w_sems.at[0, j]
            ),
            pltpu.make_async_copy(
                w_hbm.at[:, pl.ds(kv_width + first, piece)], w_ref.at[j, :, piece:], w_sems.at[1, j]
            ),
        )
        copies.append(pair)
        for copy in pair:
            copy.start()
    gain_copy.wait()
    x_copy.wait()
    rows = slots * requests
    squares = jnp.zeros((rows, 128), F32)
    for c in range(0, feats, 128):
        width = min(128, feats - c)
        x = x_ref[:, :, c : c + width].astype(F32).reshape(rows, width)
        gain = gain_ref[c : c + width].astype(F32).reshape(1, width)
        xg_ref[:, c : c + width] = (x * gain).astype(BF16)
        x = x * x
        if width < 128:
            x = jnp.concatenate([x, jnp.zeros((rows, 128 - width), F32)], axis=1)
        squares = squares + x
    sq_ref[...] = column_to_row(jnp.sum(squares, axis=1, keepdims=True), 128)
    for j in list(range(1, ranks)) + [0]:
        for copy in copies[j]:
            copy.wait()
        outs[j][...] = jnp.dot(xg_ref[...], w_ref[j], preferred_element_type=F32).astype(BF16)


def project(x, gain, weight, ranks, group, kv_mine):
    slots, requests, feats = x.shape
    rows = slots * requests
    piece = kv_mine * 128
    outs = pl.pallas_call(
        functools.partial(project_kernel, ranks, group),
        in_specs=[HBM, HBM, HBM],
        out_specs=[VMEM] * (ranks + 1),
        out_shape=[jax.ShapeDtypeStruct((rows, 2 * piece), BF16)] * ranks
        + [jax.ShapeDtypeStruct((rows // 128, 128), F32)],
        scratch_shapes=[
            pltpu.VMEM((feats,), BF16),
            pltpu.VMEM((slots, requests, feats), BF16),
            pltpu.VMEM((ranks, feats, 2 * piece), BF16),
            pltpu.VMEM((rows, feats), BF16),
            pltpu.SemaphoreType.DMA((2,)),
            pltpu.SemaphoreType.DMA((2, ranks)),
        ],
        compiler_params=pltpu.CompilerParams(vmem_limit_bytes=55889100),
        cost_estimate=pl.CostEstimate(
            flops=4 * rows * feats * piece * ranks,
            bytes_accessed=4 * feats * piece * ranks,
            transcendentals=0,
        ),
        name="project",
    )(gain, x, weight)
    return outs[:ranks], outs[ranks]


def resident_kernel(ranks, valid_ref, q_ref, sq_ref, k_hbm, v_hbm, *rest):
    outs = rest[:ranks]
    k_buf, v_buf, o_all, s_all, sems = rest[ranks:]
    residents, positions, width = k_buf.shape
    copies = []
    for r in range(residents):
        copies.append(
            (
                pltpu.make_async_copy(k_hbm.at[r], k_buf.at[r], sems.at[0, r]),
                pltpu.make_async_copy(
                    v_hbm.at[r, :, : width // 2], v_buf.at[r, :, : width // 2], sems.at[1, r]
                ),
                pltpu.make_async_copy(
                    v_hbm.at[r, :, width // 2 :], v_buf.at[r, :, width // 2 :], sems.at[2, r]
                ),
            )
        )
    for trio in copies:
        for copy in trio:
            copy.start()
    heads = q_ref.shape[1]
    kv_heads = width // 128
    group = heads // kv_heads
    pair_rows = 2 * group
    heads_mine = heads // ranks
    rank = lax.axis_index("tp")
    top_half = iota((pair_rows, 128), 0) < group
    own_block = iota((heads, width), 0) // group == iota((heads, width), 1) // 128
    scale = F32(1.0) / jnp.sqrt(F32(128.0))
    for r in range(residents):
        wide = jnp.concatenate([q_ref[r]] * kv_heads, axis=1)
        wide = jnp.where(own_block, wide, jnp.zeros_like(wide))
        if heads < 128:
            wide = jnp.concatenate([wide, jnp.zeros((128 - heads, width), BF16)], axis=0)
        copies[r][0].wait()
        scores = lax.dot_general(
            k_buf[r], wide, (((1,), (1,)), ((), ())), preferred_element_type=F32
        )
        scores = jnp.transpose(scores)[:heads]
        valid = iota((heads, positions), 1) < valid_ref[r]
        scores = jnp.where(valid, scores * scale, ABSENT)
        peak = jnp.max(scores, axis=1, keepdims=True).astype(BF16).astype(F32)
        weights = jnp.where(valid, jnp.exp(scores - peak), 0.0)
        high, low = split_bf16(jnp.sum(weights, axis=1, keepdims=True))
        s_all[r, 0] = column_to_row(peak, heads_mine)
        s_all[r, 1] = column_to_row(high.astype(F32), heads_mine)
        s_all[r, 2] = column_to_row(low.astype(F32), heads_mine)
        weights = weights.astype(BF16)
        for p in range(kv_heads // 2):
            if p * 4 % kv_heads == 0:
                copies[r][1 + p * 4 // kv_heads].wait()
            rows = slice(p * pair_rows, (p + 1) * pair_rows)
            both = jnp.dot(
                weights[rows], v_buf[r, :, p * 256 : (p + 1) * 256], preferred_element_type=F32
            )
            o_all[r, rows, :] = jnp.where(top_half, both[:, :128], both[:, 128:])
    sq_high, sq_low = split_bf16(sq_ref[...])
    sq_rows = sq_ref.shape[0]
    filled = residents * (heads_mine + 3) + 2 * sq_rows
    for j in range(ranks):
        target = lax.rem(rank + j, ranks)
        first = pl.multiple_of(target * heads_mine, heads_mine)
        parts = [o_all[r, pl.ds(first, heads_mine), :] for r in range(residents)]
        parts += [s_all[r, i, pl.ds(target, 1), :] for i in range(3) for r in range(residents)]
        parts += [sq_high.astype(F32), sq_low.astype(F32)]
        if outs[j].shape[0] > filled:
            parts.append(jnp.zeros((outs[j].shape[0] - filled, 128), F32))
        outs[j][...] = jnp.concatenate(parts, axis=0).astype(BF16)


def attend_resident(valid, queries, squares, k_cache, v_cache, ranks):
    residents, positions, width = k_cache.shape
    heads = queries.shape[1]
    heads_mine = heads // ranks
    rows = -(-(residents * (heads_mine + 3) + 2 * squares.shape[0]) // 16) * 16
    return pl.pallas_call(
        functools.partial(resident_kernel, ranks),
        in_specs=[SMEM, VMEM, VMEM, HBM, HBM],
        out_specs=[VMEM] * ranks,
        out_shape=[jax.ShapeDtypeStruct((rows, 128), BF16)] * ranks,
        scratch_shapes=[
            pltpu.VMEM((residents, positions, width), BF16),
            pltpu.VMEM((residents, positions, width), BF16),
            pltpu.VMEM((residents, heads, 128), F32),
            pltpu.VMEM((residents, 3, ranks, 128), F32),
            pltpu.SemaphoreType.DMA((3, residents)),
        ],
        compiler_params=pltpu.CompilerParams(vmem_limit_bytes=52 * MIB),
        cost_estimate=pl.CostEstimate(
            flops=4 * residents * heads * positions * 128,
            bytes_accessed=4 * residents * positions * width,
            transcendentals=residents * heads * positions,
        ),
        name="attend_resident",
    )(valid, queries, squares, k_cache, v_cache)


def expand(own, rows):
    per = rows // own.shape[0]
    which = iota((rows, 128), 0) // per
    out = jnp.broadcast_to(own[0:1], (rows, 128))
    for h in range(1, own.shape[0]):
        out = jnp.where(which == h, own[h : h + 1], out)
    return out


def moved_kernel(
    insts, ranks, features, at_sq, here_ref, dest_ref, count_ref, gain_ref, cos_ref, sin_ref, *rest
):
    pieces, rest = rest[:ranks], rest[ranks:]
    payloads, rest = rest[:ranks], rest[ranks:]
    asks, out_ref, q_ref, own_ref, line_ref = rest
    here = here_ref[0]
    requests = dest_ref.shape[0]
    tokens = pieces[0].shape[0]
    piece = pieces[0].shape[1] // 2
    kv_mine = piece // 128
    heads_mine = line_ref.shape[1] // 128
    rows = requests * heads_mine
    scale = F32(1.0) / jnp.sqrt(F32(128.0))
    gain = gain_ref[...].astype(F32)

    row_request = iota((rows, tokens), 0) // heads_mine
    limit = jnp.zeros((rows, tokens), jnp.int32)
    for r in range(requests):
        dest = dest_ref[r, here]
        limit = jnp.where(row_request == r, count_ref[r, here], limit)
        place = jnp.int32(0)
        for s in range(insts):
            for c in range(requests):
                place += jnp.where((dest_ref[c, s] == dest) & (here > s), 1, 0).astype(jnp.int32)
        ask = asks[dest, place].astype(F32)
        at = slice(r * heads_mine, (r + 1) * heads_mine)
        q_ref[at, :] = ask[:heads_mine]
        own_ref[0, at, :] = expand(ask[heads_mine : heads_mine + kv_mine], heads_mine)
        own_ref[1, at, :] = expand(ask[heads_mine + kv_mine : heads_mine + 2 * kv_mine], heads_mine)

    squares = None
    blocks = tokens // 128
    for t in range(ranks):
        both = payloads[t][at_sq : at_sq + 2 * blocks, :].astype(F32)
        both = both[:blocks] + both[blocks:]
        squares = both if squares is None else squares + both
    squares = jnp.concatenate(
        [row_to_column(squares[b : b + 1], 128) for b in range(blocks)], axis=0
    )
    kv = pieces[0][...].astype(F32)
    for t in range(1, ranks):
        kv = kv + pieces[t][...].astype(F32)
    kv = kv * lax.rsqrt(squares / features + EPS)

    q = q_ref[...]
    q16 = q.astype(BF16)
    which = iota((rows, tokens), 0) % heads_mine // (heads_mine // kv_mine)
    scores = None
    for h in range(kv_mine):
        key = kv[:, h * 128 : (h + 1) * 128]
        key = key * lax.rsqrt(jnp.mean(key * key, axis=1, keepdims=True) + EPS) * gain
        key = key * cos_ref[...] + pltpu.roll(key, 64, 1) * sin_ref[...]
        part = lax.dot_general(
            q16, key.astype(BF16), (((1,), (1,)), ((), ())), preferred_element_type=F32
        )
        scores = part if scores is None else jnp.where(which == h, part, scores)
    token = iota((rows, tokens), 1)
    valid = (token % requests == row_request) & (token // requests < limit)
    scores = jnp.where(valid, scores * scale, ABSENT)
    own_score = jnp.sum(q * own_ref[0], axis=1, keepdims=True) * scale
    top = jnp.maximum(jnp.max(scores, axis=1, keepdims=True), own_score)
    weights = jnp.where(valid, jnp.exp(scores - top), 0.0)
    own_weight = jnp.exp(own_score - top)
    total = jnp.sum(weights, axis=1, keepdims=True) + own_weight
    weights = weights.astype(BF16)
    summed = None
    for h in range(kv_mine):
        value = kv[:, piece + h * 128 : piece + (h + 1) * 128].astype(BF16)
        part = jnp.dot(weights, value, preferred_element_type=F32)
        summed = part if summed is None else jnp.where(which[:, :128] == h, part, summed)
    summed = summed + own_weight.astype(BF16).astype(F32) * own_ref[1]
    result = summed / total
    for r in range(requests):
        for h in range(heads_mine):
            at = r * heads_mine + h
            line_ref[r : r + 1, h * 128 : (h + 1) * 128] = result[at : at + 1, :]
    out_ref[...] = line_ref[...].astype(BF16)


def attend_moved(here, dest, count, k_gain, cos, sin, pieces, payloads, asks, heads_mine, at_sq, features):
    requests = dest.shape[0]
    insts, ranks = asks.shape[0], len(pieces)
    rows = requests * heads_mine
    return pl.pallas_call(
        functools.partial(moved_kernel, insts, ranks, features, at_sq),
        in_specs=[SMEM] * 3 + [VMEM] * (4 + 2 * ranks),
        out_specs=VMEM,
        out_shape=jax.ShapeDtypeStruct((requests, heads_mine * 128), BF16),
        scratch_shapes=[
            pltpu.VMEM((rows, 128), F32),
            pltpu.VMEM((2, rows, 128), F32),
            pltpu.VMEM((requests, heads_mine * 128), F32),
        ],
        compiler_params=pltpu.CompilerParams(vmem_limit_bytes=16 * MIB),
        name="attend_moved",
    )(here, dest, count, k_gain, cos, sin, *pieces, *payloads, asks)


def combine_kernel(ranks, residents, ask_ref, *rest):
    payloads = rest[:ranks]
    out_ref, line_ref = rest[ranks:]
    heads_mine = line_ref.shape[1] // 128
    kv_mine = (ask_ref.shape[1] - heads_mine) // 2
    scale = F32(1.0) / jnp.sqrt(F32(128.0))
    at = residents * heads_mine
    for r in range(residents):
        q = ask_ref[r, :heads_mine, :].astype(F32)
        own_k = expand(ask_ref[r, heads_mine : heads_mine + kv_mine, :].astype(F32), heads_mine)
        own_v = expand(
            ask_ref[r, heads_mine + kv_mine : heads_mine + 2 * kv_mine, :].astype(F32), heads_mine
        )
        own_score = jnp.sum(q * own_k, axis=1, keepdims=True) * scale
        peaks, totals = [], []
        for t in range(ranks):
            stat = payloads[t][at : at + 3 * residents, :].astype(F32)
            peaks.append(row_to_column(stat[r : r + 1], heads_mine))
            total = stat[residents + r : residents + r + 1]
            total = total + stat[2 * residents + r : 2 * residents + r + 1]
            totals.append(row_to_column(total, heads_mine))
        top = own_score
        for t in range(ranks):
            top = jnp.maximum(top, peaks[t])
        own_weight = jnp.exp(own_score - top)
        denom = own_weight
        numer = own_weight.astype(BF16).astype(F32) * own_v
        for t in range(ranks):
            keep = jnp.exp(peaks[t] - top)
            denom = denom + keep * totals[t]
            numer = numer + keep * payloads[t][r * heads_mine : (r + 1) * heads_mine, :].astype(F32)
        result = numer / denom
        for h in range(heads_mine):
            line_ref[r : r + 1, h * 128 : (h + 1) * 128] = result[h : h + 1, :]
    out_ref[...] = line_ref[...].astype(BF16)


def combine_resident(asks, payloads, residents, heads_mine):
    return pl.pallas_call(
        functools.partial(combine_kernel, len(payloads), residents),
        in_specs=[VMEM] * (1 + len(payloads)),
        out_specs=VMEM,
        out_shape=jax.ShapeDtypeStruct((residents, heads_mine * 128), BF16),
        scratch_shapes=[pltpu.VMEM((residents, heads_mine * 128), F32)],
        compiler_params=pltpu.CompilerParams(vmem_limit_bytes=8 * MIB),
        name="combine_resident",
    )(asks, *payloads)


def finish_kernel(insts, here_ref, dest_ref, kept_ref, *rest):
    moved = rest[: insts - 1]
    out_ref, line_ref = rest[insts - 1 :]
    residents = kept_ref.shape[0]
    requests = dest_ref.shape[0]
    here = here_ref[0]
    line_ref[:residents, :] = kept_ref[...].astype(F32)
    place = jnp.int32(residents)
    for s in range(insts):
        for c in range(requests):
            mine = dest_ref[c, s] == here
            shift = lax.rem(here - s + insts, insts)
            for j in range(1, insts):

                @pl.when(mine & (shift == j))
                def _():
                    line_ref[pl.ds(place, 1), :] = moved[j - 1][c : c + 1, :].astype(F32)

            place += jnp.where(mine, 1, 0).astype(jnp.int32)
    out_ref[...] = line_ref[...].astype(BF16)


def finish(here, dest, kept, moved):
    residents, width = kept.shape
    rows = residents + dest.shape[0]
    return pl.pallas_call(
        functools.partial(finish_kernel, len(moved) + 1),
        in_specs=[SMEM, SMEM, VMEM] + [VMEM] * len(moved),
        out_specs=VMEM,
        out_shape=jax.ShapeDtypeStruct((rows, width), BF16),
        scratch_shapes=[pltpu.VMEM((rows, width), F32)],
        compiler_params=pltpu.CompilerParams(vmem_limit_bytes=8 * MIB),
        name="finish",
    )(here, dest, kept, *moved)


def shifted(x, axis, j, n):
    return lax.ppermute(x, axis, [(i, (i + j) % n) for i in range(n)])


def rotation(slots, requests, head_size):
    half = head_size // 2
    freq = THETA ** (-np.arange(half) * 2.0 / head_size)
    angle = np.repeat(np.arange(slots), requests)[:, None] * freq[None, :]
    cos, sin = np.cos(angle), np.sin(angle)
    return (
        np.concatenate([cos, cos], axis=1).astype(np.float32),
        np.concatenate([-sin, sin], axis=1).astype(np.float32),
    )


def per_device(
    mig_hidden,
    mig_dest,
    mig_count,
    attn_gain,
    kv_weight,
    k_gain,
    query,
    new_kv,
    k_cache,
    v_cache,
    lengths,
):
    insts = lax.axis_size("inst")
    ranks = lax.axis_size("tp")
    here = lax.axis_index("inst").astype(jnp.int32).reshape(1)
    rank = lax.axis_index("tp")
    head_size = k_gain.shape[0]
    slots, requests, feats = mig_hidden.shape[1:]
    residents = k_cache.shape[1]
    decoded = query.shape[1]
    heads = query.shape[2] // head_size
    kv_heads = kv_weight.shape[1] // 2 // head_size
    heads_mine = heads // ranks
    group = heads // kv_heads
    kv_mine = max(1, heads_mine // group)

    queries = query[0].reshape(decoded, heads, head_size)
    own = new_kv[0].reshape(decoded, 2, kv_heads, head_size)
    my_queries = lax.dynamic_slice_in_dim(queries, rank * heads_mine, heads_mine, 1)
    my_own = lax.dynamic_slice_in_dim(own, rank * heads_mine // group, kv_mine, 2)
    asks = jnp.concatenate(
        [my_queries, my_own.reshape(decoded, 2 * kv_mine, head_size)], axis=1
    )
    asked = jnp.broadcast_to(asks[residents:], (insts,) + asks[residents:].shape)
    asked = lax.all_to_all(asked, "inst", 0, 0, tiled=True)

    pieces, squares = project(
        mig_hidden[0], attn_gain, kv_weight, ranks, group, kv_mine
    )
    pieces = [pieces[0]] + [shifted(pieces[j], "tp", j, ranks) for j in range(1, ranks)]
    valid = lengths[0] - rank * k_cache.shape[2]
    payloads = attend_resident(valid, queries, squares, k_cache[0], v_cache[0], ranks)
    payloads = [payloads[0]] + [shifted(payloads[j], "tp", j, ranks) for j in range(1, ranks)]
    kept = combine_resident(asks, payloads, residents, heads_mine)
    dest, count = mig_dest.T, mig_count.T
    cos, sin = rotation(slots, requests, head_size)
    moved = attend_moved(
        here,
        dest,
        count,
        k_gain.reshape(1, head_size),
        cos,
        sin,
        pieces,
        payloads,
        asked,
        heads_mine,
        residents * (heads_mine + 3),
        feats * ranks,
    )
    moved = [shifted(moved, "inst", j, insts) for j in range(1, insts)]
    return finish(here, dest, kept, moved)[None]


def solution(mesh):
    placed = (
        P(("group", "inst"), None, None, "tp"),
        P("group", None),
        P("group", None),
        P("tp"),
        P("tp", None),
        P(),
        P(("group", "inst"), None, None),
        P(("group", "inst"), None, None),
        P(("group", "inst"), None, "tp", None),
        P(("group", "inst"), None, "tp", None),
        P(("group", "inst"), None),
    )
    return jax.shard_map(
        per_device,
        mesh=mesh,
        in_specs=placed,
        out_specs=P(("group", "inst"), None, "tp"),
        check_vma=False,
    )
```

```python
import functools

import jax
import jax.numpy as jnp
import numpy as np
from jax import lax
from jax.experimental import pallas as pl
from jax.experimental.pallas import tpu as pltpu
from jax.sharding import PartitionSpec as P

EPS = 1e-06
THETA = 1000000.0
ABSENT = -1e30
F32 = jnp.float32
BF16 = jnp.bfloat16
MIB = 1024 * 1024
CHUNK = 256

VMEM = pl.BlockSpec(memory_space=pltpu.VMEM)
SMEM = pl.BlockSpec(memory_space=pltpu.SMEM)
HBM = pl.BlockSpec(memory_space=pltpu.HBM)


def iota(shape, dim):
    return lax.broadcasted_iota(jnp.int32, shape, dim)


def column_to_row(column, period):
    n = column.shape[0]
    spread = jnp.where(iota((n, 128), 0) % period == iota((n, 128), 1), column, 0.0)
    return jnp.sum(spread.reshape(n // period, period, 128), axis=1)


def row_to_column(row, n):
    return jnp.sum(
        jnp.where(iota((n, 128), 0) == iota((n, 128), 1), row, 0.0), axis=1, keepdims=True
    )


def split_bf16(x):
    high = x.astype(BF16)
    return high, (x - high.astype(F32)).astype(BF16)


def project_kernel(ranks, group, gain_hbm, x_hbm, w_hbm, q_hbm, own_hbm, *rest):
    outs, ask_ref = rest[:ranks], rest[ranks]
    gain_ref, x_ref, w_ref, acc_ref, in_sems, w_sems = rest[ranks + 1 :]
    slots, requests, feats = x_ref.shape
    rows = slots * requests
    piece = outs[0].shape[1] // 2
    kv_width = w_hbm.shape[1] // 2
    heads_mine = kv_width // 128 * group // ranks
    rank = lax.axis_index("tp")

    def first_column(target):
        return pl.multiple_of(target * heads_mine // group * 128, 128)

    gain_copy = pltpu.make_async_copy(gain_hbm, gain_ref, in_sems.at[0])
    gain_copy.start()
    x_copy = pltpu.make_async_copy(x_hbm, x_ref, in_sems.at[1])
    x_copy.start()
    cuts = list(range(0, feats, CHUNK)) + [feats]
    chunks = list(zip(cuts[:-1], cuts[1:]))
    copies = []
    for i, (low, high) in enumerate(chunks):
        copies.append(
            pltpu.make_async_copy(
                w_hbm.at[low:high, :], w_ref.at[low:high, :], w_sems.at[i]
            )
        )
        copies[-1].start()
    mine = heads_mine * 128
    q_first = pl.multiple_of(rank * mine, 128)
    asking = [
        pltpu.make_async_copy(
            q_hbm.at[:, pl.ds(q_first, mine)], ask_ref.at[:, :mine], in_sems.at[2]
        )
    ]
    for i in range(2):
        asking.append(
            pltpu.make_async_copy(
                own_hbm.at[:, pl.ds(i * kv_width + first_column(rank), piece)],
                ask_ref.at[:, mine + i * piece : mine + (i + 1) * piece],
                in_sems.at[3 + i],
            )
        )
    for copy in asking:
        copy.start()
    gain_copy.wait()
    x_copy.wait()
    squares = jnp.zeros((rows, 128), F32)
    for i, (low, high) in enumerate(chunks):
        parts = []
        for c in range(low, high, 128):
            width = min(128, high - c)
            x = x_ref[:, :, c : c + width].astype(F32).reshape(rows, width)
            gain = gain_ref[c : c + width].astype(F32).reshape(1, width)
            parts.append((x * gain).astype(BF16))
            x = x * x
            if width < 128:
                x = jnp.concatenate([x, jnp.zeros((rows, 128 - width), F32)], axis=1)
            squares = squares + x
        xg = parts[0] if len(parts) == 1 else jnp.concatenate(parts, axis=1)
        copies[i].wait()
        for n in range(0, 2 * kv_width, 512):
            part = jnp.dot(xg, w_ref[low:high, n : n + 512], preferred_element_type=F32)
            if i == 0:
                acc_ref[:, n : n + 512] = part
            else:
                acc_ref[:, n : n + 512] += part
    sq = column_to_row(jnp.sum(squares, axis=1, keepdims=True), 128)
    high, low = split_bf16(sq)
    tail = jnp.concatenate([high.astype(F32), low.astype(F32)], axis=0)
    if outs[0].shape[0] - rows > tail.shape[0]:
        fill = outs[0].shape[0] - rows - tail.shape[0]
        tail = jnp.concatenate([tail, jnp.zeros((fill, 128), F32)], axis=0)
    extra = jnp.concatenate([tail.astype(BF16)] * (2 * piece // 128), axis=1)
    for j in range(ranks):
        first = first_column(rank ^ j)
        outs[j][:rows, :piece] = acc_ref[:, pl.ds(first, piece)].astype(BF16)
        outs[j][:rows, piece:] = acc_ref[:, pl.ds(kv_width + first, piece)].astype(BF16)
        outs[j][rows:, :] = extra
    for copy in asking:
        copy.wait()


def project(x, gain, weight, query, own, ranks, group, kv_mine):
    slots, requests, feats = x.shape
    rows = slots * requests
    piece = kv_mine * 128
    extra = -(-2 * (rows // 128) // 8) * 8
    decoded, q_width = query.shape
    outs = pl.pallas_call(
        functools.partial(project_kernel, ranks, group),
        in_specs=[HBM] * 5,
        out_specs=[VMEM] * (ranks + 1),
        out_shape=[jax.ShapeDtypeStruct((rows + extra, 2 * piece), BF16)] * ranks
        + [jax.ShapeDtypeStruct((decoded, q_width // ranks + 2 * piece), BF16)],
        scratch_shapes=[
            pltpu.VMEM((feats,), BF16),
            pltpu.VMEM((slots, requests, feats), BF16),
            pltpu.VMEM(weight.shape, BF16),
            pltpu.VMEM((rows, weight.shape[1]), F32),
            pltpu.SemaphoreType.DMA((5,)),
            pltpu.SemaphoreType.DMA((-(-feats // CHUNK),)),
        ],
        compiler_params=pltpu.CompilerParams(vmem_limit_bytes=60 * MIB),
        cost_estimate=pl.CostEstimate(
            flops=2 * rows * feats * weight.shape[1],
            bytes_accessed=2 * feats * weight.shape[1],
            transcendentals=0,
        ),
        name="project",
    )(gain, x, weight, query, own)
    return outs[:ranks], outs[ranks]


def resident_kernel(ranks, heads, len_hbm, q_hbm, k_hbm, v_hbm, *rest):
    outs = rest[:ranks]
    len_ref, q_ref, q_all, k_buf, v_buf, o_all, s_all, in_sems, sems = rest[ranks:]
    len_copy = pltpu.make_async_copy(len_hbm, len_ref, in_sems.at[0])
    len_copy.start()
    q_copy = pltpu.make_async_copy(q_hbm, q_ref, in_sems.at[1])
    q_copy.start()
    residents, positions, width = k_buf.shape
    half = width // 2
    copies = []
    for r in range(residents):
        trio = [pltpu.make_async_copy(k_hbm.at[r], k_buf.at[r], sems.at[0, r])]
        for i in range(2):
            at = slice(i * half, (i + 1) * half)
            trio.append(
                pltpu.make_async_copy(v_hbm.at[r, :, at], v_buf.at[r, :, at], sems.at[1 + i, r])
            )
        copies.append(trio)
    for trio in copies:
        for copy in trio:
            copy.start()
    kv_heads = width // 128
    group = heads // kv_heads
    pair_rows = 2 * group
    heads_mine = heads // ranks
    rank = lax.axis_index("tp")
    top_half = iota((pair_rows, 128), 0) < group
    scale = F32(1.0) / jnp.sqrt(F32(128.0))
    q_copy.wait()
    q_lines = q_ref[...].astype(F32)
    for r in range(residents):
        for h in range(heads):
            q_all[r, h : h + 1, :] = q_lines[r : r + 1, h * 128 : (h + 1) * 128]
    len_copy.wait()
    for r in range(residents):
        valid = rank * positions + iota((pair_rows, positions), 1) < len_ref[0, r]
        copies[r][0].wait()
        weights, peaks, totals = [], [], []
        for p in range(kv_heads // 2):
            q = q_all[r, p * pair_rows : (p + 1) * pair_rows, :]
            zero = jnp.zeros_like(q)
            lhs = jnp.concatenate(
                [jnp.where(top_half, q, zero), jnp.where(top_half, zero, q)], axis=1
            ).astype(BF16)
            scores = lax.dot_general(
                lhs,
                k_buf[r, :, p * 256 : (p + 1) * 256],
                (((1,), (1,)), ((), ())),
                preferred_element_type=F32,
            )
            scores = jnp.where(valid, scores * scale, ABSENT)
            peak = jnp.max(scores, axis=1, keepdims=True).astype(BF16).astype(F32)
            weight = jnp.where(valid, jnp.exp(scores - peak), 0.0)
            peaks.append(peak)
            totals.append(jnp.sum(weight, axis=1, keepdims=True))
            weights.append(weight.astype(BF16))
        high, low = split_bf16(jnp.concatenate(totals, axis=0))
        s_all[r, 0] = column_to_row(jnp.concatenate(peaks, axis=0), heads_mine)
        s_all[r, 1] = column_to_row(high.astype(F32), heads_mine)
        s_all[r, 2] = column_to_row(low.astype(F32), heads_mine)
        for p in range(kv_heads // 2):
            if p * 4 % kv_heads == 0:
                copies[r][1 + p * 4 // kv_heads].wait()
            both = jnp.dot(
                weights[p], v_buf[r, :, p * 256 : (p + 1) * 256], preferred_element_type=F32
            )
            o_all[r, p * pair_rows : (p + 1) * pair_rows, :] = jnp.where(
                top_half, both[:, :128], both[:, 128:]
            )
    filled = residents * (heads_mine + 3)
    for j in range(ranks):
        target = rank ^ j
        first = pl.multiple_of(target * heads_mine, heads_mine)
        parts = [o_all[r, pl.ds(first, heads_mine), :] for r in range(residents)]
        parts += [s_all[r, i, pl.ds(target, 1), :] for i in range(3) for r in range(residents)]
        if outs[j].shape[0] > filled:
            parts.append(jnp.zeros((outs[j].shape[0] - filled, 128), F32))
        outs[j][...] = jnp.concatenate(parts, axis=0).astype(BF16)


def attend_resident(lengths, query, k_cache, v_cache, ranks):
    residents, positions, width = k_cache.shape
    heads = query.shape[1] // 128
    heads_mine = heads // ranks
    rows = -(-(residents * (heads_mine + 3)) // 16) * 16
    return pl.pallas_call(
        functools.partial(resident_kernel, ranks, heads),
        in_specs=[HBM] * 4,
        out_specs=[VMEM] * ranks,
        out_shape=[jax.ShapeDtypeStruct((rows, 128), BF16)] * ranks,
        scratch_shapes=[
            pltpu.SMEM(lengths.shape, jnp.int32),
            pltpu.VMEM(query.shape, BF16),
            pltpu.VMEM((residents, heads, 128), F32),
            pltpu.VMEM((residents, positions, width), BF16),
            pltpu.VMEM((residents, positions, width), BF16),
            pltpu.VMEM((residents, heads, 128), F32),
            pltpu.VMEM((residents, 3, ranks, 128), F32),
            pltpu.SemaphoreType.DMA((2,)),
            pltpu.SemaphoreType.DMA((3, residents)),
        ],
        compiler_params=pltpu.CompilerParams(vmem_limit_bytes=60 * MIB),
        cost_estimate=pl.CostEstimate(
            flops=4 * residents * heads * positions * 128,
            bytes_accessed=4 * residents * positions * width,
            transcendentals=residents * heads * positions,
        ),
        name="attend_resident",
    )(lengths, query, k_cache, v_cache)


def block_of(blocks, b):
    step = b.bit_length() - 1
    array = blocks[step]
    return array if step == 0 else array.at[b - (1 << step)]


def prepare_kernel(insts, steps, residents, kv_mine, dest_ref, count_ref, gain_ref, cos_ref, sin_ref, *rest):
    asks, rest = rest[:steps], rest[steps:]
    q_out, own_out, limit_out, cos_out, sin_out, place_out, line_ref, q_ref, k_ref = rest
    requests = dest_ref.shape[0]
    rows = q_out.shape[0]
    heads_mine = rows // requests
    per = heads_mine // kv_mine
    decoded = asks[0].shape[0]
    here = lax.axis_index("inst")
    ask_row = iota((decoded, line_ref.shape[1]), 0)
    limit = jnp.zeros((rows, 128), jnp.int32)
    for r in range(requests):
        dest = dest_ref[r, here]
        limit = jnp.where(iota((rows, 128), 0) // heads_mine == r, count_ref[r, here], limit)
        place = jnp.int32(residents)
        for s in range(insts):
            for c in range(requests):
                place += jnp.where((dest_ref[c, s] == dest) & (here > s), 1, 0).astype(jnp.int32)
        for b in range(1, insts):

            @pl.when(here ^ b == dest)
            def _():
                ask = block_of(asks, b)[...].astype(F32)
                line_ref[r : r + 1, :] = jnp.sum(
                    jnp.where(ask_row == place, ask, 0.0), axis=0, keepdims=True
                )

        line = line_ref[r : r + 1, :]
        for h in range(heads_mine):
            at = r * heads_mine + h
            k_at = (heads_mine + h // per) * 128
            v_at = k_at + kv_mine * 128
            q_ref[at : at + 1, :] = line[:, h * 128 : (h + 1) * 128]
            k_ref[at : at + 1, :] = line[:, k_at : k_at + 128]
            own_out[0, at : at + 1, :] = line[:, v_at : v_at + 128]
    scale = F32(1.0) / jnp.sqrt(F32(128.0))
    q = q_ref[...]
    q_out[...] = q.astype(BF16)
    own_out[1] = jnp.broadcast_to(
        jnp.sum(q * k_ref[...], axis=1, keepdims=True) * scale, (rows, 128)
    )
    limit_out[...] = limit
    gain = gain_ref[...].astype(F32)
    cos_out[...] = cos_ref[...] * gain
    sin_out[...] = sin_ref[...] * pltpu.roll(jnp.broadcast_to(gain, (8, 128)), 64, 1)[:1]
    places = jnp.full(place_out.shape, -1, jnp.int32)
    row = iota(place_out.shape, 0)
    place = jnp.int32(residents)
    for s in range(insts):
        for c in range(requests):
            mine = dest_ref[c, s] == here
            places = jnp.where((row == (here ^ s) * requests + c) & mine, place, places)
            place += jnp.where(mine, 1, 0).astype(jnp.int32)
    place_out[...] = places


def prepare(dest, count, k_gain, cos, sin, asks, residents, heads_mine, kv_mine):
    requests, insts = dest.shape
    rows = requests * heads_mine
    return pl.pallas_call(
        functools.partial(prepare_kernel, insts, len(asks), residents, kv_mine),
        in_specs=[SMEM] * 2 + [VMEM] * (3 + len(asks)),
        out_specs=[VMEM] * 6,
        out_shape=[
            jax.ShapeDtypeStruct((rows, 128), BF16),
            jax.ShapeDtypeStruct((2, rows, 128), F32),
            jax.ShapeDtypeStruct((rows, 128), jnp.int32),
            jax.ShapeDtypeStruct(cos.shape, F32),
            jax.ShapeDtypeStruct(sin.shape, F32),
            jax.ShapeDtypeStruct((insts * requests, 128), jnp.int32),
        ],
        scratch_shapes=[
            pltpu.VMEM((requests, asks[0].shape[1]), F32),
            pltpu.VMEM((rows, 128), F32),
            pltpu.VMEM((rows, 128), F32),
        ],
        compiler_params=pltpu.CompilerParams(vmem_limit_bytes=16 * MIB),
        name="prepare",
    )(dest, count, k_gain, cos, sin, *asks)


def moved_kernel(ranks, features, q_ref, own_ref, limit_ref, cos_ref, sin_ref, *rest):
    pieces = rest[:ranks]
    _, out_ref, line_ref = rest[ranks:]
    requests = out_ref.shape[0]
    tokens = cos_ref.shape[0]
    piece = pieces[0].shape[1] // 2
    kv_mine = piece // 128
    rows = q_ref.shape[0]
    heads_mine = rows // requests
    scale = F32(1.0) / jnp.sqrt(F32(128.0))

    tail = pieces[0][tokens:, :].astype(F32)
    for t in range(1, ranks):
        tail = tail + pieces[t][tokens:, :].astype(F32)
    blocks = tokens // 128
    squares = tail[:blocks, :128] + tail[blocks : 2 * blocks, :128]
    squares = jnp.concatenate(
        [row_to_column(squares[b : b + 1], 128) for b in range(blocks)], axis=0
    )
    token_scale = lax.rsqrt(squares / features + EPS)

    def column_block(c):
        total = pieces[0][:tokens, c : c + 128].astype(F32)
        for t in range(1, ranks):
            total = total + pieces[t][:tokens, c : c + 128].astype(F32)
        return total * token_scale

    q = q_ref[...]
    which = iota((rows, tokens), 0) % heads_mine // (heads_mine // kv_mine)
    scores = None
    for h in range(kv_mine):
        key = column_block(h * 128)
        key = key * lax.rsqrt(jnp.mean(key * key, axis=1, keepdims=True) + EPS)
        key = key * cos_ref[...] + pltpu.roll(key, 64, 1) * sin_ref[...]
        part = lax.dot_general(
            q, key.astype(BF16), (((1,), (1,)), ((), ())), preferred_element_type=F32
        )
        scores = part if scores is None else jnp.where(which == h, part, scores)
    token = iota((rows, tokens), 1)
    limit = jnp.concatenate([limit_ref[...]] * (tokens // 128), axis=1)
    valid = (token % requests == iota((rows, tokens), 0) // heads_mine) & (
        token // requests < limit
    )
    scores = jnp.where(valid, scores * scale, ABSENT)
    own_score = own_ref[1]
    top = jnp.maximum(jnp.max(scores, axis=1, keepdims=True), own_score)
    weights = jnp.where(
        valid, jnp.exp(scores - jnp.concatenate([top] * (tokens // 128), axis=1)), 0.0
    )
    own_weight = jnp.exp(own_score - top)
    total = jnp.sum(weights, axis=1, keepdims=True) + own_weight
    weights = weights.astype(BF16)
    summed = None
    for h in range(kv_mine):
        value = column_block(piece + h * 128).astype(BF16)
        part = jnp.dot(weights, value, preferred_element_type=F32)
        summed = part if summed is None else jnp.where(which[:, :128] == h, part, summed)
    summed = summed + own_weight.astype(BF16).astype(F32) * own_ref[0]
    result = summed / total
    for r in range(requests):
        for h in range(heads_mine):
            at = r * heads_mine + h
            line_ref[r : r + 1, h * 128 : (h + 1) * 128] = result[at : at + 1, :]
    out_ref[...] = line_ref[...].astype(BF16)


def attend_moved(prepared, pieces, after, requests, features):
    rows = prepared[0].shape[0]
    width = rows // requests * 128
    return pl.pallas_call(
        functools.partial(moved_kernel, len(pieces), features),
        in_specs=[VMEM] * (len(prepared) + len(pieces) + 1),
        out_specs=VMEM,
        out_shape=jax.ShapeDtypeStruct((requests, width), BF16),
        scratch_shapes=[pltpu.VMEM((requests, width), F32)],
        compiler_params=pltpu.CompilerParams(vmem_limit_bytes=16 * MIB),
        name="attend_moved",
    )(*prepared, *pieces, after)


def combine_kernel(ranks, residents, kv_mine, ask_ref, *rest):
    payloads = rest[:ranks]
    out_ref, q_ref, own_ref = rest[ranks:]
    heads_mine = q_ref.shape[0]
    per = heads_mine // kv_mine
    scale = F32(1.0) / jnp.sqrt(F32(128.0))
    at = residents * heads_mine
    ask = ask_ref[...].astype(F32)
    for r in range(residents):
        for h in range(heads_mine):
            k_at = (heads_mine + h // per) * 128
            v_at = k_at + kv_mine * 128
            q_ref[h : h + 1, :] = ask[r : r + 1, h * 128 : (h + 1) * 128]
            own_ref[0, h : h + 1, :] = ask[r : r + 1, k_at : k_at + 128]
            own_ref[1, h : h + 1, :] = ask[r : r + 1, v_at : v_at + 128]
        own_score = jnp.sum(q_ref[...] * own_ref[0], axis=1, keepdims=True) * scale
        peaks, totals = [], []
        for t in range(ranks):
            stat = payloads[t][at : at + 3 * residents, :].astype(F32)
            peaks.append(row_to_column(stat[r : r + 1], heads_mine))
            total = stat[residents + r : residents + r + 1]
            total = total + stat[2 * residents + r : 2 * residents + r + 1]
            totals.append(row_to_column(total, heads_mine))
        top = own_score
        for t in range(ranks):
            top = jnp.maximum(top, peaks[t])
        own_weight = jnp.exp(own_score - top)
        denom = own_weight
        numer = own_weight.astype(BF16).astype(F32) * own_ref[1]
        for t in range(ranks):
            keep = jnp.exp(peaks[t] - top)
            denom = denom + keep * totals[t]
            numer = numer + keep * payloads[t][r * heads_mine : (r + 1) * heads_mine, :].astype(F32)
        result = numer / denom
        for h in range(heads_mine):
            out_ref[r : r + 1, h * 128 : (h + 1) * 128] = result[h : h + 1, :]


def combine_resident(asks, payloads, residents, heads_mine, kv_mine):
    return pl.pallas_call(
        functools.partial(combine_kernel, len(payloads), residents, kv_mine),
        in_specs=[VMEM] * (1 + len(payloads)),
        out_specs=VMEM,
        out_shape=jax.ShapeDtypeStruct((residents, heads_mine * 128), F32),
        scratch_shapes=[
            pltpu.VMEM((heads_mine, 128), F32),
            pltpu.VMEM((2, heads_mine, 128), F32),
        ],
        compiler_params=pltpu.CompilerParams(vmem_limit_bytes=8 * MIB),
        name="combine_resident",
    )(asks, *payloads)


def finish_kernel(insts, steps, kept_ref, place_ref, *rest):
    moved = rest[:steps]
    out_ref = rest[steps]
    residents = kept_ref.shape[0]
    decoded, width = out_ref.shape
    requests = decoded - residents
    row = iota((decoded, 128), 0)
    arrived = [block_of(moved, b)[...].astype(F32) for b in range(1, insts)]
    for c in range(0, width, 128):
        kept = kept_ref[:, c : c + 128]
        line = jnp.concatenate([kept, jnp.zeros((requests, 128), F32)], axis=0)
        for b in range(1, insts):
            for i in range(requests):
                at = b * requests + i
                line = jnp.where(
                    place_ref[at : at + 1, :] == row, arrived[b - 1][i : i + 1, c : c + 128], line
                )
        out_ref[:, c : c + 128] = line.astype(BF16)


def finish(kept, places, moved, insts, requests):
    residents, width = kept.shape
    return pl.pallas_call(
        functools.partial(finish_kernel, insts, len(moved)),
        in_specs=[VMEM] * (2 + len(moved)),
        out_specs=VMEM,
        out_shape=jax.ShapeDtypeStruct((residents + requests, width), BF16),
        compiler_params=pltpu.CompilerParams(vmem_limit_bytes=8 * MIB),
        name="finish",
    )(kept, places, *moved)


def swapped(x, axis, j, n):
    return lax.ppermute(x, axis, [(i, i ^ j) for i in range(n)])


def gather(x, axis, n):
    held, blocks = x, []
    for step in range(n.bit_length() - 1):
        blocks.append(swapped(held, axis, 1 << step, n))
        if 2 << step < n:
            one = blocks[-1]
            held = jnp.stack([held, one]) if step == 0 else jnp.concatenate([held, one])
    return blocks


def rotation(slots, requests, head_size):
    half = head_size // 2
    freq = THETA ** (-np.arange(half) * 2.0 / head_size)
    angle = np.repeat(np.arange(slots), requests)[:, None] * freq[None, :]
    cos, sin = np.cos(angle), np.sin(angle)
    return (
        np.concatenate([cos, cos], axis=1).astype(np.float32),
        np.concatenate([-sin, sin], axis=1).astype(np.float32),
    )


def per_device(
    mig_hidden,
    mig_dest,
    mig_count,
    attn_gain,
    kv_weight,
    k_gain,
    query,
    new_kv,
    k_cache,
    v_cache,
    lengths,
):
    insts = lax.axis_size("inst")
    ranks = lax.axis_size("tp")
    head_size = k_gain.shape[0]
    slots, requests, feats = mig_hidden.shape[1:]
    residents = k_cache.shape[1]
    heads = query.shape[2] // head_size
    kv_heads = kv_weight.shape[1] // 2 // head_size
    heads_mine = heads // ranks
    group = heads // kv_heads
    kv_mine = max(1, heads_mine // group)

    pieces, ask = project(
        mig_hidden[0], attn_gain, kv_weight, query[0], new_kv[0], ranks, group, kv_mine
    )
    pieces = [pieces[0]] + [swapped(pieces[j], "tp", j, ranks) for j in reversed(range(1, ranks))]
    asks = gather(ask, "inst", insts)
    payloads = attend_resident(lengths, query[0], k_cache[0], v_cache[0], ranks)
    payloads = [payloads[0]] + [swapped(payloads[j], "tp", j, ranks) for j in range(1, ranks)]
    kept = combine_resident(ask, payloads, residents, heads_mine, kv_mine)
    cos, sin = rotation(slots, requests, head_size)
    *prepared, places = prepare(
        mig_dest.T,
        mig_count.T,
        k_gain.reshape(1, head_size),
        cos,
        sin,
        asks,
        residents,
        heads_mine,
        kv_mine,
    )
    moved = attend_moved(prepared, pieces, kept, requests, feats * ranks)
    return finish(kept, places, gather(moved, "inst", insts), insts, requests)[None]


def solution(mesh):
    placed = (
        P(("group", "inst"), None, None, "tp"),
        P("group", None),
        P("group", None),
        P("tp"),
        P("tp", None),
        P(),
        P(("group", "inst"), None, None),
        P(("group", "inst"), None, None),
        P(("group", "inst"), None, "tp", None),
        P(("group", "inst"), None, "tp", None),
        P(("group", "inst"), None),
    )
    return jax.shard_map(
        per_device,
        mesh=mesh,
        in_specs=placed,
        out_specs=P(("group", "inst"), None, "tp"),
        check_vma=False,
    )
```

```python
import functools

import jax
import jax.numpy as jnp
import numpy as np
from jax import lax
from jax.experimental import pallas as pl
from jax.experimental.pallas import tpu as pltpu
from jax.sharding import PartitionSpec as P

EPS = 1e-06
THETA = 1000000.0
ABSENT = -1e30
F32 = jnp.float32
BF16 = jnp.bfloat16
MIB = 1024 * 1024
CHUNK = 256

VMEM = pl.BlockSpec(memory_space=pltpu.VMEM)
SMEM = pl.BlockSpec(memory_space=pltpu.SMEM)
HBM = pl.BlockSpec(memory_space=pltpu.HBM)


def iota(shape, dim):
    return lax.broadcasted_iota(jnp.int32, shape, dim)


def column_to_row(column, period):
    n = column.shape[0]
    spread = jnp.where(iota((n, 128), 0) % period == iota((n, 128), 1), column, 0.0)
    return jnp.sum(spread.reshape(n // period, period, 128), axis=1)


def row_to_column(row, n):
    return jnp.sum(
        jnp.where(iota((n, 128), 0) == iota((n, 128), 1), row, 0.0), axis=1, keepdims=True
    )


def split_bf16(x):
    high = x.astype(BF16)
    return high, (x - high.astype(F32)).astype(BF16)


def project_kernel(ranks, group, gain_hbm, x_hbm, w_hbm, q_hbm, own_hbm, *rest):
    outs, ask_ref = rest[:ranks], rest[ranks]
    gain_ref, x_ref, w_ref, acc_ref, in_sems, w_sems = rest[ranks + 1 :]
    slots, requests, feats = x_ref.shape
    rows = slots * requests
    piece = outs[0].shape[1] // 2
    kv_width = w_hbm.shape[1] // 2
    heads_mine = kv_width // 128 * group // ranks
    rank = lax.axis_index("tp")

    def first_column(target):
        return pl.multiple_of(target * heads_mine // group * 128, 128)

    gain_copy = pltpu.make_async_copy(gain_hbm, gain_ref, in_sems.at[0])
    gain_copy.start()
    x_copy = pltpu.make_async_copy(x_hbm, x_ref, in_sems.at[1])
    x_copy.start()
    cuts = list(range(0, feats, CHUNK)) + [feats]
    chunks = list(zip(cuts[:-1], cuts[1:]))
    copies = []
    for i, (low, high) in enumerate(chunks):
        copies.append(
            pltpu.make_async_copy(
                w_hbm.at[low:high, :], w_ref.at[low:high, :], w_sems.at[i]
            )
        )
        copies[-1].start()
    mine = heads_mine * 128
    q_first = pl.multiple_of(rank * mine, 128)
    asking = [
        pltpu.make_async_copy(
            q_hbm.at[:, pl.ds(q_first, mine)], ask_ref.at[:, :mine], in_sems.at[2]
        )
    ]
    for i in range(2):
        asking.append(
            pltpu.make_async_copy(
                own_hbm.at[:, pl.ds(i * kv_width + first_column(rank), piece)],
                ask_ref.at[:, mine + i * piece : mine + (i + 1) * piece],
                in_sems.at[3 + i],
            )
        )
    for copy in asking:
        copy.start()
    gain_copy.wait()
    x_copy.wait()
    squares = jnp.zeros((rows, 128), F32)
    for i, (low, high) in enumerate(chunks):
        parts = []
        for c in range(low, high, 128):
            width = min(128, high - c)
            x = x_ref[:, :, c : c + width].astype(F32).reshape(rows, width)
            gain = gain_ref[c : c + width].astype(F32).reshape(1, width)
            parts.append((x * gain).astype(BF16))
            x = x * x
            if width < 128:
                x = jnp.concatenate([x, jnp.zeros((rows, 128 - width), F32)], axis=1)
            squares = squares + x
        xg = parts[0] if len(parts) == 1 else jnp.concatenate(parts, axis=1)
        copies[i].wait()
        for n in range(0, 2 * kv_width, 512):
            part = jnp.dot(xg, w_ref[low:high, n : n + 512], preferred_element_type=F32)
            if i == 0:
                acc_ref[:, n : n + 512] = part
            else:
                acc_ref[:, n : n + 512] += part
    sq = column_to_row(jnp.sum(squares, axis=1, keepdims=True), 128)
    high, low = split_bf16(sq)
    tail = jnp.concatenate([high.astype(F32), low.astype(F32)], axis=0)
    if outs[0].shape[0] - rows > tail.shape[0]:
        fill = outs[0].shape[0] - rows - tail.shape[0]
        tail = jnp.concatenate([tail, jnp.zeros((fill, 128), F32)], axis=0)
    extra = jnp.concatenate([tail.astype(BF16)] * (2 * piece // 128), axis=1)
    for j in range(ranks):
        first = first_column(rank ^ j)
        outs[j][:rows, :piece] = acc_ref[:, pl.ds(first, piece)].astype(BF16)
        outs[j][:rows, piece:] = acc_ref[:, pl.ds(kv_width + first, piece)].astype(BF16)
        outs[j][rows:, :] = extra
    for copy in asking:
        copy.wait()


def project(x, gain, weight, query, own, ranks, group, kv_mine):
    slots, requests, feats = x.shape
    rows = slots * requests
    piece = kv_mine * 128
    extra = -(-2 * (rows // 128) // 8) * 8
    decoded, q_width = query.shape
    outs = pl.pallas_call(
        functools.partial(project_kernel, ranks, group),
        in_specs=[HBM] * 5,
        out_specs=[VMEM] * (ranks + 1),
        out_shape=[jax.ShapeDtypeStruct((rows + extra, 2 * piece), BF16)] * ranks
        + [jax.ShapeDtypeStruct((decoded, q_width // ranks + 2 * piece), BF16)],
        scratch_shapes=[
            pltpu.VMEM((feats,), BF16),
            pltpu.VMEM((slots, requests, feats), BF16),
            pltpu.VMEM(weight.shape, BF16),
            pltpu.VMEM((rows, weight.shape[1]), F32),
            pltpu.SemaphoreType.DMA((5,)),
            pltpu.SemaphoreType.DMA((-(-feats // CHUNK),)),
        ],
        compiler_params=pltpu.CompilerParams(vmem_limit_bytes=60 * MIB),
        cost_estimate=pl.CostEstimate(
            flops=2 * rows * feats * weight.shape[1],
            bytes_accessed=2 * feats * weight.shape[1],
            transcendentals=0,
        ),
        name="project",
    )(gain, x, weight, query, own)
    return outs[:ranks], outs[ranks]


def resident_kernel(ranks, heads, len_hbm, q_hbm, k_hbm, v_hbm, *rest):
    outs = rest[:ranks]
    len_ref, q_ref, q_all, k_buf, v_buf, o_all, s_all, in_sems, sems = rest[ranks:]
    len_copy = pltpu.make_async_copy(len_hbm, len_ref, in_sems.at[0])
    len_copy.start()
    q_copy = pltpu.make_async_copy(q_hbm, q_ref, in_sems.at[1])
    q_copy.start()
    residents, positions, width = k_buf.shape
    copies = []
    for r in range(residents):
        copies.append(
            (
                pltpu.make_async_copy(k_hbm.at[r], k_buf.at[r], sems.at[0, r]),
                pltpu.make_async_copy(v_hbm.at[r], v_buf.at[r], sems.at[1, r]),
            )
        )
    for pair in copies:
        for copy in pair:
            copy.start()
    kv_heads = width // 128
    group = heads // kv_heads
    pair_rows = 2 * group
    heads_mine = heads // ranks
    rank = lax.axis_index("tp")
    top_half = iota((pair_rows, 128), 0) < group
    scale = F32(1.0) / jnp.sqrt(F32(128.0))
    q_copy.wait()
    q_lines = q_ref[...].astype(F32)
    for r in range(residents):
        for h in range(heads):
            q_all[r, h : h + 1, :] = q_lines[r : r + 1, h * 128 : (h + 1) * 128]
    len_copy.wait()
    for r in range(residents):
        valid = rank * positions + iota((pair_rows, positions), 1) < len_ref[0, r]
        copies[r][0].wait()
        weights, peaks, totals = [], [], []
        for p in range(kv_heads // 2):
            q = q_all[r, p * pair_rows : (p + 1) * pair_rows, :]
            zero = jnp.zeros_like(q)
            lhs = jnp.concatenate(
                [jnp.where(top_half, q, zero), jnp.where(top_half, zero, q)], axis=1
            ).astype(BF16)
            scores = lax.dot_general(
                lhs,
                k_buf[r, :, p * 256 : (p + 1) * 256],
                (((1,), (1,)), ((), ())),
                preferred_element_type=F32,
            )
            scores = jnp.where(valid, scores * scale, ABSENT)
            peak = jnp.max(scores, axis=1, keepdims=True).astype(BF16).astype(F32)
            weight = jnp.where(valid, jnp.exp(scores - peak), 0.0)
            peaks.append(peak)
            totals.append(jnp.sum(weight, axis=1, keepdims=True))
            weights.append(weight.astype(BF16))
        high, low = split_bf16(jnp.concatenate(totals, axis=0))
        s_all[r, 0] = column_to_row(jnp.concatenate(peaks, axis=0), heads_mine)
        s_all[r, 1] = column_to_row(high.astype(F32), heads_mine)
        s_all[r, 2] = column_to_row(low.astype(F32), heads_mine)
        copies[r][1].wait()
        for p in range(kv_heads // 2):
            both = jnp.dot(
                weights[p], v_buf[r, :, p * 256 : (p + 1) * 256], preferred_element_type=F32
            )
            o_all[r, p * pair_rows : (p + 1) * pair_rows, :] = jnp.where(
                top_half, both[:, :128], both[:, 128:]
            )
    filled = residents * (heads_mine + 3)
    for j in range(ranks):
        target = rank ^ j
        first = pl.multiple_of(target * heads_mine, heads_mine)
        parts = [o_all[r, pl.ds(first, heads_mine), :] for r in range(residents)]
        parts += [s_all[r, i, pl.ds(target, 1), :] for i in range(3) for r in range(residents)]
        if outs[j].shape[0] > filled:
            parts.append(jnp.zeros((outs[j].shape[0] - filled, 128), F32))
        outs[j][...] = jnp.concatenate(parts, axis=0).astype(BF16)


def attend_resident(lengths, query, k_cache, v_cache, ranks):
    residents, positions, width = k_cache.shape
    heads = query.shape[1] // 128
    heads_mine = heads // ranks
    rows = -(-(residents * (heads_mine + 3)) // 16) * 16
    return pl.pallas_call(
        functools.partial(resident_kernel, ranks, heads),
        in_specs=[HBM] * 4,
        out_specs=[VMEM] * ranks,
        out_shape=[jax.ShapeDtypeStruct((rows, 128), BF16)] * ranks,
        scratch_shapes=[
            pltpu.SMEM(lengths.shape, jnp.int32),
            pltpu.VMEM(query.shape, BF16),
            pltpu.VMEM((residents, heads, 128), F32),
            pltpu.VMEM((residents, positions, width), BF16),
            pltpu.VMEM((residents, positions, width), BF16),
            pltpu.VMEM((residents, heads, 128), F32),
            pltpu.VMEM((residents, 3, ranks, 128), F32),
            pltpu.SemaphoreType.DMA((2,)),
            pltpu.SemaphoreType.DMA((2, residents)),
        ],
        compiler_params=pltpu.CompilerParams(vmem_limit_bytes=60 * MIB),
        cost_estimate=pl.CostEstimate(
            flops=4 * residents * heads * positions * 128,
            bytes_accessed=4 * residents * positions * width,
            transcendentals=residents * heads * positions,
        ),
        name="attend_resident",
    )(lengths, query, k_cache, v_cache)


def block_of(blocks, b):
    step = b.bit_length() - 1
    array = blocks[step]
    return array if step == 0 else array.at[b - (1 << step)]


def prepare_kernel(insts, steps, residents, kv_mine, dest_ref, count_ref, gain_ref, cos_ref, sin_ref, *rest):
    asks, rest = rest[:steps], rest[steps:]
    q_out, own_out, limit_out, cos_out, sin_out, place_out, line_ref, q_ref, k_ref = rest
    requests = dest_ref.shape[0]
    rows = q_out.shape[0]
    heads_mine = rows // requests
    per = heads_mine // kv_mine
    decoded = asks[0].shape[0]
    here = lax.axis_index("inst")
    ask_row = iota((decoded, line_ref.shape[1]), 0)
    limit = jnp.zeros((rows, 128), jnp.int32)
    for r in range(requests):
        dest = dest_ref[r, here]
        limit = jnp.where(iota((rows, 128), 0) // heads_mine == r, count_ref[r, here], limit)
        place = jnp.int32(residents)
        for s in range(insts):
            for c in range(requests):
                place += jnp.where((dest_ref[c, s] == dest) & (here > s), 1, 0).astype(jnp.int32)
        for b in range(1, insts):

            @pl.when(here ^ b == dest)
            def _():
                ask = block_of(asks, b)[...].astype(F32)
                line_ref[r : r + 1, :] = jnp.sum(
                    jnp.where(ask_row == place, ask, 0.0), axis=0, keepdims=True
                )

        line = line_ref[r : r + 1, :]
        for h in range(heads_mine):
            at = r * heads_mine + h
            k_at = (heads_mine + h // per) * 128
            v_at = k_at + kv_mine * 128
            q_ref[at : at + 1, :] = line[:, h * 128 : (h + 1) * 128]
            k_ref[at : at + 1, :] = line[:, k_at : k_at + 128]
            own_out[0, at : at + 1, :] = line[:, v_at : v_at + 128]
    scale = F32(1.0) / jnp.sqrt(F32(128.0))
    q = q_ref[...]
    q_out[...] = q.astype(BF16)
    own_out[1] = jnp.broadcast_to(
        jnp.sum(q * k_ref[...], axis=1, keepdims=True) * scale, (rows, 128)
    )
    limit_out[...] = limit
    gain = gain_ref[...].astype(F32)
    cos_out[...] = cos_ref[...] * gain
    sin_out[...] = sin_ref[...] * pltpu.roll(jnp.broadcast_to(gain, (8, 128)), 64, 1)[:1]
    places = jnp.full(place_out.shape, -1, jnp.int32)
    row = iota(place_out.shape, 0)
    place = jnp.int32(residents)
    for s in range(insts):
        for c in range(requests):
            mine = dest_ref[c, s] == here
            places = jnp.where((row == (here ^ s) * requests + c) & mine, place, places)
            place += jnp.where(mine, 1, 0).astype(jnp.int32)
    place_out[...] = places


def prepare(dest, count, k_gain, cos, sin, asks, residents, heads_mine, kv_mine):
    requests, insts = dest.shape
    rows = requests * heads_mine
    return pl.pallas_call(
        functools.partial(prepare_kernel, insts, len(asks), residents, kv_mine),
        in_specs=[SMEM] * 2 + [VMEM] * (3 + len(asks)),
        out_specs=[VMEM] * 6,
        out_shape=[
            jax.ShapeDtypeStruct((rows, 128), BF16),
            jax.ShapeDtypeStruct((2, rows, 128), F32),
            jax.ShapeDtypeStruct((rows, 128), jnp.int32),
            jax.ShapeDtypeStruct(cos.shape, F32),
            jax.ShapeDtypeStruct(sin.shape, F32),
            jax.ShapeDtypeStruct((insts * requests, 128), jnp.int32),
        ],
        scratch_shapes=[
            pltpu.VMEM((requests, asks[0].shape[1]), F32),
            pltpu.VMEM((rows, 128), F32),
            pltpu.VMEM((rows, 128), F32),
        ],
        compiler_params=pltpu.CompilerParams(vmem_limit_bytes=16 * MIB),
        name="prepare",
    )(dest, count, k_gain, cos, sin, *asks)


def moved_kernel(ranks, features, q_ref, own_ref, limit_ref, cos_ref, sin_ref, *rest):
    pieces = rest[:ranks]
    _, out_ref, line_ref = rest[ranks:]
    requests = out_ref.shape[0]
    tokens = cos_ref.shape[0]
    piece = pieces[0].shape[1] // 2
    kv_mine = piece // 128
    rows = q_ref.shape[0]
    heads_mine = rows // requests
    scale = F32(1.0) / jnp.sqrt(F32(128.0))

    tail = pieces[0][tokens:, :].astype(F32)
    for t in range(1, ranks):
        tail = tail + pieces[t][tokens:, :].astype(F32)
    blocks = tokens // 128
    squares = tail[:blocks, :128] + tail[blocks : 2 * blocks, :128]
    squares = jnp.concatenate(
        [row_to_column(squares[b : b + 1], 128) for b in range(blocks)], axis=0
    )
    token_scale = lax.rsqrt(squares / features + EPS)

    def column_block(c):
        total = pieces[0][:tokens, c : c + 128].astype(F32)
        for t in range(1, ranks):
            total = total + pieces[t][:tokens, c : c + 128].astype(F32)
        return total * token_scale

    q = q_ref[...]
    which = iota((rows, tokens), 0) % heads_mine // (heads_mine // kv_mine)
    scores = None
    for h in range(kv_mine):
        key = column_block(h * 128)
        key = key * lax.rsqrt(jnp.mean(key * key, axis=1, keepdims=True) + EPS)
        key = key * cos_ref[...] + pltpu.roll(key, 64, 1) * sin_ref[...]
        part = lax.dot_general(
            q, key.astype(BF16), (((1,), (1,)), ((), ())), preferred_element_type=F32
        )
        scores = part if scores is None else jnp.where(which == h, part, scores)
    token = iota((rows, tokens), 1)
    limit = jnp.concatenate([limit_ref[...]] * (tokens // 128), axis=1)
    valid = (token % requests == iota((rows, tokens), 0) // heads_mine) & (
        token // requests < limit
    )
    scores = jnp.where(valid, scores * scale, ABSENT)
    own_score = own_ref[1]
    top = jnp.maximum(jnp.max(scores, axis=1, keepdims=True), own_score)
    weights = jnp.where(
        valid, jnp.exp(scores - jnp.concatenate([top] * (tokens // 128), axis=1)), 0.0
    )
    own_weight = jnp.exp(own_score - top)
    total = jnp.sum(weights, axis=1, keepdims=True) + own_weight
    weights = weights.astype(BF16)
    summed = None
    for h in range(kv_mine):
        value = column_block(piece + h * 128).astype(BF16)
        part = jnp.dot(weights, value, preferred_element_type=F32)
        summed = part if summed is None else jnp.where(which[:, :128] == h, part, summed)
    summed = summed + own_weight.astype(BF16).astype(F32) * own_ref[0]
    result = summed / total
    for r in range(requests):
        for h in range(heads_mine):
            at = r * heads_mine + h
            line_ref[r : r + 1, h * 128 : (h + 1) * 128] = result[at : at + 1, :]
    out_ref[...] = line_ref[...].astype(BF16)


def attend_moved(prepared, pieces, after, requests, features):
    rows = prepared[0].shape[0]
    width = rows // requests * 128
    return pl.pallas_call(
        functools.partial(moved_kernel, len(pieces), features),
        in_specs=[VMEM] * (len(prepared) + len(pieces) + 1),
        out_specs=VMEM,
        out_shape=jax.ShapeDtypeStruct((requests, width), BF16),
        scratch_shapes=[pltpu.VMEM((requests, width), F32)],
        compiler_params=pltpu.CompilerParams(vmem_limit_bytes=16 * MIB),
        name="attend_moved",
    )(*prepared, *pieces, after)


def combine_kernel(ranks, residents, kv_mine, ask_ref, *rest):
    payloads = rest[:ranks]
    out_ref, q_ref, own_ref = rest[ranks:]
    heads_mine = q_ref.shape[0]
    per = heads_mine // kv_mine
    scale = F32(1.0) / jnp.sqrt(F32(128.0))
    at = residents * heads_mine
    ask = ask_ref[...].astype(F32)
    for r in range(residents):
        for h in range(heads_mine):
            k_at = (heads_mine + h // per) * 128
            v_at = k_at + kv_mine * 128
            q_ref[h : h + 1, :] = ask[r : r + 1, h * 128 : (h + 1) * 128]
            own_ref[0, h : h + 1, :] = ask[r : r + 1, k_at : k_at + 128]
            own_ref[1, h : h + 1, :] = ask[r : r + 1, v_at : v_at + 128]
        own_score = jnp.sum(q_ref[...] * own_ref[0], axis=1, keepdims=True) * scale
        peaks, totals = [], []
        for t in range(ranks):
            stat = payloads[t][at : at + 3 * residents, :].astype(F32)
            peaks.append(row_to_column(stat[r : r + 1], heads_mine))
            total = stat[residents + r : residents + r + 1]
            total = total + stat[2 * residents + r : 2 * residents + r + 1]
            totals.append(row_to_column(total, heads_mine))
        top = own_score
        for t in range(ranks):
            top = jnp.maximum(top, peaks[t])
        own_weight = jnp.exp(own_score - top)
        denom = own_weight
        numer = own_weight.astype(BF16).astype(F32) * own_ref[1]
        for t in range(ranks):
            keep = jnp.exp(peaks[t] - top)
            denom = denom + keep * totals[t]
            numer = numer + keep * payloads[t][r * heads_mine : (r + 1) * heads_mine, :].astype(F32)
        result = numer / denom
        for h in range(heads_mine):
            out_ref[r : r + 1, h * 128 : (h + 1) * 128] = result[h : h + 1, :]


def combine_resident(asks, payloads, residents, heads_mine, kv_mine):
    return pl.pallas_call(
        functools.partial(combine_kernel, len(payloads), residents, kv_mine),
        in_specs=[VMEM] * (1 + len(payloads)),
        out_specs=VMEM,
        out_shape=jax.ShapeDtypeStruct((residents, heads_mine * 128), F32),
        scratch_shapes=[
            pltpu.VMEM((heads_mine, 128), F32),
            pltpu.VMEM((2, heads_mine, 128), F32),
        ],
        compiler_params=pltpu.CompilerParams(vmem_limit_bytes=8 * MIB),
        name="combine_resident",
    )(asks, *payloads)


def finish_kernel(kept_ref, place_ref, *rest):
    moved, out_ref = rest[:-1], rest[-1]
    residents = kept_ref.shape[0]
    decoded, width = out_ref.shape
    requests = decoded - residents
    row = iota((decoded, 128), 0)
    arrived = [ref[...].astype(F32) for ref in moved]
    for c in range(0, width, 128):
        kept = kept_ref[:, c : c + 128]
        line = jnp.concatenate([kept, jnp.zeros((requests, 128), F32)], axis=0)
        for b in range(len(moved)):
            for i in range(requests):
                at = (b + 1) * requests + i
                line = jnp.where(
                    place_ref[at : at + 1, :] == row, arrived[b][i : i + 1, c : c + 128], line
                )
        out_ref[:, c : c + 128] = line.astype(BF16)


def finish(kept, places, moved, requests):
    residents, width = kept.shape
    return pl.pallas_call(
        finish_kernel,
        in_specs=[VMEM] * (2 + len(moved)),
        out_specs=VMEM,
        out_shape=jax.ShapeDtypeStruct((residents + requests, width), BF16),
        compiler_params=pltpu.CompilerParams(vmem_limit_bytes=8 * MIB),
        name="finish",
    )(kept, places, *moved)


def swapped(x, axis, j, n):
    return lax.ppermute(x, axis, [(i, i ^ j) for i in range(n)])


def gather(x, axis, n):
    held, blocks = x, []
    for step in range(n.bit_length() - 1):
        blocks.append(swapped(held, axis, 1 << step, n))
        if 2 << step < n:
            one = blocks[-1]
            held = jnp.stack([held, one]) if step == 0 else jnp.concatenate([held, one])
    return blocks


def rotation(slots, requests, head_size):
    half = head_size // 2
    freq = THETA ** (-np.arange(half) * 2.0 / head_size)
    angle = np.repeat(np.arange(slots), requests)[:, None] * freq[None, :]
    cos, sin = np.cos(angle), np.sin(angle)
    return (
        np.concatenate([cos, cos], axis=1).astype(np.float32),
        np.concatenate([-sin, sin], axis=1).astype(np.float32),
    )


def per_device(
    mig_hidden,
    mig_dest,
    mig_count,
    attn_gain,
    kv_weight,
    k_gain,
    query,
    new_kv,
    k_cache,
    v_cache,
    lengths,
):
    insts = lax.axis_size("inst")
    ranks = lax.axis_size("tp")
    head_size = k_gain.shape[0]
    slots, requests, feats = mig_hidden.shape[1:]
    residents = k_cache.shape[1]
    heads = query.shape[2] // head_size
    kv_heads = kv_weight.shape[1] // 2 // head_size
    heads_mine = heads // ranks
    group = heads // kv_heads
    kv_mine = max(1, heads_mine // group)

    pieces, ask = project(
        mig_hidden[0], attn_gain, kv_weight, query[0], new_kv[0], ranks, group, kv_mine
    )
    pieces = [pieces[0]] + [swapped(pieces[j], "tp", j, ranks) for j in reversed(range(1, ranks))]
    asks = gather(ask, "inst", insts)
    payloads = attend_resident(lengths, query[0], k_cache[0], v_cache[0], ranks)
    payloads = [payloads[0]] + [swapped(payloads[j], "tp", j, ranks) for j in range(1, ranks)]
    kept = combine_resident(ask, payloads, residents, heads_mine, kv_mine)
    cos, sin = rotation(slots, requests, head_size)
    *prepared, places = prepare(
        mig_dest.T,
        mig_count.T,
        k_gain.reshape(1, head_size),
        cos,
        sin,
        asks,
        residents,
        heads_mine,
        kv_mine,
    )
    moved = attend_moved(prepared, pieces, payloads[1], requests, feats * ranks)
    moved = [swapped(moved, "inst", b, insts) for b in range(1, insts)]
    return finish(kept, places, moved, requests)[None]


def solution(mesh):
    placed = (
        P(("group", "inst"), None, None, "tp"),
        P("group", None),
        P("group", None),
        P("tp"),
        P("tp", None),
        P(),
        P(("group", "inst"), None, None),
        P(("group", "inst"), None, None),
        P(("group", "inst"), None, "tp", None),
        P(("group", "inst"), None, "tp", None),
        P(("group", "inst"), None),
    )
    return jax.shard_map(
        per_device,
        mesh=mesh,
        in_specs=placed,
        out_specs=P(("group", "inst"), None, "tp"),
        check_vma=False,
    )
```

```python
import functools

import jax
import jax.numpy as jnp
import numpy as np
from jax import lax
from jax.experimental import pallas as pl
from jax.experimental.pallas import tpu as pltpu
from jax.sharding import PartitionSpec as P

EPS = 1e-06
THETA = 1000000.0
ABSENT = -1e30
F32 = jnp.float32
BF16 = jnp.bfloat16
MIB = 1024 * 1024
CHUNK = 512

VMEM = pl.BlockSpec(memory_space=pltpu.VMEM)
SMEM = pl.BlockSpec(memory_space=pltpu.SMEM)
HBM = pl.BlockSpec(memory_space=pltpu.HBM)


def iota(shape, dim):
    return lax.broadcasted_iota(jnp.int32, shape, dim)


def column_to_row(column, period):
    n = column.shape[0]
    spread = jnp.where(iota((n, 128), 0) % period == iota((n, 128), 1), column, 0.0)
    return jnp.sum(spread.reshape(n // period, period, 128), axis=1)


def row_to_column(row, n):
    return jnp.sum(
        jnp.where(iota((n, 128), 0) == iota((n, 128), 1), row, 0.0), axis=1, keepdims=True
    )


def split_bf16(x):
    high = x.astype(BF16)
    return high, (x - high.astype(F32)).astype(BF16)


def project_kernel(ranks, group, gain_hbm, x_hbm, w_hbm, q_hbm, own_hbm, *rest):
    outs, ask_ref = rest[:ranks], rest[ranks]
    gain_ref, x_ref, w_ref, acc_ref, in_sems, w_sems = rest[ranks + 1 :]
    slots, requests, feats = x_ref.shape
    rows = slots * requests
    piece = outs[0].shape[1] // 2
    kv_width = w_hbm.shape[1] // 2
    heads_mine = kv_width // 128 * group // ranks
    rank = lax.axis_index("tp")

    def first_column(target):
        return pl.multiple_of(target * heads_mine // group * 128, 128)

    gain_copy = pltpu.make_async_copy(gain_hbm, gain_ref, in_sems.at[0])
    gain_copy.start()
    x_copy = pltpu.make_async_copy(x_hbm, x_ref, in_sems.at[1])
    x_copy.start()
    cuts = list(range(0, feats, CHUNK)) + [feats]
    chunks = list(zip(cuts[:-1], cuts[1:]))
    copies = []
    for i, (low, high) in enumerate(chunks):
        copies.append(
            pltpu.make_async_copy(
                w_hbm.at[low:high, :], w_ref.at[low:high, :], w_sems.at[i]
            )
        )
        copies[-1].start()
    mine = heads_mine * 128
    q_first = pl.multiple_of(rank * mine, 128)
    asking = [
        pltpu.make_async_copy(
            q_hbm.at[:, pl.ds(q_first, mine)], ask_ref.at[:, :mine], in_sems.at[2]
        )
    ]
    for i in range(2):
        asking.append(
            pltpu.make_async_copy(
                own_hbm.at[:, pl.ds(i * kv_width + first_column(rank), piece)],
                ask_ref.at[:, mine + i * piece : mine + (i + 1) * piece],
                in_sems.at[3 + i],
            )
        )
    for copy in asking:
        copy.start()
    gain_copy.wait()
    x_copy.wait()
    squares = jnp.zeros((rows, 128), F32)
    for i, (low, high) in enumerate(chunks):
        parts = []
        for c in range(low, high, 128):
            width = min(128, high - c)
            x = x_ref[:, :, c : c + width].astype(F32).reshape(rows, width)
            gain = gain_ref[c : c + width].astype(F32).reshape(1, width)
            parts.append((x * gain).astype(BF16))
            x = x * x
            if width < 128:
                x = jnp.concatenate([x, jnp.zeros((rows, 128 - width), F32)], axis=1)
            squares = squares + x
        xg = parts[0] if len(parts) == 1 else jnp.concatenate(parts, axis=1)
        copies[i].wait()
        for n in range(0, 2 * kv_width, 512):
            part = jnp.dot(xg, w_ref[low:high, n : n + 512], preferred_element_type=F32)
            if i == 0:
                acc_ref[:, n : n + 512] = part
            else:
                acc_ref[:, n : n + 512] += part
    sq = column_to_row(jnp.sum(squares, axis=1, keepdims=True), 128)
    high, low = split_bf16(sq)
    tail = jnp.concatenate([high.astype(F32), low.astype(F32)], axis=0)
    if outs[0].shape[0] - rows > tail.shape[0]:
        fill = outs[0].shape[0] - rows - tail.shape[0]
        tail = jnp.concatenate([tail, jnp.zeros((fill, 128), F32)], axis=0)
    extra = jnp.concatenate([tail.astype(BF16)] * (2 * piece // 128), axis=1)
    for j in range(ranks):
        first = first_column(rank ^ j)
        outs[j][:rows, :piece] = acc_ref[:, pl.ds(first, piece)].astype(BF16)
        outs[j][:rows, piece:] = acc_ref[:, pl.ds(kv_width + first, piece)].astype(BF16)
        outs[j][rows:, :] = extra
    for copy in asking:
        copy.wait()


def project(x, gain, weight, query, own, ranks, group, kv_mine):
    slots, requests, feats = x.shape
    rows = slots * requests
    piece = kv_mine * 128
    extra = -(-2 * (rows // 128) // 8) * 8
    decoded, q_width = query.shape
    outs = pl.pallas_call(
        functools.partial(project_kernel, ranks, group),
        in_specs=[HBM] * 5,
        out_specs=[VMEM] * (ranks + 1),
        out_shape=[jax.ShapeDtypeStruct((rows + extra, 2 * piece), BF16)] * ranks
        + [jax.ShapeDtypeStruct((decoded, q_width // ranks + 2 * piece), BF16)],
        scratch_shapes=[
            pltpu.VMEM((feats,), BF16),
            pltpu.VMEM((slots, requests, feats), BF16),
            pltpu.VMEM(weight.shape, BF16),
            pltpu.VMEM((rows, weight.shape[1]), F32),
            pltpu.SemaphoreType.DMA((5,)),
            pltpu.SemaphoreType.DMA((-(-feats // CHUNK),)),
        ],
        compiler_params=pltpu.CompilerParams(vmem_limit_bytes=60 * MIB),
        cost_estimate=pl.CostEstimate(
            flops=2 * rows * feats * weight.shape[1],
            bytes_accessed=2 * feats * weight.shape[1],
            transcendentals=0,
        ),
        name="project",
    )(gain, x, weight, query, own)
    return outs[:ranks], outs[ranks]


def resident_kernel(ranks, len_hbm, q_hbm, k_hbm, v_hbm, *rest):
    outs = rest[:ranks]
    len_ref, q_ref, k_buf, v_buf, o_all, s_all, in_sems, sems = rest[ranks:]
    residents, positions, width = k_buf.shape
    len_copy = pltpu.make_async_copy(len_hbm, len_ref, in_sems.at[0])
    q_copy = pltpu.make_async_copy(q_hbm, q_ref, in_sems.at[1])
    k_copies = [
        pltpu.make_async_copy(k_hbm.at[r], k_buf.at[r], sems.at[0, r]) for r in range(residents)
    ]
    v_copies = [
        pltpu.make_async_copy(v_hbm.at[r], v_buf.at[r], sems.at[1, r]) for r in range(residents)
    ]
    len_copy.start()
    q_copy.start()
    for r in range(residents + 1):
        if r < residents:
            k_copies[r].start()
        if r > 0:
            v_copies[r - 1].start()
    heads = q_ref.shape[1]
    kv_heads = width // 128
    group = heads // kv_heads
    pair_rows = 2 * group
    heads_mine = heads // ranks
    rank = lax.axis_index("tp")
    top_half = iota((pair_rows, 128), 0) < group
    pairs = [slice(p * pair_rows, (p + 1) * pair_rows) for p in range(kv_heads // 2)]
    position = rank * positions + iota((heads, positions), 1)
    scale = F32(1.0) / jnp.sqrt(F32(128.0))
    diagonal = iota((heads, 128), 0) % heads_mine == iota((heads, 128), 1)

    def scores_of(r):
        parts = []
        for p, rows in enumerate(pairs):
            q = q_ref[r, rows, :]
            zero = jnp.zeros_like(q)
            lhs = jnp.concatenate(
                [jnp.where(top_half, q, zero), jnp.where(top_half, zero, q)], axis=1
            )
            parts.append(
                lax.dot_general(
                    lhs,
                    k_buf[r, :, p * 256 : (p + 1) * 256],
                    (((1,), (1,)), ((), ())),
                    preferred_element_type=F32,
                )
            )
        return jnp.concatenate(parts, axis=0)

    def to_rows(column):
        spread = jnp.where(diagonal, column, 0.0)
        return jnp.sum(spread.reshape(ranks, heads_mine, 128), axis=1)

    def weights_of(r, scores):
        valid = position < len_ref[0, r]
        scores = jnp.where(valid, scores * scale, ABSENT)
        peak = jnp.max(scores, axis=1, keepdims=True).astype(BF16).astype(F32)
        weights = jnp.where(valid, jnp.exp(scores - peak), 0.0)
        total = to_rows(jnp.sum(weights, axis=1, keepdims=True))
        high, low = split_bf16(total)
        s_all[r, 0] = to_rows(peak)
        s_all[r, 1] = high.astype(F32)
        s_all[r, 2] = low.astype(F32)
        return weights.astype(BF16)

    def add_values(r, weights):
        for p, rows in enumerate(pairs):
            both = jnp.dot(
                weights[rows], v_buf[r, :, p * 256 : (p + 1) * 256], preferred_element_type=F32
            )
            o_all[r, rows, :] = jnp.where(top_half, both[:, :128], both[:, 128:])

    len_copy.wait()
    q_copy.wait()
    k_copies[0].wait()
    scores = scores_of(0)
    for r in range(residents):
        following = None
        if r + 1 < residents:
            k_copies[r + 1].wait()
            following = scores_of(r + 1)
        weights = weights_of(r, scores)
        v_copies[r].wait()
        add_values(r, weights)
        scores = following
    filled = residents * (heads_mine + 3)
    for j in range(ranks):
        target = rank ^ j
        first = pl.multiple_of(target * heads_mine, heads_mine)
        parts = [o_all[r, pl.ds(first, heads_mine), :] for r in range(residents)]
        parts += [s_all[r, i, pl.ds(target, 1), :] for i in range(3) for r in range(residents)]
        if outs[j].shape[0] > filled:
            parts.append(jnp.zeros((outs[j].shape[0] - filled, 128), F32))
        outs[j][...] = jnp.concatenate(parts, axis=0).astype(BF16)


def attend_resident(lengths, queries, k_cache, v_cache, ranks):
    residents, positions, width = k_cache.shape
    heads = queries.shape[1]
    heads_mine = heads // ranks
    rows = -(-(residents * (heads_mine + 3)) // 16) * 16
    return pl.pallas_call(
        functools.partial(resident_kernel, ranks),
        in_specs=[HBM] * 4,
        out_specs=[VMEM] * ranks,
        out_shape=[jax.ShapeDtypeStruct((rows, 128), BF16)] * ranks,
        scratch_shapes=[
            pltpu.SMEM(lengths.shape, jnp.int32),
            pltpu.VMEM(queries.shape, BF16),
            pltpu.VMEM((residents, positions, width), BF16),
            pltpu.VMEM((residents, positions, width), BF16),
            pltpu.VMEM((residents, heads, 128), F32),
            pltpu.VMEM((residents, 3, ranks, 128), F32),
            pltpu.SemaphoreType.DMA((2,)),
            pltpu.SemaphoreType.DMA((2, residents)),
        ],
        compiler_params=pltpu.CompilerParams(vmem_limit_bytes=60 * MIB),
        cost_estimate=pl.CostEstimate(
            flops=4 * residents * heads * positions * 128,
            bytes_accessed=4 * residents * positions * width,
            transcendentals=residents * heads * positions,
        ),
        name="attend_resident",
    )(lengths, queries, k_cache, v_cache)


def block_of(blocks, b):
    step = b.bit_length() - 1
    array = blocks[step]
    return array if step == 0 else array.at[b - (1 << step)]


def prepare_kernel(insts, steps, residents, kv_mine, dest_ref, count_ref, gain_ref, cos_ref, sin_ref, *rest):
    asks, rest = rest[:steps], rest[steps:]
    q_out, own_out, limit_out, cos_out, sin_out, place_out, line_ref, q_ref, k_ref = rest
    requests = dest_ref.shape[0]
    rows = q_out.shape[0]
    heads_mine = rows // requests
    per = heads_mine // kv_mine
    decoded = asks[0].shape[0]
    here = lax.axis_index("inst")
    ask_row = iota((decoded, line_ref.shape[1]), 0)
    limit = jnp.zeros((rows, 128), jnp.int32)
    for r in range(requests):
        dest = dest_ref[r, here]
        limit = jnp.where(iota((rows, 128), 0) // heads_mine == r, count_ref[r, here], limit)
        place = jnp.int32(residents)
        for s in range(insts):
            for c in range(requests):
                place += jnp.where((dest_ref[c, s] == dest) & (here > s), 1, 0).astype(jnp.int32)
        for b in range(1, insts):

            @pl.when(here ^ b == dest)
            def _():
                ask = block_of(asks, b)[...].astype(F32)
                line_ref[r : r + 1, :] = jnp.sum(
                    jnp.where(ask_row == place, ask, 0.0), axis=0, keepdims=True
                )

        line = line_ref[r : r + 1, :]
        for h in range(heads_mine):
            at = r * heads_mine + h
            k_at = (heads_mine + h // per) * 128
            v_at = k_at + kv_mine * 128
            q_ref[at : at + 1, :] = line[:, h * 128 : (h + 1) * 128]
            k_ref[at : at + 1, :] = line[:, k_at : k_at + 128]
            own_out[0, at : at + 1, :] = line[:, v_at : v_at + 128]
    scale = F32(1.0) / jnp.sqrt(F32(128.0))
    q = q_ref[...]
    q_out[...] = q.astype(BF16)
    own_out[1] = jnp.broadcast_to(
        jnp.sum(q * k_ref[...], axis=1, keepdims=True) * scale, (rows, 128)
    )
    limit_out[...] = limit
    gain = gain_ref[...].astype(F32)
    cos_out[...] = cos_ref[...] * gain
    sin_out[...] = sin_ref[...] * pltpu.roll(jnp.broadcast_to(gain, (8, 128)), 64, 1)[:1]
    places = jnp.full(place_out.shape, -1, jnp.int32)
    row = iota(place_out.shape, 0)
    place = jnp.int32(residents)
    for s in range(insts):
        for c in range(requests):
            mine = dest_ref[c, s] == here
            places = jnp.where((row == (here ^ s) * requests + c) & mine, place, places)
            place += jnp.where(mine, 1, 0).astype(jnp.int32)
    place_out[...] = places


def prepare(dest, count, k_gain, cos, sin, asks, residents, heads_mine, kv_mine):
    requests, insts = dest.shape
    rows = requests * heads_mine
    return pl.pallas_call(
        functools.partial(prepare_kernel, insts, len(asks), residents, kv_mine),
        in_specs=[SMEM] * 2 + [VMEM] * (3 + len(asks)),
        out_specs=[VMEM] * 6,
        out_shape=[
            jax.ShapeDtypeStruct((rows, 128), BF16),
            jax.ShapeDtypeStruct((2, rows, 128), F32),
            jax.ShapeDtypeStruct((rows, 128), jnp.int32),
            jax.ShapeDtypeStruct(cos.shape, F32),
            jax.ShapeDtypeStruct(sin.shape, F32),
            jax.ShapeDtypeStruct((insts * requests, 128), jnp.int32),
        ],
        scratch_shapes=[
            pltpu.VMEM((requests, asks[0].shape[1]), F32),
            pltpu.VMEM((rows, 128), F32),
            pltpu.VMEM((rows, 128), F32),
        ],
        compiler_params=pltpu.CompilerParams(vmem_limit_bytes=16 * MIB),
        name="prepare",
    )(dest, count, k_gain, cos, sin, *asks)


def moved_kernel(ranks, features, q_ref, own_ref, limit_ref, cos_ref, sin_ref, *rest):
    pieces = rest[:ranks]
    out_ref, line_ref = rest[ranks:]
    requests = out_ref.shape[0]
    tokens = cos_ref.shape[0]
    piece = pieces[0].shape[1] // 2
    kv_mine = piece // 128
    rows = q_ref.shape[0]
    heads_mine = rows // requests
    scale = F32(1.0) / jnp.sqrt(F32(128.0))

    tail = pieces[0][tokens:, :].astype(F32)
    for t in range(1, ranks):
        tail = tail + pieces[t][tokens:, :].astype(F32)
    blocks = tokens // 128
    squares = tail[:blocks, :128] + tail[blocks : 2 * blocks, :128]
    squares = jnp.concatenate(
        [row_to_column(squares[b : b + 1], 128) for b in range(blocks)], axis=0
    )
    token_scale = lax.rsqrt(squares / features + EPS)

    def column_block(c):
        total = pieces[0][:tokens, c : c + 128].astype(F32)
        for t in range(1, ranks):
            total = total + pieces[t][:tokens, c : c + 128].astype(F32)
        return total * token_scale

    q = q_ref[...]
    which = iota((rows, tokens), 0) % heads_mine // (heads_mine // kv_mine)
    scores = None
    for h in range(kv_mine):
        key = column_block(h * 128)
        key = key * lax.rsqrt(jnp.mean(key * key, axis=1, keepdims=True) + EPS)
        key = key * cos_ref[...] + pltpu.roll(key, 64, 1) * sin_ref[...]
        part = lax.dot_general(
            q, key.astype(BF16), (((1,), (1,)), ((), ())), preferred_element_type=F32
        )
        scores = part if scores is None else jnp.where(which == h, part, scores)
    token = iota((rows, tokens), 1)
    limit = jnp.concatenate([limit_ref[...]] * (tokens // 128), axis=1)
    valid = (token % requests == iota((rows, tokens), 0) // heads_mine) & (
        token // requests < limit
    )
    scores = jnp.where(valid, scores * scale, ABSENT)
    own_score = own_ref[1]
    top = jnp.maximum(jnp.max(scores, axis=1, keepdims=True), own_score)
    weights = jnp.where(
        valid, jnp.exp(scores - jnp.concatenate([top] * (tokens // 128), axis=1)), 0.0
    )
    own_weight = jnp.exp(own_score - top)
    total = jnp.sum(weights, axis=1, keepdims=True) + own_weight
    weights = weights.astype(BF16)
    summed = None
    for h in range(kv_mine):
        value = column_block(piece + h * 128).astype(BF16)
        part = jnp.dot(weights, value, preferred_element_type=F32)
        summed = part if summed is None else jnp.where(which[:, :128] == h, part, summed)
    summed = summed + own_weight.astype(BF16).astype(F32) * own_ref[0]
    result = summed / total
    for r in range(requests):
        for h in range(heads_mine):
            at = r * heads_mine + h
            line_ref[r : r + 1, h * 128 : (h + 1) * 128] = result[at : at + 1, :]
    out_ref[...] = line_ref[...].astype(BF16)


def attend_moved(prepared, pieces, requests, features):
    rows = prepared[0].shape[0]
    width = rows // requests * 128
    return pl.pallas_call(
        functools.partial(moved_kernel, len(pieces), features),
        in_specs=[VMEM] * (len(prepared) + len(pieces)),
        out_specs=VMEM,
        out_shape=jax.ShapeDtypeStruct((requests, width), BF16),
        scratch_shapes=[pltpu.VMEM((requests, width), F32)],
        compiler_params=pltpu.CompilerParams(vmem_limit_bytes=16 * MIB),
        name="attend_moved",
    )(*prepared, *pieces)


def combine_kernel(ranks, residents, kv_mine, ask_ref, *rest):
    payloads = rest[:ranks]
    out_ref, q_ref, own_ref = rest[ranks:]
    heads_mine = q_ref.shape[0]
    per = heads_mine // kv_mine
    scale = F32(1.0) / jnp.sqrt(F32(128.0))
    at = residents * heads_mine
    ask = ask_ref[...].astype(F32)
    for r in range(residents):
        for h in range(heads_mine):
            k_at = (heads_mine + h // per) * 128
            v_at = k_at + kv_mine * 128
            q_ref[h : h + 1, :] = ask[r : r + 1, h * 128 : (h + 1) * 128]
            own_ref[0, h : h + 1, :] = ask[r : r + 1, k_at : k_at + 128]
            own_ref[1, h : h + 1, :] = ask[r : r + 1, v_at : v_at + 128]
        own_score = jnp.sum(q_ref[...] * own_ref[0], axis=1, keepdims=True) * scale
        peaks, totals = [], []
        for t in range(ranks):
            stat = payloads[t][at : at + 3 * residents, :].astype(F32)
            peaks.append(row_to_column(stat[r : r + 1], heads_mine))
            total = stat[residents + r : residents + r + 1]
            total = total + stat[2 * residents + r : 2 * residents + r + 1]
            totals.append(row_to_column(total, heads_mine))
        top = own_score
        for t in range(ranks):
            top = jnp.maximum(top, peaks[t])
        own_weight = jnp.exp(own_score - top)
        denom = own_weight
        numer = own_weight.astype(BF16).astype(F32) * own_ref[1]
        for t in range(ranks):
            keep = jnp.exp(peaks[t] - top)
            denom = denom + keep * totals[t]
            numer = numer + keep * payloads[t][r * heads_mine : (r + 1) * heads_mine, :].astype(F32)
        result = numer / denom
        for h in range(heads_mine):
            out_ref[r : r + 1, h * 128 : (h + 1) * 128] = result[h : h + 1, :]


def combine_resident(asks, payloads, residents, heads_mine, kv_mine):
    return pl.pallas_call(
        functools.partial(combine_kernel, len(payloads), residents, kv_mine),
        in_specs=[VMEM] * (1 + len(payloads)),
        out_specs=VMEM,
        out_shape=jax.ShapeDtypeStruct((residents, heads_mine * 128), F32),
        scratch_shapes=[
            pltpu.VMEM((heads_mine, 128), F32),
            pltpu.VMEM((2, heads_mine, 128), F32),
        ],
        compiler_params=pltpu.CompilerParams(vmem_limit_bytes=8 * MIB),
        name="combine_resident",
    )(asks, *payloads)


def finish_kernel(kept_ref, place_ref, *rest):
    moved, out_ref = rest[:-1], rest[-1]
    residents = kept_ref.shape[0]
    decoded, width = out_ref.shape
    requests = decoded - residents
    row = iota((decoded, 128), 0)
    arrived = [ref[...].astype(F32) for ref in moved]
    for c in range(0, width, 128):
        kept = kept_ref[:, c : c + 128]
        line = jnp.concatenate([kept, jnp.zeros((requests, 128), F32)], axis=0)
        for b in range(len(moved)):
            for i in range(requests):
                at = (b + 1) * requests + i
                line = jnp.where(
                    place_ref[at : at + 1, :] == row, arrived[b][i : i + 1, c : c + 128], line
                )
        out_ref[:, c : c + 128] = line.astype(BF16)


def finish(kept, places, moved, requests):
    residents, width = kept.shape
    return pl.pallas_call(
        finish_kernel,
        in_specs=[VMEM] * (2 + len(moved)),
        out_specs=VMEM,
        out_shape=jax.ShapeDtypeStruct((residents + requests, width), BF16),
        compiler_params=pltpu.CompilerParams(vmem_limit_bytes=8 * MIB),
        name="finish",
    )(kept, places, *moved)


def swapped(x, axis, j, n):
    return lax.ppermute(x, axis, [(i, i ^ j) for i in range(n)])


def gather(x, axis, n):
    held, blocks = x, []
    for step in range(n.bit_length() - 1):
        blocks.append(swapped(held, axis, 1 << step, n))
        if 2 << step < n:
            one = blocks[-1]
            held = jnp.stack([held, one]) if step == 0 else jnp.concatenate([held, one])
    return blocks


def rotation(slots, requests, head_size):
    half = head_size // 2
    freq = THETA ** (-np.arange(half) * 2.0 / head_size)
    angle = np.repeat(np.arange(slots), requests)[:, None] * freq[None, :]
    cos, sin = np.cos(angle), np.sin(angle)
    return (
        np.concatenate([cos, cos], axis=1).astype(np.float32),
        np.concatenate([-sin, sin], axis=1).astype(np.float32),
    )


def per_device(
    mig_hidden,
    mig_dest,
    mig_count,
    attn_gain,
    kv_weight,
    k_gain,
    query,
    new_kv,
    k_cache,
    v_cache,
    lengths,
):
    insts = lax.axis_size("inst")
    ranks = lax.axis_size("tp")
    head_size = k_gain.shape[0]
    slots, requests, feats = mig_hidden.shape[1:]
    residents = k_cache.shape[1]
    heads = query.shape[2] // head_size
    kv_heads = kv_weight.shape[1] // 2 // head_size
    heads_mine = heads // ranks
    group = heads // kv_heads
    kv_mine = max(1, heads_mine // group)

    pieces, ask = project(
        mig_hidden[0], attn_gain, kv_weight, query[0], new_kv[0], ranks, group, kv_mine
    )
    pieces = [pieces[0]] + [swapped(pieces[j], "tp", j, ranks) for j in reversed(range(1, ranks))]
    asks = gather(ask, "inst", insts)
    queries = query[0].reshape(query.shape[1], heads, head_size)
    payloads = attend_resident(lengths, queries, k_cache[0], v_cache[0], ranks)
    payloads = [payloads[0]] + [swapped(payloads[j], "tp", j, ranks) for j in range(1, ranks)]
    cos, sin = rotation(slots, requests, head_size)
    *prepared, places = prepare(
        mig_dest.T,
        mig_count.T,
        k_gain.reshape(1, head_size),
        cos,
        sin,
        asks,
        residents,
        heads_mine,
        kv_mine,
    )
    prepared[0], payloads[0] = lax.optimization_barrier((prepared[0], payloads[0]))
    moved = attend_moved(prepared, pieces, requests, feats * ranks)
    kept = combine_resident(ask, payloads, residents, heads_mine, kv_mine)
    moved = [swapped(moved, "inst", b, insts) for b in range(1, insts)]
    return finish(kept, places, moved, requests)[None]


def solution(mesh):
    placed = (
        P(("group", "inst"), None, None, "tp"),
        P("group", None),
        P("group", None),
        P("tp"),
        P("tp", None),
        P(),
        P(("group", "inst"), None, None),
        P(("group", "inst"), None, None),
        P(("group", "inst"), None, "tp", None),
        P(("group", "inst"), None, "tp", None),
        P(("group", "inst"), None),
    )
    return jax.shard_map(
        per_device,
        mesh=mesh,
        in_specs=placed,
        out_specs=P(("group", "inst"), None, "tp"),
        check_vma=False,
    )
```

```python
import functools

import jax
import jax.numpy as jnp
import numpy as np
from jax import lax
from jax.experimental import pallas as pl
from jax.experimental.pallas import tpu as pltpu
from jax.sharding import PartitionSpec as P

EPS = 1e-06
THETA = 1000000.0
ABSENT = -1e30
F32 = jnp.float32
BF16 = jnp.bfloat16
MIB = 1024 * 1024
CHUNK = 512

VMEM = pl.BlockSpec(memory_space=pltpu.VMEM)
SMEM = pl.BlockSpec(memory_space=pltpu.SMEM)
HBM = pl.BlockSpec(memory_space=pltpu.HBM)


def iota(shape, dim):
    return lax.broadcasted_iota(jnp.int32, shape, dim)


def column_to_row(column, period):
    n = column.shape[0]
    spread = jnp.where(iota((n, 128), 0) % period == iota((n, 128), 1), column, 0.0)
    return jnp.sum(spread.reshape(n // period, period, 128), axis=1)


def row_to_column(row, n):
    return jnp.sum(
        jnp.where(iota((n, 128), 0) == iota((n, 128), 1), row, 0.0), axis=1, keepdims=True
    )


def split_bf16(x):
    high = x.astype(BF16)
    return high, (x - high.astype(F32)).astype(BF16)


def project_kernel(ranks, group, gain_hbm, x_hbm, w_hbm, q_hbm, own_hbm, *rest):
    outs, ask_ref = rest[:ranks], rest[ranks]
    gain_ref, x_ref, w_ref, acc_ref, in_sems, w_sems = rest[ranks + 1 :]
    slots, requests, feats = x_ref.shape
    rows = slots * requests
    piece = outs[0].shape[1] // 2
    kv_width = w_hbm.shape[1] // 2
    heads_mine = kv_width // 128 * group // ranks
    rank = lax.axis_index("tp")

    def first_column(target):
        return pl.multiple_of(target * heads_mine // group * 128, 128)

    gain_copy = pltpu.make_async_copy(gain_hbm, gain_ref, in_sems.at[0])
    gain_copy.start()
    x_copy = pltpu.make_async_copy(x_hbm, x_ref, in_sems.at[1])
    x_copy.start()
    cuts = list(range(0, feats, CHUNK)) + [feats]
    chunks = list(zip(cuts[:-1], cuts[1:]))
    copies = []
    for i, (low, high) in enumerate(chunks):
        copies.append(
            pltpu.make_async_copy(
                w_hbm.at[low:high, :], w_ref.at[low:high, :], w_sems.at[i]
            )
        )
        copies[-1].start()
    mine = heads_mine * 128
    q_first = pl.multiple_of(rank * mine, 128)
    asking = [
        pltpu.make_async_copy(
            q_hbm.at[:, pl.ds(q_first, mine)], ask_ref.at[:, :mine], in_sems.at[2]
        )
    ]
    for i in range(2):
        asking.append(
            pltpu.make_async_copy(
                own_hbm.at[:, pl.ds(i * kv_width + first_column(rank), piece)],
                ask_ref.at[:, mine + i * piece : mine + (i + 1) * piece],
                in_sems.at[3 + i],
            )
        )
    for copy in asking:
        copy.start()
    gain_copy.wait()
    x_copy.wait()
    squares = jnp.zeros((rows, 128), F32)
    for i, (low, high) in enumerate(chunks):
        parts = []
        for c in range(low, high, 128):
            width = min(128, high - c)
            x = x_ref[:, :, c : c + width].astype(F32).reshape(rows, width)
            gain = gain_ref[c : c + width].astype(F32).reshape(1, width)
            parts.append((x * gain).astype(BF16))
            x = x * x
            if width < 128:
                x = jnp.concatenate([x, jnp.zeros((rows, 128 - width), F32)], axis=1)
            squares = squares + x
        xg = parts[0] if len(parts) == 1 else jnp.concatenate(parts, axis=1)
        copies[i].wait()
        for n in range(0, 2 * kv_width, 512):
            part = jnp.dot(xg, w_ref[low:high, n : n + 512], preferred_element_type=F32)
            if i == 0:
                acc_ref[:, n : n + 512] = part
            else:
                acc_ref[:, n : n + 512] += part
    sq = column_to_row(jnp.sum(squares, axis=1, keepdims=True), 128)
    high, low = split_bf16(sq)
    tail = jnp.concatenate([high.astype(F32), low.astype(F32)], axis=0)
    if outs[0].shape[0] - rows > tail.shape[0]:
        fill = outs[0].shape[0] - rows - tail.shape[0]
        tail = jnp.concatenate([tail, jnp.zeros((fill, 128), F32)], axis=0)
    extra = jnp.concatenate([tail.astype(BF16)] * (2 * piece // 128), axis=1)
    for j in range(ranks):
        first = first_column(rank ^ j)
        outs[j][:rows, :piece] = acc_ref[:, pl.ds(first, piece)].astype(BF16)
        outs[j][:rows, piece:] = acc_ref[:, pl.ds(kv_width + first, piece)].astype(BF16)
        outs[j][rows:, :] = extra
    for copy in asking:
        copy.wait()


def project(x, gain, weight, query, own, ranks, group, kv_mine):
    slots, requests, feats = x.shape
    rows = slots * requests
    piece = kv_mine * 128
    extra = -(-2 * (rows // 128) // 8) * 8
    decoded, q_width = query.shape
    outs = pl.pallas_call(
        functools.partial(project_kernel, ranks, group),
        in_specs=[HBM] * 5,
        out_specs=[VMEM] * (ranks + 1),
        out_shape=[jax.ShapeDtypeStruct((rows + extra, 2 * piece), BF16)] * ranks
        + [jax.ShapeDtypeStruct((decoded, q_width // ranks + 2 * piece), BF16)],
        scratch_shapes=[
            pltpu.VMEM((feats,), BF16),
            pltpu.VMEM((slots, requests, feats), BF16),
            pltpu.VMEM(weight.shape, BF16),
            pltpu.VMEM((rows, weight.shape[1]), F32),
            pltpu.SemaphoreType.DMA((5,)),
            pltpu.SemaphoreType.DMA((-(-feats // CHUNK),)),
        ],
        compiler_params=pltpu.CompilerParams(vmem_limit_bytes=56 * MIB),
        cost_estimate=pl.CostEstimate(
            flops=2 * rows * feats * weight.shape[1],
            bytes_accessed=2 * feats * weight.shape[1],
            transcendentals=0,
        ),
        name="project",
    )(gain, x, weight, query, own)
    return outs[:ranks], outs[ranks]


def resident_kernel(ranks, len_hbm, q_hbm, k_hbm, v_hbm, *rest):
    outs = rest[:ranks]
    len_ref, q_ref, q_all, k_buf, v_buf, o_all, s_all, in_sems, sems = rest[ranks:]
    residents, positions, width = k_buf.shape
    len_copy = pltpu.make_async_copy(len_hbm, len_ref, in_sems.at[0])
    q_copy = pltpu.make_async_copy(q_hbm, q_ref, in_sems.at[1])
    len_copy.start()
    q_copy.start()
    copies = []
    for r in range(residents):
        copies.append(
            (
                pltpu.make_async_copy(k_hbm.at[r], k_buf.at[r], sems.at[0, r]),
                pltpu.make_async_copy(v_hbm.at[r], v_buf.at[r], sems.at[1, r]),
            )
        )
    for pair in copies:
        for copy in pair:
            copy.start()
    heads = q_ref.shape[1] // 128
    kv_heads = width // 128
    group = heads // kv_heads
    pair_rows = 2 * group
    heads_mine = heads // ranks
    rank = lax.axis_index("tp")
    top_half = iota((pair_rows, 128), 0) < group
    position = iota((pair_rows, positions), 1)
    scale = F32(1.0) / jnp.sqrt(F32(128.0))
    diagonal = iota((heads, 128), 0) % heads_mine == iota((heads, 128), 1)

    def to_rows(columns):
        spread = jnp.where(diagonal, jnp.concatenate(columns, axis=0), 0.0)
        return jnp.sum(spread.reshape(ranks, heads_mine, 128), axis=1)

    len_copy.wait()
    q_copy.wait()
    for h in range(heads):
        q_all[h * 8 : h * 8 + residents, :] = q_ref[:residents, h * 128 : (h + 1) * 128].astype(F32)
    peaks, totals = [], []
    for r in range(residents):
        q_mine = q_all[pl.ds(r, heads, stride=8), :]
        peaks.append([])
        totals.append([])
        valid = position < len_ref[0, r] - rank * positions
        copies[r][0].wait()
        weights = []
        for p in range(kv_heads // 2):
            q = q_mine[p * pair_rows : (p + 1) * pair_rows].astype(BF16)
            zero = jnp.zeros_like(q)
            lhs = jnp.concatenate(
                [jnp.where(top_half, q, zero), jnp.where(top_half, zero, q)], axis=1
            )
            scores = lax.dot_general(
                lhs,
                k_buf[r, :, p * 256 : (p + 1) * 256],
                (((1,), (1,)), ((), ())),
                preferred_element_type=F32,
            )
            scores = jnp.where(valid, scores * scale, ABSENT)
            peak = jnp.max(scores, axis=1, keepdims=True).astype(BF16).astype(F32)
            weight = jnp.where(valid, jnp.exp(scores - peak), 0.0)
            peaks[r].append(peak)
            totals[r].append(jnp.sum(weight, axis=1, keepdims=True))
            weights.append(weight.astype(BF16))
        copies[r][1].wait()
        for p in range(kv_heads // 2):
            both = jnp.dot(
                weights[p], v_buf[r, :, p * 256 : (p + 1) * 256], preferred_element_type=F32
            )
            o_all[r, p * pair_rows : (p + 1) * pair_rows, :] = jnp.where(
                top_half, both[:, :128], both[:, 128:]
            )
    for r in range(residents):
        s_all[r, 0] = to_rows(peaks[r])
        high, low = split_bf16(to_rows(totals[r]))
        s_all[r, 1] = high.astype(F32)
        s_all[r, 2] = low.astype(F32)
    filled = residents * (heads_mine + 3)
    for j in range(ranks):
        target = rank ^ j
        first = pl.multiple_of(target * heads_mine, heads_mine)
        parts = [o_all[r, pl.ds(first, heads_mine), :] for r in range(residents)]
        parts += [s_all[r, i, pl.ds(target, 1), :] for i in range(3) for r in range(residents)]
        if outs[j].shape[0] > filled:
            parts.append(jnp.zeros((outs[j].shape[0] - filled, 128), F32))
        outs[j][...] = jnp.concatenate(parts, axis=0).astype(BF16)


def attend_resident(lengths, query, k_cache, v_cache, ranks):
    residents, positions, width = k_cache.shape
    heads = query.shape[1] // 128
    heads_mine = heads // ranks
    rows = -(-(residents * (heads_mine + 3)) // 16) * 16
    return pl.pallas_call(
        functools.partial(resident_kernel, ranks),
        in_specs=[HBM] * 4,
        out_specs=[VMEM] * ranks,
        out_shape=[jax.ShapeDtypeStruct((rows, 128), BF16)] * ranks,
        scratch_shapes=[
            pltpu.SMEM(lengths.shape, jnp.int32),
            pltpu.VMEM(query.shape, BF16),
            pltpu.VMEM((heads * 8, 128), F32),
            pltpu.VMEM((residents, positions, width), BF16),
            pltpu.VMEM((residents, positions, width), BF16),
            pltpu.VMEM((residents, heads, 128), F32),
            pltpu.VMEM((residents, 3, ranks, 128), F32),
            pltpu.SemaphoreType.DMA((2,)),
            pltpu.SemaphoreType.DMA((2, residents)),
        ],
        compiler_params=pltpu.CompilerParams(vmem_limit_bytes=56 * MIB),
        cost_estimate=pl.CostEstimate(
            flops=4 * residents * heads * positions * 128,
            bytes_accessed=4 * residents * positions * width,
            transcendentals=residents * heads * positions,
        ),
        name="attend_resident",
    )(lengths, query, k_cache, v_cache)


def expand(own, rows):
    which = iota((rows, 128), 0) // (rows // own.shape[0])
    out = jnp.broadcast_to(own[0:1], (rows, 128))
    for h in range(1, own.shape[0]):
        out = jnp.where(which == h, own[h : h + 1], out)
    return out


def heads_of(line, heads_mine, kv_mine):
    per = heads_mine // kv_mine
    blocks = [line[:, c : c + 128] for c in range(0, line.shape[1], 128)]
    q = jnp.concatenate(blocks[:heads_mine], axis=0)
    k = blocks[heads_mine : heads_mine + kv_mine]
    v = blocks[heads_mine + kv_mine :]
    return (
        q,
        expand(jnp.concatenate(k, axis=0), heads_mine),
        expand(jnp.concatenate(v, axis=0), heads_mine),
    )


def prepare_kernel(insts, residents, kv_mine, dest_ref, count_ref, gain_ref, cos_ref, sin_ref, *rest):
    asks, rest = rest[: insts - 1], rest[insts - 1 :]
    q_out, own_out, limit_out, cos_out, sin_out, place_out, line_ref, q_ref, k_ref = rest
    requests = dest_ref.shape[0]
    rows = q_out.shape[0]
    heads_mine = rows // requests
    here = lax.axis_index("inst")
    ask_row = iota(asks[0].shape, 0)
    limit = jnp.zeros((rows, 128), jnp.int32)
    for r in range(requests):
        dest = dest_ref[r, here]
        limit = jnp.where(iota((rows, 128), 0) // heads_mine == r, count_ref[r, here], limit)
        place = jnp.int32(residents)
        for s in range(insts):
            for c in range(requests):
                place += jnp.where((dest_ref[c, s] == dest) & (here > s), 1, 0).astype(jnp.int32)
        for b in range(1, insts):

            @pl.when(here ^ b == dest)
            def _():
                ask = asks[b - 1][...].astype(F32)
                line_ref[r : r + 1, :] = jnp.sum(
                    jnp.where(ask_row == place, ask, 0.0), axis=0, keepdims=True
                )

        at = slice(r * heads_mine, (r + 1) * heads_mine)
        q_ref[at, :], k_ref[at, :], own_out[0, at, :] = heads_of(
            line_ref[r : r + 1, :], heads_mine, kv_mine
        )
    scale = F32(1.0) / jnp.sqrt(F32(128.0))
    q = q_ref[...]
    q_out[...] = q.astype(BF16)
    own_out[1] = jnp.broadcast_to(
        jnp.sum(q * k_ref[...], axis=1, keepdims=True) * scale, (rows, 128)
    )
    limit_out[...] = limit
    gain = gain_ref[...].astype(F32)
    cos_out[...] = cos_ref[...] * gain
    sin_out[...] = sin_ref[...] * pltpu.roll(jnp.broadcast_to(gain, (8, 128)), 64, 1)[:1]
    places = jnp.full(place_out.shape, -1, jnp.int32)
    row = iota(place_out.shape, 0)
    place = jnp.int32(residents)
    for s in range(insts):
        for c in range(requests):
            mine = dest_ref[c, s] == here
            places = jnp.where((row == (here ^ s) * requests + c) & mine, place, places)
            place += jnp.where(mine, 1, 0).astype(jnp.int32)
    place_out[...] = places


def prepare(dest, count, k_gain, cos, sin, asks, residents, heads_mine, kv_mine):
    requests, insts = dest.shape
    rows = requests * heads_mine
    return pl.pallas_call(
        functools.partial(prepare_kernel, insts, residents, kv_mine),
        in_specs=[SMEM] * 2 + [VMEM] * (3 + len(asks)),
        out_specs=[VMEM] * 6,
        out_shape=[
            jax.ShapeDtypeStruct((rows, 128), BF16),
            jax.ShapeDtypeStruct((2, rows, 128), F32),
            jax.ShapeDtypeStruct((rows, 128), jnp.int32),
            jax.ShapeDtypeStruct(cos.shape, F32),
            jax.ShapeDtypeStruct(sin.shape, F32),
            jax.ShapeDtypeStruct((insts * requests, 128), jnp.int32),
        ],
        scratch_shapes=[
            pltpu.VMEM((requests, asks[0].shape[1]), F32),
            pltpu.VMEM((rows, 128), F32),
            pltpu.VMEM((rows, 128), F32),
        ],
        compiler_params=pltpu.CompilerParams(vmem_limit_bytes=16 * MIB),
        name="prepare",
    )(dest, count, k_gain, cos, sin, *asks)


def moved_kernel(ranks, features, q_ref, own_ref, limit_ref, cos_ref, sin_ref, *rest):
    pieces = rest[:ranks]
    out_ref, line_ref = rest[ranks:]
    requests = out_ref.shape[0]
    tokens = cos_ref.shape[0]
    piece = pieces[0].shape[1] // 2
    kv_mine = piece // 128
    rows = q_ref.shape[0]
    heads_mine = rows // requests
    scale = F32(1.0) / jnp.sqrt(F32(128.0))

    tail = pieces[0][tokens:, :].astype(F32)
    for t in range(1, ranks):
        tail = tail + pieces[t][tokens:, :].astype(F32)
    blocks = tokens // 128
    squares = tail[:blocks, :128] + tail[blocks : 2 * blocks, :128]
    squares = jnp.concatenate(
        [row_to_column(squares[b : b + 1], 128) for b in range(blocks)], axis=0
    )
    token_scale = lax.rsqrt(squares / features + EPS)

    def column_block(c):
        total = pieces[0][:tokens, c : c + 128].astype(F32)
        for t in range(1, ranks):
            total = total + pieces[t][:tokens, c : c + 128].astype(F32)
        return total * token_scale

    q = q_ref[...]
    which = iota((rows, tokens), 0) % heads_mine // (heads_mine // kv_mine)
    scores = None
    for h in range(kv_mine):
        key = column_block(h * 128)
        key = key * lax.rsqrt(jnp.mean(key * key, axis=1, keepdims=True) + EPS)
        key = key * cos_ref[...] + pltpu.roll(key, 64, 1) * sin_ref[...]
        part = lax.dot_general(
            q, key.astype(BF16), (((1,), (1,)), ((), ())), preferred_element_type=F32
        )
        scores = part if scores is None else jnp.where(which == h, part, scores)
    token = iota((rows, tokens), 1)
    limit = jnp.concatenate([limit_ref[...]] * (tokens // 128), axis=1)
    valid = (token % requests == iota((rows, tokens), 0) // heads_mine) & (
        token // requests < limit
    )
    scores = jnp.where(valid, scores * scale, ABSENT)
    own_score = own_ref[1]
    top = jnp.maximum(jnp.max(scores, axis=1, keepdims=True), own_score)
    weights = jnp.where(
        valid, jnp.exp(scores - jnp.concatenate([top] * (tokens // 128), axis=1)), 0.0
    )
    own_weight = jnp.exp(own_score - top)
    total = jnp.sum(weights, axis=1, keepdims=True) + own_weight
    weights = weights.astype(BF16)
    summed = None
    for h in range(kv_mine):
        value = column_block(piece + h * 128).astype(BF16)
        part = jnp.dot(weights, value, preferred_element_type=F32)
        summed = part if summed is None else jnp.where(which[:, :128] == h, part, summed)
    summed = summed + own_weight.astype(BF16).astype(F32) * own_ref[0]
    result = summed / total
    for r in range(requests):
        for h in range(heads_mine):
            at = r * heads_mine + h
            line_ref[r : r + 1, h * 128 : (h + 1) * 128] = result[at : at + 1, :]
    out_ref[...] = line_ref[...].astype(BF16)


def attend_moved(prepared, pieces, requests, features):
    rows = prepared[0].shape[0]
    width = rows // requests * 128
    return pl.pallas_call(
        functools.partial(moved_kernel, len(pieces), features),
        in_specs=[VMEM] * (len(prepared) + len(pieces)),
        out_specs=VMEM,
        out_shape=jax.ShapeDtypeStruct((requests, width), BF16),
        scratch_shapes=[pltpu.VMEM((requests, width), F32)],
        compiler_params=pltpu.CompilerParams(vmem_limit_bytes=16 * MIB),
        cost_estimate=pl.CostEstimate(
            flops=4 * rows * rows * 128 * 64, bytes_accessed=4 * 1024 * 1024, transcendentals=rows * 128
        ),
        name="attend_moved",
    )(*prepared, *pieces)


def combine_kernel(ranks, residents, kv_mine, ask_ref, *rest):
    payloads = rest[:ranks]
    out_ref = rest[ranks]
    heads_mine = out_ref.shape[1] // 128
    scale = F32(1.0) / jnp.sqrt(F32(128.0))
    at = residents * heads_mine
    ask = ask_ref[...].astype(F32)
    for r in range(residents):
        q, own_k, own_v = heads_of(ask[r : r + 1], heads_mine, kv_mine)
        own_score = jnp.sum(q * own_k, axis=1, keepdims=True) * scale
        peaks, totals = [], []
        for t in range(ranks):
            stat = payloads[t][at : at + 3 * residents, :].astype(F32)
            peaks.append(row_to_column(stat[r : r + 1], heads_mine))
            total = stat[residents + r : residents + r + 1]
            total = total + stat[2 * residents + r : 2 * residents + r + 1]
            totals.append(row_to_column(total, heads_mine))
        top = own_score
        for t in range(ranks):
            top = jnp.maximum(top, peaks[t])
        own_weight = jnp.exp(own_score - top)
        denom = own_weight
        numer = own_weight.astype(BF16).astype(F32) * own_v
        for t in range(ranks):
            keep = jnp.exp(peaks[t] - top)
            denom = denom + keep * totals[t]
            numer = numer + keep * payloads[t][r * heads_mine : (r + 1) * heads_mine, :].astype(F32)
        result = numer / denom
        for h in range(heads_mine):
            out_ref[r : r + 1, h * 128 : (h + 1) * 128] = result[h : h + 1, :]


def combine_resident(asks, payloads, residents, heads_mine, kv_mine):
    return pl.pallas_call(
        functools.partial(combine_kernel, len(payloads), residents, kv_mine),
        in_specs=[VMEM] * (1 + len(payloads)),
        out_specs=VMEM,
        out_shape=jax.ShapeDtypeStruct((residents, heads_mine * 128), F32),
        compiler_params=pltpu.CompilerParams(vmem_limit_bytes=8 * MIB),
        name="combine_resident",
    )(asks, *payloads)


def finish_kernel(kept_ref, place_ref, *rest):
    moved, out_ref = rest[:-1], rest[-1]
    residents = kept_ref.shape[0]
    decoded, width = out_ref.shape
    requests = decoded - residents
    row = iota((decoded, 128), 0)
    arrived = [ref[...].astype(F32) for ref in moved]
    for c in range(0, width, 128):
        kept = kept_ref[:, c : c + 128]
        line = jnp.concatenate([kept, jnp.zeros((requests, 128), F32)], axis=0)
        for b in range(len(moved)):
            for i in range(requests):
                at = (b + 1) * requests + i
                line = jnp.where(
                    place_ref[at : at + 1, :] == row, arrived[b][i : i + 1, c : c + 128], line
                )
        out_ref[:, c : c + 128] = line.astype(BF16)


def finish(kept, places, moved, requests):
    residents, width = kept.shape
    return pl.pallas_call(
        finish_kernel,
        in_specs=[VMEM] * (2 + len(moved)),
        out_specs=VMEM,
        out_shape=jax.ShapeDtypeStruct((residents + requests, width), BF16),
        compiler_params=pltpu.CompilerParams(vmem_limit_bytes=8 * MIB),
        name="finish",
    )(kept, places, *moved)


def swapped(x, axis, j, n):
    return lax.ppermute(x, axis, [(i, i ^ j) for i in range(n)])


def rotation(slots, requests, head_size):
    half = head_size // 2
    freq = THETA ** (-np.arange(half) * 2.0 / head_size)
    angle = np.repeat(np.arange(slots), requests)[:, None] * freq[None, :]
    cos, sin = np.cos(angle), np.sin(angle)
    return (
        np.concatenate([cos, cos], axis=1).astype(np.float32),
        np.concatenate([-sin, sin], axis=1).astype(np.float32),
    )


def per_device(
    mig_hidden,
    mig_dest,
    mig_count,
    attn_gain,
    kv_weight,
    k_gain,
    query,
    new_kv,
    k_cache,
    v_cache,
    lengths,
):
    insts = lax.axis_size("inst")
    ranks = lax.axis_size("tp")
    head_size = k_gain.shape[0]
    slots, requests, feats = mig_hidden.shape[1:]
    residents = k_cache.shape[1]
    heads = query.shape[2] // head_size
    kv_heads = kv_weight.shape[1] // 2 // head_size
    heads_mine = heads // ranks
    group = heads // kv_heads
    kv_mine = max(1, heads_mine // group)

    pieces, ask = project(
        mig_hidden[0], attn_gain, kv_weight, query[0], new_kv[0], ranks, group, kv_mine
    )
    last = ranks - 1
    far = swapped(pieces[last], "tp", last, ranks)
    asks = [swapped(ask, "inst", b, insts) for b in range(1, insts)]
    asks[0], *near = lax.optimization_barrier((asks[0], *pieces[1:last]))
    near = [swapped(near[j - 1], "tp", j, ranks) for j in reversed(range(1, last))]
    pieces = [pieces[0], far] + near
    payloads = attend_resident(lengths, query[0], k_cache[0], v_cache[0], ranks)
    own_payload = payloads[0]
    payloads = [swapped(payloads[j], "tp", j, ranks) for j in reversed(range(1, ranks))]
    cos, sin = rotation(slots, requests, head_size)
    *prepared, places = prepare(
        mig_dest.T,
        mig_count.T,
        k_gain.reshape(1, head_size),
        cos,
        sin,
        asks,
        residents,
        heads_mine,
        kv_mine,
    )
    prepared[0], own_payload = lax.optimization_barrier((prepared[0], own_payload))
    moved = attend_moved(prepared, pieces, requests, feats * ranks)
    kept = combine_resident(ask, [own_payload] + payloads, residents, heads_mine, kv_mine)
    moved = [swapped(moved, "inst", b, insts) for b in reversed(range(1, insts))][::-1]
    return finish(kept, places, moved, requests)[None]


def solution(mesh):
    placed = (
        P(("group", "inst"), None, None, "tp"),
        P("group", None),
        P("group", None),
        P("tp"),
        P("tp", None),
        P(),
        P(("group", "inst"), None, None),
        P(("group", "inst"), None, None),
        P(("group", "inst"), None, "tp", None),
        P(("group", "inst"), None, "tp", None),
        P(("group", "inst"), None),
    )
    return jax.shard_map(
        per_device,
        mesh=mesh,
        in_specs=placed,
        out_specs=P(("group", "inst"), None, "tp"),
        check_vma=False,
    )
```

```python
import functools

import jax
import jax.numpy as jnp
import numpy as np
from jax import lax
from jax.experimental import pallas as pl
from jax.experimental.pallas import tpu as pltpu
from jax.sharding import PartitionSpec as P

EPS = 1e-06
THETA = 1000000.0
ABSENT = -1e30
F32 = jnp.float32
BF16 = jnp.bfloat16
MIB = 1024 * 1024
CHUNK = 512
AHEAD = 3

VMEM = pl.BlockSpec(memory_space=pltpu.VMEM)
SMEM = pl.BlockSpec(memory_space=pltpu.SMEM)
HBM = pl.BlockSpec(memory_space=pltpu.HBM)


def iota(shape, dim):
    return lax.broadcasted_iota(jnp.int32, shape, dim)


def column_to_row(column, period):
    n = column.shape[0]
    spread = jnp.where(iota((n, 128), 0) % period == iota((n, 128), 1), column, 0.0)
    return jnp.sum(spread.reshape(n // period, period, 128), axis=1)


def row_to_column(row, n):
    return jnp.sum(
        jnp.where(iota((n, 128), 0) == iota((n, 128), 1), row, 0.0), axis=1, keepdims=True
    )


def split_bf16(x):
    high = x.astype(BF16)
    return high, (x - high.astype(F32)).astype(BF16)


def project_kernel(ranks, group, gain_hbm, x_hbm, w_hbm, q_hbm, own_hbm, *rest):
    outs, ask_ref = rest[:ranks], rest[ranks]
    gain_ref, x_ref, w_ref, acc_ref, in_sems, w_sems = rest[ranks + 1 :]
    slots, requests, feats = x_ref.shape
    rows = slots * requests
    piece = outs[0].shape[1] // 2
    kv_width = w_hbm.shape[1] // 2
    heads_mine = kv_width // 128 * group // ranks
    rank = lax.axis_index("tp")

    def first_column(target):
        return pl.multiple_of(target * heads_mine // group * 128, 128)

    gain_copy = pltpu.make_async_copy(gain_hbm, gain_ref, in_sems.at[0])
    gain_copy.start()
    x_copy = pltpu.make_async_copy(x_hbm, x_ref, in_sems.at[1])
    x_copy.start()
    cuts = list(range(0, feats, CHUNK)) + [feats]
    chunks = list(zip(cuts[:-1], cuts[1:]))
    copies = []
    for i, (low, high) in enumerate(chunks):
        copies.append(
            pltpu.make_async_copy(w_hbm.at[low:high, :], w_ref.at[low:high, :], w_sems.at[i])
        )
    copies[0].start()
    mine = heads_mine * 128
    q_first = pl.multiple_of(rank * mine, 128)
    asking = [
        pltpu.make_async_copy(
            q_hbm.at[:, pl.ds(q_first, mine)], ask_ref.at[:, :mine], in_sems.at[2]
        )
    ]
    for i in range(2):
        asking.append(
            pltpu.make_async_copy(
                own_hbm.at[:, pl.ds(i * kv_width + first_column(rank), piece)],
                ask_ref.at[:, mine + i * piece : mine + (i + 1) * piece],
                in_sems.at[3 + i],
            )
        )
    for copy in asking:
        copy.start()
    gain_copy.wait()
    x_copy.wait()
    if len(copies) > 1:
        copies[1].start()
    squares = jnp.zeros((rows, 128), F32)
    for i, (low, high) in enumerate(chunks):
        parts = []
        for c in range(low, high, 128):
            width = min(128, high - c)
            x = x_ref[:, :, c : c + width].astype(F32).reshape(rows, width)
            gain = gain_ref[c : c + width].astype(F32).reshape(1, width)
            parts.append((x * gain).astype(BF16))
            x = x * x
            if width < 128:
                x = jnp.concatenate([x, jnp.zeros((rows, 128 - width), F32)], axis=1)
            squares = squares + x
        xg = parts[0] if len(parts) == 1 else jnp.concatenate(parts, axis=1)
        copies[i].wait()
        if i + 2 < len(copies):
            copies[i + 2].start()
        for n in range(0, 2 * kv_width, 512):
            part = jnp.dot(xg, w_ref[low:high, n : n + 512], preferred_element_type=F32)
            if i == 0:
                acc_ref[:, n : n + 512] = part
            else:
                acc_ref[:, n : n + 512] += part
    sq = column_to_row(jnp.sum(squares, axis=1, keepdims=True), 128)
    high, low = split_bf16(sq)
    tail = jnp.concatenate([high.astype(F32), low.astype(F32)], axis=0)
    fill = outs[1].shape[0] - rows - tail.shape[0]
    if fill:
        tail = jnp.concatenate([tail, jnp.zeros((fill, 128), F32)], axis=0)
    extra = jnp.concatenate([tail.astype(BF16)] * (2 * piece // 128), axis=1)
    for j in range(ranks):
        first = first_column(rank ^ j)
        outs[j][:rows, :piece] = acc_ref[:, pl.ds(first, piece)].astype(BF16)
        outs[j][:rows, piece:] = acc_ref[:, pl.ds(kv_width + first, piece)].astype(BF16)
        outs[j][rows:, :] = extra
    for copy in asking:
        copy.wait()


def project(x, gain, weight, query, own, ranks, group, kv_mine):
    slots, requests, feats = x.shape
    rows = slots * requests
    piece = kv_mine * 128
    extra = -(-2 * (rows // 128) // 8) * 8
    decoded, q_width = query.shape
    outs = pl.pallas_call(
        functools.partial(project_kernel, ranks, group),
        in_specs=[HBM] * 5,
        out_specs=[VMEM] * (ranks + 1),
        out_shape=[jax.ShapeDtypeStruct((rows + extra, 2 * piece), BF16)] * ranks
        + [jax.ShapeDtypeStruct((decoded, q_width // ranks + 2 * piece), BF16)],
        scratch_shapes=[
            pltpu.VMEM((feats,), BF16),
            pltpu.VMEM((slots, requests, feats), BF16),
            pltpu.VMEM(weight.shape, BF16),
            pltpu.VMEM((rows, weight.shape[1]), F32),
            pltpu.SemaphoreType.DMA((5,)),
            pltpu.SemaphoreType.DMA((-(-feats // CHUNK),)),
        ],
        compiler_params=pltpu.CompilerParams(vmem_limit_bytes=56 * MIB),
        cost_estimate=pl.CostEstimate(
            flops=2 * rows * feats * weight.shape[1],
            bytes_accessed=2 * feats * weight.shape[1],
            transcendentals=0,
        ),
        name="project",
    )(gain, x, weight, query, own)
    return outs[:ranks], outs[ranks]


def resident_kernel(ranks, len_hbm, q_hbm, k_hbm, v_hbm, *rest):
    outs = rest[:ranks]
    len_ref, q_ref, q_all, k_buf, v_buf, s_buf, o_all, s_all, in_sems, sems = rest[ranks:]
    residents, positions, width = k_buf.shape
    half = positions // 2
    chunks = []
    for r in range(residents):
        for hbm, buf in ((k_hbm, k_buf), (v_hbm, v_buf)):
            for i in range(2):
                at = slice(i * half, (i + 1) * half)
                chunks.append(
                    pltpu.make_async_copy(
                        hbm.at[r, at, :], buf.at[r, at, :], sems.at[len(chunks)]
                    )
                )
    for chunk in chunks[:AHEAD]:
        chunk.start()
    q_copy = pltpu.make_async_copy(q_hbm, q_ref, in_sems.at[0])
    len_copy = pltpu.make_async_copy(len_hbm, len_ref, in_sems.at[1])
    q_copy.start()
    len_copy.start()

    def arrived(i):
        chunks[i].wait()
        if i + AHEAD < len(chunks):
            chunks[i + AHEAD].start()

    heads = q_ref.shape[1] // 128
    kv_heads = width // 128
    group = heads // kv_heads
    pair_rows = 2 * group
    heads_mine = heads // ranks
    rank = lax.axis_index("tp")
    top_half = iota((pair_rows, 128), 0) < group
    position = rank * positions + iota((pair_rows, positions), 1)
    scale = F32(1.0) / jnp.sqrt(F32(128.0))
    diagonal = iota((heads, 128), 0) % heads_mine == iota((heads, 128), 1)
    pairs = [slice(p * pair_rows, (p + 1) * pair_rows) for p in range(kv_heads // 2)]

    def to_rows(columns):
        spread = jnp.where(diagonal, jnp.concatenate(columns, axis=0), 0.0)
        return jnp.sum(spread.reshape(ranks, heads_mine, 128), axis=1)

    q_copy.wait()
    len_copy.wait()
    for h in range(heads):
        q_all[h * 8 : h * 8 + residents, :] = q_ref[:residents, h * 128 : (h + 1) * 128].astype(F32)
    peaks, totals = [], []
    for r in range(residents):
        q_mine = q_all[pl.ds(r, heads, stride=8), :]
        peaks.append([])
        totals.append([])
        valid = position < len_ref[0:1, r : r + 1]
        both_of = []
        for rows in pairs:
            q = q_mine[rows].astype(BF16)
            zero = jnp.zeros_like(q)
            both_of.append(
                jnp.concatenate(
                    [jnp.where(top_half, q, zero), jnp.where(top_half, zero, q)], axis=1
                )
            )
        for i in range(2):
            arrived(4 * r + i)
            at = slice(i * half, (i + 1) * half)
            for p, rows in enumerate(pairs):
                s_buf[rows, at] = lax.dot_general(
                    both_of[p],
                    k_buf[r, at, p * 256 : (p + 1) * 256],
                    (((1,), (1,)), ((), ())),
                    preferred_element_type=F32,
                )
        weights = []
        for rows in pairs:
            scores = jnp.where(valid, s_buf[rows, :] * scale, ABSENT)
            peak = jnp.max(scores, axis=1, keepdims=True).astype(BF16).astype(F32)
            weight = jnp.where(valid, jnp.exp(scores - peak), 0.0)
            peaks[r].append(peak)
            totals[r].append(jnp.sum(weight, axis=1, keepdims=True))
            weights.append(weight.astype(BF16))
        for i in range(2):
            arrived(4 * r + 2 + i)
            at = slice(i * half, (i + 1) * half)
            for p, rows in enumerate(pairs):
                both = jnp.dot(
                    weights[p][:, at],
                    v_buf[r, at, p * 256 : (p + 1) * 256],
                    preferred_element_type=F32,
                )
                part = jnp.where(top_half, both[:, :128], both[:, 128:])
                if i == 0:
                    o_all[r, rows, :] = part
                else:
                    o_all[r, rows, :] += part
    for r in range(residents):
        s_all[r, 0] = to_rows(peaks[r])
        high, low = split_bf16(to_rows(totals[r]))
        s_all[r, 1] = high.astype(F32)
        s_all[r, 2] = low.astype(F32)
    filled = residents * (heads_mine + 3)
    for j in range(ranks):
        target = rank ^ j
        first = pl.multiple_of(target * heads_mine, heads_mine)
        parts = [o_all[r, pl.ds(first, heads_mine), :] for r in range(residents)]
        parts += [s_all[r, i, pl.ds(target, 1), :] for i in range(3) for r in range(residents)]
        if outs[j].shape[0] > filled:
            parts.append(jnp.zeros((outs[j].shape[0] - filled, 128), F32))
        outs[j][...] = jnp.concatenate(parts, axis=0).astype(BF16)


def attend_resident(lengths, query, k_cache, v_cache, ranks):
    residents, positions, width = k_cache.shape
    heads = query.shape[1] // 128
    heads_mine = heads // ranks
    rows = -(-(residents * (heads_mine + 3)) // 16) * 16
    return pl.pallas_call(
        functools.partial(resident_kernel, ranks),
        in_specs=[HBM] * 4,
        out_specs=[VMEM] * ranks,
        out_shape=[jax.ShapeDtypeStruct((rows, 128), BF16)] * ranks,
        scratch_shapes=[
            pltpu.VMEM(lengths.shape, jnp.int32),
            pltpu.VMEM(query.shape, BF16),
            pltpu.VMEM((heads * 8, 128), F32),
            pltpu.VMEM((residents, positions, width), BF16),
            pltpu.VMEM((residents, positions, width), BF16),
            pltpu.VMEM((heads, positions), F32),
            pltpu.VMEM((residents, heads, 128), F32),
            pltpu.VMEM((residents, 3, ranks, 128), F32),
            pltpu.SemaphoreType.DMA((2,)),
            pltpu.SemaphoreType.DMA((4 * residents,)),
        ],
        compiler_params=pltpu.CompilerParams(vmem_limit_bytes=56 * MIB),
        cost_estimate=pl.CostEstimate(
            flops=4 * residents * heads * positions * 128,
            bytes_accessed=4 * residents * positions * width,
            transcendentals=residents * heads * positions,
        ),
        name="attend_resident",
    )(lengths, query, k_cache, v_cache)


def expand(own, rows):
    which = iota((rows, 128), 0) // (rows // own.shape[0])
    out = jnp.broadcast_to(own[0:1], (rows, 128))
    for h in range(1, own.shape[0]):
        out = jnp.where(which == h, own[h : h + 1], out)
    return out


def heads_of(line, heads_mine, kv_mine):
    per = heads_mine // kv_mine
    blocks = [line[:, c : c + 128] for c in range(0, line.shape[1], 128)]
    q = jnp.concatenate(blocks[:heads_mine], axis=0)
    k = blocks[heads_mine : heads_mine + kv_mine]
    v = blocks[heads_mine + kv_mine :]
    return (
        q,
        expand(jnp.concatenate(k, axis=0), heads_mine),
        expand(jnp.concatenate(v, axis=0), heads_mine),
    )


def prepare_kernel(insts, residents, kv_mine, dest_ref, count_ref, gain_ref, cos_ref, sin_ref, *rest):
    asks, rest = rest[: insts - 1], rest[insts - 1 :]
    q_out, own_out, limit_out, cos_out, sin_out, place_out, line_ref, q_ref, k_ref = rest
    requests = dest_ref.shape[0]
    rows = q_out.shape[0]
    heads_mine = rows // requests
    here = lax.axis_index("inst")
    ask_row = iota(asks[0].shape, 0)
    limit = jnp.zeros((rows, 128), jnp.int32)
    for r in range(requests):
        dest = dest_ref[r, here]
        limit = jnp.where(iota((rows, 128), 0) // heads_mine == r, count_ref[r, here], limit)
        place = jnp.int32(residents)
        for s in range(insts):
            for c in range(requests):
                place += jnp.where((dest_ref[c, s] == dest) & (here > s), 1, 0).astype(jnp.int32)
        for b in range(1, insts):

            @pl.when(here ^ b == dest)
            def _():
                ask = asks[b - 1][...].astype(F32)
                line_ref[r : r + 1, :] = jnp.sum(
                    jnp.where(ask_row == place, ask, 0.0), axis=0, keepdims=True
                )

        at = slice(r * heads_mine, (r + 1) * heads_mine)
        q_ref[at, :], k_ref[at, :], own_out[0, at, :] = heads_of(
            line_ref[r : r + 1, :], heads_mine, kv_mine
        )
    scale = F32(1.0) / jnp.sqrt(F32(128.0))
    q = q_ref[...]
    q_out[...] = q.astype(BF16)
    own_out[1] = jnp.broadcast_to(
        jnp.sum(q * k_ref[...], axis=1, keepdims=True) * scale, (rows, 128)
    )
    limit_out[...] = limit
    gain = gain_ref[...].astype(F32)
    cos_out[...] = cos_ref[...] * gain
    sin_out[...] = sin_ref[...] * pltpu.roll(jnp.broadcast_to(gain, (8, 128)), 64, 1)[:1]
    places = jnp.full(place_out.shape, -1, jnp.int32)
    row = iota(place_out.shape, 0)
    place = jnp.int32(residents)
    for s in range(insts):
        for c in range(requests):
            mine = dest_ref[c, s] == here
            places = jnp.where((row == (here ^ s) * requests + c) & mine, place, places)
            place += jnp.where(mine, 1, 0).astype(jnp.int32)
    place_out[...] = places


def prepare(dest, count, k_gain, cos, sin, asks, residents, heads_mine, kv_mine):
    requests, insts = dest.shape
    rows = requests * heads_mine
    return pl.pallas_call(
        functools.partial(prepare_kernel, insts, residents, kv_mine),
        in_specs=[SMEM] * 2 + [VMEM] * (3 + len(asks)),
        out_specs=[VMEM] * 6,
        out_shape=[
            jax.ShapeDtypeStruct((rows, 128), BF16),
            jax.ShapeDtypeStruct((2, rows, 128), F32),
            jax.ShapeDtypeStruct((rows, 128), jnp.int32),
            jax.ShapeDtypeStruct(cos.shape, F32),
            jax.ShapeDtypeStruct(sin.shape, F32),
            jax.ShapeDtypeStruct((insts * requests, 128), jnp.int32),
        ],
        scratch_shapes=[
            pltpu.VMEM((requests, asks[0].shape[1]), F32),
            pltpu.VMEM((rows, 128), F32),
            pltpu.VMEM((rows, 128), F32),
        ],
        compiler_params=pltpu.CompilerParams(vmem_limit_bytes=16 * MIB),
        name="prepare",
    )(dest, count, k_gain, cos, sin, *asks)


def moved_kernel(ranks, features, q_ref, own_ref, limit_ref, cos_ref, sin_ref, *rest):
    pieces = rest[:ranks]
    out_ref, line_ref = rest[ranks:]
    requests = out_ref.shape[0]
    tokens = cos_ref.shape[0]
    piece = pieces[0].shape[1] // 2
    kv_mine = piece // 128
    rows = q_ref.shape[0]
    heads_mine = rows // requests
    scale = F32(1.0) / jnp.sqrt(F32(128.0))

    blocks = tokens // 128
    last = tokens + 2 * blocks
    tail = pieces[0][tokens:last, :128].astype(F32)
    for t in range(1, ranks):
        tail = tail + pieces[t][tokens:last, :128].astype(F32)
    squares = tail[:blocks] + tail[blocks:]
    squares = jnp.concatenate(
        [row_to_column(squares[b : b + 1], 128) for b in range(blocks)], axis=0
    )
    token_scale = lax.rsqrt(squares / features + EPS)

    def column_block(c):
        total = pieces[0][:tokens, c : c + 128].astype(F32)
        for t in range(1, ranks):
            total = total + pieces[t][:tokens, c : c + 128].astype(F32)
        return total * token_scale

    q = q_ref[...]
    which = iota((rows, tokens), 0) % heads_mine // (heads_mine // kv_mine)
    scores = None
    for h in range(kv_mine):
        key = column_block(h * 128)
        key = key * lax.rsqrt(jnp.mean(key * key, axis=1, keepdims=True) + EPS)
        key = key * cos_ref[...] + pltpu.roll(key, 64, 1) * sin_ref[...]
        part = lax.dot_general(
            q, key.astype(BF16), (((1,), (1,)), ((), ())), preferred_element_type=F32
        )
        scores = part if scores is None else jnp.where(which == h, part, scores)
    token = iota((rows, tokens), 1)
    limit = jnp.concatenate([limit_ref[...]] * (tokens // 128), axis=1)
    valid = (token % requests == iota((rows, tokens), 0) // heads_mine) & (
        token // requests < limit
    )
    scores = jnp.where(valid, scores * scale, ABSENT)
    own_score = own_ref[1]
    top = jnp.maximum(jnp.max(scores, axis=1, keepdims=True), own_score)
    weights = jnp.where(
        valid, jnp.exp(scores - jnp.concatenate([top] * (tokens // 128), axis=1)), 0.0
    )
    own_weight = jnp.exp(own_score - top)
    total = jnp.sum(weights, axis=1, keepdims=True) + own_weight
    weights = weights.astype(BF16)
    summed = None
    for h in range(kv_mine):
        value = column_block(piece + h * 128).astype(BF16)
        part = jnp.dot(weights, value, preferred_element_type=F32)
        summed = part if summed is None else jnp.where(which[:, :128] == h, part, summed)
    summed = summed + own_weight.astype(BF16).astype(F32) * own_ref[0]
    result = summed / total
    for r in range(requests):
        for h in range(heads_mine):
            at = r * heads_mine + h
            line_ref[r : r + 1, h * 128 : (h + 1) * 128] = result[at : at + 1, :]
    out_ref[...] = line_ref[...].astype(BF16)


def attend_moved(prepared, pieces, requests, features):
    rows = prepared[0].shape[0]
    width = rows // requests * 128
    return pl.pallas_call(
        functools.partial(moved_kernel, len(pieces), features),
        in_specs=[VMEM] * (len(prepared) + len(pieces)),
        out_specs=VMEM,
        out_shape=jax.ShapeDtypeStruct((requests, width), BF16),
        scratch_shapes=[pltpu.VMEM((requests, width), F32)],
        compiler_params=pltpu.CompilerParams(vmem_limit_bytes=16 * MIB),
        cost_estimate=pl.CostEstimate(
            flops=4 * rows * rows * 128 * 64, bytes_accessed=4 * 1024 * 1024, transcendentals=rows * 128
        ),
        name="attend_moved",
    )(*prepared, *pieces)


def combine_kernel(ranks, residents, kv_mine, ask_ref, *rest):
    refs, out_ref = rest[:ranks], rest[ranks]
    heads_mine = out_ref.shape[1] // 128
    scale = F32(1.0) / jnp.sqrt(F32(128.0))
    payloads = [ref[...].astype(F32) for ref in refs]
    at = residents * heads_mine
    ask = ask_ref[...].astype(F32)
    for r in range(residents):
        q, own_k, own_v = heads_of(ask[r : r + 1], heads_mine, kv_mine)
        own_score = jnp.sum(q * own_k, axis=1, keepdims=True) * scale
        peaks, totals = [], []
        for payload in payloads:
            stat = payload[at : at + 3 * residents]
            peaks.append(row_to_column(stat[r : r + 1], heads_mine))
            total = stat[residents + r : residents + r + 1]
            total = total + stat[2 * residents + r : 2 * residents + r + 1]
            totals.append(row_to_column(total, heads_mine))
        top = own_score
        for peak in peaks:
            top = jnp.maximum(top, peak)
        own_weight = jnp.exp(own_score - top)
        denom = own_weight
        numer = own_weight.astype(BF16).astype(F32) * own_v
        for peak, total, payload in zip(peaks, totals, payloads):
            keep = jnp.exp(peak - top)
            denom = denom + keep * total
            numer = numer + keep * payload[r * heads_mine : (r + 1) * heads_mine]
        result = numer / denom
        for h in range(heads_mine):
            out_ref[r : r + 1, h * 128 : (h + 1) * 128] = result[h : h + 1, :]


def combine_resident(ask, payloads, residents, heads_mine, kv_mine):
    return pl.pallas_call(
        functools.partial(combine_kernel, len(payloads), residents, kv_mine),
        in_specs=[VMEM] * (1 + len(payloads)),
        out_specs=VMEM,
        out_shape=jax.ShapeDtypeStruct((residents, heads_mine * 128), F32),
        compiler_params=pltpu.CompilerParams(vmem_limit_bytes=8 * MIB),
        name="combine_resident",
    )(ask, *payloads)


def finish_kernel(kept_ref, place_ref, *rest):
    moved, out_ref = rest[:-1], rest[-1]
    residents = kept_ref.shape[0]
    decoded, width = out_ref.shape
    requests = decoded - residents
    row = iota((decoded, 128), 0)
    arrived = [ref[...].astype(F32) for ref in moved]
    for c in range(0, width, 128):
        kept = kept_ref[:, c : c + 128]
        line = jnp.concatenate([kept, jnp.zeros((requests, 128), F32)], axis=0)
        for b in range(len(moved)):
            for i in range(requests):
                at = (b + 1) * requests + i
                line = jnp.where(
                    place_ref[at : at + 1, :] == row, arrived[b][i : i + 1, c : c + 128], line
                )
        out_ref[:, c : c + 128] = line.astype(BF16)


def finish(kept, places, moved, requests):
    residents, width = kept.shape
    return pl.pallas_call(
        finish_kernel,
        in_specs=[VMEM] * (2 + len(moved)),
        out_specs=VMEM,
        out_shape=jax.ShapeDtypeStruct((residents + requests, width), BF16),
        compiler_params=pltpu.CompilerParams(vmem_limit_bytes=8 * MIB),
        name="finish",
    )(kept, places, *moved)


def swapped(x, axis, j, n):
    return lax.ppermute(x, axis, [(i, i ^ j) for i in range(n)])


def rotation(slots, requests, head_size):
    half = head_size // 2
    freq = THETA ** (-np.arange(half) * 2.0 / head_size)
    angle = np.repeat(np.arange(slots), requests)[:, None] * freq[None, :]
    cos, sin = np.cos(angle), np.sin(angle)
    return (
        np.concatenate([cos, cos], axis=1).astype(np.float32),
        np.concatenate([-sin, sin], axis=1).astype(np.float32),
    )


def per_device(
    mig_hidden,
    mig_dest,
    mig_count,
    attn_gain,
    kv_weight,
    k_gain,
    query,
    new_kv,
    k_cache,
    v_cache,
    lengths,
):
    insts = lax.axis_size("inst")
    ranks = lax.axis_size("tp")
    head_size = k_gain.shape[0]
    slots, requests, feats = mig_hidden.shape[1:]
    residents = k_cache.shape[1]
    heads = query.shape[2] // head_size
    kv_heads = kv_weight.shape[1] // 2 // head_size
    heads_mine = heads // ranks
    group = heads // kv_heads
    kv_mine = max(1, heads_mine // group)

    pieces, ask = project(
        mig_hidden[0], attn_gain, kv_weight, query[0], new_kv[0], ranks, group, kv_mine
    )
    last = ranks - 1
    far = swapped(pieces[last], "tp", last, ranks)
    asks = [swapped(ask, "inst", b, insts) for b in range(1, insts)]
    asks[0], *others = lax.optimization_barrier((asks[0], *pieces[1:last]))
    others = [swapped(others[j - 1], "tp", j, ranks) for j in reversed(range(1, last))]
    pieces = [pieces[0], far] + others
    payloads = attend_resident(lengths, query[0], k_cache[0], v_cache[0], ranks)
    own_payload = payloads[0]
    payloads = [swapped(payloads[j], "tp", j, ranks) for j in reversed(range(1, ranks))]
    cos, sin = rotation(slots, requests, head_size)
    *prepared, places = prepare(
        mig_dest.T,
        mig_count.T,
        k_gain.reshape(1, head_size),
        cos,
        sin,
        asks,
        residents,
        heads_mine,
        kv_mine,
    )
    prepared[0], own_payload = lax.optimization_barrier((prepared[0], own_payload))
    moved = attend_moved(prepared, pieces, requests, feats * ranks)
    kept = combine_resident(ask, [own_payload] + payloads, residents, heads_mine, kv_mine)
    moved = [swapped(moved, "inst", b, insts) for b in reversed(range(1, insts))][::-1]
    return finish(kept, places, moved, requests)[None]


def solution(mesh):
    placed = (
        P(("group", "inst"), None, None, "tp"),
        P("group", None),
        P("group", None),
        P("tp"),
        P("tp", None),
        P(),
        P(("group", "inst"), None, None),
        P(("group", "inst"), None, None),
        P(("group", "inst"), None, "tp", None),
        P(("group", "inst"), None, "tp", None),
        P(("group", "inst"), None),
    )
    return jax.shard_map(
        per_device,
        mesh=mesh,
        in_specs=placed,
        out_specs=P(("group", "inst"), None, "tp"),
        check_vma=False,
    )
```

```python
import functools

import jax
import jax.numpy as jnp
import numpy as np
from jax import lax
from jax.experimental import pallas as pl
from jax.experimental.pallas import tpu as pltpu
from jax.sharding import PartitionSpec as P

EPS = 1e-06
THETA = 1000000.0
ABSENT = -1e30
F32 = jnp.float32
BF16 = jnp.bfloat16
MIB = 1024 * 1024
CHUNK = 512
AHEAD = 4

VMEM = pl.BlockSpec(memory_space=pltpu.VMEM)
SMEM = pl.BlockSpec(memory_space=pltpu.SMEM)
HBM = pl.BlockSpec(memory_space=pltpu.HBM)


def iota(shape, dim):
    return lax.broadcasted_iota(jnp.int32, shape, dim)


def column_to_row(column, period):
    n = column.shape[0]
    spread = jnp.where(iota((n, 128), 0) % period == iota((n, 128), 1), column, 0.0)
    return jnp.sum(spread.reshape(n // period, period, 128), axis=1)


def row_to_column(row, n):
    return jnp.sum(
        jnp.where(iota((n, 128), 0) == iota((n, 128), 1), row, 0.0), axis=1, keepdims=True
    )


def split_bf16(x):
    high = x.astype(BF16)
    return high, (x - high.astype(F32)).astype(BF16)


def project_kernel(ranks, group, gain_hbm, x_hbm, w_hbm, q_hbm, own_hbm, *rest):
    outs, ask_ref = rest[:ranks], rest[ranks]
    gain_ref, x_ref, w_ref, acc_ref, in_sems, w_sems = rest[ranks + 1 :]
    slots, requests, feats = x_ref.shape
    rows = slots * requests
    piece = outs[0].shape[1] // 2
    kv_width = w_hbm.shape[1] // 2
    heads_mine = kv_width // 128 * group // ranks
    rank = lax.axis_index("tp")

    def first_column(target):
        return pl.multiple_of(target * heads_mine // group * 128, 128)

    gain_copy = pltpu.make_async_copy(gain_hbm, gain_ref, in_sems.at[0])
    gain_copy.start()
    x_copy = pltpu.make_async_copy(x_hbm, x_ref, in_sems.at[1])
    x_copy.start()
    cuts = list(range(0, feats, CHUNK)) + [feats]
    chunks = list(zip(cuts[:-1], cuts[1:]))
    copies = []
    for i, (low, high) in enumerate(chunks):
        copies.append(
            pltpu.make_async_copy(w_hbm.at[low:high, :], w_ref.at[low:high, :], w_sems.at[i])
        )
        copies[-1].start()
    mine = heads_mine * 128
    q_first = pl.multiple_of(rank * mine, 128)
    asking = [
        pltpu.make_async_copy(
            q_hbm.at[:, pl.ds(q_first, mine)], ask_ref.at[:, :mine], in_sems.at[2]
        )
    ]
    for i in range(2):
        asking.append(
            pltpu.make_async_copy(
                own_hbm.at[:, pl.ds(i * kv_width + first_column(rank), piece)],
                ask_ref.at[:, mine + i * piece : mine + (i + 1) * piece],
                in_sems.at[3 + i],
            )
        )
    for copy in asking:
        copy.start()
    gain_copy.wait()
    x_copy.wait()
    squares = jnp.zeros((rows, 128), F32)
    for i, (low, high) in enumerate(chunks):
        parts = []
        for c in range(low, high, 128):
            width = min(128, high - c)
            x = x_ref[:, :, c : c + width].astype(F32).reshape(rows, width)
            gain = gain_ref[c : c + width].astype(F32).reshape(1, width)
            parts.append((x * gain).astype(BF16))
            x = x * x
            if width < 128:
                x = jnp.concatenate([x, jnp.zeros((rows, 128 - width), F32)], axis=1)
            squares = squares + x
        xg = parts[0] if len(parts) == 1 else jnp.concatenate(parts, axis=1)
        copies[i].wait()
        for n in range(0, 2 * kv_width, 512):
            part = jnp.dot(xg, w_ref[low:high, n : n + 512], preferred_element_type=F32)
            if i == 0:
                acc_ref[:, n : n + 512] = part
            else:
                acc_ref[:, n : n + 512] += part
    sq = column_to_row(jnp.sum(squares, axis=1, keepdims=True), 128)
    high, low = split_bf16(sq)
    tail = jnp.concatenate([high.astype(F32), low.astype(F32)], axis=0)
    fill = outs[1].shape[0] - rows - tail.shape[0]
    if fill:
        tail = jnp.concatenate([tail, jnp.zeros((fill, 128), F32)], axis=0)
    extra = jnp.concatenate([tail.astype(BF16)] * (2 * piece // 128), axis=1)
    for j in range(ranks):
        first = first_column(rank ^ j)
        outs[j][:rows, :piece] = acc_ref[:, pl.ds(first, piece)].astype(BF16)
        outs[j][:rows, piece:] = acc_ref[:, pl.ds(kv_width + first, piece)].astype(BF16)
        outs[j][rows:, :] = extra
    for copy in asking:
        copy.wait()


def project(x, gain, weight, query, own, ranks, group, kv_mine):
    slots, requests, feats = x.shape
    rows = slots * requests
    piece = kv_mine * 128
    extra = -(-2 * (rows // 128) // 8) * 8
    decoded, q_width = query.shape
    outs = pl.pallas_call(
        functools.partial(project_kernel, ranks, group),
        in_specs=[HBM] * 5,
        out_specs=[VMEM] * (ranks + 1),
        out_shape=[jax.ShapeDtypeStruct((rows + extra, 2 * piece), BF16)] * ranks
        + [jax.ShapeDtypeStruct((decoded, q_width // ranks + 2 * piece), BF16)],
        scratch_shapes=[
            pltpu.VMEM((feats,), BF16),
            pltpu.VMEM((slots, requests, feats), BF16),
            pltpu.VMEM(weight.shape, BF16),
            pltpu.VMEM((rows, weight.shape[1]), F32),
            pltpu.SemaphoreType.DMA((5,)),
            pltpu.SemaphoreType.DMA((-(-feats // CHUNK),)),
        ],
        compiler_params=pltpu.CompilerParams(vmem_limit_bytes=56 * MIB),
        cost_estimate=pl.CostEstimate(
            flops=2 * rows * feats * weight.shape[1],
            bytes_accessed=2 * feats * weight.shape[1],
            transcendentals=0,
        ),
        name="project",
    )(gain, x, weight, query, own)
    return outs[:ranks], outs[ranks]


def resident_kernel(ranks, len_hbm, q_hbm, k_hbm, v_hbm, *rest):
    outs = rest[:ranks]
    len_ref, q_ref, q_all, k_buf, v_buf, wide_ref, s_buf, w_buf, o_all, s_all, in_sems, sems = rest[
        ranks:
    ]
    residents, positions, width = k_buf.shape
    half = positions // 2
    chunks = []
    for r in range(residents):
        for hbm, buf in ((k_hbm, k_buf), (v_hbm, v_buf)):
            for i in range(2):
                at = slice(i * half, (i + 1) * half)
                chunks.append(
                    pltpu.make_async_copy(
                        hbm.at[r, at, :], buf.at[r, at, :], sems.at[len(chunks)]
                    )
                )
    for chunk in chunks[:AHEAD]:
        chunk.start()
    q_copy = pltpu.make_async_copy(q_hbm, q_ref, in_sems.at[0])
    len_copy = pltpu.make_async_copy(len_hbm, len_ref, in_sems.at[1])
    q_copy.start()
    len_copy.start()

    def arrived(i):
        chunks[i].wait()
        if i + AHEAD < len(chunks):
            chunks[i + AHEAD].start()

    heads = q_ref.shape[1] // 128
    kv_heads = width // 128
    group = heads // kv_heads
    heads_mine = heads // ranks
    rank = lax.axis_index("tp")
    position = rank * positions + iota((16, positions), 1)
    scale = F32(1.0) / jnp.sqrt(F32(128.0))
    diagonal = iota((heads, 128), 0) % heads_mine == iota((heads, 128), 1)
    own_block = iota((heads, width), 0) // group == iota((heads, width), 1) // 128

    def to_rows(columns):
        spread = jnp.where(diagonal, jnp.concatenate(columns, axis=0), 0.0)
        return jnp.sum(spread.reshape(ranks, heads_mine, 128), axis=1)

    q_copy.wait()
    len_copy.wait()
    for h in range(heads):
        q_all[h * 8 : h * 8 + residents, :] = q_ref[:residents, h * 128 : (h + 1) * 128].astype(F32)
    peaks, totals = [], []
    for r in range(residents):
        q = q_all[pl.ds(r, heads, stride=8), :].astype(BF16)
        wide = jnp.concatenate([q] * kv_heads, axis=1)
        wide_ref[...] = jnp.where(own_block, wide, jnp.zeros_like(wide))
        peaks.append([])
        totals.append([])
        valid = position < len_ref[0:1, r : r + 1]
        for i in range(2):
            arrived(4 * r + i)
            at = slice(i * half, (i + 1) * half)
            s_buf[:, at] = lax.dot_general(
                wide_ref[...],
                k_buf[r, at, :],
                (((1,), (1,)), ((), ())),
                preferred_element_type=F32,
            )
        for c in range(0, heads, 16):
            rows = slice(c, c + 16)
            scores = jnp.where(valid, s_buf[rows, :] * scale, ABSENT)
            peak = jnp.max(scores, axis=1, keepdims=True).astype(BF16).astype(F32)
            weight = jnp.where(valid, jnp.exp(scores - peak), 0.0)
            peaks[r].append(peak)
            totals[r].append(jnp.sum(weight, axis=1, keepdims=True))
            w_buf[rows, :] = weight.astype(BF16)
        for i in range(2):
            arrived(4 * r + 2 + i)
            at = slice(i * half, (i + 1) * half)
            part = jnp.dot(w_buf[:, at], v_buf[r, at, :], preferred_element_type=F32)
            for g in range(kv_heads):
                rows = slice(g * group, (g + 1) * group)
                block = part[rows, g * 128 : (g + 1) * 128]
                if i == 0:
                    o_all[r, rows, :] = block
                else:
                    o_all[r, rows, :] += block
    for r in range(residents):
        s_all[r, 0] = to_rows(peaks[r])
        high, low = split_bf16(to_rows(totals[r]))
        s_all[r, 1] = high.astype(F32)
        s_all[r, 2] = low.astype(F32)
    filled = residents * (heads_mine + 3)
    for j in range(ranks):
        target = rank ^ j
        first = pl.multiple_of(target * heads_mine, heads_mine)
        parts = [o_all[r, pl.ds(first, heads_mine), :] for r in range(residents)]
        parts += [s_all[r, i, pl.ds(target, 1), :] for i in range(3) for r in range(residents)]
        if outs[j].shape[0] > filled:
            parts.append(jnp.zeros((outs[j].shape[0] - filled, 128), F32))
        outs[j][...] = jnp.concatenate(parts, axis=0).astype(BF16)


def attend_resident(lengths, query, k_cache, v_cache, ranks):
    residents, positions, width = k_cache.shape
    heads = query.shape[1] // 128
    heads_mine = heads // ranks
    rows = -(-(residents * (heads_mine + 3)) // 16) * 16
    return pl.pallas_call(
        functools.partial(resident_kernel, ranks),
        in_specs=[HBM] * 4,
        out_specs=[VMEM] * ranks,
        out_shape=[jax.ShapeDtypeStruct((rows, 128), BF16)] * ranks,
        scratch_shapes=[
            pltpu.VMEM(lengths.shape, jnp.int32),
            pltpu.VMEM(query.shape, BF16),
            pltpu.VMEM((heads * 8, 128), F32),
            pltpu.VMEM((residents, positions, width), BF16),
            pltpu.VMEM((residents, positions, width), BF16),
            pltpu.VMEM((heads, width), BF16),
            pltpu.VMEM((heads, positions), F32),
            pltpu.VMEM((heads, positions), BF16),
            pltpu.VMEM((residents, heads, 128), F32),
            pltpu.VMEM((residents, 3, ranks, 128), F32),
            pltpu.SemaphoreType.DMA((2,)),
            pltpu.SemaphoreType.DMA((4 * residents,)),
        ],
        compiler_params=pltpu.CompilerParams(vmem_limit_bytes=56 * MIB),
        cost_estimate=pl.CostEstimate(
            flops=4 * residents * heads * positions * 128,
            bytes_accessed=4 * residents * positions * width,
            transcendentals=residents * heads * positions,
        ),
        name="attend_resident",
    )(lengths, query, k_cache, v_cache)


def expand(own, rows):
    which = iota((rows, 128), 0) // (rows // own.shape[0])
    out = jnp.broadcast_to(own[0:1], (rows, 128))
    for h in range(1, own.shape[0]):
        out = jnp.where(which == h, own[h : h + 1], out)
    return out


def heads_of(line, heads_mine, kv_mine):
    per = heads_mine // kv_mine
    blocks = [line[:, c : c + 128] for c in range(0, line.shape[1], 128)]
    q = jnp.concatenate(blocks[:heads_mine], axis=0)
    k = blocks[heads_mine : heads_mine + kv_mine]
    v = blocks[heads_mine + kv_mine :]
    return (
        q,
        expand(jnp.concatenate(k, axis=0), heads_mine),
        expand(jnp.concatenate(v, axis=0), heads_mine),
    )


def prepare_kernel(insts, residents, kv_mine, dest_ref, count_ref, gain_ref, cos_ref, sin_ref, *rest):
    asks, rest = rest[: insts - 1], rest[insts - 1 :]
    q_out, own_out, limit_out, cos_out, sin_out, place_out, line_ref, q_ref, k_ref = rest
    requests = dest_ref.shape[0]
    rows = q_out.shape[0]
    heads_mine = rows // requests
    here = lax.axis_index("inst")
    ask_row = iota(asks[0].shape, 0)
    limit = jnp.zeros((rows, 128), jnp.int32)
    for r in range(requests):
        dest = dest_ref[r, here]
        limit = jnp.where(iota((rows, 128), 0) // heads_mine == r, count_ref[r, here], limit)
        place = jnp.int32(residents)
        for s in range(insts):
            for c in range(requests):
                place += jnp.where((dest_ref[c, s] == dest) & (here > s), 1, 0).astype(jnp.int32)
        for b in range(1, insts):

            @pl.when(here ^ b == dest)
            def _():
                ask = asks[b - 1][...].astype(F32)
                line_ref[r : r + 1, :] = jnp.sum(
                    jnp.where(ask_row == place, ask, 0.0), axis=0, keepdims=True
                )

        at = slice(r * heads_mine, (r + 1) * heads_mine)
        q_ref[at, :], k_ref[at, :], own_out[0, at, :] = heads_of(
            line_ref[r : r + 1, :], heads_mine, kv_mine
        )
    scale = F32(1.0) / jnp.sqrt(F32(128.0))
    q = q_ref[...]
    q_out[...] = q.astype(BF16)
    own_out[1] = jnp.broadcast_to(
        jnp.sum(q * k_ref[...], axis=1, keepdims=True) * scale, (rows, 128)
    )
    limit_out[...] = limit
    gain = gain_ref[...].astype(F32)
    cos_out[...] = cos_ref[...] * gain
    sin_out[...] = sin_ref[...] * pltpu.roll(jnp.broadcast_to(gain, (8, 128)), 64, 1)[:1]
    places = jnp.full(place_out.shape, -1, jnp.int32)
    row = iota(place_out.shape, 0)
    place = jnp.int32(residents)
    for s in range(insts):
        for c in range(requests):
            mine = dest_ref[c, s] == here
            places = jnp.where((row == (here ^ s) * requests + c) & mine, place, places)
            place += jnp.where(mine, 1, 0).astype(jnp.int32)
    place_out[...] = places


def prepare(dest, count, k_gain, cos, sin, asks, residents, heads_mine, kv_mine):
    requests, insts = dest.shape
    rows = requests * heads_mine
    return pl.pallas_call(
        functools.partial(prepare_kernel, insts, residents, kv_mine),
        in_specs=[SMEM] * 2 + [VMEM] * (3 + len(asks)),
        out_specs=[VMEM] * 6,
        out_shape=[
            jax.ShapeDtypeStruct((rows, 128), BF16),
            jax.ShapeDtypeStruct((2, rows, 128), F32),
            jax.ShapeDtypeStruct((rows, 128), jnp.int32),
            jax.ShapeDtypeStruct(cos.shape, F32),
            jax.ShapeDtypeStruct(sin.shape, F32),
            jax.ShapeDtypeStruct((insts * requests, 128), jnp.int32),
        ],
        scratch_shapes=[
            pltpu.VMEM((requests, asks[0].shape[1]), F32),
            pltpu.VMEM((rows, 128), F32),
            pltpu.VMEM((rows, 128), F32),
        ],
        compiler_params=pltpu.CompilerParams(vmem_limit_bytes=16 * MIB),
        name="prepare",
    )(dest, count, k_gain, cos, sin, *asks)


def moved_kernel(ranks, features, q_ref, own_ref, limit_ref, cos_ref, sin_ref, *rest):
    pieces = rest[:ranks]
    out_ref, line_ref = rest[ranks:]
    requests = out_ref.shape[0]
    tokens = cos_ref.shape[0]
    piece = pieces[0].shape[1] // 2
    kv_mine = piece // 128
    rows = q_ref.shape[0]
    heads_mine = rows // requests
    scale = F32(1.0) / jnp.sqrt(F32(128.0))

    blocks = tokens // 128
    last = tokens + 2 * blocks
    tail = pieces[0][tokens:last, :128].astype(F32)
    for t in range(1, ranks):
        tail = tail + pieces[t][tokens:last, :128].astype(F32)
    squares = tail[:blocks] + tail[blocks:]
    squares = jnp.concatenate(
        [row_to_column(squares[b : b + 1], 128) for b in range(blocks)], axis=0
    )
    token_scale = lax.rsqrt(squares / features + EPS)

    def column_block(c):
        total = pieces[0][:tokens, c : c + 128].astype(F32)
        for t in range(1, ranks):
            total = total + pieces[t][:tokens, c : c + 128].astype(F32)
        return total * token_scale

    q = q_ref[...]
    which = iota((rows, tokens), 0) % heads_mine // (heads_mine // kv_mine)
    scores = None
    for h in range(kv_mine):
        key = column_block(h * 128)
        key = key * lax.rsqrt(jnp.mean(key * key, axis=1, keepdims=True) + EPS)
        key = key * cos_ref[...] + pltpu.roll(key, 64, 1) * sin_ref[...]
        part = lax.dot_general(
            q, key.astype(BF16), (((1,), (1,)), ((), ())), preferred_element_type=F32
        )
        scores = part if scores is None else jnp.where(which == h, part, scores)
    token = iota((rows, tokens), 1)
    limit = jnp.concatenate([limit_ref[...]] * (tokens // 128), axis=1)
    valid = (token % requests == iota((rows, tokens), 0) // heads_mine) & (
        token // requests < limit
    )
    scores = jnp.where(valid, scores * scale, ABSENT)
    own_score = own_ref[1]
    top = jnp.maximum(jnp.max(scores, axis=1, keepdims=True), own_score)
    weights = jnp.where(
        valid, jnp.exp(scores - jnp.concatenate([top] * (tokens // 128), axis=1)), 0.0
    )
    own_weight = jnp.exp(own_score - top)
    total = jnp.sum(weights, axis=1, keepdims=True) + own_weight
    weights = weights.astype(BF16)
    summed = None
    for h in range(kv_mine):
        value = column_block(piece + h * 128).astype(BF16)
        part = jnp.dot(weights, value, preferred_element_type=F32)
        summed = part if summed is None else jnp.where(which[:, :128] == h, part, summed)
    summed = summed + own_weight.astype(BF16).astype(F32) * own_ref[0]
    result = summed / total
    for r in range(requests):
        for h in range(heads_mine):
            at = r * heads_mine + h
            line_ref[r : r + 1, h * 128 : (h + 1) * 128] = result[at : at + 1, :]
    out_ref[...] = line_ref[...].astype(BF16)


def attend_moved(prepared, pieces, requests, features):
    rows = prepared[0].shape[0]
    width = rows // requests * 128
    return pl.pallas_call(
        functools.partial(moved_kernel, len(pieces), features),
        in_specs=[VMEM] * (len(prepared) + len(pieces)),
        out_specs=VMEM,
        out_shape=jax.ShapeDtypeStruct((requests, width), BF16),
        scratch_shapes=[pltpu.VMEM((requests, width), F32)],
        compiler_params=pltpu.CompilerParams(vmem_limit_bytes=16 * MIB),
        cost_estimate=pl.CostEstimate(
            flops=4 * rows * rows * 128 * 64, bytes_accessed=4 * 1024 * 1024, transcendentals=rows * 128
        ),
        name="attend_moved",
    )(*prepared, *pieces)


def combine_kernel(ranks, residents, kv_mine, ask_ref, *rest):
    refs, out_ref = rest[:ranks], rest[ranks]
    heads_mine = out_ref.shape[1] // 128
    scale = F32(1.0) / jnp.sqrt(F32(128.0))
    payloads = [ref[...].astype(F32) for ref in refs]
    at = residents * heads_mine
    ask = ask_ref[...].astype(F32)
    for r in range(residents):
        q, own_k, own_v = heads_of(ask[r : r + 1], heads_mine, kv_mine)
        own_score = jnp.sum(q * own_k, axis=1, keepdims=True) * scale
        peaks, totals = [], []
        for payload in payloads:
            stat = payload[at : at + 3 * residents]
            peaks.append(row_to_column(stat[r : r + 1], heads_mine))
            total = stat[residents + r : residents + r + 1]
            total = total + stat[2 * residents + r : 2 * residents + r + 1]
            totals.append(row_to_column(total, heads_mine))
        top = own_score
        for peak in peaks:
            top = jnp.maximum(top, peak)
        own_weight = jnp.exp(own_score - top)
        denom = own_weight
        numer = own_weight.astype(BF16).astype(F32) * own_v
        for peak, total, payload in zip(peaks, totals, payloads):
            keep = jnp.exp(peak - top)
            denom = denom + keep * total
            numer = numer + keep * payload[r * heads_mine : (r + 1) * heads_mine]
        result = numer / denom
        for h in range(heads_mine):
            out_ref[r : r + 1, h * 128 : (h + 1) * 128] = result[h : h + 1, :]


def combine_resident(ask, payloads, residents, heads_mine, kv_mine):
    return pl.pallas_call(
        functools.partial(combine_kernel, len(payloads), residents, kv_mine),
        in_specs=[VMEM] * (1 + len(payloads)),
        out_specs=VMEM,
        out_shape=jax.ShapeDtypeStruct((residents, heads_mine * 128), F32),
        compiler_params=pltpu.CompilerParams(vmem_limit_bytes=8 * MIB),
        name="combine_resident",
    )(ask, *payloads)


def finish_kernel(kept_ref, place_ref, *rest):
    moved, out_ref = rest[:-1], rest[-1]
    residents = kept_ref.shape[0]
    decoded, width = out_ref.shape
    requests = decoded - residents
    row = iota((decoded, 128), 0)
    arrived = [ref[...].astype(F32) for ref in moved]
    for c in range(0, width, 128):
        kept = kept_ref[:, c : c + 128]
        line = jnp.concatenate([kept, jnp.zeros((requests, 128), F32)], axis=0)
        for b in range(len(moved)):
            for i in range(requests):
                at = (b + 1) * requests + i
                line = jnp.where(
                    place_ref[at : at + 1, :] == row, arrived[b][i : i + 1, c : c + 128], line
                )
        out_ref[:, c : c + 128] = line.astype(BF16)


def finish(kept, places, moved, requests):
    residents, width = kept.shape
    return pl.pallas_call(
        finish_kernel,
        in_specs=[VMEM] * (2 + len(moved)),
        out_specs=VMEM,
        out_shape=jax.ShapeDtypeStruct((residents + requests, width), BF16),
        compiler_params=pltpu.CompilerParams(vmem_limit_bytes=8 * MIB),
        name="finish",
    )(kept, places, *moved)


def swapped(x, axis, j, n):
    return lax.ppermute(x, axis, [(i, i ^ j) for i in range(n)])


def rotation(slots, requests, head_size):
    half = head_size // 2
    freq = THETA ** (-np.arange(half) * 2.0 / head_size)
    angle = np.repeat(np.arange(slots), requests)[:, None] * freq[None, :]
    cos, sin = np.cos(angle), np.sin(angle)
    return (
        np.concatenate([cos, cos], axis=1).astype(np.float32),
        np.concatenate([-sin, sin], axis=1).astype(np.float32),
    )


def per_device(
    mig_hidden,
    mig_dest,
    mig_count,
    attn_gain,
    kv_weight,
    k_gain,
    query,
    new_kv,
    k_cache,
    v_cache,
    lengths,
):
    insts = lax.axis_size("inst")
    ranks = lax.axis_size("tp")
    head_size = k_gain.shape[0]
    slots, requests, feats = mig_hidden.shape[1:]
    residents = k_cache.shape[1]
    heads = query.shape[2] // head_size
    kv_heads = kv_weight.shape[1] // 2 // head_size
    heads_mine = heads // ranks
    group = heads // kv_heads
    kv_mine = max(1, heads_mine // group)

    pieces, ask = project(
        mig_hidden[0], attn_gain, kv_weight, query[0], new_kv[0], ranks, group, kv_mine
    )
    last = ranks - 1
    far = swapped(pieces[last], "tp", last, ranks)
    asks = [swapped(ask, "inst", b, insts) for b in range(1, insts)]
    asks[0], *others = lax.optimization_barrier((asks[0], *pieces[1:last]))
    others = [swapped(others[j - 1], "tp", j, ranks) for j in reversed(range(1, last))]
    pieces = [pieces[0], far] + others
    payloads = attend_resident(lengths, query[0], k_cache[0], v_cache[0], ranks)
    own_payload = payloads[0]
    payloads = [swapped(payloads[j], "tp", j, ranks) for j in reversed(range(1, ranks))]
    cos, sin = rotation(slots, requests, head_size)
    *prepared, places = prepare(
        mig_dest.T,
        mig_count.T,
        k_gain.reshape(1, head_size),
        cos,
        sin,
        asks,
        residents,
        heads_mine,
        kv_mine,
    )
    prepared[0], own_payload = lax.optimization_barrier((prepared[0], own_payload))
    moved = attend_moved(prepared, pieces, requests, feats * ranks)
    kept = combine_resident(ask, [own_payload] + payloads, residents, heads_mine, kv_mine)
    moved = [swapped(moved, "inst", b, insts) for b in reversed(range(1, insts))][::-1]
    return finish(kept, places, moved, requests)[None]


def solution(mesh):
    placed = (
        P(("group", "inst"), None, None, "tp"),
        P("group", None),
        P("group", None),
        P("tp"),
        P("tp", None),
        P(),
        P(("group", "inst"), None, None),
        P(("group", "inst"), None, None),
        P(("group", "inst"), None, "tp", None),
        P(("group", "inst"), None, "tp", None),
        P(("group", "inst"), None),
    )
    return jax.shard_map(
        per_device,
        mesh=mesh,
        in_specs=placed,
        out_specs=P(("group", "inst"), None, "tp"),
        check_vma=False,
    )
```

```python
import functools

import jax
import jax.numpy as jnp
import numpy as np
from jax import lax
from jax.experimental import pallas as pl
from jax.experimental.pallas import tpu as pltpu
from jax.sharding import PartitionSpec as P

EPS = 1e-06
THETA = 1000000.0
ABSENT = -1e30
F32 = jnp.float32
BF16 = jnp.bfloat16
MIB = 1024 * 1024
CHUNK = 512
AHEAD = 4

VMEM = pl.BlockSpec(memory_space=pltpu.VMEM)
SMEM = pl.BlockSpec(memory_space=pltpu.SMEM)
HBM = pl.BlockSpec(memory_space=pltpu.HBM)


def iota(shape, dim):
    return lax.broadcasted_iota(jnp.int32, shape, dim)


def column_to_row(column, period):
    n = column.shape[0]
    spread = jnp.where(iota((n, 128), 0) % period == iota((n, 128), 1), column, 0.0)
    return jnp.sum(spread.reshape(n // period, period, 128), axis=1)


def row_to_column(row, n):
    return jnp.sum(
        jnp.where(iota((n, 128), 0) == iota((n, 128), 1), row, 0.0), axis=1, keepdims=True
    )


def split_bf16(x):
    high = x.astype(BF16)
    return high, (x - high.astype(F32)).astype(BF16)


def project_kernel(ranks, group, gain_hbm, x_hbm, w_hbm, q_hbm, own_hbm, *rest):
    outs, ask_ref = rest[:ranks], rest[ranks]
    gain_ref, x_ref, w_ref, acc_ref, in_sems, w_sems = rest[ranks + 1 :]
    slots, requests, feats = x_ref.shape
    rows = slots * requests
    piece = outs[0].shape[1] // 2
    kv_width = w_hbm.shape[1] // 2
    heads_mine = kv_width // 128 * group // ranks
    rank = lax.axis_index("tp")

    def first_column(target):
        return pl.multiple_of(target * heads_mine // group * 128, 128)

    gain_copy = pltpu.make_async_copy(gain_hbm, gain_ref, in_sems.at[0])
    gain_copy.start()
    x_copy = pltpu.make_async_copy(x_hbm, x_ref, in_sems.at[1])
    x_copy.start()
    cuts = list(range(0, feats, CHUNK)) + [feats]
    chunks = list(zip(cuts[:-1], cuts[1:]))
    copies = []
    for i, (low, high) in enumerate(chunks):
        copies.append(
            pltpu.make_async_copy(w_hbm.at[low:high, :], w_ref.at[low:high, :], w_sems.at[i])
        )
        copies[-1].start()
    mine = heads_mine * 128
    q_first = pl.multiple_of(rank * mine, 128)
    asking = [
        pltpu.make_async_copy(
            q_hbm.at[:, pl.ds(q_first, mine)], ask_ref.at[:, :mine], in_sems.at[2]
        )
    ]
    for i in range(2):
        asking.append(
            pltpu.make_async_copy(
                own_hbm.at[:, pl.ds(i * kv_width + first_column(rank), piece)],
                ask_ref.at[:, mine + i * piece : mine + (i + 1) * piece],
                in_sems.at[3 + i],
            )
        )
    for copy in asking:
        copy.start()
    gain_copy.wait()
    x_copy.wait()
    squares = jnp.zeros((rows, 128), F32)
    for i, (low, high) in enumerate(chunks):
        parts = []
        for c in range(low, high, 128):
            width = min(128, high - c)
            x = x_ref[:, :, c : c + width].astype(F32).reshape(rows, width)
            gain = gain_ref[c : c + width].astype(F32).reshape(1, width)
            parts.append((x * gain).astype(BF16))
            x = x * x
            if width < 128:
                x = jnp.concatenate([x, jnp.zeros((rows, 128 - width), F32)], axis=1)
            squares = squares + x
        xg = parts[0] if len(parts) == 1 else jnp.concatenate(parts, axis=1)
        copies[i].wait()
        for n in range(0, 2 * kv_width, 512):
            part = jnp.dot(xg, w_ref[low:high, n : n + 512], preferred_element_type=F32)
            if i == 0:
                acc_ref[:, n : n + 512] = part
            else:
                acc_ref[:, n : n + 512] += part
    sq = column_to_row(jnp.sum(squares, axis=1, keepdims=True), 128)
    high, low = split_bf16(sq)
    tail = jnp.concatenate([high.astype(F32), low.astype(F32)], axis=0)
    fill = outs[1].shape[0] - rows - tail.shape[0]
    if fill:
        tail = jnp.concatenate([tail, jnp.zeros((fill, 128), F32)], axis=0)
    extra = jnp.concatenate([tail.astype(BF16)] * (2 * piece // 128), axis=1)
    for j in range(ranks):
        first = first_column(rank ^ j)
        outs[j][:rows, :piece] = acc_ref[:, pl.ds(first, piece)].astype(BF16)
        outs[j][:rows, piece:] = acc_ref[:, pl.ds(kv_width + first, piece)].astype(BF16)
        outs[j][rows:, :] = extra
    for copy in asking:
        copy.wait()


def project(x, gain, weight, query, own, ranks, group, kv_mine):
    slots, requests, feats = x.shape
    rows = slots * requests
    piece = kv_mine * 128
    extra = -(-2 * (rows // 128) // 8) * 8
    decoded, q_width = query.shape
    outs = pl.pallas_call(
        functools.partial(project_kernel, ranks, group),
        in_specs=[HBM] * 5,
        out_specs=[VMEM] * (ranks + 1),
        out_shape=[jax.ShapeDtypeStruct((rows + extra, 2 * piece), BF16)] * ranks
        + [jax.ShapeDtypeStruct((decoded, q_width // ranks + 2 * piece), BF16)],
        scratch_shapes=[
            pltpu.VMEM((feats,), BF16),
            pltpu.VMEM((slots, requests, feats), BF16),
            pltpu.VMEM(weight.shape, BF16),
            pltpu.VMEM((rows, weight.shape[1]), F32),
            pltpu.SemaphoreType.DMA((5,)),
            pltpu.SemaphoreType.DMA((-(-feats // CHUNK),)),
        ],
        compiler_params=pltpu.CompilerParams(vmem_limit_bytes=56 * MIB),
        cost_estimate=pl.CostEstimate(
            flops=2 * rows * feats * weight.shape[1],
            bytes_accessed=2 * feats * weight.shape[1],
            transcendentals=0,
        ),
        name="project",
    )(gain, x, weight, query, own)
    return outs[:ranks], outs[ranks]


def resident_kernel(ranks, len_hbm, q_hbm, k_hbm, v_hbm, *rest):
    outs = rest[:ranks]
    len_ref, q_ref, q_all, k_buf, v_buf, wide_ref, s_buf, w_buf, o_all, s_all, in_sems, sems = rest[
        ranks:
    ]
    residents, positions, width = k_buf.shape
    half = positions // 2
    chunks = []
    for r in range(residents):
        for hbm, buf in ((k_hbm, k_buf), (v_hbm, v_buf)):
            for i in range(2):
                at = slice(i * half, (i + 1) * half)
                chunks.append(
                    pltpu.make_async_copy(
                        hbm.at[r, at, :], buf.at[r, at, :], sems.at[len(chunks)]
                    )
                )
    for chunk in chunks[:AHEAD]:
        chunk.start()
    q_copy = pltpu.make_async_copy(q_hbm, q_ref, in_sems.at[0])
    len_copy = pltpu.make_async_copy(len_hbm, len_ref, in_sems.at[1])
    q_copy.start()
    len_copy.start()

    def arrived(i):
        chunks[i].wait()
        if i + AHEAD < len(chunks):
            chunks[i + AHEAD].start()

    heads = q_ref.shape[1] // 128
    kv_heads = width // 128
    group = heads // kv_heads
    heads_mine = heads // ranks
    rank = lax.axis_index("tp")
    position = rank * positions + iota((16, positions), 1)
    scale = F32(1.0) / jnp.sqrt(F32(128.0))
    diagonal = iota((heads, 128), 0) % heads_mine == iota((heads, 128), 1)
    own_block = iota((heads, width), 0) // group == iota((heads, width), 1) // 128

    def to_rows(columns):
        spread = jnp.where(diagonal, jnp.concatenate(columns, axis=0), 0.0)
        return jnp.sum(spread.reshape(ranks, heads_mine, 128), axis=1)

    q_copy.wait()
    for h in range(heads):
        q_all[h * 8 : h * 8 + residents, :] = q_ref[:residents, h * 128 : (h + 1) * 128].astype(F32)
    peaks, totals = [], []
    for r in range(residents):
        q = q_all[pl.ds(r, heads, stride=8), :].astype(BF16)
        wide = jnp.concatenate([q] * kv_heads, axis=1)
        wide_ref[...] = jnp.where(own_block, wide, jnp.zeros_like(wide))
        peaks.append([])
        totals.append([])
        for i in range(2):
            arrived(4 * r + i)
            at = slice(i * half, (i + 1) * half)
            s_buf[:, at] = lax.dot_general(
                wide_ref[...],
                k_buf[r, at, :],
                (((1,), (1,)), ((), ())),
                preferred_element_type=F32,
            )
        if r == 0:
            len_copy.wait()
        valid = position < len_ref[0:1, r : r + 1]
        for c in range(0, heads, 16):
            rows = slice(c, c + 16)
            scores = jnp.where(valid, s_buf[rows, :] * scale, ABSENT)
            peak = jnp.max(scores, axis=1, keepdims=True).astype(BF16).astype(F32)
            weight = jnp.where(valid, jnp.exp(scores - peak), 0.0)
            peaks[r].append(peak)
            totals[r].append(jnp.sum(weight, axis=1, keepdims=True))
            w_buf[rows, :] = weight.astype(BF16)
        for i in range(2):
            arrived(4 * r + 2 + i)
            at = slice(i * half, (i + 1) * half)
            part = jnp.dot(w_buf[:, at], v_buf[r, at, :], preferred_element_type=F32)
            for g in range(kv_heads):
                rows = slice(g * group, (g + 1) * group)
                block = part[rows, g * 128 : (g + 1) * 128]
                if i == 0:
                    o_all[r, rows, :] = block
                else:
                    o_all[r, rows, :] += block
    for r in range(residents):
        s_all[r, 0] = to_rows(peaks[r])
        high, low = split_bf16(to_rows(totals[r]))
        s_all[r, 1] = high.astype(F32)
        s_all[r, 2] = low.astype(F32)
    filled = residents * (heads_mine + 3)
    for j in range(ranks):
        target = rank ^ j
        first = pl.multiple_of(target * heads_mine, heads_mine)
        parts = [o_all[r, pl.ds(first, heads_mine), :] for r in range(residents)]
        parts += [s_all[r, i, pl.ds(target, 1), :] for i in range(3) for r in range(residents)]
        if outs[j].shape[0] > filled:
            parts.append(jnp.zeros((outs[j].shape[0] - filled, 128), F32))
        outs[j][...] = jnp.concatenate(parts, axis=0).astype(BF16)


def attend_resident(lengths, query, k_cache, v_cache, ranks):
    residents, positions, width = k_cache.shape
    heads = query.shape[1] // 128
    heads_mine = heads // ranks
    rows = -(-(residents * (heads_mine + 3)) // 16) * 16
    return pl.pallas_call(
        functools.partial(resident_kernel, ranks),
        in_specs=[HBM] * 4,
        out_specs=[VMEM] * ranks,
        out_shape=[jax.ShapeDtypeStruct((rows, 128), BF16)] * ranks,
        scratch_shapes=[
            pltpu.VMEM(lengths.shape, jnp.int32),
            pltpu.VMEM(query.shape, BF16),
            pltpu.VMEM((heads * 8, 128), F32),
            pltpu.VMEM((residents, positions, width), BF16),
            pltpu.VMEM((residents, positions, width), BF16),
            pltpu.VMEM((heads, width), BF16),
            pltpu.VMEM((heads, positions), F32),
            pltpu.VMEM((heads, positions), BF16),
            pltpu.VMEM((residents, heads, 128), F32),
            pltpu.VMEM((residents, 3, ranks, 128), F32),
            pltpu.SemaphoreType.DMA((2,)),
            pltpu.SemaphoreType.DMA((4 * residents,)),
        ],
        compiler_params=pltpu.CompilerParams(vmem_limit_bytes=56 * MIB),
        cost_estimate=pl.CostEstimate(
            flops=4 * residents * heads * positions * 128,
            bytes_accessed=4 * residents * positions * width,
            transcendentals=residents * heads * positions,
        ),
        name="attend_resident",
    )(lengths, query, k_cache, v_cache)


def expand(own, rows):
    which = iota((rows, 128), 0) // (rows // own.shape[0])
    out = jnp.broadcast_to(own[0:1], (rows, 128))
    for h in range(1, own.shape[0]):
        out = jnp.where(which == h, own[h : h + 1], out)
    return out


def heads_of(line, heads_mine, kv_mine):
    per = heads_mine // kv_mine
    blocks = [line[:, c : c + 128] for c in range(0, line.shape[1], 128)]
    q = jnp.concatenate(blocks[:heads_mine], axis=0)
    k = blocks[heads_mine : heads_mine + kv_mine]
    v = blocks[heads_mine + kv_mine :]
    return (
        q,
        expand(jnp.concatenate(k, axis=0), heads_mine),
        expand(jnp.concatenate(v, axis=0), heads_mine),
    )


def prepare_kernel(insts, residents, kv_mine, dest_ref, count_ref, gain_ref, cos_ref, sin_ref, *rest):
    asks, rest = rest[: insts - 1], rest[insts - 1 :]
    q_out, own_out, limit_out, cos_out, sin_out, place_out, line_ref, q_ref, k_ref = rest
    requests = dest_ref.shape[0]
    rows = q_out.shape[0]
    heads_mine = rows // requests
    here = lax.axis_index("inst")
    ask_row = iota(asks[0].shape, 0)
    limit = jnp.zeros((rows, 128), jnp.int32)
    for r in range(requests):
        dest = dest_ref[r, here]
        limit = jnp.where(iota((rows, 128), 0) // heads_mine == r, count_ref[r, here], limit)
        place = jnp.int32(residents)
        for s in range(insts):
            for c in range(requests):
                place += jnp.where((dest_ref[c, s] == dest) & (here > s), 1, 0).astype(jnp.int32)
        for b in range(1, insts):

            @pl.when(here ^ b == dest)
            def _():
                ask = asks[b - 1][...].astype(F32)
                line_ref[r : r + 1, :] = jnp.sum(
                    jnp.where(ask_row == place, ask, 0.0), axis=0, keepdims=True
                )

        at = slice(r * heads_mine, (r + 1) * heads_mine)
        q_ref[at, :], k_ref[at, :], own_out[0, at, :] = heads_of(
            line_ref[r : r + 1, :], heads_mine, kv_mine
        )
    scale = F32(1.0) / jnp.sqrt(F32(128.0))
    q = q_ref[...]
    q_out[...] = q.astype(BF16)
    own_out[1] = jnp.broadcast_to(
        jnp.sum(q * k_ref[...], axis=1, keepdims=True) * scale, (rows, 128)
    )
    limit_out[...] = limit
    gain = gain_ref[...].astype(F32)
    cos_out[...] = cos_ref[...] * gain
    sin_out[...] = sin_ref[...] * pltpu.roll(jnp.broadcast_to(gain, (8, 128)), 64, 1)[:1]
    places = jnp.full(place_out.shape, -1, jnp.int32)
    row = iota(place_out.shape, 0)
    place = jnp.int32(residents)
    for s in range(insts):
        for c in range(requests):
            mine = dest_ref[c, s] == here
            places = jnp.where((row == (here ^ s) * requests + c) & mine, place, places)
            place += jnp.where(mine, 1, 0).astype(jnp.int32)
    place_out[...] = places


def prepare(dest, count, k_gain, cos, sin, asks, residents, heads_mine, kv_mine):
    requests, insts = dest.shape
    rows = requests * heads_mine
    return pl.pallas_call(
        functools.partial(prepare_kernel, insts, residents, kv_mine),
        in_specs=[SMEM] * 2 + [VMEM] * (3 + len(asks)),
        out_specs=[VMEM] * 6,
        out_shape=[
            jax.ShapeDtypeStruct((rows, 128), BF16),
            jax.ShapeDtypeStruct((2, rows, 128), F32),
            jax.ShapeDtypeStruct((rows, 128), jnp.int32),
            jax.ShapeDtypeStruct(cos.shape, F32),
            jax.ShapeDtypeStruct(sin.shape, F32),
            jax.ShapeDtypeStruct((insts * requests, 128), jnp.int32),
        ],
        scratch_shapes=[
            pltpu.VMEM((requests, asks[0].shape[1]), F32),
            pltpu.VMEM((rows, 128), F32),
            pltpu.VMEM((rows, 128), F32),
        ],
        compiler_params=pltpu.CompilerParams(vmem_limit_bytes=16 * MIB),
        name="prepare",
    )(dest, count, k_gain, cos, sin, *asks)


def moved_kernel(ranks, features, q_ref, own_ref, limit_ref, cos_ref, sin_ref, *rest):
    pieces = rest[:ranks]
    out_ref, line_ref = rest[ranks:]
    requests = out_ref.shape[0]
    tokens = cos_ref.shape[0]
    piece = pieces[0].shape[1] // 2
    kv_mine = piece // 128
    rows = q_ref.shape[0]
    heads_mine = rows // requests
    scale = F32(1.0) / jnp.sqrt(F32(128.0))

    blocks = tokens // 128
    last = tokens + 2 * blocks
    tail = pieces[0][tokens:last, :128].astype(F32)
    for t in range(1, ranks):
        tail = tail + pieces[t][tokens:last, :128].astype(F32)
    squares = tail[:blocks] + tail[blocks:]
    squares = jnp.concatenate(
        [row_to_column(squares[b : b + 1], 128) for b in range(blocks)], axis=0
    )
    token_scale = lax.rsqrt(squares / features + EPS)

    def column_block(c):
        total = pieces[0][:tokens, c : c + 128].astype(F32)
        for t in range(1, ranks):
            total = total + pieces[t][:tokens, c : c + 128].astype(F32)
        return total * token_scale

    q = q_ref[...]
    which = iota((rows, tokens), 0) % heads_mine // (heads_mine // kv_mine)
    scores = None
    for h in range(kv_mine):
        key = column_block(h * 128)
        key = key * lax.rsqrt(jnp.mean(key * key, axis=1, keepdims=True) + EPS)
        key = key * cos_ref[...] + pltpu.roll(key, 64, 1) * sin_ref[...]
        part = lax.dot_general(
            q, key.astype(BF16), (((1,), (1,)), ((), ())), preferred_element_type=F32
        )
        scores = part if scores is None else jnp.where(which == h, part, scores)
    token = iota((rows, tokens), 1)
    limit = jnp.concatenate([limit_ref[...]] * (tokens // 128), axis=1)
    valid = (token % requests == iota((rows, tokens), 0) // heads_mine) & (
        token // requests < limit
    )
    scores = jnp.where(valid, scores * scale, ABSENT)
    own_score = own_ref[1]
    top = jnp.maximum(jnp.max(scores, axis=1, keepdims=True), own_score)
    weights = jnp.where(
        valid, jnp.exp(scores - jnp.concatenate([top] * (tokens // 128), axis=1)), 0.0
    )
    own_weight = jnp.exp(own_score - top)
    total = jnp.sum(weights, axis=1, keepdims=True) + own_weight
    weights = weights.astype(BF16)
    summed = None
    for h in range(kv_mine):
        value = column_block(piece + h * 128).astype(BF16)
        part = jnp.dot(weights, value, preferred_element_type=F32)
        summed = part if summed is None else jnp.where(which[:, :128] == h, part, summed)
    summed = summed + own_weight.astype(BF16).astype(F32) * own_ref[0]
    result = summed / total
    for r in range(requests):
        for h in range(heads_mine):
            at = r * heads_mine + h
            line_ref[r : r + 1, h * 128 : (h + 1) * 128] = result[at : at + 1, :]
    out_ref[...] = line_ref[...].astype(BF16)


def attend_moved(prepared, pieces, requests, features):
    rows = prepared[0].shape[0]
    width = rows // requests * 128
    return pl.pallas_call(
        functools.partial(moved_kernel, len(pieces), features),
        in_specs=[VMEM] * (len(prepared) + len(pieces)),
        out_specs=VMEM,
        out_shape=jax.ShapeDtypeStruct((requests, width), BF16),
        scratch_shapes=[pltpu.VMEM((requests, width), F32)],
        compiler_params=pltpu.CompilerParams(vmem_limit_bytes=16 * MIB),
        cost_estimate=pl.CostEstimate(
            flops=4 * rows * rows * 128 * 64, bytes_accessed=4 * 1024 * 1024, transcendentals=rows * 128
        ),
        name="attend_moved",
    )(*prepared, *pieces)


def combine_kernel(ranks, residents, kv_mine, ask_ref, *rest):
    refs, out_ref = rest[:ranks], rest[ranks]
    heads_mine = out_ref.shape[1] // 128
    scale = F32(1.0) / jnp.sqrt(F32(128.0))
    payloads = [ref[...].astype(F32) for ref in refs]
    at = residents * heads_mine
    ask = ask_ref[...].astype(F32)
    for r in range(residents):
        q, own_k, own_v = heads_of(ask[r : r + 1], heads_mine, kv_mine)
        own_score = jnp.sum(q * own_k, axis=1, keepdims=True) * scale
        peaks, totals = [], []
        for payload in payloads:
            stat = payload[at : at + 3 * residents]
            peaks.append(row_to_column(stat[r : r + 1], heads_mine))
            total = stat[residents + r : residents + r + 1]
            total = total + stat[2 * residents + r : 2 * residents + r + 1]
            totals.append(row_to_column(total, heads_mine))
        top = own_score
        for peak in peaks:
            top = jnp.maximum(top, peak)
        own_weight = jnp.exp(own_score - top)
        denom = own_weight
        numer = own_weight.astype(BF16).astype(F32) * own_v
        for peak, total, payload in zip(peaks, totals, payloads):
            keep = jnp.exp(peak - top)
            denom = denom + keep * total
            numer = numer + keep * payload[r * heads_mine : (r + 1) * heads_mine]
        result = numer / denom
        for h in range(heads_mine):
            out_ref[r : r + 1, h * 128 : (h + 1) * 128] = result[h : h + 1, :]


def combine_resident(ask, payloads, residents, heads_mine, kv_mine):
    return pl.pallas_call(
        functools.partial(combine_kernel, len(payloads), residents, kv_mine),
        in_specs=[VMEM] * (1 + len(payloads)),
        out_specs=VMEM,
        out_shape=jax.ShapeDtypeStruct((residents, heads_mine * 128), F32),
        compiler_params=pltpu.CompilerParams(vmem_limit_bytes=8 * MIB),
        name="combine_resident",
    )(ask, *payloads)


def finish_kernel(kept_ref, place_ref, *rest):
    moved, out_ref = rest[:-1], rest[-1]
    residents = kept_ref.shape[0]
    decoded, width = out_ref.shape
    requests = decoded - residents
    row = iota((decoded, 128), 0)
    arrived = [ref[...].astype(F32) for ref in moved]
    for c in range(0, width, 128):
        kept = kept_ref[:, c : c + 128]
        line = jnp.concatenate([kept, jnp.zeros((requests, 128), F32)], axis=0)
        for b in range(len(moved)):
            for i in range(requests):
                at = (b + 1) * requests + i
                line = jnp.where(
                    place_ref[at : at + 1, :] == row, arrived[b][i : i + 1, c : c + 128], line
                )
        out_ref[:, c : c + 128] = line.astype(BF16)


def finish(kept, places, moved, requests):
    residents, width = kept.shape
    return pl.pallas_call(
        finish_kernel,
        in_specs=[VMEM] * (2 + len(moved)),
        out_specs=VMEM,
        out_shape=jax.ShapeDtypeStruct((residents + requests, width), BF16),
        compiler_params=pltpu.CompilerParams(vmem_limit_bytes=8 * MIB),
        name="finish",
    )(kept, places, *moved)


def swapped(x, axis, j, n):
    return lax.ppermute(x, axis, [(i, i ^ j) for i in range(n)])


def rotation(slots, requests, head_size):
    half = head_size // 2
    freq = THETA ** (-np.arange(half) * 2.0 / head_size)
    angle = np.repeat(np.arange(slots), requests)[:, None] * freq[None, :]
    cos, sin = np.cos(angle), np.sin(angle)
    return (
        np.concatenate([cos, cos], axis=1).astype(np.float32),
        np.concatenate([-sin, sin], axis=1).astype(np.float32),
    )


def per_device(
    mig_hidden,
    mig_dest,
    mig_count,
    attn_gain,
    kv_weight,
    k_gain,
    query,
    new_kv,
    k_cache,
    v_cache,
    lengths,
):
    insts = lax.axis_size("inst")
    ranks = lax.axis_size("tp")
    head_size = k_gain.shape[0]
    slots, requests, feats = mig_hidden.shape[1:]
    residents = k_cache.shape[1]
    heads = query.shape[2] // head_size
    kv_heads = kv_weight.shape[1] // 2 // head_size
    heads_mine = heads // ranks
    group = heads // kv_heads
    kv_mine = max(1, heads_mine // group)

    pieces, ask = project(
        mig_hidden[0], attn_gain, kv_weight, query[0], new_kv[0], ranks, group, kv_mine
    )
    last = ranks - 1
    far = swapped(pieces[last], "tp", last, ranks)
    asks = [swapped(ask, "inst", b, insts) for b in range(1, insts)]
    asks[0], *others = lax.optimization_barrier((asks[0], *pieces[1:last]))
    others = [swapped(others[j - 1], "tp", j, ranks) for j in reversed(range(1, last))]
    pieces = [pieces[0], far] + others
    payloads = attend_resident(lengths, query[0], k_cache[0], v_cache[0], ranks)
    own_payload = swapped(payloads[0], "tp", 0, ranks)
    payloads = [swapped(payloads[j], "tp", j, ranks) for j in reversed(range(1, ranks))]
    cos, sin = rotation(slots, requests, head_size)
    *prepared, places = prepare(
        mig_dest.T,
        mig_count.T,
        k_gain.reshape(1, head_size),
        cos,
        sin,
        asks,
        residents,
        heads_mine,
        kv_mine,
    )
    prepared[0], own_payload = lax.optimization_barrier((prepared[0], own_payload))
    moved = attend_moved(prepared, pieces, requests, feats * ranks)
    kept = combine_resident(ask, [own_payload] + payloads, residents, heads_mine, kv_mine)
    moved = [swapped(moved, "inst", b, insts) for b in reversed(range(1, insts))][::-1]
    return finish(kept, places, moved, requests)[None]


def solution(mesh):
    placed = (
        P(("group", "inst"), None, None, "tp"),
        P("group", None),
        P("group", None),
        P("tp"),
        P("tp", None),
        P(),
        P(("group", "inst"), None, None),
        P(("group", "inst"), None, None),
        P(("group", "inst"), None, "tp", None),
        P(("group", "inst"), None, "tp", None),
        P(("group", "inst"), None),
    )
    return jax.shard_map(
        per_device,
        mesh=mesh,
        in_specs=placed,
        out_specs=P(("group", "inst"), None, "tp"),
        check_vma=False,
    )
```

```python
import functools

import jax
import jax.numpy as jnp
import numpy as np
from jax import lax
from jax.experimental import pallas as pl
from jax.experimental.pallas import tpu as pltpu
from jax.sharding import PartitionSpec as P

EPS = 1e-06
THETA = 1000000.0
ABSENT = -1e30
F32 = jnp.float32
BF16 = jnp.bfloat16
MIB = 1024 * 1024
CHUNK = 512

VMEM = pl.BlockSpec(memory_space=pltpu.VMEM)
SMEM = pl.BlockSpec(memory_space=pltpu.SMEM)
HBM = pl.BlockSpec(memory_space=pltpu.HBM)


def iota(shape, dim):
    return lax.broadcasted_iota(jnp.int32, shape, dim)


def column_to_row(column, period):
    n = column.shape[0]
    spread = jnp.where(iota((n, 128), 0) % period == iota((n, 128), 1), column, 0.0)
    return jnp.sum(spread.reshape(n // period, period, 128), axis=1)


def row_to_column(row, n):
    return jnp.sum(
        jnp.where(iota((n, 128), 0) == iota((n, 128), 1), row, 0.0), axis=1, keepdims=True
    )


def split_bf16(x):
    high = x.astype(BF16)
    return high, (x - high.astype(F32)).astype(BF16)


def project_kernel(ranks, group, gain_hbm, x_hbm, w_hbm, q_hbm, own_hbm, *rest):
    outs, ask_ref = rest[:ranks], rest[ranks]
    gain_ref, x_ref, w_ref, acc_ref, in_sems, w_sems = rest[ranks + 1 :]
    slots, requests, feats = x_ref.shape
    rows = slots * requests
    piece = outs[0].shape[1] // 2
    kv_width = w_hbm.shape[1] // 2
    heads_mine = kv_width // 128 * group // ranks
    rank = lax.axis_index("tp")

    def first_column(target):
        return pl.multiple_of(target * heads_mine // group * 128, 128)

    gain_copy = pltpu.make_async_copy(gain_hbm, gain_ref, in_sems.at[0])
    gain_copy.start()
    x_copy = pltpu.make_async_copy(x_hbm, x_ref, in_sems.at[1])
    x_copy.start()
    cuts = list(range(0, feats, CHUNK)) + [feats]
    chunks = list(zip(cuts[:-1], cuts[1:]))
    copies = []
    for i, (low, high) in enumerate(chunks):
        copies.append(
            pltpu.make_async_copy(w_hbm.at[low:high, :], w_ref.at[low:high, :], w_sems.at[i])
        )
        copies[-1].start()
    mine = heads_mine * 128
    q_first = pl.multiple_of(rank * mine, 128)
    asking = [
        pltpu.make_async_copy(
            q_hbm.at[:, pl.ds(q_first, mine)], ask_ref.at[:, :mine], in_sems.at[2]
        )
    ]
    for i in range(2):
        asking.append(
            pltpu.make_async_copy(
                own_hbm.at[:, pl.ds(i * kv_width + first_column(rank), piece)],
                ask_ref.at[:, mine + i * piece : mine + (i + 1) * piece],
                in_sems.at[3 + i],
            )
        )
    for copy in asking:
        copy.start()
    gain_copy.wait()
    x_copy.wait()
    squares = jnp.zeros((rows, 128), F32)
    for i, (low, high) in enumerate(chunks):
        parts = []
        for c in range(low, high, 128):
            width = min(128, high - c)
            x = x_ref[:, :, c : c + width].astype(F32).reshape(rows, width)
            gain = gain_ref[c : c + width].astype(F32).reshape(1, width)
            parts.append((x * gain).astype(BF16))
            x = x * x
            if width < 128:
                x = jnp.concatenate([x, jnp.zeros((rows, 128 - width), F32)], axis=1)
            squares = squares + x
        xg = parts[0] if len(parts) == 1 else jnp.concatenate(parts, axis=1)
        copies[i].wait()
        for n in range(0, 2 * kv_width, 512):
            part = jnp.dot(xg, w_ref[low:high, n : n + 512], preferred_element_type=F32)
            if i == 0:
                acc_ref[:, n : n + 512] = part
            else:
                acc_ref[:, n : n + 512] += part
    sq = column_to_row(jnp.sum(squares, axis=1, keepdims=True), 128)
    high, low = split_bf16(sq)
    tail = jnp.concatenate([high.astype(F32), low.astype(F32)], axis=0)
    fill = outs[1].shape[0] - rows - tail.shape[0]
    if fill:
        tail = jnp.concatenate([tail, jnp.zeros((fill, 128), F32)], axis=0)
    extra = jnp.concatenate([tail.astype(BF16)] * (2 * piece // 128), axis=1)
    for j in range(ranks):
        first = first_column(rank ^ j)
        outs[j][:rows, :piece] = acc_ref[:, pl.ds(first, piece)].astype(BF16)
        outs[j][:rows, piece:] = acc_ref[:, pl.ds(kv_width + first, piece)].astype(BF16)
        outs[j][rows:, :] = extra
    for copy in asking:
        copy.wait()


def project(x, gain, weight, query, own, ranks, group, kv_mine):
    slots, requests, feats = x.shape
    rows = slots * requests
    piece = kv_mine * 128
    extra = -(-2 * (rows // 128) // 8) * 8
    decoded, q_width = query.shape
    outs = pl.pallas_call(
        functools.partial(project_kernel, ranks, group),
        in_specs=[HBM] * 5,
        out_specs=[VMEM] * (ranks + 1),
        out_shape=[jax.ShapeDtypeStruct((rows + extra, 2 * piece), BF16)] * ranks
        + [jax.ShapeDtypeStruct((decoded, q_width // ranks + 2 * piece), BF16)],
        scratch_shapes=[
            pltpu.VMEM((feats,), BF16),
            pltpu.VMEM((slots, requests, feats), BF16),
            pltpu.VMEM(weight.shape, BF16),
            pltpu.VMEM((rows, weight.shape[1]), F32),
            pltpu.SemaphoreType.DMA((5,)),
            pltpu.SemaphoreType.DMA((-(-feats // CHUNK),)),
        ],
        compiler_params=pltpu.CompilerParams(vmem_limit_bytes=56 * MIB),
        cost_estimate=pl.CostEstimate(
            flops=2 * rows * feats * weight.shape[1],
            bytes_accessed=2 * feats * weight.shape[1],
            transcendentals=0,
        ),
        name="project",
    )(gain, x, weight, query, own)
    return outs[:ranks], outs[ranks]


def resident_kernel(ranks, len_hbm, q_hbm, k_hbm, v_hbm, *rest):
    outs = rest[:ranks]
    len_ref, q_ref, q_all, k_buf, v_buf, wide_ref, s_buf, w_buf, o_all, s_all, in_sems, sems = rest[
        ranks:
    ]
    residents, positions, width = k_buf.shape
    half = positions // 2
    halves = [slice(i * half, (i + 1) * half) for i in range(2)]

    def copies(which, hbm, buf):
        return [
            [
                pltpu.make_async_copy(hbm.at[r, at, :], buf.at[r, at, :], sems.at[which, r, i])
                for i, at in enumerate(halves)
            ]
            for r in range(residents)
        ]

    k_copies, v_copies = copies(0, k_hbm, k_buf), copies(1, v_hbm, v_buf)
    len_copy = pltpu.make_async_copy(len_hbm, len_ref, in_sems.at[0])
    q_copy = pltpu.make_async_copy(q_hbm, q_ref, in_sems.at[1])
    len_copy.start()
    k_copies[0][0].start()
    q_copy.start()
    heads = q_ref.shape[1] // 128
    kv_heads = width // 128
    group = heads // kv_heads
    heads_mine = heads // ranks
    rank = lax.axis_index("tp")
    position = iota((16, positions), 1)
    scale = F32(1.0) / jnp.sqrt(F32(128.0))
    diagonal = iota((heads, 128), 0) % heads_mine == iota((heads, 128), 1)
    own_block = iota((heads, width), 0) // group == iota((heads, width), 1) // 128

    def to_rows(columns):
        spread = jnp.where(diagonal, jnp.concatenate(columns, axis=0), 0.0)
        return jnp.sum(spread.reshape(ranks, heads_mine, 128), axis=1)

    len_copy.wait()
    counts = [len_ref[0, r] - rank * positions for r in range(residents)]
    for r in range(residents):
        for of in (k_copies, v_copies):
            for i in range(2):
                if r > 0 or i > 0 or of is v_copies:
                    pl.when(counts[r] > i * half)(of[r][i].start)
    q_copy.wait()
    for h in range(heads):
        q_all[h * 8 : h * 8 + residents, :] = q_ref[:residents, h * 128 : (h + 1) * 128].astype(F32)
    k_copies[0][0].wait()
    for r in range(residents):
        some = counts[r] > 0

        @pl.when(some)
        def _():
            q = q_all[pl.ds(r, heads, stride=8), :].astype(BF16)
            wide = jnp.concatenate([q] * kv_heads, axis=1)
            wide_ref[...] = jnp.where(own_block, wide, jnp.zeros_like(wide))

        for i, at in enumerate(halves):

            @pl.when(counts[r] > i * half)
            def _():
                if r > 0 or i > 0:
                    k_copies[r][i].wait()
                s_buf[:, at] = lax.dot_general(
                    wide_ref[...],
                    k_buf[r, at, :],
                    (((1,), (1,)), ((), ())),
                    preferred_element_type=F32,
                )

        @pl.when(some)
        def _():
            valid = position < counts[r]
            peaks, totals = [], []
            for c in range(0, heads, 16):
                rows = slice(c, c + 16)
                scores = jnp.where(valid, s_buf[rows, :] * scale, ABSENT)
                peak = jnp.max(scores, axis=1, keepdims=True).astype(BF16).astype(F32)
                weight = jnp.where(valid, jnp.exp(scores - peak), 0.0)
                peaks.append(peak)
                totals.append(jnp.sum(weight, axis=1, keepdims=True))
                w_buf[rows, :] = weight.astype(BF16)
            s_all[r, 0] = to_rows(peaks)
            high, low = split_bf16(to_rows(totals))
            s_all[r, 1] = high.astype(F32)
            s_all[r, 2] = low.astype(F32)

        @pl.when(jnp.logical_not(some))
        def _():
            s_all[r, 0] = jnp.full((ranks, 128), ABSENT, F32)
            s_all[r, 1] = jnp.zeros((ranks, 128), F32)
            s_all[r, 2] = jnp.zeros((ranks, 128), F32)
            o_all[r] = jnp.zeros((heads, 128), F32)

        for i, at in enumerate(halves):

            @pl.when(counts[r] > i * half)
            def _():
                v_copies[r][i].wait()
                part = jnp.dot(w_buf[:, at], v_buf[r, at, :], preferred_element_type=F32)
                for g in range(kv_heads):
                    rows = slice(g * group, (g + 1) * group)
                    block = part[rows, g * 128 : (g + 1) * 128]
                    if i == 0:
                        o_all[r, rows, :] = block
                    else:
                        o_all[r, rows, :] += block

    filled = residents * (heads_mine + 3)
    for j in range(ranks):
        target = rank ^ j
        first = pl.multiple_of(target * heads_mine, heads_mine)
        parts = [o_all[r, pl.ds(first, heads_mine), :] for r in range(residents)]
        parts += [s_all[r, i, pl.ds(target, 1), :] for i in range(3) for r in range(residents)]
        if outs[j].shape[0] > filled:
            parts.append(jnp.zeros((outs[j].shape[0] - filled, 128), F32))
        outs[j][...] = jnp.concatenate(parts, axis=0).astype(BF16)


def attend_resident(lengths, query, k_cache, v_cache, ranks):
    residents, positions, width = k_cache.shape
    heads = query.shape[1] // 128
    heads_mine = heads // ranks
    rows = -(-(residents * (heads_mine + 3)) // 16) * 16
    return pl.pallas_call(
        functools.partial(resident_kernel, ranks),
        in_specs=[HBM] * 4,
        out_specs=[VMEM] * ranks,
        out_shape=[jax.ShapeDtypeStruct((rows, 128), BF16)] * ranks,
        scratch_shapes=[
            pltpu.SMEM(lengths.shape, jnp.int32),
            pltpu.VMEM(query.shape, BF16),
            pltpu.VMEM((heads * 8, 128), F32),
            pltpu.VMEM((residents, positions, width), BF16),
            pltpu.VMEM((residents, positions, width), BF16),
            pltpu.VMEM((heads, width), BF16),
            pltpu.VMEM((heads, positions), F32),
            pltpu.VMEM((heads, positions), BF16),
            pltpu.VMEM((residents, heads, 128), F32),
            pltpu.VMEM((residents, 3, ranks, 128), F32),
            pltpu.SemaphoreType.DMA((2,)),
            pltpu.SemaphoreType.DMA((2, residents, 2)),
        ],
        compiler_params=pltpu.CompilerParams(vmem_limit_bytes=56 * MIB),
        cost_estimate=pl.CostEstimate(
            flops=4 * residents * heads * positions * 128,
            bytes_accessed=4 * residents * positions * width,
            transcendentals=residents * heads * positions,
        ),
        name="attend_resident",
    )(lengths, query, k_cache, v_cache)


def expand(own, rows):
    which = iota((rows, 128), 0) // (rows // own.shape[0])
    out = jnp.broadcast_to(own[0:1], (rows, 128))
    for h in range(1, own.shape[0]):
        out = jnp.where(which == h, own[h : h + 1], out)
    return out


def heads_of(line, heads_mine, kv_mine):
    per = heads_mine // kv_mine
    blocks = [line[:, c : c + 128] for c in range(0, line.shape[1], 128)]
    q = jnp.concatenate(blocks[:heads_mine], axis=0)
    k = blocks[heads_mine : heads_mine + kv_mine]
    v = blocks[heads_mine + kv_mine :]
    return (
        q,
        expand(jnp.concatenate(k, axis=0), heads_mine),
        expand(jnp.concatenate(v, axis=0), heads_mine),
    )


def prepare_kernel(insts, residents, kv_mine, dest_ref, count_ref, gain_ref, cos_ref, sin_ref, *rest):
    asks, rest = rest[: insts - 1], rest[insts - 1 :]
    q_out, own_out, limit_out, cos_out, sin_out, place_out, line_ref, q_ref, k_ref = rest
    requests = dest_ref.shape[0]
    rows = q_out.shape[0]
    heads_mine = rows // requests
    here = lax.axis_index("inst")
    ask_row = iota(asks[0].shape, 0)
    limit = jnp.zeros((rows, 128), jnp.int32)
    for r in range(requests):
        dest = dest_ref[r, here]
        limit = jnp.where(iota((rows, 128), 0) // heads_mine == r, count_ref[r, here], limit)
        place = jnp.int32(residents)
        for s in range(insts):
            for c in range(requests):
                place += jnp.where((dest_ref[c, s] == dest) & (here > s), 1, 0).astype(jnp.int32)
        for b in range(1, insts):

            @pl.when(here ^ b == dest)
            def _():
                ask = asks[b - 1][...].astype(F32)
                line_ref[r : r + 1, :] = jnp.sum(
                    jnp.where(ask_row == place, ask, 0.0), axis=0, keepdims=True
                )

        at = slice(r * heads_mine, (r + 1) * heads_mine)
        q_ref[at, :], k_ref[at, :], own_out[0, at, :] = heads_of(
            line_ref[r : r + 1, :], heads_mine, kv_mine
        )
    scale = F32(1.0) / jnp.sqrt(F32(128.0))
    q = q_ref[...]
    q_out[...] = q.astype(BF16)
    own_out[1] = jnp.broadcast_to(
        jnp.sum(q * k_ref[...], axis=1, keepdims=True) * scale, (rows, 128)
    )
    limit_out[...] = limit
    gain = gain_ref[...].astype(F32)
    cos_out[...] = cos_ref[...] * gain
    sin_out[...] = sin_ref[...] * pltpu.roll(jnp.broadcast_to(gain, (8, 128)), 64, 1)[:1]
    places = jnp.full(place_out.shape, -1, jnp.int32)
    row = iota(place_out.shape, 0)
    place = jnp.int32(residents)
    for s in range(insts):
        for c in range(requests):
            mine = dest_ref[c, s] == here
            places = jnp.where((row == (here ^ s) * requests + c) & mine, place, places)
            place += jnp.where(mine, 1, 0).astype(jnp.int32)
    place_out[...] = places


def prepare(dest, count, k_gain, cos, sin, asks, residents, heads_mine, kv_mine):
    requests, insts = dest.shape
    rows = requests * heads_mine
    return pl.pallas_call(
        functools.partial(prepare_kernel, insts, residents, kv_mine),
        in_specs=[SMEM] * 2 + [VMEM] * (3 + len(asks)),
        out_specs=[VMEM] * 6,
        out_shape=[
            jax.ShapeDtypeStruct((rows, 128), BF16),
            jax.ShapeDtypeStruct((2, rows, 128), F32),
            jax.ShapeDtypeStruct((rows, 128), jnp.int32),
            jax.ShapeDtypeStruct(cos.shape, F32),
            jax.ShapeDtypeStruct(sin.shape, F32),
            jax.ShapeDtypeStruct((insts * requests, 128), jnp.int32),
        ],
        scratch_shapes=[
            pltpu.VMEM((requests, asks[0].shape[1]), F32),
            pltpu.VMEM((rows, 128), F32),
            pltpu.VMEM((rows, 128), F32),
        ],
        compiler_params=pltpu.CompilerParams(vmem_limit_bytes=16 * MIB),
        name="prepare",
    )(dest, count, k_gain, cos, sin, *asks)


def moved_kernel(ranks, features, q_ref, own_ref, limit_ref, cos_ref, sin_ref, *rest):
    pieces = rest[:ranks]
    out_ref, line_ref = rest[ranks:]
    requests = out_ref.shape[0]
    tokens = cos_ref.shape[0]
    piece = pieces[0].shape[1] // 2
    kv_mine = piece // 128
    rows = q_ref.shape[0]
    heads_mine = rows // requests
    scale = F32(1.0) / jnp.sqrt(F32(128.0))

    blocks = tokens // 128
    last = tokens + 2 * blocks
    tail = pieces[0][tokens:last, :128].astype(F32)
    for t in range(1, ranks):
        tail = tail + pieces[t][tokens:last, :128].astype(F32)
    squares = tail[:blocks] + tail[blocks:]
    squares = jnp.concatenate(
        [row_to_column(squares[b : b + 1], 128) for b in range(blocks)], axis=0
    )
    token_scale = lax.rsqrt(squares / features + EPS)

    def column_block(c):
        total = pieces[0][:tokens, c : c + 128].astype(F32)
        for t in range(1, ranks):
            total = total + pieces[t][:tokens, c : c + 128].astype(F32)
        return total * token_scale

    q = q_ref[...]
    which = iota((rows, tokens), 0) % heads_mine // (heads_mine // kv_mine)
    scores = None
    for h in range(kv_mine):
        key = column_block(h * 128)
        key = key * lax.rsqrt(jnp.mean(key * key, axis=1, keepdims=True) + EPS)
        key = key * cos_ref[...] + pltpu.roll(key, 64, 1) * sin_ref[...]
        part = lax.dot_general(
            q, key.astype(BF16), (((1,), (1,)), ((), ())), preferred_element_type=F32
        )
        scores = part if scores is None else jnp.where(which == h, part, scores)
    token = iota((rows, tokens), 1)
    limit = jnp.concatenate([limit_ref[...]] * (tokens // 128), axis=1)
    valid = (token % requests == iota((rows, tokens), 0) // heads_mine) & (
        token // requests < limit
    )
    scores = jnp.where(valid, scores * scale, ABSENT)
    own_score = own_ref[1]
    top = jnp.maximum(jnp.max(scores, axis=1, keepdims=True), own_score)
    weights = jnp.where(
        valid, jnp.exp(scores - jnp.concatenate([top] * (tokens // 128), axis=1)), 0.0
    )
    own_weight = jnp.exp(own_score - top)
    total = jnp.sum(weights, axis=1, keepdims=True) + own_weight
    weights = weights.astype(BF16)
    summed = None
    for h in range(kv_mine):
        value = column_block(piece + h * 128).astype(BF16)
        part = jnp.dot(weights, value, preferred_element_type=F32)
        summed = part if summed is None else jnp.where(which[:, :128] == h, part, summed)
    summed = summed + own_weight.astype(BF16).astype(F32) * own_ref[0]
    result = summed / total
    for r in range(requests):
        for h in range(heads_mine):
            at = r * heads_mine + h
            line_ref[r : r + 1, h * 128 : (h + 1) * 128] = result[at : at + 1, :]
    out_ref[...] = line_ref[...].astype(BF16)


def attend_moved(prepared, pieces, requests, features):
    rows = prepared[0].shape[0]
    width = rows // requests * 128
    return pl.pallas_call(
        functools.partial(moved_kernel, len(pieces), features),
        in_specs=[VMEM] * (len(prepared) + len(pieces)),
        out_specs=VMEM,
        out_shape=jax.ShapeDtypeStruct((requests, width), BF16),
        scratch_shapes=[pltpu.VMEM((requests, width), F32)],
        compiler_params=pltpu.CompilerParams(vmem_limit_bytes=16 * MIB),
        cost_estimate=pl.CostEstimate(
            flops=4 * rows * rows * 128 * 64, bytes_accessed=4 * 1024 * 1024, transcendentals=rows * 128
        ),
        name="attend_moved",
    )(*prepared, *pieces)


def combine_kernel(ranks, residents, kv_mine, ask_ref, *rest):
    refs, out_ref = rest[:ranks], rest[ranks]
    heads_mine = out_ref.shape[1] // 128
    scale = F32(1.0) / jnp.sqrt(F32(128.0))
    payloads = [ref[...].astype(F32) for ref in refs]
    at = residents * heads_mine
    ask = ask_ref[...].astype(F32)
    for r in range(residents):
        q, own_k, own_v = heads_of(ask[r : r + 1], heads_mine, kv_mine)
        own_score = jnp.sum(q * own_k, axis=1, keepdims=True) * scale
        peaks, totals = [], []
        for payload in payloads:
            stat = payload[at : at + 3 * residents]
            peaks.append(row_to_column(stat[r : r + 1], heads_mine))
            total = stat[residents + r : residents + r + 1]
            total = total + stat[2 * residents + r : 2 * residents + r + 1]
            totals.append(row_to_column(total, heads_mine))
        top = own_score
        for peak in peaks:
            top = jnp.maximum(top, peak)
        own_weight = jnp.exp(own_score - top)
        denom = own_weight
        numer = own_weight.astype(BF16).astype(F32) * own_v
        for peak, total, payload in zip(peaks, totals, payloads):
            keep = jnp.exp(peak - top)
            denom = denom + keep * total
            numer = numer + keep * payload[r * heads_mine : (r + 1) * heads_mine]
        result = numer / denom
        for h in range(heads_mine):
            out_ref[r : r + 1, h * 128 : (h + 1) * 128] = result[h : h + 1, :]


def combine_resident(ask, payloads, residents, heads_mine, kv_mine):
    return pl.pallas_call(
        functools.partial(combine_kernel, len(payloads), residents, kv_mine),
        in_specs=[VMEM] * (1 + len(payloads)),
        out_specs=VMEM,
        out_shape=jax.ShapeDtypeStruct((residents, heads_mine * 128), F32),
        compiler_params=pltpu.CompilerParams(vmem_limit_bytes=8 * MIB),
        name="combine_resident",
    )(ask, *payloads)


def finish_kernel(kept_ref, place_ref, *rest):
    moved, out_ref = rest[:-1], rest[-1]
    residents = kept_ref.shape[0]
    decoded, width = out_ref.shape
    requests = decoded - residents
    row = iota((decoded, 128), 0)
    arrived = [ref[...].astype(F32) for ref in moved]
    for c in range(0, width, 128):
        kept = kept_ref[:, c : c + 128]
        line = jnp.concatenate([kept, jnp.zeros((requests, 128), F32)], axis=0)
        for b in range(len(moved)):
            for i in range(requests):
                at = (b + 1) * requests + i
                line = jnp.where(
                    place_ref[at : at + 1, :] == row, arrived[b][i : i + 1, c : c + 128], line
                )
        out_ref[:, c : c + 128] = line.astype(BF16)


def finish(kept, places, moved, requests):
    residents, width = kept.shape
    return pl.pallas_call(
        finish_kernel,
        in_specs=[VMEM] * (2 + len(moved)),
        out_specs=VMEM,
        out_shape=jax.ShapeDtypeStruct((residents + requests, width), BF16),
        compiler_params=pltpu.CompilerParams(vmem_limit_bytes=8 * MIB),
        name="finish",
    )(kept, places, *moved)


def swapped(x, axis, j, n):
    return lax.ppermute(x, axis, [(i, i ^ j) for i in range(n)])


def rotation(slots, requests, head_size):
    half = head_size // 2
    freq = THETA ** (-np.arange(half) * 2.0 / head_size)
    angle = np.repeat(np.arange(slots), requests)[:, None] * freq[None, :]
    cos, sin = np.cos(angle), np.sin(angle)
    return (
        np.concatenate([cos, cos], axis=1).astype(np.float32),
        np.concatenate([-sin, sin], axis=1).astype(np.float32),
    )


def per_device(
    mig_hidden,
    mig_dest,
    mig_count,
    attn_gain,
    kv_weight,
    k_gain,
    query,
    new_kv,
    k_cache,
    v_cache,
    lengths,
):
    insts = lax.axis_size("inst")
    ranks = lax.axis_size("tp")
    head_size = k_gain.shape[0]
    slots, requests, feats = mig_hidden.shape[1:]
    residents = k_cache.shape[1]
    heads = query.shape[2] // head_size
    kv_heads = kv_weight.shape[1] // 2 // head_size
    heads_mine = heads // ranks
    group = heads // kv_heads
    kv_mine = max(1, heads_mine // group)

    pieces, ask = project(
        mig_hidden[0], attn_gain, kv_weight, query[0], new_kv[0], ranks, group, kv_mine
    )
    last = ranks - 1
    far = swapped(pieces[last], "tp", last, ranks)
    asks = [swapped(ask, "inst", b, insts) for b in range(1, insts)]
    asks[0], *others = lax.optimization_barrier((asks[0], *pieces[1:last]))
    others = [swapped(others[j - 1], "tp", j, ranks) for j in reversed(range(1, last))]
    pieces = [pieces[0], far] + others
    payloads = attend_resident(lengths, query[0], k_cache[0], v_cache[0], ranks)
    own_payload = payloads[0]
    payloads = [swapped(payloads[j], "tp", j, ranks) for j in reversed(range(1, ranks))]
    cos, sin = rotation(slots, requests, head_size)
    *prepared, places = prepare(
        mig_dest.T,
        mig_count.T,
        k_gain.reshape(1, head_size),
        cos,
        sin,
        asks,
        residents,
        heads_mine,
        kv_mine,
    )
    prepared[0], own_payload = lax.optimization_barrier((prepared[0], own_payload))
    moved = attend_moved(prepared, pieces, requests, feats * ranks)
    kept = combine_resident(ask, [own_payload] + payloads, residents, heads_mine, kv_mine)
    moved = [swapped(moved, "inst", b, insts) for b in reversed(range(1, insts))][::-1]
    return finish(kept, places, moved, requests)[None]


def solution(mesh):
    placed = (
        P(("group", "inst"), None, None, "tp"),
        P("group", None),
        P("group", None),
        P("tp"),
        P("tp", None),
        P(),
        P(("group", "inst"), None, None),
        P(("group", "inst"), None, None),
        P(("group", "inst"), None, "tp", None),
        P(("group", "inst"), None, "tp", None),
        P(("group", "inst"), None),
    )
    return jax.shard_map(
        per_device,
        mesh=mesh,
        in_specs=placed,
        out_specs=P(("group", "inst"), None, "tp"),
        check_vma=False,
    )
```

```python
import functools

import jax
import jax.numpy as jnp
import numpy as np
from jax import lax
from jax.experimental import pallas as pl
from jax.experimental.pallas import tpu as pltpu
from jax.sharding import PartitionSpec as P

EPS = 1e-06
THETA = 1000000.0
ABSENT = -1e30
F32 = jnp.float32
BF16 = jnp.bfloat16
MIB = 1024 * 1024
CHUNK = 512

VMEM = pl.BlockSpec(memory_space=pltpu.VMEM)
SMEM = pl.BlockSpec(memory_space=pltpu.SMEM)
HBM = pl.BlockSpec(memory_space=pltpu.HBM)


def iota(shape, dim):
    return lax.broadcasted_iota(jnp.int32, shape, dim)


def column_to_row(column, period):
    n = column.shape[0]
    spread = jnp.where(iota((n, 128), 0) % period == iota((n, 128), 1), column, 0.0)
    return jnp.sum(spread.reshape(n // period, period, 128), axis=1)


def row_to_column(row, n):
    return jnp.sum(
        jnp.where(iota((n, 128), 0) == iota((n, 128), 1), row, 0.0), axis=1, keepdims=True
    )


def split_bf16(x):
    high = x.astype(BF16)
    return high, (x - high.astype(F32)).astype(BF16)


def project_kernel(ranks, group, gain_hbm, x_hbm, w_hbm, q_hbm, own_hbm, *rest):
    outs, ask_ref = rest[:ranks], rest[ranks]
    gain_ref, x_ref, w_ref, acc_ref, in_sems, w_sems = rest[ranks + 1 :]
    slots, requests, feats = x_ref.shape
    rows = slots * requests
    piece = outs[0].shape[1] // 2
    kv_width = w_hbm.shape[1] // 2
    heads_mine = kv_width // 128 * group // ranks
    rank = lax.axis_index("tp")

    def first_column(target):
        return pl.multiple_of(target * heads_mine // group * 128, 128)

    gain_copy = pltpu.make_async_copy(gain_hbm, gain_ref, in_sems.at[0])
    gain_copy.start()
    x_copy = pltpu.make_async_copy(x_hbm, x_ref, in_sems.at[1])
    x_copy.start()
    cuts = list(range(0, feats, CHUNK)) + [feats]
    chunks = list(zip(cuts[:-1], cuts[1:]))
    copies = []
    for i, (low, high) in enumerate(chunks):
        copies.append(
            pltpu.make_async_copy(w_hbm.at[low:high, :], w_ref.at[low:high, :], w_sems.at[i])
        )
        copies[-1].start()
    mine = heads_mine * 128
    q_first = pl.multiple_of(rank * mine, 128)
    asking = [
        pltpu.make_async_copy(
            q_hbm.at[:, pl.ds(q_first, mine)], ask_ref.at[:, :mine], in_sems.at[2]
        )
    ]
    for i in range(2):
        asking.append(
            pltpu.make_async_copy(
                own_hbm.at[:, pl.ds(i * kv_width + first_column(rank), piece)],
                ask_ref.at[:, mine + i * piece : mine + (i + 1) * piece],
                in_sems.at[3 + i],
            )
        )
    for copy in asking:
        copy.start()
    gain_copy.wait()
    x_copy.wait()
    squares = jnp.zeros((rows, 128), F32)
    for i, (low, high) in enumerate(chunks):
        parts = []
        for c in range(low, high, 128):
            width = min(128, high - c)
            x = x_ref[:, :, c : c + width].astype(F32).reshape(rows, width)
            gain = gain_ref[c : c + width].astype(F32).reshape(1, width)
            parts.append((x * gain).astype(BF16))
            x = x * x
            if width < 128:
                x = jnp.concatenate([x, jnp.zeros((rows, 128 - width), F32)], axis=1)
            squares = squares + x
        xg = parts[0] if len(parts) == 1 else jnp.concatenate(parts, axis=1)
        copies[i].wait()
        for n in range(0, 2 * kv_width, 512):
            part = jnp.dot(xg, w_ref[low:high, n : n + 512], preferred_element_type=F32)
            if i == 0:
                acc_ref[:, n : n + 512] = part
            else:
                acc_ref[:, n : n + 512] += part
    sq = column_to_row(jnp.sum(squares, axis=1, keepdims=True), 128)
    high, low = split_bf16(sq)
    tail = jnp.concatenate([high.astype(F32), low.astype(F32)], axis=0)
    fill = outs[1].shape[0] - rows - tail.shape[0]
    if fill:
        tail = jnp.concatenate([tail, jnp.zeros((fill, 128), F32)], axis=0)
    extra = jnp.concatenate([tail.astype(BF16)] * (2 * piece // 128), axis=1)
    for j in range(ranks):
        first = first_column(rank ^ j)
        outs[j][:rows, :piece] = acc_ref[:, pl.ds(first, piece)].astype(BF16)
        outs[j][:rows, piece:] = acc_ref[:, pl.ds(kv_width + first, piece)].astype(BF16)
        outs[j][rows:, :] = extra
    for copy in asking:
        copy.wait()


def project(x, gain, weight, query, own, ranks, group, kv_mine):
    slots, requests, feats = x.shape
    rows = slots * requests
    piece = kv_mine * 128
    extra = -(-2 * (rows // 128) // 8) * 8
    decoded, q_width = query.shape
    outs = pl.pallas_call(
        functools.partial(project_kernel, ranks, group),
        in_specs=[HBM] * 5,
        out_specs=[VMEM] * (ranks + 1),
        out_shape=[jax.ShapeDtypeStruct((rows + extra, 2 * piece), BF16)] * ranks
        + [jax.ShapeDtypeStruct((decoded, q_width // ranks + 2 * piece), BF16)],
        scratch_shapes=[
            pltpu.VMEM((feats,), BF16),
            pltpu.VMEM((slots, requests, feats), BF16),
            pltpu.VMEM(weight.shape, BF16),
            pltpu.VMEM((rows, weight.shape[1]), F32),
            pltpu.SemaphoreType.DMA((5,)),
            pltpu.SemaphoreType.DMA((-(-feats // CHUNK),)),
        ],
        compiler_params=pltpu.CompilerParams(vmem_limit_bytes=56 * MIB),
        cost_estimate=pl.CostEstimate(
            flops=2 * rows * feats * weight.shape[1],
            bytes_accessed=2 * feats * weight.shape[1],
            transcendentals=0,
        ),
        name="project",
    )(gain, x, weight, query, own)
    return outs[:ranks], outs[ranks]


def resident_kernel(ranks, len_hbm, q_hbm, k_hbm, v_hbm, *rest):
    out, len_ref, q_ref, q_all, k_buf, v_buf, wide_ref, s_buf, w_buf, o_all, s_all, in_sems, sems = (
        rest
    )
    residents, positions, width = k_buf.shape
    half = positions // 2
    halves = [slice(i * half, (i + 1) * half) for i in range(2)]

    def copies(which, hbm, buf):
        return [
            [
                pltpu.make_async_copy(hbm.at[r, at, :], buf.at[r, at, :], sems.at[which, r, i])
                for i, at in enumerate(halves)
            ]
            for r in range(residents)
        ]

    k_copies, v_copies = copies(0, k_hbm, k_buf), copies(1, v_hbm, v_buf)
    len_copy = pltpu.make_async_copy(len_hbm, len_ref, in_sems.at[0])
    q_copy = pltpu.make_async_copy(q_hbm, q_ref, in_sems.at[1])
    len_copy.start()
    q_copy.start()
    rank = lax.axis_index("tp")

    @pl.when(rank == 0)
    def _():
        for r in range(residents):
            for of in (k_copies, v_copies):
                for copy in of[r]:
                    copy.start()

    heads = q_ref.shape[1] // 128
    kv_heads = width // 128
    group = heads // kv_heads
    heads_mine = heads // ranks
    position = iota((16, positions), 1)
    scale = F32(1.0) / jnp.sqrt(F32(128.0))
    diagonal = iota((heads, 128), 0) % heads_mine == iota((heads, 128), 1)
    own_block = iota((heads, width), 0) // group == iota((heads, width), 1) // 128

    def to_rows(columns):
        spread = jnp.where(diagonal, jnp.concatenate(columns, axis=0), 0.0)
        return jnp.sum(spread.reshape(ranks, heads_mine, 128), axis=1)

    len_copy.wait()
    counts = [len_ref[0, r] - rank * positions for r in range(residents)]
    for r in range(residents):
        for of in (k_copies, v_copies):
            for i in range(2):
                pl.when((rank > 0) & (counts[r] > i * half))(of[r][i].start)
    q_copy.wait()
    for h in range(heads):
        q_all[h * 8 : h * 8 + residents, :] = q_ref[:residents, h * 128 : (h + 1) * 128].astype(F32)
    for r in range(residents):
        some = (rank == 0) | (counts[r] > 0)

        @pl.when(some)
        def _():
            q = q_all[pl.ds(r, heads, stride=8), :].astype(BF16)
            wide = jnp.concatenate([q] * kv_heads, axis=1)
            wide_ref[...] = jnp.where(own_block, wide, jnp.zeros_like(wide))

        for i, at in enumerate(halves):

            @pl.when((rank == 0) | (counts[r] > i * half))
            def _():
                k_copies[r][i].wait()
                s_buf[:, at] = lax.dot_general(
                    wide_ref[...],
                    k_buf[r, at, :],
                    (((1,), (1,)), ((), ())),
                    preferred_element_type=F32,
                )

        @pl.when(some)
        def _():
            valid = position < counts[r]
            peaks, totals = [], []
            for c in range(0, heads, 16):
                rows = slice(c, c + 16)
                scores = jnp.where(valid, s_buf[rows, :] * scale, ABSENT)
                peak = jnp.max(scores, axis=1, keepdims=True).astype(BF16).astype(F32)
                weight = jnp.where(valid, jnp.exp(scores - peak), 0.0)
                peaks.append(peak)
                totals.append(jnp.sum(weight, axis=1, keepdims=True))
                w_buf[rows, :] = weight.astype(BF16)
            s_all[r, 0] = to_rows(peaks)
            high, low = split_bf16(to_rows(totals))
            s_all[r, 1] = high.astype(F32)
            s_all[r, 2] = low.astype(F32)

        @pl.when(jnp.logical_not(some))
        def _():
            s_all[r, 0] = jnp.full((ranks, 128), ABSENT, F32)
            s_all[r, 1] = jnp.zeros((ranks, 128), F32)
            s_all[r, 2] = jnp.zeros((ranks, 128), F32)
            o_all[r] = jnp.zeros((heads, 128), F32)

        for i, at in enumerate(halves):

            @pl.when((rank == 0) | (counts[r] > i * half))
            def _():
                v_copies[r][i].wait()
                part = jnp.dot(w_buf[:, at], v_buf[r, at, :], preferred_element_type=F32)
                for g in range(kv_heads):
                    rows = slice(g * group, (g + 1) * group)
                    block = part[rows, g * 128 : (g + 1) * 128]
                    if i == 0:
                        o_all[r, rows, :] = block
                    else:
                        o_all[r, rows, :] += block

    filled = residents * (heads_mine + 3)
    for t in range(ranks):
        parts = [o_all[r, t * heads_mine : (t + 1) * heads_mine, :] for r in range(residents)]
        parts += [s_all[r, i, t : t + 1, :] for i in range(3) for r in range(residents)]
        if out.shape[1] > filled:
            parts.append(jnp.zeros((out.shape[1] - filled, 128), F32))
        out[t] = jnp.concatenate(parts, axis=0).astype(BF16)


def attend_resident(lengths, query, k_cache, v_cache, ranks):
    residents, positions, width = k_cache.shape
    heads = query.shape[1] // 128
    heads_mine = heads // ranks
    rows = -(-(residents * (heads_mine + 3)) // 16) * 16
    return pl.pallas_call(
        functools.partial(resident_kernel, ranks),
        in_specs=[HBM] * 4,
        out_specs=VMEM,
        out_shape=jax.ShapeDtypeStruct((ranks, rows, 128), BF16),
        scratch_shapes=[
            pltpu.SMEM(lengths.shape, jnp.int32),
            pltpu.VMEM(query.shape, BF16),
            pltpu.VMEM((heads * 8, 128), F32),
            pltpu.VMEM((residents, positions, width), BF16),
            pltpu.VMEM((residents, positions, width), BF16),
            pltpu.VMEM((heads, width), BF16),
            pltpu.VMEM((heads, positions), F32),
            pltpu.VMEM((heads, positions), BF16),
            pltpu.VMEM((residents, heads, 128), F32),
            pltpu.VMEM((residents, 3, ranks, 128), F32),
            pltpu.SemaphoreType.DMA((2,)),
            pltpu.SemaphoreType.DMA((2, residents, 2)),
        ],
        compiler_params=pltpu.CompilerParams(vmem_limit_bytes=56 * MIB),
        cost_estimate=pl.CostEstimate(
            flops=4 * residents * heads * positions * 128,
            bytes_accessed=4 * residents * positions * width,
            transcendentals=residents * heads * positions,
        ),
        name="attend_resident",
    )(lengths, query, k_cache, v_cache)


def expand(own, rows):
    which = iota((rows, 128), 0) // (rows // own.shape[0])
    out = jnp.broadcast_to(own[0:1], (rows, 128))
    for h in range(1, own.shape[0]):
        out = jnp.where(which == h, own[h : h + 1], out)
    return out


def heads_of(line, heads_mine, kv_mine):
    per = heads_mine // kv_mine
    blocks = [line[:, c : c + 128] for c in range(0, line.shape[1], 128)]
    q = jnp.concatenate(blocks[:heads_mine], axis=0)
    k = blocks[heads_mine : heads_mine + kv_mine]
    v = blocks[heads_mine + kv_mine :]
    return (
        q,
        expand(jnp.concatenate(k, axis=0), heads_mine),
        expand(jnp.concatenate(v, axis=0), heads_mine),
    )


def moved_kernel(
    insts, ranks, residents, features, dest_ref, count_ref, gain_ref, cos_ref, sin_ref, *rest
):
    asks, rest = rest[: insts - 1], rest[insts - 1 :]
    pieces, rest = rest[:ranks], rest[ranks:]
    out_ref, place_out, ask_ref, q_ref, own_ref, line_ref = rest
    requests = out_ref.shape[0]
    tokens = cos_ref.shape[0]
    piece = pieces[0].shape[1] // 2
    kv_mine = piece // 128
    rows = q_ref.shape[0]
    heads_mine = rows // requests
    scale = F32(1.0) / jnp.sqrt(F32(128.0))
    here = lax.axis_index("inst")

    ask_row = iota(asks[0].shape, 0)
    row_request = iota((rows, tokens), 0) // heads_mine
    limit = jnp.zeros((rows, tokens), jnp.int32)
    for r in range(requests):
        dest = dest_ref[r, here]
        limit = jnp.where(row_request == r, count_ref[r, here], limit)
        place = jnp.int32(residents)
        for s in range(insts):
            for c in range(requests):
                place += jnp.where((dest_ref[c, s] == dest) & (here > s), 1, 0).astype(jnp.int32)
        for b in range(1, insts):

            @pl.when(here ^ b == dest)
            def _():
                ask = asks[b - 1][...].astype(F32)
                ask_ref[r : r + 1, :] = jnp.sum(
                    jnp.where(ask_row == place, ask, 0.0), axis=0, keepdims=True
                )

        at = slice(r * heads_mine, (r + 1) * heads_mine)
        q_ref[at, :], own_ref[0, at, :], own_ref[1, at, :] = heads_of(
            ask_ref[r : r + 1, :], heads_mine, kv_mine
        )
    places = jnp.full(place_out.shape, -1, jnp.int32)
    row = iota(place_out.shape, 0)
    place = jnp.int32(residents)
    for s in range(insts):
        for c in range(requests):
            mine = dest_ref[c, s] == here
            places = jnp.where((row == (here ^ s) * requests + c) & mine, place, places)
            place += jnp.where(mine, 1, 0).astype(jnp.int32)
    place_out[...] = places

    blocks = tokens // 128
    last = tokens + 2 * blocks
    tail = pieces[0][tokens:last, :128].astype(F32)
    for t in range(1, ranks):
        tail = tail + pieces[t][tokens:last, :128].astype(F32)
    squares = tail[:blocks] + tail[blocks:]
    squares = jnp.concatenate(
        [row_to_column(squares[b : b + 1], 128) for b in range(blocks)], axis=0
    )
    token_scale = lax.rsqrt(squares / features + EPS)

    def column_block(c):
        total = pieces[0][:tokens, c : c + 128].astype(F32)
        for t in range(1, ranks):
            total = total + pieces[t][:tokens, c : c + 128].astype(F32)
        return total * token_scale

    gain = gain_ref[...].astype(F32)
    q = q_ref[...]
    q16 = q.astype(BF16)
    which = iota((rows, tokens), 0) % heads_mine // (heads_mine // kv_mine)
    scores = None
    for h in range(kv_mine):
        key = column_block(h * 128)
        key = key * lax.rsqrt(jnp.mean(key * key, axis=1, keepdims=True) + EPS) * gain
        key = key * cos_ref[...] + pltpu.roll(key, 64, 1) * sin_ref[...]
        part = lax.dot_general(
            q16, key.astype(BF16), (((1,), (1,)), ((), ())), preferred_element_type=F32
        )
        scores = part if scores is None else jnp.where(which == h, part, scores)
    token = iota((rows, tokens), 1)
    valid = (token % requests == row_request) & (token // requests < limit)
    scores = jnp.where(valid, scores * scale, ABSENT)
    own_score = jnp.sum(q * own_ref[0], axis=1, keepdims=True) * scale
    top = jnp.maximum(jnp.max(scores, axis=1, keepdims=True), own_score)
    weights = jnp.where(valid, jnp.exp(scores - top), 0.0)
    own_weight = jnp.exp(own_score - top)
    total = jnp.sum(weights, axis=1, keepdims=True) + own_weight
    weights = weights.astype(BF16)
    summed = None
    for h in range(kv_mine):
        value = column_block(piece + h * 128).astype(BF16)
        part = jnp.dot(weights, value, preferred_element_type=F32)
        summed = part if summed is None else jnp.where(which[:, :128] == h, part, summed)
    summed = summed + own_weight.astype(BF16).astype(F32) * own_ref[1]
    result = summed / total
    for r in range(requests):
        for h in range(heads_mine):
            at = r * heads_mine + h
            line_ref[r : r + 1, h * 128 : (h + 1) * 128] = result[at : at + 1, :]
    out_ref[...] = line_ref[...].astype(BF16)


def attend_moved(dest, count, k_gain, cos, sin, asks, pieces, residents, heads_mine, features):
    requests, insts = dest.shape
    rows = requests * heads_mine
    return pl.pallas_call(
        functools.partial(moved_kernel, insts, len(pieces), residents, features),
        in_specs=[SMEM] * 2 + [VMEM] * (3 + len(asks) + len(pieces)),
        out_specs=[VMEM] * 2,
        out_shape=[
            jax.ShapeDtypeStruct((requests, heads_mine * 128), BF16),
            jax.ShapeDtypeStruct((insts * requests, 128), jnp.int32),
        ],
        scratch_shapes=[
            pltpu.VMEM((requests, asks[0].shape[1]), F32),
            pltpu.VMEM((rows, 128), F32),
            pltpu.VMEM((2, rows, 128), F32),
            pltpu.VMEM((requests, heads_mine * 128), F32),
        ],
        compiler_params=pltpu.CompilerParams(vmem_limit_bytes=16 * MIB),
        name="attend_moved",
    )(dest, count, k_gain, cos, sin, *asks, *pieces)


def combine_kernel(residents, kv_mine, ask_ref, payload_ref, out_ref):
    heads_mine = out_ref.shape[1] // 128
    scale = F32(1.0) / jnp.sqrt(F32(128.0))
    payloads = [payload_ref[t].astype(F32) for t in range(payload_ref.shape[0])]
    at = residents * heads_mine
    ask = ask_ref[...].astype(F32)
    for r in range(residents):
        q, own_k, own_v = heads_of(ask[r : r + 1], heads_mine, kv_mine)
        own_score = jnp.sum(q * own_k, axis=1, keepdims=True) * scale
        peaks, totals = [], []
        for payload in payloads:
            stat = payload[at : at + 3 * residents]
            peaks.append(row_to_column(stat[r : r + 1], heads_mine))
            total = stat[residents + r : residents + r + 1]
            total = total + stat[2 * residents + r : 2 * residents + r + 1]
            totals.append(row_to_column(total, heads_mine))
        top = own_score
        for peak in peaks:
            top = jnp.maximum(top, peak)
        own_weight = jnp.exp(own_score - top)
        denom = own_weight
        numer = own_weight.astype(BF16).astype(F32) * own_v
        for peak, total, payload in zip(peaks, totals, payloads):
            keep = jnp.exp(peak - top)
            denom = denom + keep * total
            numer = numer + keep * payload[r * heads_mine : (r + 1) * heads_mine]
        result = numer / denom
        for h in range(heads_mine):
            out_ref[r : r + 1, h * 128 : (h + 1) * 128] = result[h : h + 1, :]


def combine_resident(ask, payloads, residents, heads_mine, kv_mine):
    return pl.pallas_call(
        functools.partial(combine_kernel, residents, kv_mine),
        in_specs=[VMEM] * 2,
        out_specs=VMEM,
        out_shape=jax.ShapeDtypeStruct((residents, heads_mine * 128), F32),
        compiler_params=pltpu.CompilerParams(vmem_limit_bytes=8 * MIB),
        name="combine_resident",
    )(ask, payloads)


def finish_kernel(kept_ref, place_ref, *rest):
    moved, out_ref = rest[:-1], rest[-1]
    residents = kept_ref.shape[0]
    decoded, width = out_ref.shape
    requests = decoded - residents
    row = iota((decoded, 128), 0)
    arrived = [ref[...].astype(F32) for ref in moved]
    for c in range(0, width, 128):
        kept = kept_ref[:, c : c + 128]
        line = jnp.concatenate([kept, jnp.zeros((requests, 128), F32)], axis=0)
        for b in range(len(moved)):
            for i in range(requests):
                at = (b + 1) * requests + i
                line = jnp.where(
                    place_ref[at : at + 1, :] == row, arrived[b][i : i + 1, c : c + 128], line
                )
        out_ref[:, c : c + 128] = line.astype(BF16)


def finish(kept, places, moved, requests):
    residents, width = kept.shape
    return pl.pallas_call(
        finish_kernel,
        in_specs=[VMEM] * (2 + len(moved)),
        out_specs=VMEM,
        out_shape=jax.ShapeDtypeStruct((residents + requests, width), BF16),
        compiler_params=pltpu.CompilerParams(vmem_limit_bytes=8 * MIB),
        name="finish",
    )(kept, places, *moved)


def swapped(x, axis, j, n):
    return lax.ppermute(x, axis, [(i, i ^ j) for i in range(n)])


def rotation(slots, requests, head_size):
    half = head_size // 2
    freq = THETA ** (-np.arange(half) * 2.0 / head_size)
    angle = np.repeat(np.arange(slots), requests)[:, None] * freq[None, :]
    cos, sin = np.cos(angle), np.sin(angle)
    return (
        np.concatenate([cos, cos], axis=1).astype(np.float32),
        np.concatenate([-sin, sin], axis=1).astype(np.float32),
    )


def per_device(
    mig_hidden,
    mig_dest,
    mig_count,
    attn_gain,
    kv_weight,
    k_gain,
    query,
    new_kv,
    k_cache,
    v_cache,
    lengths,
):
    insts = lax.axis_size("inst")
    ranks = lax.axis_size("tp")
    head_size = k_gain.shape[0]
    slots, requests, feats = mig_hidden.shape[1:]
    residents = k_cache.shape[1]
    heads = query.shape[2] // head_size
    kv_heads = kv_weight.shape[1] // 2 // head_size
    heads_mine = heads // ranks
    group = heads // kv_heads
    kv_mine = max(1, heads_mine // group)

    pieces, ask = project(
        mig_hidden[0], attn_gain, kv_weight, query[0], new_kv[0], ranks, group, kv_mine
    )
    last = ranks - 1
    far = swapped(pieces[last], "tp", last, ranks)
    asks = [swapped(ask, "inst", b, insts) for b in range(1, insts)]
    asks[0], *others = lax.optimization_barrier((asks[0], *pieces[1:last]))
    others = [swapped(others[j - 1], "tp", j, ranks) for j in reversed(range(1, last))]
    pieces = [pieces[0], far] + others
    payloads = attend_resident(lengths, query[0], k_cache[0], v_cache[0], ranks)
    asks, payloads = lax.optimization_barrier((asks, payloads))
    received = lax.all_to_all(payloads, "tp", 0, 0, tiled=True)
    cos, sin = rotation(slots, requests, head_size)
    moved, places = attend_moved(
        mig_dest.T,
        mig_count.T,
        k_gain.reshape(1, head_size),
        cos,
        sin,
        asks,
        pieces,
        residents,
        heads_mine,
        feats * ranks,
    )
    kept = combine_resident(ask, received, residents, heads_mine, kv_mine)
    moved = [swapped(moved, "inst", b, insts) for b in reversed(range(1, insts))][::-1]
    return finish(kept, places, moved, requests)[None]


def solution(mesh):
    placed = (
        P(("group", "inst"), None, None, "tp"),
        P("group", None),
        P("group", None),
        P("tp"),
        P("tp", None),
        P(),
        P(("group", "inst"), None, None),
        P(("group", "inst"), None, None),
        P(("group", "inst"), None, "tp", None),
        P(("group", "inst"), None, "tp", None),
        P(("group", "inst"), None),
    )
    return jax.shard_map(
        per_device,
        mesh=mesh,
        in_specs=placed,
        out_specs=P(("group", "inst"), None, "tp"),
        check_vma=False,
    )
```

```python
import functools

import jax
import jax.numpy as jnp
import numpy as np
from jax import lax
from jax.experimental import pallas as pl
from jax.experimental.pallas import tpu as pltpu
from jax.sharding import PartitionSpec as P

EPS = 1e-06
THETA = 1000000.0
ABSENT = -1e30
F32 = jnp.float32
BF16 = jnp.bfloat16
MIB = 1024 * 1024
CHUNK = 512

VMEM = pl.BlockSpec(memory_space=pltpu.VMEM)
SMEM = pl.BlockSpec(memory_space=pltpu.SMEM)
HBM = pl.BlockSpec(memory_space=pltpu.HBM)


def iota(shape, dim):
    return lax.broadcasted_iota(jnp.int32, shape, dim)


def column_to_row(column, period):
    n = column.shape[0]
    spread = jnp.where(iota((n, 128), 0) % period == iota((n, 128), 1), column, 0.0)
    return jnp.sum(spread.reshape(n // period, period, 128), axis=1)


def row_to_column(row, n):
    return jnp.sum(
        jnp.where(iota((n, 128), 0) == iota((n, 128), 1), row, 0.0), axis=1, keepdims=True
    )


def split_bf16(x):
    high = x.astype(BF16)
    return high, (x - high.astype(F32)).astype(BF16)


def project_kernel(ranks, group, gain_hbm, x_hbm, w_hbm, q_hbm, own_hbm, *rest):
    outs, ask_ref = rest[:ranks], rest[ranks]
    gain_ref, x_ref, w_ref, acc_ref, in_sems, w_sems = rest[ranks + 1 :]
    slots, requests, feats = x_ref.shape
    rows = slots * requests
    piece = outs[0].shape[1] // 2
    kv_width = w_hbm.shape[1] // 2
    heads_mine = kv_width // 128 * group // ranks
    rank = lax.axis_index("tp")

    def first_column(target):
        return pl.multiple_of(target * heads_mine // group * 128, 128)

    gain_copy = pltpu.make_async_copy(gain_hbm, gain_ref, in_sems.at[0])
    gain_copy.start()
    x_copy = pltpu.make_async_copy(x_hbm, x_ref, in_sems.at[1])
    x_copy.start()
    cuts = list(range(0, feats, CHUNK)) + [feats]
    chunks = list(zip(cuts[:-1], cuts[1:]))
    copies = []
    for i, (low, high) in enumerate(chunks):
        copies.append(
            pltpu.make_async_copy(w_hbm.at[low:high, :], w_ref.at[low:high, :], w_sems.at[i])
        )
        copies[-1].start()
    mine = heads_mine * 128
    q_first = pl.multiple_of(rank * mine, 128)
    asking = [
        pltpu.make_async_copy(
            q_hbm.at[:, pl.ds(q_first, mine)], ask_ref.at[:, :mine], in_sems.at[2]
        )
    ]
    for i in range(2):
        asking.append(
            pltpu.make_async_copy(
                own_hbm.at[:, pl.ds(i * kv_width + first_column(rank), piece)],
                ask_ref.at[:, mine + i * piece : mine + (i + 1) * piece],
                in_sems.at[3 + i],
            )
        )
    for copy in asking:
        copy.start()
    gain_copy.wait()
    x_copy.wait()
    squares = jnp.zeros((rows, 128), F32)
    for i, (low, high) in enumerate(chunks):
        parts = []
        for c in range(low, high, 128):
            width = min(128, high - c)
            x = x_ref[:, :, c : c + width].astype(F32).reshape(rows, width)
            gain = gain_ref[c : c + width].astype(F32).reshape(1, width)
            parts.append((x * gain).astype(BF16))
            x = x * x
            if width < 128:
                x = jnp.concatenate([x, jnp.zeros((rows, 128 - width), F32)], axis=1)
            squares = squares + x
        xg = parts[0] if len(parts) == 1 else jnp.concatenate(parts, axis=1)
        copies[i].wait()
        for n in range(0, 2 * kv_width, 512):
            part = jnp.dot(xg, w_ref[low:high, n : n + 512], preferred_element_type=F32)
            if i == 0:
                acc_ref[:, n : n + 512] = part
            else:
                acc_ref[:, n : n + 512] += part
    sq = column_to_row(jnp.sum(squares, axis=1, keepdims=True), 128)
    high, low = split_bf16(sq)
    tail = jnp.concatenate([high.astype(F32), low.astype(F32)], axis=0)
    fill = outs[1].shape[0] - rows - tail.shape[0]
    if fill:
        tail = jnp.concatenate([tail, jnp.zeros((fill, 128), F32)], axis=0)
    extra = jnp.concatenate([tail.astype(BF16)] * (2 * piece // 128), axis=1)
    for j in range(ranks):
        first = first_column(rank ^ j)
        outs[j][:rows, :piece] = acc_ref[:, pl.ds(first, piece)].astype(BF16)
        outs[j][:rows, piece:] = acc_ref[:, pl.ds(kv_width + first, piece)].astype(BF16)
        outs[j][rows:, :] = extra
    for copy in asking:
        copy.wait()


def project(x, gain, weight, query, own, ranks, group, kv_mine):
    slots, requests, feats = x.shape
    rows = slots * requests
    piece = kv_mine * 128
    extra = -(-2 * (rows // 128) // 8) * 8
    decoded, q_width = query.shape
    outs = pl.pallas_call(
        functools.partial(project_kernel, ranks, group),
        in_specs=[HBM] * 5,
        out_specs=[VMEM] * (ranks + 1),
        out_shape=[jax.ShapeDtypeStruct((rows + extra, 2 * piece), BF16)] * ranks
        + [jax.ShapeDtypeStruct((decoded, q_width // ranks + 2 * piece), BF16)],
        scratch_shapes=[
            pltpu.VMEM((feats,), BF16),
            pltpu.VMEM((slots, requests, feats), BF16),
            pltpu.VMEM(weight.shape, BF16),
            pltpu.VMEM((rows, weight.shape[1]), F32),
            pltpu.SemaphoreType.DMA((5,)),
            pltpu.SemaphoreType.DMA((-(-feats // CHUNK),)),
        ],
        compiler_params=pltpu.CompilerParams(vmem_limit_bytes=56 * MIB),
        cost_estimate=pl.CostEstimate(
            flops=2 * rows * feats * weight.shape[1],
            bytes_accessed=2 * feats * weight.shape[1],
            transcendentals=0,
        ),
        name="project",
    )(gain, x, weight, query, own)
    return outs[:ranks], outs[ranks]


def resident_kernel(ranks, len_ref, q_hbm, k_hbm, v_hbm, out, *rest):
    q_ref, q_wide, k_buf, v_buf, o_all, s_all, q_sem, sems = rest
    residents, positions, width = k_buf.shape
    q_copy = pltpu.make_async_copy(q_hbm, q_ref, q_sem)
    copies = []
    for r in range(residents):
        copies.append(
            (
                pltpu.make_async_copy(k_hbm.at[r], k_buf.at[r], sems.at[0, r]),
                pltpu.make_async_copy(v_hbm.at[r], v_buf.at[r], sems.at[1, r]),
            )
        )
    q_copy.start()
    for pair in copies:
        for copy in pair:
            copy.start()
    heads = q_ref.shape[0]
    kv_heads = width // 128
    group = heads // kv_heads
    pair_rows = 2 * group
    heads_mine = heads // ranks
    rank = lax.axis_index("tp")
    top_half = iota((pair_rows, 128), 0) < group
    position = rank * positions + iota((pair_rows, positions), 1)
    scale = F32(1.0) / jnp.sqrt(F32(128.0))
    diagonal = iota((heads, 128), 0) % heads_mine == iota((heads, 128), 1)

    def to_rows(columns):
        spread = jnp.where(diagonal, jnp.concatenate(columns, axis=0), 0.0)
        return jnp.sum(spread.reshape(ranks, heads_mine, 128), axis=1)

    q_copy.wait()
    q_wide[...] = q_ref[...].astype(F32)
    queries = [q_wide[:, r, :].astype(BF16) for r in range(residents)]
    for r in range(residents):
        valid = position < len_ref[0, r]
        copies[r][0].wait()
        weights, peaks, totals = [], [], []
        for p in range(kv_heads // 2):
            q = queries[r][p * pair_rows : (p + 1) * pair_rows]
            zero = jnp.zeros_like(q)
            lhs = jnp.concatenate(
                [jnp.where(top_half, q, zero), jnp.where(top_half, zero, q)], axis=1
            )
            scores = lax.dot_general(
                lhs,
                k_buf[r, :, p * 256 : (p + 1) * 256],
                (((1,), (1,)), ((), ())),
                preferred_element_type=F32,
            )
            scores = jnp.where(valid, scores * scale, ABSENT)
            peak = jnp.max(scores, axis=1, keepdims=True).astype(BF16).astype(F32)
            weight = jnp.where(valid, jnp.exp(scores - peak), 0.0)
            peaks.append(peak)
            totals.append(jnp.sum(weight, axis=1, keepdims=True))
            weights.append(weight.astype(BF16))
        s_all[r, 0] = to_rows(peaks)
        high, low = split_bf16(to_rows(totals))
        s_all[r, 1] = high.astype(F32)
        s_all[r, 2] = low.astype(F32)
        copies[r][1].wait()
        for p in range(kv_heads // 2):
            both = jnp.dot(
                weights[p], v_buf[r, :, p * 256 : (p + 1) * 256], preferred_element_type=F32
            )
            o_all[r, p * pair_rows : (p + 1) * pair_rows, :] = jnp.where(
                top_half, both[:, :128], both[:, 128:]
            )
    filled = residents * (heads_mine + 3)
    for t in range(ranks):
        parts = [o_all[r, t * heads_mine : (t + 1) * heads_mine, :] for r in range(residents)]
        parts += [s_all[r, i, t : t + 1, :] for i in range(3) for r in range(residents)]
        if out.shape[1] > filled:
            parts.append(jnp.zeros((out.shape[1] - filled, 128), F32))
        out[t] = jnp.concatenate(parts, axis=0).astype(BF16)


def attend_resident(lengths, queries, k_cache, v_cache, ranks):
    residents, positions, width = k_cache.shape
    heads = queries.shape[0]
    heads_mine = heads // ranks
    rows = -(-(residents * (heads_mine + 3)) // 16) * 16
    return pl.pallas_call(
        functools.partial(resident_kernel, ranks),
        in_specs=[SMEM, HBM, HBM, HBM],
        out_specs=VMEM,
        out_shape=jax.ShapeDtypeStruct((ranks, rows, 128), BF16),
        scratch_shapes=[
            pltpu.VMEM(queries.shape, BF16),
            pltpu.VMEM(queries.shape, F32),
            pltpu.VMEM((residents, positions, width), BF16),
            pltpu.VMEM((residents, positions, width), BF16),
            pltpu.VMEM((residents, heads, 128), F32),
            pltpu.VMEM((residents, 3, ranks, 128), F32),
            pltpu.SemaphoreType.DMA,
            pltpu.SemaphoreType.DMA((2, residents)),
        ],
        compiler_params=pltpu.CompilerParams(vmem_limit_bytes=56 * MIB),
        cost_estimate=pl.CostEstimate(
            flops=4 * residents * heads * positions * 128,
            bytes_accessed=4 * residents * positions * width,
            transcendentals=residents * heads * positions,
        ),
        name="attend_resident",
    )(lengths, queries, k_cache, v_cache)


def expand(own, rows):
    which = iota((rows, 128), 0) // (rows // own.shape[0])
    out = jnp.broadcast_to(own[0:1], (rows, 128))
    for h in range(1, own.shape[0]):
        out = jnp.where(which == h, own[h : h + 1], out)
    return out


def heads_of(line, heads_mine, kv_mine):
    per = heads_mine // kv_mine
    blocks = [line[:, c : c + 128] for c in range(0, line.shape[1], 128)]
    q = jnp.concatenate(blocks[:heads_mine], axis=0)
    k = blocks[heads_mine : heads_mine + kv_mine]
    v = blocks[heads_mine + kv_mine :]
    return (
        q,
        expand(jnp.concatenate(k, axis=0), heads_mine),
        expand(jnp.concatenate(v, axis=0), heads_mine),
    )


def moved_kernel(
    insts, ranks, residents, features, dest_ref, count_ref, gain_ref, cos_ref, sin_ref, *rest
):
    asks, rest = rest[: insts - 1], rest[insts - 1 :]
    pieces, rest = rest[:ranks], rest[ranks:]
    out_ref, place_out, ask_ref, q_ref, own_ref, line_ref = rest
    requests = out_ref.shape[0]
    tokens = cos_ref.shape[0]
    piece = pieces[0].shape[1] // 2
    kv_mine = piece // 128
    rows = q_ref.shape[0]
    heads_mine = rows // requests
    scale = F32(1.0) / jnp.sqrt(F32(128.0))
    here = lax.axis_index("inst")

    ask_row = iota(asks[0].shape, 0)
    row_request = iota((rows, tokens), 0) // heads_mine
    limit = jnp.zeros((rows, tokens), jnp.int32)
    for r in range(requests):
        dest = dest_ref[r, here]
        limit = jnp.where(row_request == r, count_ref[r, here], limit)
        place = jnp.int32(residents)
        for s in range(insts):
            for c in range(requests):
                place += jnp.where((dest_ref[c, s] == dest) & (here > s), 1, 0).astype(jnp.int32)
        for b in range(1, insts):

            @pl.when(here ^ b == dest)
            def _():
                ask = asks[b - 1][...].astype(F32)
                ask_ref[r : r + 1, :] = jnp.sum(
                    jnp.where(ask_row == place, ask, 0.0), axis=0, keepdims=True
                )

        at = slice(r * heads_mine, (r + 1) * heads_mine)
        q_ref[at, :], own_ref[0, at, :], own_ref[1, at, :] = heads_of(
            ask_ref[r : r + 1, :], heads_mine, kv_mine
        )
    places = jnp.full(place_out.shape, -1, jnp.int32)
    row = iota(place_out.shape, 0)
    place = jnp.int32(residents)
    for s in range(insts):
        for c in range(requests):
            mine = dest_ref[c, s] == here
            places = jnp.where((row == (here ^ s) * requests + c) & mine, place, places)
            place += jnp.where(mine, 1, 0).astype(jnp.int32)
    place_out[...] = places

    blocks = tokens // 128
    last = tokens + 2 * blocks
    tail = pieces[0][tokens:last, :128].astype(F32)
    for t in range(1, ranks):
        tail = tail + pieces[t][tokens:last, :128].astype(F32)
    squares = tail[:blocks] + tail[blocks:]
    squares = jnp.concatenate(
        [row_to_column(squares[b : b + 1], 128) for b in range(blocks)], axis=0
    )
    token_scale = lax.rsqrt(squares / features + EPS)

    def column_block(c):
        total = pieces[0][:tokens, c : c + 128].astype(F32)
        for t in range(1, ranks):
            total = total + pieces[t][:tokens, c : c + 128].astype(F32)
        return total * token_scale

    gain = gain_ref[...].astype(F32)
    q = q_ref[...]
    q16 = q.astype(BF16)
    which = iota((rows, tokens), 0) % heads_mine // (heads_mine // kv_mine)
    scores = None
    for h in range(kv_mine):
        key = column_block(h * 128)
        key = key * lax.rsqrt(jnp.mean(key * key, axis=1, keepdims=True) + EPS) * gain
        key = key * cos_ref[...] + pltpu.roll(key, 64, 1) * sin_ref[...]
        part = lax.dot_general(
            q16, key.astype(BF16), (((1,), (1,)), ((), ())), preferred_element_type=F32
        )
        scores = part if scores is None else jnp.where(which == h, part, scores)
    token = iota((rows, tokens), 1)
    valid = (token % requests == row_request) & (token // requests < limit)
    scores = jnp.where(valid, scores * scale, ABSENT)
    own_score = jnp.sum(q * own_ref[0], axis=1, keepdims=True) * scale
    top = jnp.maximum(jnp.max(scores, axis=1, keepdims=True), own_score)
    weights = jnp.where(valid, jnp.exp(scores - top), 0.0)
    own_weight = jnp.exp(own_score - top)
    total = jnp.sum(weights, axis=1, keepdims=True) + own_weight
    weights = weights.astype(BF16)
    summed = None
    for h in range(kv_mine):
        value = column_block(piece + h * 128).astype(BF16)
        part = jnp.dot(weights, value, preferred_element_type=F32)
        summed = part if summed is None else jnp.where(which[:, :128] == h, part, summed)
    summed = summed + own_weight.astype(BF16).astype(F32) * own_ref[1]
    result = summed / total
    for r in range(requests):
        for h in range(heads_mine):
            at = r * heads_mine + h
            line_ref[r : r + 1, h * 128 : (h + 1) * 128] = result[at : at + 1, :]
    out_ref[...] = line_ref[...].astype(BF16)


def attend_moved(dest, count, k_gain, cos, sin, asks, pieces, residents, heads_mine, features):
    requests, insts = dest.shape
    rows = requests * heads_mine
    return pl.pallas_call(
        functools.partial(moved_kernel, insts, len(pieces), residents, features),
        in_specs=[SMEM] * 2 + [VMEM] * (3 + len(asks) + len(pieces)),
        out_specs=[VMEM] * 2,
        out_shape=[
            jax.ShapeDtypeStruct((requests, heads_mine * 128), BF16),
            jax.ShapeDtypeStruct((insts * requests, 128), jnp.int32),
        ],
        scratch_shapes=[
            pltpu.VMEM((requests, asks[0].shape[1]), F32),
            pltpu.VMEM((rows, 128), F32),
            pltpu.VMEM((2, rows, 128), F32),
            pltpu.VMEM((requests, heads_mine * 128), F32),
        ],
        compiler_params=pltpu.CompilerParams(vmem_limit_bytes=16 * MIB),
        name="attend_moved",
    )(dest, count, k_gain, cos, sin, *asks, *pieces)


def combine_kernel(residents, kv_mine, ask_ref, payload_ref, out_ref):
    heads_mine = out_ref.shape[1] // 128
    scale = F32(1.0) / jnp.sqrt(F32(128.0))
    payloads = [payload_ref[t].astype(F32) for t in range(payload_ref.shape[0])]
    at = residents * heads_mine
    ask = ask_ref[...].astype(F32)
    for r in range(residents):
        q, own_k, own_v = heads_of(ask[r : r + 1], heads_mine, kv_mine)
        own_score = jnp.sum(q * own_k, axis=1, keepdims=True) * scale
        peaks, totals = [], []
        for payload in payloads:
            stat = payload[at : at + 3 * residents]
            peaks.append(row_to_column(stat[r : r + 1], heads_mine))
            total = stat[residents + r : residents + r + 1]
            total = total + stat[2 * residents + r : 2 * residents + r + 1]
            totals.append(row_to_column(total, heads_mine))
        top = own_score
        for peak in peaks:
            top = jnp.maximum(top, peak)
        own_weight = jnp.exp(own_score - top)
        denom = own_weight
        numer = own_weight.astype(BF16).astype(F32) * own_v
        for peak, total, payload in zip(peaks, totals, payloads):
            keep = jnp.exp(peak - top)
            denom = denom + keep * total
            numer = numer + keep * payload[r * heads_mine : (r + 1) * heads_mine]
        result = numer / denom
        for h in range(heads_mine):
            out_ref[r : r + 1, h * 128 : (h + 1) * 128] = result[h : h + 1, :]


def combine_resident(ask, payloads, residents, heads_mine, kv_mine):
    return pl.pallas_call(
        functools.partial(combine_kernel, residents, kv_mine),
        in_specs=[VMEM] * 2,
        out_specs=VMEM,
        out_shape=jax.ShapeDtypeStruct((residents, heads_mine * 128), F32),
        compiler_params=pltpu.CompilerParams(vmem_limit_bytes=8 * MIB),
        name="combine_resident",
    )(ask, payloads)


def finish_kernel(kept_ref, place_ref, *rest):
    moved, out_ref = rest[:-1], rest[-1]
    residents = kept_ref.shape[0]
    decoded, width = out_ref.shape
    requests = decoded - residents
    row = iota((decoded, 128), 0)
    arrived = [ref[...].astype(F32) for ref in moved]
    for c in range(0, width, 128):
        kept = kept_ref[:, c : c + 128]
        line = jnp.concatenate([kept, jnp.zeros((requests, 128), F32)], axis=0)
        for b in range(len(moved)):
            for i in range(requests):
                at = (b + 1) * requests + i
                line = jnp.where(
                    place_ref[at : at + 1, :] == row, arrived[b][i : i + 1, c : c + 128], line
                )
        out_ref[:, c : c + 128] = line.astype(BF16)


def finish(kept, places, moved, requests):
    residents, width = kept.shape
    return pl.pallas_call(
        finish_kernel,
        in_specs=[VMEM] * (2 + len(moved)),
        out_specs=VMEM,
        out_shape=jax.ShapeDtypeStruct((residents + requests, width), BF16),
        compiler_params=pltpu.CompilerParams(vmem_limit_bytes=8 * MIB),
        name="finish",
    )(kept, places, *moved)


def swapped(x, axis, j, n):
    return lax.ppermute(x, axis, [(i, i ^ j) for i in range(n)])


def rotation(slots, requests, head_size):
    half = head_size // 2
    freq = THETA ** (-np.arange(half) * 2.0 / head_size)
    angle = np.repeat(np.arange(slots), requests)[:, None] * freq[None, :]
    cos, sin = np.cos(angle), np.sin(angle)
    return (
        np.concatenate([cos, cos], axis=1).astype(np.float32),
        np.concatenate([-sin, sin], axis=1).astype(np.float32),
    )


def per_device(
    mig_hidden,
    mig_dest,
    mig_count,
    attn_gain,
    kv_weight,
    k_gain,
    query,
    new_kv,
    k_cache,
    v_cache,
    lengths,
):
    insts = lax.axis_size("inst")
    ranks = lax.axis_size("tp")
    head_size = k_gain.shape[0]
    slots, requests, feats = mig_hidden.shape[1:]
    residents = k_cache.shape[1]
    heads = query.shape[2] // head_size
    kv_heads = kv_weight.shape[1] // 2 // head_size
    heads_mine = heads // ranks
    group = heads // kv_heads
    kv_mine = max(1, heads_mine // group)

    pieces, ask = project(
        mig_hidden[0], attn_gain, kv_weight, query[0], new_kv[0], ranks, group, kv_mine
    )
    last = ranks - 1
    far = swapped(pieces[last], "tp", last, ranks)
    asks = [swapped(ask, "inst", b, insts) for b in range(1, insts)]
    asks[0], *others = lax.optimization_barrier((asks[0], *pieces[1:last]))
    others = [swapped(others[j - 1], "tp", j, ranks) for j in reversed(range(1, last))]
    pieces = [pieces[0], far] + others
    queries = jnp.transpose(query[0].reshape(query.shape[1], heads, head_size), (1, 0, 2))
    payloads = attend_resident(lengths, queries, k_cache[0], v_cache[0], ranks)
    asks, payloads = lax.optimization_barrier((asks, payloads))
    received = lax.all_to_all(payloads, "tp", 0, 0, tiled=True)
    cos, sin = rotation(slots, requests, head_size)
    moved, places = attend_moved(
        mig_dest.T,
        mig_count.T,
        k_gain.reshape(1, head_size),
        cos,
        sin,
        asks,
        pieces,
        residents,
        heads_mine,
        feats * ranks,
    )
    kept = combine_resident(ask, received, residents, heads_mine, kv_mine)
    moved = [swapped(moved, "inst", b, insts) for b in reversed(range(1, insts))][::-1]
    return finish(kept, places, moved, requests)[None]


def solution(mesh):
    placed = (
        P(("group", "inst"), None, None, "tp"),
        P("group", None),
        P("group", None),
        P("tp"),
        P("tp", None),
        P(),
        P(("group", "inst"), None, None),
        P(("group", "inst"), None, None),
        P(("group", "inst"), None, "tp", None),
        P(("group", "inst"), None, "tp", None),
        P(("group", "inst"), None),
    )
    return jax.shard_map(
        per_device,
        mesh=mesh,
        in_specs=placed,
        out_specs=P(("group", "inst"), None, "tp"),
        check_vma=False,
    )
```

```python
import functools

import jax
import jax.numpy as jnp
import numpy as np
from jax import lax
from jax.experimental import pallas as pl
from jax.experimental.pallas import tpu as pltpu
from jax.sharding import PartitionSpec as P

EPS = 1e-06
THETA = 1000000.0
ABSENT = -1e30
F32 = jnp.float32
BF16 = jnp.bfloat16
MIB = 1024 * 1024
CHUNK = 512

VMEM = pl.BlockSpec(memory_space=pltpu.VMEM)
SMEM = pl.BlockSpec(memory_space=pltpu.SMEM)
HBM = pl.BlockSpec(memory_space=pltpu.HBM)


def iota(shape, dim):
    return lax.broadcasted_iota(jnp.int32, shape, dim)


def column_to_row(column, period):
    n = column.shape[0]
    spread = jnp.where(iota((n, 128), 0) % period == iota((n, 128), 1), column, 0.0)
    return jnp.sum(spread.reshape(n // period, period, 128), axis=1)


def row_to_column(row, n):
    return jnp.sum(
        jnp.where(iota((n, 128), 0) == iota((n, 128), 1), row, 0.0), axis=1, keepdims=True
    )


def split_bf16(x):
    high = x.astype(BF16)
    return high, (x - high.astype(F32)).astype(BF16)


def project_kernel(ranks, group, gain_hbm, x_hbm, w_hbm, q_hbm, own_hbm, *rest):
    outs, ask_ref = rest[:ranks], rest[ranks]
    gain_ref, x_ref, w_ref, acc_ref, in_sems, w_sems = rest[ranks + 1 :]
    slots, requests, feats = x_ref.shape
    rows = slots * requests
    piece = outs[0].shape[1] // 2
    kv_width = w_hbm.shape[1] // 2
    heads_mine = kv_width // 128 * group // ranks
    rank = lax.axis_index("tp")

    def first_column(target):
        return pl.multiple_of(target * heads_mine // group * 128, 128)

    gain_copy = pltpu.make_async_copy(gain_hbm, gain_ref, in_sems.at[0])
    gain_copy.start()
    x_copy = pltpu.make_async_copy(x_hbm, x_ref, in_sems.at[1])
    x_copy.start()
    cuts = list(range(0, feats, CHUNK)) + [feats]
    chunks = list(zip(cuts[:-1], cuts[1:]))
    copies = []
    for i, (low, high) in enumerate(chunks):
        copies.append(
            pltpu.make_async_copy(w_hbm.at[low:high, :], w_ref.at[low:high, :], w_sems.at[i])
        )
        copies[-1].start()
    mine = heads_mine * 128
    q_first = pl.multiple_of(rank * mine, 128)
    asking = [
        pltpu.make_async_copy(
            q_hbm.at[:, pl.ds(q_first, mine)], ask_ref.at[:, :mine], in_sems.at[2]
        )
    ]
    for i in range(2):
        asking.append(
            pltpu.make_async_copy(
                own_hbm.at[:, pl.ds(i * kv_width + first_column(rank), piece)],
                ask_ref.at[:, mine + i * piece : mine + (i + 1) * piece],
                in_sems.at[3 + i],
            )
        )
    for copy in asking:
        copy.start()
    gain_copy.wait()
    x_copy.wait()
    squares = jnp.zeros((rows, 128), F32)
    for i, (low, high) in enumerate(chunks):
        parts = []
        for c in range(low, high, 128):
            width = min(128, high - c)
            x = x_ref[:, :, c : c + width].astype(F32).reshape(rows, width)
            gain = gain_ref[c : c + width].astype(F32).reshape(1, width)
            parts.append((x * gain).astype(BF16))
            x = x * x
            if width < 128:
                x = jnp.concatenate([x, jnp.zeros((rows, 128 - width), F32)], axis=1)
            squares = squares + x
        xg = parts[0] if len(parts) == 1 else jnp.concatenate(parts, axis=1)
        copies[i].wait()
        for n in range(0, 2 * kv_width, 512):
            part = jnp.dot(xg, w_ref[low:high, n : n + 512], preferred_element_type=F32)
            if i == 0:
                acc_ref[:, n : n + 512] = part
            else:
                acc_ref[:, n : n + 512] += part
    sq = column_to_row(jnp.sum(squares, axis=1, keepdims=True), 128)
    high, low = split_bf16(sq)
    tail = jnp.concatenate([high.astype(F32), low.astype(F32)], axis=0)
    fill = outs[1].shape[0] - rows - tail.shape[0]
    if fill:
        tail = jnp.concatenate([tail, jnp.zeros((fill, 128), F32)], axis=0)
    extra = jnp.concatenate([tail.astype(BF16)] * (2 * piece // 128), axis=1)
    for j in range(ranks):
        first = first_column(rank ^ j)
        outs[j][:rows, :piece] = acc_ref[:, pl.ds(first, piece)].astype(BF16)
        outs[j][:rows, piece:] = acc_ref[:, pl.ds(kv_width + first, piece)].astype(BF16)
        outs[j][rows:, :] = extra
    for copy in asking:
        copy.wait()


def project(x, gain, weight, query, own, ranks, group, kv_mine):
    slots, requests, feats = x.shape
    rows = slots * requests
    piece = kv_mine * 128
    extra = -(-2 * (rows // 128) // 8) * 8
    decoded, q_width = query.shape
    outs = pl.pallas_call(
        functools.partial(project_kernel, ranks, group),
        in_specs=[HBM] * 5,
        out_specs=[VMEM] * (ranks + 1),
        out_shape=[jax.ShapeDtypeStruct((rows + extra, 2 * piece), BF16)] * ranks
        + [jax.ShapeDtypeStruct((decoded, q_width // ranks + 2 * piece), BF16)],
        scratch_shapes=[
            pltpu.VMEM((feats,), BF16),
            pltpu.VMEM((slots, requests, feats), BF16),
            pltpu.VMEM(weight.shape, BF16),
            pltpu.VMEM((rows, weight.shape[1]), F32),
            pltpu.SemaphoreType.DMA((5,)),
            pltpu.SemaphoreType.DMA((-(-feats // CHUNK),)),
        ],
        compiler_params=pltpu.CompilerParams(vmem_limit_bytes=56 * MIB),
        cost_estimate=pl.CostEstimate(
            flops=2 * rows * feats * weight.shape[1],
            bytes_accessed=2 * feats * weight.shape[1],
            transcendentals=0,
        ),
        name="project",
    )(gain, x, weight, query, own)
    return outs[:ranks], outs[ranks]


def resident_kernel(ranks, len_ref, q_ref, k_hbm, v_hbm, out, *rest):
    q_wide, q_all, k_buf, v_buf, o_all, m_all, l_all, s_all, sems = rest
    residents, positions, width = k_buf.shape
    copies = []
    for r in range(residents):
        copies.append(
            (
                pltpu.make_async_copy(k_hbm.at[r], k_buf.at[r], sems.at[0, r]),
                pltpu.make_async_copy(v_hbm.at[r], v_buf.at[r], sems.at[1, r]),
            )
        )
    for pair in copies:
        for copy in pair:
            copy.start()
    heads = q_ref.shape[0]
    kv_heads = width // 128
    group = heads // kv_heads
    pair_rows = 2 * group
    heads_mine = heads // ranks
    rank = lax.axis_index("tp")
    top_half = iota((pair_rows, 128), 0) < group
    position = rank * positions + iota((pair_rows, positions), 1)
    scale = F32(1.0) / jnp.sqrt(F32(128.0))
    diagonal = iota((heads, 128), 0) % heads_mine == iota((heads, 128), 1)

    def to_rows(column):
        spread = jnp.where(diagonal, column, 0.0)
        return jnp.sum(spread.reshape(ranks, heads_mine, 128), axis=1)

    q_wide[...] = q_ref[...].astype(F32)
    for r in range(residents):
        q_all[r] = q_wide[:, r, :].astype(BF16)
    for r in range(residents):
        valid = position < len_ref[0, r]
        copies[r][0].wait()
        weights = []
        for p in range(kv_heads // 2):
            rows = slice(p * pair_rows, (p + 1) * pair_rows)
            q = q_all[r, rows, :]
            zero = jnp.zeros_like(q)
            lhs = jnp.concatenate(
                [jnp.where(top_half, q, zero), jnp.where(top_half, zero, q)], axis=1
            )
            scores = lax.dot_general(
                lhs,
                k_buf[r, :, p * 256 : (p + 1) * 256],
                (((1,), (1,)), ((), ())),
                preferred_element_type=F32,
            )
            scores = jnp.where(valid, scores * scale, ABSENT)
            peak = jnp.max(scores, axis=1, keepdims=True).astype(BF16).astype(F32)
            weight = jnp.where(valid, jnp.exp(scores - peak), 0.0)
            m_all[r, rows, :] = peak
            l_all[r, rows, :] = jnp.sum(weight, axis=1, keepdims=True)
            weights.append(weight.astype(BF16))
        copies[r][1].wait()
        for p in range(kv_heads // 2):
            both = jnp.dot(
                weights[p], v_buf[r, :, p * 256 : (p + 1) * 256], preferred_element_type=F32
            )
            o_all[r, p * pair_rows : (p + 1) * pair_rows, :] = jnp.where(
                top_half, both[:, :128], both[:, 128:]
            )
    for r in range(residents):
        s_all[r, 0] = to_rows(m_all[r])
        high, low = split_bf16(to_rows(l_all[r]))
        s_all[r, 1] = high.astype(F32)
        s_all[r, 2] = low.astype(F32)
    filled = residents * (heads_mine + 3)
    for t in range(ranks):
        parts = [o_all[r, t * heads_mine : (t + 1) * heads_mine, :] for r in range(residents)]
        parts += [s_all[r, i, t : t + 1, :] for i in range(3) for r in range(residents)]
        if out.shape[1] > filled:
            parts.append(jnp.zeros((out.shape[1] - filled, 128), F32))
        out[t] = jnp.concatenate(parts, axis=0).astype(BF16)


def attend_resident(lengths, queries, k_cache, v_cache, ranks):
    residents, positions, width = k_cache.shape
    heads = queries.shape[0]
    heads_mine = heads // ranks
    rows = -(-(residents * (heads_mine + 3)) // 16) * 16
    return pl.pallas_call(
        functools.partial(resident_kernel, ranks),
        in_specs=[SMEM, VMEM, HBM, HBM],
        out_specs=VMEM,
        out_shape=jax.ShapeDtypeStruct((ranks, rows, 128), BF16),
        scratch_shapes=[
            pltpu.VMEM(queries.shape, F32),
            pltpu.VMEM((residents, heads, 128), BF16),
            pltpu.VMEM((residents, positions, width), BF16),
            pltpu.VMEM((residents, positions, width), BF16),
            pltpu.VMEM((residents, heads, 128), F32),
            pltpu.VMEM((residents, heads, 1), F32),
            pltpu.VMEM((residents, heads, 1), F32),
            pltpu.VMEM((residents, 3, ranks, 128), F32),
            pltpu.SemaphoreType.DMA((2, residents)),
        ],
        compiler_params=pltpu.CompilerParams(vmem_limit_bytes=56 * MIB),
        cost_estimate=pl.CostEstimate(
            flops=4 * residents * heads * positions * 128,
            bytes_accessed=4 * residents * positions * width,
            transcendentals=residents * heads * positions,
        ),
        name="attend_resident",
    )(lengths, queries, k_cache, v_cache)


def expand(own, rows):
    which = iota((rows, 128), 0) // (rows // own.shape[0])
    out = jnp.broadcast_to(own[0:1], (rows, 128))
    for h in range(1, own.shape[0]):
        out = jnp.where(which == h, own[h : h + 1], out)
    return out


def heads_of(line, heads_mine, kv_mine):
    per = heads_mine // kv_mine
    blocks = [line[:, c : c + 128] for c in range(0, line.shape[1], 128)]
    q = jnp.concatenate(blocks[:heads_mine], axis=0)
    k = blocks[heads_mine : heads_mine + kv_mine]
    v = blocks[heads_mine + kv_mine :]
    return (
        q,
        expand(jnp.concatenate(k, axis=0), heads_mine),
        expand(jnp.concatenate(v, axis=0), heads_mine),
    )


def moved_kernel(
    insts, ranks, residents, features, dest_ref, count_ref, gain_ref, cos_ref, sin_ref, *rest
):
    asks, rest = rest[: insts - 1], rest[insts - 1 :]
    pieces, rest = rest[:ranks], rest[ranks:]
    out_ref, place_out, ask_ref, q_ref, own_ref, line_ref = rest
    requests = out_ref.shape[0]
    tokens = cos_ref.shape[0]
    piece = pieces[0].shape[1] // 2
    kv_mine = piece // 128
    rows = q_ref.shape[0]
    heads_mine = rows // requests
    scale = F32(1.0) / jnp.sqrt(F32(128.0))
    here = lax.axis_index("inst")

    ask_row = iota(asks[0].shape, 0)
    row_request = iota((rows, tokens), 0) // heads_mine
    limit = jnp.zeros((rows, tokens), jnp.int32)
    for r in range(requests):
        dest = dest_ref[r, here]
        limit = jnp.where(row_request == r, count_ref[r, here], limit)
        place = jnp.int32(residents)
        for s in range(insts):
            for c in range(requests):
                place += jnp.where((dest_ref[c, s] == dest) & (here > s), 1, 0).astype(jnp.int32)
        for b in range(1, insts):

            @pl.when(here ^ b == dest)
            def _():
                ask = asks[b - 1][...].astype(F32)
                ask_ref[r : r + 1, :] = jnp.sum(
                    jnp.where(ask_row == place, ask, 0.0), axis=0, keepdims=True
                )

        at = slice(r * heads_mine, (r + 1) * heads_mine)
        q_ref[at, :], own_ref[0, at, :], own_ref[1, at, :] = heads_of(
            ask_ref[r : r + 1, :], heads_mine, kv_mine
        )
    places = jnp.full(place_out.shape, -1, jnp.int32)
    row = iota(place_out.shape, 0)
    place = jnp.int32(residents)
    for s in range(insts):
        for c in range(requests):
            mine = dest_ref[c, s] == here
            places = jnp.where((row == (here ^ s) * requests + c) & mine, place, places)
            place += jnp.where(mine, 1, 0).astype(jnp.int32)
    place_out[...] = places

    blocks = tokens // 128
    last = tokens + 2 * blocks
    tail = pieces[0][tokens:last, :128].astype(F32)
    for t in range(1, ranks):
        tail = tail + pieces[t][tokens:last, :128].astype(F32)
    squares = tail[:blocks] + tail[blocks:]
    squares = jnp.concatenate(
        [row_to_column(squares[b : b + 1], 128) for b in range(blocks)], axis=0
    )
    token_scale = lax.rsqrt(squares / features + EPS)

    def column_block(c):
        total = pieces[0][:tokens, c : c + 128].astype(F32)
        for t in range(1, ranks):
            total = total + pieces[t][:tokens, c : c + 128].astype(F32)
        return total * token_scale

    gain = gain_ref[...].astype(F32)
    q = q_ref[...]
    q16 = q.astype(BF16)
    which = iota((rows, tokens), 0) % heads_mine // (heads_mine // kv_mine)
    scores = None
    for h in range(kv_mine):
        key = column_block(h * 128)
        key = key * lax.rsqrt(jnp.mean(key * key, axis=1, keepdims=True) + EPS) * gain
        key = key * cos_ref[...] + pltpu.roll(key, 64, 1) * sin_ref[...]
        part = lax.dot_general(
            q16, key.astype(BF16), (((1,), (1,)), ((), ())), preferred_element_type=F32
        )
        scores = part if scores is None else jnp.where(which == h, part, scores)
    token = iota((rows, tokens), 1)
    valid = (token % requests == row_request) & (token // requests < limit)
    scores = jnp.where(valid, scores * scale, ABSENT)
    own_score = jnp.sum(q * own_ref[0], axis=1, keepdims=True) * scale
    top = jnp.maximum(jnp.max(scores, axis=1, keepdims=True), own_score)
    weights = jnp.where(valid, jnp.exp(scores - top), 0.0)
    own_weight = jnp.exp(own_score - top)
    total = jnp.sum(weights, axis=1, keepdims=True) + own_weight
    weights = weights.astype(BF16)
    summed = None
    for h in range(kv_mine):
        value = column_block(piece + h * 128).astype(BF16)
        part = jnp.dot(weights, value, preferred_element_type=F32)
        summed = part if summed is None else jnp.where(which[:, :128] == h, part, summed)
    summed = summed + own_weight.astype(BF16).astype(F32) * own_ref[1]
    result = summed / total
    for r in range(requests):
        for h in range(heads_mine):
            at = r * heads_mine + h
            line_ref[r : r + 1, h * 128 : (h + 1) * 128] = result[at : at + 1, :]
    out_ref[...] = line_ref[...].astype(BF16)


def attend_moved(dest, count, k_gain, cos, sin, asks, pieces, residents, heads_mine, features):
    requests, insts = dest.shape
    rows = requests * heads_mine
    return pl.pallas_call(
        functools.partial(moved_kernel, insts, len(pieces), residents, features),
        in_specs=[SMEM] * 2 + [VMEM] * (3 + len(asks) + len(pieces)),
        out_specs=[VMEM] * 2,
        out_shape=[
            jax.ShapeDtypeStruct((requests, heads_mine * 128), BF16),
            jax.ShapeDtypeStruct((insts * requests, 128), jnp.int32),
        ],
        scratch_shapes=[
            pltpu.VMEM((requests, asks[0].shape[1]), F32),
            pltpu.VMEM((rows, 128), F32),
            pltpu.VMEM((2, rows, 128), F32),
            pltpu.VMEM((requests, heads_mine * 128), F32),
        ],
        compiler_params=pltpu.CompilerParams(vmem_limit_bytes=16 * MIB),
        name="attend_moved",
    )(dest, count, k_gain, cos, sin, *asks, *pieces)


def combine_kernel(residents, kv_mine, ask_ref, payload_ref, out_ref):
    heads_mine = out_ref.shape[1] // 128
    scale = F32(1.0) / jnp.sqrt(F32(128.0))
    payloads = [payload_ref[t].astype(F32) for t in range(payload_ref.shape[0])]
    at = residents * heads_mine
    ask = ask_ref[...].astype(F32)
    for r in range(residents):
        q, own_k, own_v = heads_of(ask[r : r + 1], heads_mine, kv_mine)
        own_score = jnp.sum(q * own_k, axis=1, keepdims=True) * scale
        peaks, totals = [], []
        for payload in payloads:
            stat = payload[at : at + 3 * residents]
            peaks.append(row_to_column(stat[r : r + 1], heads_mine))
            total = stat[residents + r : residents + r + 1]
            total = total + stat[2 * residents + r : 2 * residents + r + 1]
            totals.append(row_to_column(total, heads_mine))
        top = own_score
        for peak in peaks:
            top = jnp.maximum(top, peak)
        own_weight = jnp.exp(own_score - top)
        denom = own_weight
        numer = own_weight.astype(BF16).astype(F32) * own_v
        for peak, total, payload in zip(peaks, totals, payloads):
            keep = jnp.exp(peak - top)
            denom = denom + keep * total
            numer = numer + keep * payload[r * heads_mine : (r + 1) * heads_mine]
        result = numer / denom
        for h in range(heads_mine):
            out_ref[r : r + 1, h * 128 : (h + 1) * 128] = result[h : h + 1, :]


def combine_resident(ask, payloads, residents, heads_mine, kv_mine):
    return pl.pallas_call(
        functools.partial(combine_kernel, residents, kv_mine),
        in_specs=[VMEM] * 2,
        out_specs=VMEM,
        out_shape=jax.ShapeDtypeStruct((residents, heads_mine * 128), F32),
        compiler_params=pltpu.CompilerParams(vmem_limit_bytes=8 * MIB),
        name="combine_resident",
    )(ask, payloads)


def finish_kernel(kept_ref, place_ref, *rest):
    moved, out_ref = rest[:-1], rest[-1]
    residents = kept_ref.shape[0]
    decoded, width = out_ref.shape
    requests = decoded - residents
    row = iota((decoded, 128), 0)
    arrived = [ref[...].astype(F32) for ref in moved]
    for c in range(0, width, 128):
        kept = kept_ref[:, c : c + 128]
        line = jnp.concatenate([kept, jnp.zeros((requests, 128), F32)], axis=0)
        for b in range(len(moved)):
            for i in range(requests):
                at = (b + 1) * requests + i
                line = jnp.where(
                    place_ref[at : at + 1, :] == row, arrived[b][i : i + 1, c : c + 128], line
                )
        out_ref[:, c : c + 128] = line.astype(BF16)


def finish(kept, places, moved, requests):
    residents, width = kept.shape
    return pl.pallas_call(
        finish_kernel,
        in_specs=[VMEM] * (2 + len(moved)),
        out_specs=VMEM,
        out_shape=jax.ShapeDtypeStruct((residents + requests, width), BF16),
        compiler_params=pltpu.CompilerParams(vmem_limit_bytes=8 * MIB),
        name="finish",
    )(kept, places, *moved)


def swapped(x, axis, j, n):
    return lax.ppermute(x, axis, [(i, i ^ j) for i in range(n)])


def rotation(slots, requests, head_size):
    half = head_size // 2
    freq = THETA ** (-np.arange(half) * 2.0 / head_size)
    angle = np.repeat(np.arange(slots), requests)[:, None] * freq[None, :]
    cos, sin = np.cos(angle), np.sin(angle)
    return (
        np.concatenate([cos, cos], axis=1).astype(np.float32),
        np.concatenate([-sin, sin], axis=1).astype(np.float32),
    )


def per_device(
    mig_hidden,
    mig_dest,
    mig_count,
    attn_gain,
    kv_weight,
    k_gain,
    query,
    new_kv,
    k_cache,
    v_cache,
    lengths,
):
    insts = lax.axis_size("inst")
    ranks = lax.axis_size("tp")
    head_size = k_gain.shape[0]
    slots, requests, feats = mig_hidden.shape[1:]
    residents = k_cache.shape[1]
    heads = query.shape[2] // head_size
    kv_heads = kv_weight.shape[1] // 2 // head_size
    heads_mine = heads // ranks
    group = heads // kv_heads
    kv_mine = max(1, heads_mine // group)

    pieces, ask = project(
        mig_hidden[0], attn_gain, kv_weight, query[0], new_kv[0], ranks, group, kv_mine
    )
    last = ranks - 1
    far = swapped(pieces[last], "tp", last, ranks)
    asks = [swapped(ask, "inst", b, insts) for b in range(1, insts)]
    asks[0], *others = lax.optimization_barrier((asks[0], *pieces[1:last]))
    others = [swapped(others[j - 1], "tp", j, ranks) for j in reversed(range(1, last))]
    pieces = [pieces[0], far] + others
    queries = jnp.transpose(query[0].reshape(query.shape[1], heads, head_size), (1, 0, 2))
    payloads = attend_resident(lengths, queries, k_cache[0], v_cache[0], ranks)
    asks, payloads = lax.optimization_barrier((asks, payloads))
    received = lax.all_to_all(payloads, "tp", 0, 0, tiled=True)
    cos, sin = rotation(slots, requests, head_size)
    moved, places = attend_moved(
        mig_dest.T,
        mig_count.T,
        k_gain.reshape(1, head_size),
        cos,
        sin,
        asks,
        pieces,
        residents,
        heads_mine,
        feats * ranks,
    )
    kept = combine_resident(ask, received, residents, heads_mine, kv_mine)
    moved = [swapped(moved, "inst", b, insts) for b in reversed(range(1, insts))][::-1]
    return finish(kept, places, moved, requests)[None]


def solution(mesh):
    placed = (
        P(("group", "inst"), None, None, "tp"),
        P("group", None),
        P("group", None),
        P("tp"),
        P("tp", None),
        P(),
        P(("group", "inst"), None, None),
        P(("group", "inst"), None, None),
        P(("group", "inst"), None, "tp", None),
        P(("group", "inst"), None, "tp", None),
        P(("group", "inst"), None),
    )
    return jax.shard_map(
        per_device,
        mesh=mesh,
        in_specs=placed,
        out_specs=P(("group", "inst"), None, "tp"),
        check_vma=False,
    )
```

```python
import functools

import jax
import jax.numpy as jnp
import numpy as np
from jax import lax
from jax.experimental import pallas as pl
from jax.experimental.pallas import tpu as pltpu
from jax.sharding import PartitionSpec as P

EPS = 1e-06
THETA = 1000000.0
ABSENT = -1e30
F32 = jnp.float32
BF16 = jnp.bfloat16
MIB = 1024 * 1024
CHUNK = 512

VMEM = pl.BlockSpec(memory_space=pltpu.VMEM)
SMEM = pl.BlockSpec(memory_space=pltpu.SMEM)
HBM = pl.BlockSpec(memory_space=pltpu.HBM)


def iota(shape, dim):
    return lax.broadcasted_iota(jnp.int32, shape, dim)


def column_to_row(column, period):
    n = column.shape[0]
    spread = jnp.where(iota((n, 128), 0) % period == iota((n, 128), 1), column, 0.0)
    return jnp.sum(spread.reshape(n // period, period, 128), axis=1)


def row_to_column(row, n):
    return jnp.sum(
        jnp.where(iota((n, 128), 0) == iota((n, 128), 1), row, 0.0), axis=1, keepdims=True
    )


def split_bf16(x):
    high = x.astype(BF16)
    return high, (x - high.astype(F32)).astype(BF16)


def project_kernel(ranks, group, gain_hbm, x_hbm, w_hbm, q_hbm, own_hbm, *rest):
    outs, ask_ref = rest[:ranks], rest[ranks]
    gain_ref, x_ref, w_ref, acc_ref, in_sems, w_sems = rest[ranks + 1 :]
    slots, requests, feats = x_ref.shape
    rows = slots * requests
    piece = outs[0].shape[1] // 2
    kv_width = w_hbm.shape[1] // 2
    heads_mine = kv_width // 128 * group // ranks
    rank = lax.axis_index("tp")

    def first_column(target):
        return pl.multiple_of(target * heads_mine // group * 128, 128)

    gain_copy = pltpu.make_async_copy(gain_hbm, gain_ref, in_sems.at[0])
    gain_copy.start()
    x_copy = pltpu.make_async_copy(x_hbm, x_ref, in_sems.at[1])
    x_copy.start()
    cuts = list(range(0, feats, CHUNK)) + [feats]
    chunks = list(zip(cuts[:-1], cuts[1:]))
    copies = []
    for i, (low, high) in enumerate(chunks):
        copies.append(
            pltpu.make_async_copy(w_hbm.at[low:high, :], w_ref.at[low:high, :], w_sems.at[i])
        )
        copies[-1].start()
    mine = heads_mine * 128
    q_first = pl.multiple_of(rank * mine, 128)
    asking = [
        pltpu.make_async_copy(
            q_hbm.at[:, pl.ds(q_first, mine)], ask_ref.at[:, :mine], in_sems.at[2]
        )
    ]
    for i in range(2):
        asking.append(
            pltpu.make_async_copy(
                own_hbm.at[:, pl.ds(i * kv_width + first_column(rank), piece)],
                ask_ref.at[:, mine + i * piece : mine + (i + 1) * piece],
                in_sems.at[3 + i],
            )
        )
    for copy in asking:
        copy.start()
    gain_copy.wait()
    x_copy.wait()
    squares = jnp.zeros((rows, 128), F32)
    for i, (low, high) in enumerate(chunks):
        parts = []
        for c in range(low, high, 128):
            width = min(128, high - c)
            x = x_ref[:, :, c : c + width].astype(F32).reshape(rows, width)
            gain = gain_ref[c : c + width].astype(F32).reshape(1, width)
            parts.append((x * gain).astype(BF16))
            x = x * x
            if width < 128:
                x = jnp.concatenate([x, jnp.zeros((rows, 128 - width), F32)], axis=1)
            squares = squares + x
        xg = parts[0] if len(parts) == 1 else jnp.concatenate(parts, axis=1)
        copies[i].wait()
        for n in range(0, 2 * kv_width, 512):
            part = jnp.dot(xg, w_ref[low:high, n : n + 512], preferred_element_type=F32)
            if i == 0:
                acc_ref[:, n : n + 512] = part
            else:
                acc_ref[:, n : n + 512] += part
    sq = column_to_row(jnp.sum(squares, axis=1, keepdims=True), 128)
    high, low = split_bf16(sq)
    tail = jnp.concatenate([high.astype(F32), low.astype(F32)], axis=0)
    fill = outs[1].shape[0] - rows - tail.shape[0]
    if fill:
        tail = jnp.concatenate([tail, jnp.zeros((fill, 128), F32)], axis=0)
    extra = jnp.concatenate([tail.astype(BF16)] * (2 * piece // 128), axis=1)
    for j in range(ranks):
        first = first_column(rank ^ j)
        outs[j][:rows, :piece] = acc_ref[:, pl.ds(first, piece)].astype(BF16)
        outs[j][:rows, piece:] = acc_ref[:, pl.ds(kv_width + first, piece)].astype(BF16)
        outs[j][rows:, :] = extra
    for copy in asking:
        copy.wait()


def project(x, gain, weight, query, own, ranks, group, kv_mine):
    slots, requests, feats = x.shape
    rows = slots * requests
    piece = kv_mine * 128
    extra = -(-2 * (rows // 128) // 8) * 8
    decoded, q_width = query.shape
    outs = pl.pallas_call(
        functools.partial(project_kernel, ranks, group),
        in_specs=[HBM] * 5,
        out_specs=[VMEM] * (ranks + 1),
        out_shape=[jax.ShapeDtypeStruct((rows + extra, 2 * piece), BF16)] * ranks
        + [jax.ShapeDtypeStruct((decoded, q_width // ranks + 2 * piece), BF16)],
        scratch_shapes=[
            pltpu.VMEM((feats,), BF16),
            pltpu.VMEM((slots, requests, feats), BF16),
            pltpu.VMEM(weight.shape, BF16),
            pltpu.VMEM((rows, weight.shape[1]), F32),
            pltpu.SemaphoreType.DMA((5,)),
            pltpu.SemaphoreType.DMA((-(-feats // CHUNK),)),
        ],
        compiler_params=pltpu.CompilerParams(vmem_limit_bytes=56 * MIB),
        cost_estimate=pl.CostEstimate(
            flops=2 * rows * feats * weight.shape[1],
            bytes_accessed=2 * feats * weight.shape[1],
            transcendentals=0,
        ),
        name="project",
    )(gain, x, weight, query, own)
    return outs[:ranks], outs[ranks]


def resident_kernel(ranks, len_ref, q_ref, k_hbm, v_hbm, out, *rest):
    q_wide, q_all, k_buf, v_buf, o_all, m_all, l_all, s_all, sems = rest
    residents, positions, width = k_buf.shape
    copies = []
    for r in range(residents):
        copies.append(
            (
                pltpu.make_async_copy(k_hbm.at[r], k_buf.at[r], sems.at[0, r]),
                pltpu.make_async_copy(v_hbm.at[r], v_buf.at[r], sems.at[1, r]),
            )
        )
    for pair in copies:
        for copy in pair:
            copy.start()
    heads = q_ref.shape[0]
    kv_heads = width // 128
    group = heads // kv_heads
    pair_rows = 2 * group
    heads_mine = heads // ranks
    rank = lax.axis_index("tp")
    top_half = iota((pair_rows, 128), 0) < group
    position = rank * positions + iota((pair_rows, positions), 1)
    scale = F32(1.0) / jnp.sqrt(F32(128.0))
    diagonal = iota((heads, 128), 0) % heads_mine == iota((heads, 128), 1)

    def to_rows(column):
        spread = jnp.where(diagonal, column, 0.0)
        return jnp.sum(spread.reshape(ranks, heads_mine, 128), axis=1)

    q_wide[...] = q_ref[...].astype(F32)
    for r in range(residents):
        q_all[r] = q_wide[:, r, :].astype(BF16)
    for r in range(residents):
        valid = position < len_ref[0, r]
        copies[r][0].wait()
        weights = []
        for p in range(kv_heads // 2):
            rows = slice(p * pair_rows, (p + 1) * pair_rows)
            q = q_all[r, rows, :]
            zero = jnp.zeros_like(q)
            lhs = jnp.concatenate(
                [jnp.where(top_half, q, zero), jnp.where(top_half, zero, q)], axis=1
            )
            scores = lax.dot_general(
                lhs,
                k_buf[r, :, p * 256 : (p + 1) * 256],
                (((1,), (1,)), ((), ())),
                preferred_element_type=F32,
            )
            scores = jnp.where(valid, scores * scale, ABSENT)
            peak = jnp.max(scores, axis=1, keepdims=True).astype(BF16).astype(F32)
            weight = jnp.where(valid, jnp.exp(scores - peak), 0.0)
            m_all[r, rows, :] = peak
            l_all[r, rows, :] = jnp.sum(weight, axis=1, keepdims=True)
            weights.append(weight.astype(BF16))
        copies[r][1].wait()
        for p in range(kv_heads // 2):
            both = jnp.dot(
                weights[p], v_buf[r, :, p * 256 : (p + 1) * 256], preferred_element_type=F32
            )
            o_all[r, p * pair_rows : (p + 1) * pair_rows, :] = jnp.where(
                top_half, both[:, :128], both[:, 128:]
            )
    for r in range(residents):
        s_all[r, 0] = to_rows(m_all[r])
        high, low = split_bf16(to_rows(l_all[r]))
        s_all[r, 1] = high.astype(F32)
        s_all[r, 2] = low.astype(F32)
    filled = residents * (heads_mine + 3)
    for t in range(ranks):
        parts = [o_all[r, t * heads_mine : (t + 1) * heads_mine, :] for r in range(residents)]
        parts += [s_all[r, i, t : t + 1, :] for i in range(3) for r in range(residents)]
        if out.shape[1] > filled:
            parts.append(jnp.zeros((out.shape[1] - filled, 128), F32))
        out[t] = jnp.concatenate(parts, axis=0).astype(BF16)


def attend_resident(lengths, queries, k_cache, v_cache, ranks):
    residents, positions, width = k_cache.shape
    heads = queries.shape[0]
    heads_mine = heads // ranks
    rows = -(-(residents * (heads_mine + 3)) // 16) * 16
    return pl.pallas_call(
        functools.partial(resident_kernel, ranks),
        in_specs=[SMEM, VMEM, HBM, HBM],
        out_specs=VMEM,
        out_shape=jax.ShapeDtypeStruct((ranks, rows, 128), BF16),
        scratch_shapes=[
            pltpu.VMEM(queries.shape, F32),
            pltpu.VMEM((residents, heads, 128), BF16),
            pltpu.VMEM((residents, positions, width), BF16),
            pltpu.VMEM((residents, positions, width), BF16),
            pltpu.VMEM((residents, heads, 128), F32),
            pltpu.VMEM((residents, heads, 1), F32),
            pltpu.VMEM((residents, heads, 1), F32),
            pltpu.VMEM((residents, 3, ranks, 128), F32),
            pltpu.SemaphoreType.DMA((2, residents)),
        ],
        compiler_params=pltpu.CompilerParams(vmem_limit_bytes=56 * MIB),
        cost_estimate=pl.CostEstimate(
            flops=4 * residents * heads * positions * 128,
            bytes_accessed=4 * residents * positions * width,
            transcendentals=residents * heads * positions,
        ),
        name="attend_resident",
    )(lengths, queries, k_cache, v_cache)


def expand(own, rows):
    which = iota((rows, 128), 0) // (rows // own.shape[0])
    out = jnp.broadcast_to(own[0:1], (rows, 128))
    for h in range(1, own.shape[0]):
        out = jnp.where(which == h, own[h : h + 1], out)
    return out


def heads_of(line, heads_mine, kv_mine):
    per = heads_mine // kv_mine
    blocks = [line[:, c : c + 128] for c in range(0, line.shape[1], 128)]
    q = jnp.concatenate(blocks[:heads_mine], axis=0)
    k = blocks[heads_mine : heads_mine + kv_mine]
    v = blocks[heads_mine + kv_mine :]
    return (
        q,
        expand(jnp.concatenate(k, axis=0), heads_mine),
        expand(jnp.concatenate(v, axis=0), heads_mine),
    )


def moved_kernel(
    insts, ranks, residents, features, dest_ref, count_ref, gain_ref, cos_ref, sin_ref, *rest
):
    asks, rest = rest[: insts - 1], rest[insts - 1 :]
    pieces, rest = rest[:ranks], rest[ranks:]
    out_ref, place_out, ask_ref, q_ref, own_ref, line_ref = rest
    requests = out_ref.shape[0]
    tokens = cos_ref.shape[0]
    piece = pieces[0].shape[1] // 2
    kv_mine = piece // 128
    rows = q_ref.shape[0]
    heads_mine = rows // requests
    scale = F32(1.0) / jnp.sqrt(F32(128.0))
    here = lax.axis_index("inst")

    ask_row = iota(asks[0].shape, 0)
    row_request = iota((rows, tokens), 0) // heads_mine
    limit = jnp.zeros((rows, tokens), jnp.int32)
    for r in range(requests):
        dest = dest_ref[r, here]
        limit = jnp.where(row_request == r, count_ref[r, here], limit)
        place = jnp.int32(residents)
        for s in range(insts):
            for c in range(requests):
                place += jnp.where((dest_ref[c, s] == dest) & (here > s), 1, 0).astype(jnp.int32)
        for b in range(1, insts):

            @pl.when(here ^ b == dest)
            def _():
                ask = asks[b - 1][...].astype(F32)
                ask_ref[r : r + 1, :] = jnp.sum(
                    jnp.where(ask_row == place, ask, 0.0), axis=0, keepdims=True
                )

        at = slice(r * heads_mine, (r + 1) * heads_mine)
        q_ref[at, :], own_ref[0, at, :], own_ref[1, at, :] = heads_of(
            ask_ref[r : r + 1, :], heads_mine, kv_mine
        )
    places = jnp.full(place_out.shape, -1, jnp.int32)
    row = iota(place_out.shape, 0)
    place = jnp.int32(residents)
    for s in range(insts):
        for c in range(requests):
            mine = dest_ref[c, s] == here
            places = jnp.where((row == (here ^ s) * requests + c) & mine, place, places)
            place += jnp.where(mine, 1, 0).astype(jnp.int32)
    place_out[...] = places

    blocks = tokens // 128
    last = tokens + 2 * blocks
    tail = pieces[0][tokens:last, :128].astype(F32)
    for t in range(1, ranks):
        tail = tail + pieces[t][tokens:last, :128].astype(F32)
    squares = tail[:blocks] + tail[blocks:]
    squares = jnp.concatenate(
        [row_to_column(squares[b : b + 1], 128) for b in range(blocks)], axis=0
    )
    token_scale = lax.rsqrt(squares / features + EPS)

    def column_block(c):
        total = pieces[0][:tokens, c : c + 128].astype(F32)
        for t in range(1, ranks):
            total = total + pieces[t][:tokens, c : c + 128].astype(F32)
        return total * token_scale

    gain = gain_ref[...].astype(F32)
    q = q_ref[...]
    q16 = q.astype(BF16)
    which = iota((rows, tokens), 0) % heads_mine // (heads_mine // kv_mine)
    scores = None
    for h in range(kv_mine):
        key = column_block(h * 128)
        key = key * lax.rsqrt(jnp.mean(key * key, axis=1, keepdims=True) + EPS) * gain
        key = key * cos_ref[...] + pltpu.roll(key, 64, 1) * sin_ref[...]
        part = lax.dot_general(
            q16, key.astype(BF16), (((1,), (1,)), ((), ())), preferred_element_type=F32
        )
        scores = part if scores is None else jnp.where(which == h, part, scores)
    token = iota((rows, tokens), 1)
    valid = (token % requests == row_request) & (token // requests < limit)
    scores = jnp.where(valid, scores * scale, ABSENT)
    own_score = jnp.sum(q * own_ref[0], axis=1, keepdims=True) * scale
    top = jnp.maximum(jnp.max(scores, axis=1, keepdims=True), own_score)
    weights = jnp.where(valid, jnp.exp(scores - top), 0.0)
    own_weight = jnp.exp(own_score - top)
    total = jnp.sum(weights, axis=1, keepdims=True) + own_weight
    weights = weights.astype(BF16)
    summed = None
    for h in range(kv_mine):
        value = column_block(piece + h * 128).astype(BF16)
        part = jnp.dot(weights, value, preferred_element_type=F32)
        summed = part if summed is None else jnp.where(which[:, :128] == h, part, summed)
    summed = summed + own_weight.astype(BF16).astype(F32) * own_ref[1]
    result = summed / total
    for r in range(requests):
        for h in range(heads_mine):
            at = r * heads_mine + h
            line_ref[r : r + 1, h * 128 : (h + 1) * 128] = result[at : at + 1, :]
    out_ref[...] = line_ref[...].astype(BF16)


def attend_moved(dest, count, k_gain, cos, sin, asks, pieces, residents, heads_mine, features):
    requests, insts = dest.shape
    rows = requests * heads_mine
    return pl.pallas_call(
        functools.partial(moved_kernel, insts, len(pieces), residents, features),
        in_specs=[SMEM] * 2 + [VMEM] * (3 + len(asks) + len(pieces)),
        out_specs=[VMEM] * 2,
        out_shape=[
            jax.ShapeDtypeStruct((requests, heads_mine * 128), BF16),
            jax.ShapeDtypeStruct((insts * requests, 128), jnp.int32),
        ],
        scratch_shapes=[
            pltpu.VMEM((requests, asks[0].shape[1]), F32),
            pltpu.VMEM((rows, 128), F32),
            pltpu.VMEM((2, rows, 128), F32),
            pltpu.VMEM((requests, heads_mine * 128), F32),
        ],
        compiler_params=pltpu.CompilerParams(vmem_limit_bytes=16 * MIB),
        name="attend_moved",
    )(dest, count, k_gain, cos, sin, *asks, *pieces)


def combine_kernel(residents, kv_mine, ask_ref, payload_ref, out_ref):
    heads_mine = out_ref.shape[1] // 128
    scale = F32(1.0) / jnp.sqrt(F32(128.0))
    payloads = [payload_ref[t].astype(F32) for t in range(payload_ref.shape[0])]
    at = residents * heads_mine
    ask = ask_ref[...].astype(F32)
    for r in range(residents):
        q, own_k, own_v = heads_of(ask[r : r + 1], heads_mine, kv_mine)
        own_score = jnp.sum(q * own_k, axis=1, keepdims=True) * scale
        peaks, totals = [], []
        for payload in payloads:
            stat = payload[at : at + 3 * residents]
            peaks.append(row_to_column(stat[r : r + 1], heads_mine))
            total = stat[residents + r : residents + r + 1]
            total = total + stat[2 * residents + r : 2 * residents + r + 1]
            totals.append(row_to_column(total, heads_mine))
        top = own_score
        for peak in peaks:
            top = jnp.maximum(top, peak)
        own_weight = jnp.exp(own_score - top)
        denom = own_weight
        numer = own_weight.astype(BF16).astype(F32) * own_v
        for peak, total, payload in zip(peaks, totals, payloads):
            keep = jnp.exp(peak - top)
            denom = denom + keep * total
            numer = numer + keep * payload[r * heads_mine : (r + 1) * heads_mine]
        result = numer / denom
        for h in range(heads_mine):
            out_ref[r : r + 1, h * 128 : (h + 1) * 128] = result[h : h + 1, :]


def combine_resident(ask, payloads, residents, heads_mine, kv_mine):
    return pl.pallas_call(
        functools.partial(combine_kernel, residents, kv_mine),
        in_specs=[VMEM] * 2,
        out_specs=VMEM,
        out_shape=jax.ShapeDtypeStruct((residents, heads_mine * 128), F32),
        compiler_params=pltpu.CompilerParams(vmem_limit_bytes=8 * MIB),
        name="combine_resident",
    )(ask, payloads)


def finish_kernel(kept_ref, place_ref, *rest):
    moved, out_ref = rest[:-1], rest[-1]
    residents = kept_ref.shape[0]
    decoded, width = out_ref.shape
    requests = decoded - residents
    row = iota((decoded, 128), 0)
    arrived = [ref[...].astype(F32) for ref in moved]
    for c in range(0, width, 128):
        kept = kept_ref[:, c : c + 128]
        line = jnp.concatenate([kept, jnp.zeros((requests, 128), F32)], axis=0)
        for b in range(len(moved)):
            for i in range(requests):
                at = (b + 1) * requests + i
                line = jnp.where(
                    place_ref[at : at + 1, :] == row, arrived[b][i : i + 1, c : c + 128], line
                )
        out_ref[:, c : c + 128] = line.astype(BF16)


def finish(kept, places, moved, requests):
    residents, width = kept.shape
    return pl.pallas_call(
        finish_kernel,
        in_specs=[VMEM] * (2 + len(moved)),
        out_specs=VMEM,
        out_shape=jax.ShapeDtypeStruct((residents + requests, width), BF16),
        compiler_params=pltpu.CompilerParams(vmem_limit_bytes=8 * MIB),
        name="finish",
    )(kept, places, *moved)


def swapped(x, axis, j, n):
    return lax.ppermute(x, axis, [(i, i ^ j) for i in range(n)])


def rotation(slots, requests, head_size):
    half = head_size // 2
    freq = THETA ** (-np.arange(half) * 2.0 / head_size)
    angle = np.repeat(np.arange(slots), requests)[:, None] * freq[None, :]
    cos, sin = np.cos(angle), np.sin(angle)
    return (
        np.concatenate([cos, cos], axis=1).astype(np.float32),
        np.concatenate([-sin, sin], axis=1).astype(np.float32),
    )


def per_device(
    mig_hidden,
    mig_dest,
    mig_count,
    attn_gain,
    kv_weight,
    k_gain,
    query,
    new_kv,
    k_cache,
    v_cache,
    lengths,
):
    insts = lax.axis_size("inst")
    ranks = lax.axis_size("tp")
    head_size = k_gain.shape[0]
    slots, requests, feats = mig_hidden.shape[1:]
    residents = k_cache.shape[1]
    heads = query.shape[2] // head_size
    kv_heads = kv_weight.shape[1] // 2 // head_size
    heads_mine = heads // ranks
    group = heads // kv_heads
    kv_mine = max(1, heads_mine // group)

    pieces, ask = project(
        mig_hidden[0], attn_gain, kv_weight, query[0], new_kv[0], ranks, group, kv_mine
    )
    order = sorted(range(1, ranks), key=lambda j: (j == 1, abs(j - ranks // 2), j))
    sent = {j: swapped(pieces[j], "tp", j, ranks) for j in order}
    pieces = [pieces[0]] + [sent[j] for j in order]
    asks = [swapped(ask, "inst", b, insts) for b in range(1, insts)]
    queries = jnp.transpose(query[0].reshape(query.shape[1], heads, head_size), (1, 0, 2))
    payloads = attend_resident(lengths, queries, k_cache[0], v_cache[0], ranks)
    asks, payloads = lax.optimization_barrier((asks, payloads))
    received = lax.all_to_all(payloads, "tp", 0, 0, tiled=True)
    cos, sin = rotation(slots, requests, head_size)
    moved, places = attend_moved(
        mig_dest.T,
        mig_count.T,
        k_gain.reshape(1, head_size),
        cos,
        sin,
        asks,
        pieces,
        residents,
        heads_mine,
        feats * ranks,
    )
    kept = combine_resident(ask, received, residents, heads_mine, kv_mine)
    moved = [swapped(moved, "inst", b, insts) for b in reversed(range(1, insts))][::-1]
    return finish(kept, places, moved, requests)[None]


def solution(mesh):
    placed = (
        P(("group", "inst"), None, None, "tp"),
        P("group", None),
        P("group", None),
        P("tp"),
        P("tp", None),
        P(),
        P(("group", "inst"), None, None),
        P(("group", "inst"), None, None),
        P(("group", "inst"), None, "tp", None),
        P(("group", "inst"), None, "tp", None),
        P(("group", "inst"), None),
    )
    return jax.shard_map(
        per_device,
        mesh=mesh,
        in_specs=placed,
        out_specs=P(("group", "inst"), None, "tp"),
        check_vma=False,
    )
```

```python
import functools

import jax
import jax.numpy as jnp
import numpy as np
from jax import lax
from jax.experimental import pallas as pl
from jax.experimental.pallas import tpu as pltpu
from jax.sharding import PartitionSpec as P

EPS = 1e-06
THETA = 1000000.0
ABSENT = -1e30
F32 = jnp.float32
BF16 = jnp.bfloat16
MIB = 1024 * 1024
CHUNK = 512

VMEM = pl.BlockSpec(memory_space=pltpu.VMEM)
SMEM = pl.BlockSpec(memory_space=pltpu.SMEM)
HBM = pl.BlockSpec(memory_space=pltpu.HBM)


def iota(shape, dim):
    return lax.broadcasted_iota(jnp.int32, shape, dim)


def column_to_row(column, period):
    n = column.shape[0]
    spread = jnp.where(iota((n, 128), 0) % period == iota((n, 128), 1), column, 0.0)
    return jnp.sum(spread.reshape(n // period, period, 128), axis=1)


def row_to_column(row, n):
    return jnp.sum(
        jnp.where(iota((n, 128), 0) == iota((n, 128), 1), row, 0.0), axis=1, keepdims=True
    )


def split_bf16(x):
    high = x.astype(BF16)
    return high, (x - high.astype(F32)).astype(BF16)


def project_kernel(ranks, group, gain_hbm, x_hbm, w_hbm, q_hbm, own_hbm, *rest):
    outs, ask_ref = rest[:ranks], rest[ranks]
    gain_ref, x_ref, w_ref, acc_ref, in_sems, w_sems = rest[ranks + 1 :]
    slots, requests, feats = x_ref.shape
    rows = slots * requests
    piece = outs[0].shape[1] // 2
    kv_width = w_hbm.shape[1] // 2
    heads_mine = kv_width // 128 * group // ranks
    rank = lax.axis_index("tp")

    def first_column(target):
        return pl.multiple_of(target * heads_mine // group * 128, 128)

    gain_copy = pltpu.make_async_copy(gain_hbm, gain_ref, in_sems.at[0])
    gain_copy.start()
    x_copy = pltpu.make_async_copy(x_hbm, x_ref, in_sems.at[1])
    x_copy.start()
    cuts = list(range(0, feats, CHUNK)) + [feats]
    chunks = list(zip(cuts[:-1], cuts[1:]))
    copies = []
    for i, (low, high) in enumerate(chunks):
        copies.append(
            pltpu.make_async_copy(w_hbm.at[low:high, :], w_ref.at[low:high, :], w_sems.at[i])
        )
        copies[-1].start()
    mine = heads_mine * 128
    q_first = pl.multiple_of(rank * mine, 128)
    asking = [
        pltpu.make_async_copy(
            q_hbm.at[:, pl.ds(q_first, mine)], ask_ref.at[:, :mine], in_sems.at[2]
        )
    ]
    for i in range(2):
        asking.append(
            pltpu.make_async_copy(
                own_hbm.at[:, pl.ds(i * kv_width + first_column(rank), piece)],
                ask_ref.at[:, mine + i * piece : mine + (i + 1) * piece],
                in_sems.at[3 + i],
            )
        )
    for copy in asking:
        copy.start()
    gain_copy.wait()
    x_copy.wait()
    squares = jnp.zeros((rows, 128), F32)
    for i, (low, high) in enumerate(chunks):
        parts = []
        for c in range(low, high, 128):
            width = min(128, high - c)
            x = x_ref[:, :, c : c + width].astype(F32).reshape(rows, width)
            gain = gain_ref[c : c + width].astype(F32).reshape(1, width)
            parts.append((x * gain).astype(BF16))
            x = x * x
            if width < 128:
                x = jnp.concatenate([x, jnp.zeros((rows, 128 - width), F32)], axis=1)
            squares = squares + x
        xg = parts[0] if len(parts) == 1 else jnp.concatenate(parts, axis=1)
        copies[i].wait()
        for n in range(0, 2 * kv_width, 512):
            part = jnp.dot(xg, w_ref[low:high, n : n + 512], preferred_element_type=F32)
            if i == 0:
                acc_ref[:, n : n + 512] = part
            else:
                acc_ref[:, n : n + 512] += part
    sq = column_to_row(jnp.sum(squares, axis=1, keepdims=True), 128)
    high, low = split_bf16(sq)
    tail = jnp.concatenate([high.astype(F32), low.astype(F32)], axis=0)
    fill = outs[1].shape[0] - rows - tail.shape[0]
    if fill:
        tail = jnp.concatenate([tail, jnp.zeros((fill, 128), F32)], axis=0)
    extra = jnp.concatenate([tail.astype(BF16)] * (2 * piece // 128), axis=1)
    for j in range(ranks):
        first = first_column(rank ^ j)
        outs[j][:rows, :piece] = acc_ref[:, pl.ds(first, piece)].astype(BF16)
        outs[j][:rows, piece:] = acc_ref[:, pl.ds(kv_width + first, piece)].astype(BF16)
        outs[j][rows:, :] = extra
    for copy in asking:
        copy.wait()


def project(x, gain, weight, query, own, ranks, group, kv_mine):
    slots, requests, feats = x.shape
    rows = slots * requests
    piece = kv_mine * 128
    extra = -(-2 * (rows // 128) // 8) * 8
    decoded, q_width = query.shape
    outs = pl.pallas_call(
        functools.partial(project_kernel, ranks, group),
        in_specs=[HBM] * 5,
        out_specs=[VMEM] * (ranks + 1),
        out_shape=[jax.ShapeDtypeStruct((rows + extra, 2 * piece), BF16)] * ranks
        + [jax.ShapeDtypeStruct((decoded, q_width // ranks + 2 * piece), BF16)],
        scratch_shapes=[
            pltpu.VMEM((feats,), BF16),
            pltpu.VMEM((slots, requests, feats), BF16),
            pltpu.VMEM(weight.shape, BF16),
            pltpu.VMEM((rows, weight.shape[1]), F32),
            pltpu.SemaphoreType.DMA((5,)),
            pltpu.SemaphoreType.DMA((-(-feats // CHUNK),)),
        ],
        compiler_params=pltpu.CompilerParams(vmem_limit_bytes=56 * MIB),
        cost_estimate=pl.CostEstimate(
            flops=2 * rows * feats * weight.shape[1],
            bytes_accessed=2 * feats * weight.shape[1],
            transcendentals=0,
        ),
        name="project",
    )(gain, x, weight, query, own)
    return outs[:ranks], outs[ranks]


def resident_kernel(ranks, len_ref, q_ref, k_hbm, v_hbm, *rest):
    outs, rest = rest[:ranks], rest[ranks:]
    q_wide, q_all, k_buf, v_buf, o_all, m_all, l_all, s_all, sems = rest
    residents, positions, width = k_buf.shape
    copies = []
    for r in range(residents):
        copies.append(
            (
                pltpu.make_async_copy(k_hbm.at[r], k_buf.at[r], sems.at[0, r]),
                pltpu.make_async_copy(v_hbm.at[r], v_buf.at[r], sems.at[1, r]),
            )
        )
    rank = lax.axis_index("tp")
    held = [(rank == 0) | (len_ref[0, r] > rank * positions) for r in range(residents)]
    for r in range(residents):

        @pl.when(held[r])
        def _():
            for copy in copies[r]:
                copy.start()

    heads = q_ref.shape[0]
    kv_heads = width // 128
    group = heads // kv_heads
    pair_rows = 2 * group
    heads_mine = heads // ranks
    top_half = iota((pair_rows, 128), 0) < group
    position = rank * positions + iota((pair_rows, positions), 1)
    scale = F32(1.0) / jnp.sqrt(F32(128.0))
    diagonal = iota((heads, 128), 0) % heads_mine == iota((heads, 128), 1)

    def to_rows(column):
        spread = jnp.where(diagonal, column, 0.0)
        return jnp.sum(spread.reshape(ranks, heads_mine, 128), axis=1)

    q_wide[...] = q_ref[...].astype(F32)
    for r in range(residents):
        q_all[r] = q_wide[:, r, :].astype(BF16)
    def attend(r):
        valid = position < len_ref[0, r]
        copies[r][0].wait()
        weights = []
        for p in range(kv_heads // 2):
            rows = slice(p * pair_rows, (p + 1) * pair_rows)
            q = q_all[r, rows, :]
            zero = jnp.zeros_like(q)
            lhs = jnp.concatenate(
                [jnp.where(top_half, q, zero), jnp.where(top_half, zero, q)], axis=1
            )
            scores = lax.dot_general(
                lhs,
                k_buf[r, :, p * 256 : (p + 1) * 256],
                (((1,), (1,)), ((), ())),
                preferred_element_type=F32,
            )
            scores = jnp.where(valid, scores * scale, ABSENT)
            peak = jnp.max(scores, axis=1, keepdims=True).astype(BF16).astype(F32)
            weight = jnp.where(valid, jnp.exp(scores - peak), 0.0)
            m_all[r, rows, :] = peak
            l_all[r, rows, :] = jnp.sum(weight, axis=1, keepdims=True)
            weights.append(weight.astype(BF16))
        copies[r][1].wait()
        for p in range(kv_heads // 2):
            both = jnp.dot(
                weights[p], v_buf[r, :, p * 256 : (p + 1) * 256], preferred_element_type=F32
            )
            o_all[r, p * pair_rows : (p + 1) * pair_rows, :] = jnp.where(
                top_half, both[:, :128], both[:, 128:]
            )

    for r in range(residents):
        pl.when(held[r])(functools.partial(attend, r))

        @pl.when(jnp.logical_not(held[r]))
        def _():
            o_all[r] = jnp.zeros((heads, 128), F32)
            m_all[r] = jnp.full((heads, 1), ABSENT, F32)
            l_all[r] = jnp.zeros((heads, 1), F32)

    for r in range(residents):
        s_all[r, 0] = to_rows(m_all[r])
        high, low = split_bf16(to_rows(l_all[r]))
        s_all[r, 1] = high.astype(F32)
        s_all[r, 2] = low.astype(F32)
    filled = residents * (heads_mine + 3)
    for j in range(ranks):
        target = rank ^ j
        first = pl.multiple_of(target * heads_mine, heads_mine)
        parts = [o_all[r, pl.ds(first, heads_mine), :] for r in range(residents)]
        parts += [s_all[r, i, pl.ds(target, 1), :] for i in range(3) for r in range(residents)]
        if outs[j].shape[0] > filled:
            parts.append(jnp.zeros((outs[j].shape[0] - filled, 128), F32))
        outs[j][...] = jnp.concatenate(parts, axis=0).astype(BF16)


def attend_resident(lengths, queries, k_cache, v_cache, ranks):
    residents, positions, width = k_cache.shape
    heads = queries.shape[0]
    heads_mine = heads // ranks
    rows = -(-(residents * (heads_mine + 3)) // 16) * 16
    return pl.pallas_call(
        functools.partial(resident_kernel, ranks),
        in_specs=[SMEM, VMEM, HBM, HBM],
        out_specs=[VMEM] * ranks,
        out_shape=[jax.ShapeDtypeStruct((rows, 128), BF16)] * ranks,
        scratch_shapes=[
            pltpu.VMEM(queries.shape, F32),
            pltpu.VMEM((residents, heads, 128), BF16),
            pltpu.VMEM((residents, positions, width), BF16),
            pltpu.VMEM((residents, positions, width), BF16),
            pltpu.VMEM((residents, heads, 128), F32),
            pltpu.VMEM((residents, heads, 1), F32),
            pltpu.VMEM((residents, heads, 1), F32),
            pltpu.VMEM((residents, 3, ranks, 128), F32),
            pltpu.SemaphoreType.DMA((2, residents)),
        ],
        compiler_params=pltpu.CompilerParams(vmem_limit_bytes=56 * MIB),
        cost_estimate=pl.CostEstimate(
            flops=4 * residents * heads * positions * 128,
            bytes_accessed=4 * residents * positions * width,
            transcendentals=residents * heads * positions,
        ),
        name="attend_resident",
    )(lengths, queries, k_cache, v_cache)


def expand(own, rows):
    which = iota((rows, 128), 0) // (rows // own.shape[0])
    out = jnp.broadcast_to(own[0:1], (rows, 128))
    for h in range(1, own.shape[0]):
        out = jnp.where(which == h, own[h : h + 1], out)
    return out


def heads_of(line, heads_mine, kv_mine):
    per = heads_mine // kv_mine
    blocks = [line[:, c : c + 128] for c in range(0, line.shape[1], 128)]
    q = jnp.concatenate(blocks[:heads_mine], axis=0)
    k = blocks[heads_mine : heads_mine + kv_mine]
    v = blocks[heads_mine + kv_mine :]
    return (
        q,
        expand(jnp.concatenate(k, axis=0), heads_mine),
        expand(jnp.concatenate(v, axis=0), heads_mine),
    )


def moved_kernel(
    insts, ranks, residents, features, dest_ref, count_ref, gain_ref, cos_ref, sin_ref, *rest
):
    asks, rest = rest[: insts - 1], rest[insts - 1 :]
    pieces, rest = rest[:ranks], rest[ranks:]
    out_ref, place_out, ask_ref, q_ref, own_ref, line_ref = rest
    requests = out_ref.shape[0]
    tokens = cos_ref.shape[0]
    piece = pieces[0].shape[1] // 2
    kv_mine = piece // 128
    rows = q_ref.shape[0]
    heads_mine = rows // requests
    scale = F32(1.0) / jnp.sqrt(F32(128.0))
    here = lax.axis_index("inst")

    ask_row = iota(asks[0].shape, 0)
    row_request = iota((rows, tokens), 0) // heads_mine
    limit = jnp.zeros((rows, tokens), jnp.int32)
    for r in range(requests):
        dest = dest_ref[r, here]
        limit = jnp.where(row_request == r, count_ref[r, here], limit)
        place = jnp.int32(residents)
        for s in range(insts):
            for c in range(requests):
                place += jnp.where((dest_ref[c, s] == dest) & (here > s), 1, 0).astype(jnp.int32)
        for b in range(1, insts):

            @pl.when(here ^ b == dest)
            def _():
                ask = asks[b - 1][...].astype(F32)
                ask_ref[r : r + 1, :] = jnp.sum(
                    jnp.where(ask_row == place, ask, 0.0), axis=0, keepdims=True
                )

        at = slice(r * heads_mine, (r + 1) * heads_mine)
        q_ref[at, :], own_ref[0, at, :], own_ref[1, at, :] = heads_of(
            ask_ref[r : r + 1, :], heads_mine, kv_mine
        )
    places = jnp.full(place_out.shape, -1, jnp.int32)
    row = iota(place_out.shape, 0)
    place = jnp.int32(residents)
    for s in range(insts):
        for c in range(requests):
            mine = dest_ref[c, s] == here
            places = jnp.where((row == (here ^ s) * requests + c) & mine, place, places)
            place += jnp.where(mine, 1, 0).astype(jnp.int32)
    place_out[...] = places

    blocks = tokens // 128
    last = tokens + 2 * blocks
    tail = pieces[0][tokens:last, :128].astype(F32)
    for t in range(1, ranks):
        tail = tail + pieces[t][tokens:last, :128].astype(F32)
    squares = tail[:blocks] + tail[blocks:]
    squares = jnp.concatenate(
        [row_to_column(squares[b : b + 1], 128) for b in range(blocks)], axis=0
    )
    token_scale = lax.rsqrt(squares / features + EPS)

    def column_block(c):
        total = pieces[0][:tokens, c : c + 128].astype(F32)
        for t in range(1, ranks):
            total = total + pieces[t][:tokens, c : c + 128].astype(F32)
        return total * token_scale

    gain = gain_ref[...].astype(F32)
    q = q_ref[...]
    q16 = q.astype(BF16)
    which = iota((rows, tokens), 0) % heads_mine // (heads_mine // kv_mine)
    scores = None
    for h in range(kv_mine):
        key = column_block(h * 128)
        key = key * lax.rsqrt(jnp.mean(key * key, axis=1, keepdims=True) + EPS) * gain
        key = key * cos_ref[...] + pltpu.roll(key, 64, 1) * sin_ref[...]
        part = lax.dot_general(
            q16, key.astype(BF16), (((1,), (1,)), ((), ())), preferred_element_type=F32
        )
        scores = part if scores is None else jnp.where(which == h, part, scores)
    token = iota((rows, tokens), 1)
    valid = (token % requests == row_request) & (token // requests < limit)
    scores = jnp.where(valid, scores * scale, ABSENT)
    own_score = jnp.sum(q * own_ref[0], axis=1, keepdims=True) * scale
    top = jnp.maximum(jnp.max(scores, axis=1, keepdims=True), own_score)
    weights = jnp.where(valid, jnp.exp(scores - top), 0.0)
    own_weight = jnp.exp(own_score - top)
    total = jnp.sum(weights, axis=1, keepdims=True) + own_weight
    weights = weights.astype(BF16)
    summed = None
    for h in range(kv_mine):
        value = column_block(piece + h * 128).astype(BF16)
        part = jnp.dot(weights, value, preferred_element_type=F32)
        summed = part if summed is None else jnp.where(which[:, :128] == h, part, summed)
    summed = summed + own_weight.astype(BF16).astype(F32) * own_ref[1]
    result = summed / total
    for r in range(requests):
        for h in range(heads_mine):
            at = r * heads_mine + h
            line_ref[r : r + 1, h * 128 : (h + 1) * 128] = result[at : at + 1, :]
    out_ref[...] = line_ref[...].astype(BF16)


def attend_moved(dest, count, k_gain, cos, sin, asks, pieces, residents, heads_mine, features):
    requests, insts = dest.shape
    rows = requests * heads_mine
    return pl.pallas_call(
        functools.partial(moved_kernel, insts, len(pieces), residents, features),
        in_specs=[SMEM] * 2 + [VMEM] * (3 + len(asks) + len(pieces)),
        out_specs=[VMEM] * 2,
        out_shape=[
            jax.ShapeDtypeStruct((requests, heads_mine * 128), BF16),
            jax.ShapeDtypeStruct((insts * requests, 128), jnp.int32),
        ],
        scratch_shapes=[
            pltpu.VMEM((requests, asks[0].shape[1]), F32),
            pltpu.VMEM((rows, 128), F32),
            pltpu.VMEM((2, rows, 128), F32),
            pltpu.VMEM((requests, heads_mine * 128), F32),
        ],
        compiler_params=pltpu.CompilerParams(vmem_limit_bytes=16 * MIB),
        name="attend_moved",
    )(dest, count, k_gain, cos, sin, *asks, *pieces)


def combine_kernel(residents, kv_mine, ask_ref, *rest):
    refs, out_ref = rest[:-1], rest[-1]
    heads_mine = out_ref.shape[1] // 128
    scale = F32(1.0) / jnp.sqrt(F32(128.0))
    payloads = [ref[...].astype(F32) for ref in refs]
    at = residents * heads_mine
    ask = ask_ref[...].astype(F32)
    for r in range(residents):
        q, own_k, own_v = heads_of(ask[r : r + 1], heads_mine, kv_mine)
        own_score = jnp.sum(q * own_k, axis=1, keepdims=True) * scale
        peaks, totals = [], []
        for payload in payloads:
            stat = payload[at : at + 3 * residents]
            peaks.append(row_to_column(stat[r : r + 1], heads_mine))
            total = stat[residents + r : residents + r + 1]
            total = total + stat[2 * residents + r : 2 * residents + r + 1]
            totals.append(row_to_column(total, heads_mine))
        top = own_score
        for peak in peaks:
            top = jnp.maximum(top, peak)
        own_weight = jnp.exp(own_score - top)
        denom = own_weight
        numer = own_weight.astype(BF16).astype(F32) * own_v
        for peak, total, payload in zip(peaks, totals, payloads):
            keep = jnp.exp(peak - top)
            denom = denom + keep * total
            numer = numer + keep * payload[r * heads_mine : (r + 1) * heads_mine]
        result = numer / denom
        for h in range(heads_mine):
            out_ref[r : r + 1, h * 128 : (h + 1) * 128] = result[h : h + 1, :]


def combine_resident(ask, payloads, residents, heads_mine, kv_mine):
    return pl.pallas_call(
        functools.partial(combine_kernel, residents, kv_mine),
        in_specs=[VMEM] * (1 + len(payloads)),
        out_specs=VMEM,
        out_shape=jax.ShapeDtypeStruct((residents, heads_mine * 128), F32),
        compiler_params=pltpu.CompilerParams(vmem_limit_bytes=8 * MIB),
        name="combine_resident",
    )(ask, *payloads)


def finish_kernel(kept_ref, place_ref, *rest):
    moved, out_ref = rest[:-1], rest[-1]
    residents = kept_ref.shape[0]
    decoded, width = out_ref.shape
    requests = decoded - residents
    row = iota((decoded, 128), 0)
    arrived = [ref[...].astype(F32) for ref in moved]
    for c in range(0, width, 128):
        kept = kept_ref[:, c : c + 128]
        line = jnp.concatenate([kept, jnp.zeros((requests, 128), F32)], axis=0)
        for b in range(len(moved)):
            for i in range(requests):
                at = (b + 1) * requests + i
                line = jnp.where(
                    place_ref[at : at + 1, :] == row, arrived[b][i : i + 1, c : c + 128], line
                )
        out_ref[:, c : c + 128] = line.astype(BF16)


def finish(kept, places, moved, requests):
    residents, width = kept.shape
    return pl.pallas_call(
        finish_kernel,
        in_specs=[VMEM] * (2 + len(moved)),
        out_specs=VMEM,
        out_shape=jax.ShapeDtypeStruct((residents + requests, width), BF16),
        compiler_params=pltpu.CompilerParams(vmem_limit_bytes=8 * MIB),
        name="finish",
    )(kept, places, *moved)


def swapped(x, axis, j, n):
    return lax.ppermute(x, axis, [(i, i ^ j) for i in range(n)])


def rotation(slots, requests, head_size):
    half = head_size // 2
    freq = THETA ** (-np.arange(half) * 2.0 / head_size)
    angle = np.repeat(np.arange(slots), requests)[:, None] * freq[None, :]
    cos, sin = np.cos(angle), np.sin(angle)
    return (
        np.concatenate([cos, cos], axis=1).astype(np.float32),
        np.concatenate([-sin, sin], axis=1).astype(np.float32),
    )


def per_device(
    mig_hidden,
    mig_dest,
    mig_count,
    attn_gain,
    kv_weight,
    k_gain,
    query,
    new_kv,
    k_cache,
    v_cache,
    lengths,
):
    insts = lax.axis_size("inst")
    ranks = lax.axis_size("tp")
    head_size = k_gain.shape[0]
    slots, requests, feats = mig_hidden.shape[1:]
    residents = k_cache.shape[1]
    heads = query.shape[2] // head_size
    kv_heads = kv_weight.shape[1] // 2 // head_size
    heads_mine = heads // ranks
    group = heads // kv_heads
    kv_mine = max(1, heads_mine // group)

    pieces, ask = project(
        mig_hidden[0], attn_gain, kv_weight, query[0], new_kv[0], ranks, group, kv_mine
    )
    order = sorted(range(1, ranks), key=lambda j: (j == 1, abs(j - ranks // 2), j))
    sent = {j: swapped(pieces[j], "tp", j, ranks) for j in order}
    pieces = [pieces[0]] + [sent[j] for j in order]
    asks = [swapped(ask, "inst", b, insts) for b in range(1, insts)]
    queries = jnp.transpose(query[0].reshape(query.shape[1], heads, head_size), (1, 0, 2))
    payloads = attend_resident(lengths, queries, k_cache[0], v_cache[0], ranks)
    asks, payloads = lax.optimization_barrier((asks, payloads))
    order = sorted(range(1, ranks), key=lambda j: (j > 1, -j))
    received = [payloads[0]] + [swapped(payloads[j], "tp", j, ranks) for j in order]
    cos, sin = rotation(slots, requests, head_size)
    moved, places = attend_moved(
        mig_dest.T,
        mig_count.T,
        k_gain.reshape(1, head_size),
        cos,
        sin,
        asks,
        pieces,
        residents,
        heads_mine,
        feats * ranks,
    )
    kept = combine_resident(ask, received, residents, heads_mine, kv_mine)
    moved = [swapped(moved, "inst", b, insts) for b in reversed(range(1, insts))][::-1]
    return finish(kept, places, moved, requests)[None]


def solution(mesh):
    placed = (
        P(("group", "inst"), None, None, "tp"),
        P("group", None),
        P("group", None),
        P("tp"),
        P("tp", None),
        P(),
        P(("group", "inst"), None, None),
        P(("group", "inst"), None, None),
        P(("group", "inst"), None, "tp", None),
        P(("group", "inst"), None, "tp", None),
        P(("group", "inst"), None),
    )
    return jax.shard_map(
        per_device,
        mesh=mesh,
        in_specs=placed,
        out_specs=P(("group", "inst"), None, "tp"),
        check_vma=False,
    )
```

```python
import functools

import jax
import jax.numpy as jnp
import numpy as np
from jax import lax
from jax.experimental import pallas as pl
from jax.experimental.pallas import tpu as pltpu
from jax.sharding import PartitionSpec as P

EPS = 1e-06
THETA = 1000000.0
ABSENT = -1e30
F32 = jnp.float32
BF16 = jnp.bfloat16
MIB = 1024 * 1024
CHUNK = 512

VMEM = pl.BlockSpec(memory_space=pltpu.VMEM)
SMEM = pl.BlockSpec(memory_space=pltpu.SMEM)
HBM = pl.BlockSpec(memory_space=pltpu.HBM)


def iota(shape, dim):
    return lax.broadcasted_iota(jnp.int32, shape, dim)


def column_to_row(column, period):
    n = column.shape[0]
    spread = jnp.where(iota((n, 128), 0) % period == iota((n, 128), 1), column, 0.0)
    return jnp.sum(spread.reshape(n // period, period, 128), axis=1)


def row_to_column(row, n):
    return jnp.sum(
        jnp.where(iota((n, 128), 0) == iota((n, 128), 1), row, 0.0), axis=1, keepdims=True
    )


def split_bf16(x):
    high = x.astype(BF16)
    return high, (x - high.astype(F32)).astype(BF16)


def project_kernel(ranks, group, gain_hbm, x_hbm, w_hbm, q_hbm, own_hbm, *rest):
    outs, ask_ref = rest[:ranks], rest[ranks]
    gain_ref, x_ref, w_ref, acc_ref, in_sems, w_sems = rest[ranks + 1 :]
    slots, requests, feats = x_ref.shape
    rows = slots * requests
    piece = outs[0].shape[1] // 2
    kv_width = w_hbm.shape[1] // 2
    heads_mine = kv_width // 128 * group // ranks
    rank = lax.axis_index("tp")

    def first_column(target):
        return pl.multiple_of(target * heads_mine // group * 128, 128)

    gain_copy = pltpu.make_async_copy(gain_hbm, gain_ref, in_sems.at[0])
    gain_copy.start()
    x_copy = pltpu.make_async_copy(x_hbm, x_ref, in_sems.at[1])
    x_copy.start()
    cuts = list(range(0, feats, CHUNK)) + [feats]
    chunks = list(zip(cuts[:-1], cuts[1:]))
    copies = []
    for i, (low, high) in enumerate(chunks):
        copies.append(
            pltpu.make_async_copy(w_hbm.at[low:high, :], w_ref.at[low:high, :], w_sems.at[i])
        )
        copies[-1].start()
    mine = heads_mine * 128
    q_first = pl.multiple_of(rank * mine, 128)
    asking = [
        pltpu.make_async_copy(
            q_hbm.at[:, pl.ds(q_first, mine)], ask_ref.at[:, :mine], in_sems.at[2]
        )
    ]
    for i in range(2):
        asking.append(
            pltpu.make_async_copy(
                own_hbm.at[:, pl.ds(i * kv_width + first_column(rank), piece)],
                ask_ref.at[:, mine + i * piece : mine + (i + 1) * piece],
                in_sems.at[3 + i],
            )
        )
    for copy in asking:
        copy.start()
    gain_copy.wait()
    x_copy.wait()
    squares = jnp.zeros((rows, 128), F32)
    for i, (low, high) in enumerate(chunks):
        parts = []
        for c in range(low, high, 128):
            width = min(128, high - c)
            x = x_ref[:, :, c : c + width].astype(F32).reshape(rows, width)
            gain = gain_ref[c : c + width].astype(F32).reshape(1, width)
            parts.append((x * gain).astype(BF16))
            x = x * x
            if width < 128:
                x = jnp.concatenate([x, jnp.zeros((rows, 128 - width), F32)], axis=1)
            squares = squares + x
        xg = parts[0] if len(parts) == 1 else jnp.concatenate(parts, axis=1)
        copies[i].wait()
        for n in range(0, 2 * kv_width, 512):
            part = jnp.dot(xg, w_ref[low:high, n : n + 512], preferred_element_type=F32)
            if i == 0:
                acc_ref[:, n : n + 512] = part
            else:
                acc_ref[:, n : n + 512] += part
    sq = column_to_row(jnp.sum(squares, axis=1, keepdims=True), 128)
    high, low = split_bf16(sq)
    tail = jnp.concatenate([high.astype(F32), low.astype(F32)], axis=0)
    fill = outs[1].shape[0] - rows - tail.shape[0]
    if fill:
        tail = jnp.concatenate([tail, jnp.zeros((fill, 128), F32)], axis=0)
    extra = jnp.concatenate([tail.astype(BF16)] * (2 * piece // 128), axis=1)
    for j in range(ranks):
        first = first_column(rank ^ j)
        outs[j][:rows, :piece] = acc_ref[:, pl.ds(first, piece)].astype(BF16)
        outs[j][:rows, piece:] = acc_ref[:, pl.ds(kv_width + first, piece)].astype(BF16)
        outs[j][rows:, :] = extra
    for copy in asking:
        copy.wait()


def project(x, gain, weight, query, own, ranks, group, kv_mine):
    slots, requests, feats = x.shape
    rows = slots * requests
    piece = kv_mine * 128
    extra = -(-2 * (rows // 128) // 8) * 8
    decoded, q_width = query.shape
    outs = pl.pallas_call(
        functools.partial(project_kernel, ranks, group),
        in_specs=[HBM] * 5,
        out_specs=[VMEM] * (ranks + 1),
        out_shape=[jax.ShapeDtypeStruct((rows + extra, 2 * piece), BF16)] * ranks
        + [jax.ShapeDtypeStruct((decoded, q_width // ranks + 2 * piece), BF16)],
        scratch_shapes=[
            pltpu.VMEM((feats,), BF16),
            pltpu.VMEM((slots, requests, feats), BF16),
            pltpu.VMEM(weight.shape, BF16),
            pltpu.VMEM((rows, weight.shape[1]), F32),
            pltpu.SemaphoreType.DMA((5,)),
            pltpu.SemaphoreType.DMA((-(-feats // CHUNK),)),
        ],
        compiler_params=pltpu.CompilerParams(vmem_limit_bytes=56 * MIB),
        cost_estimate=pl.CostEstimate(
            flops=2 * rows * feats * weight.shape[1],
            bytes_accessed=2 * feats * weight.shape[1],
            transcendentals=0,
        ),
        name="project",
    )(gain, x, weight, query, own)
    return outs[:ranks], outs[ranks]


def resident_kernel(ranks, len_ref, q_ref, k_hbm, v_hbm, *rest):
    outs, rest = rest[:ranks], rest[ranks:]
    q_wide, q_all, k_buf, v_buf, o_all, m_all, l_all, s_all, sems = rest
    residents, positions, width = k_buf.shape
    copies = []
    for r in range(residents):
        copies.append(
            (
                pltpu.make_async_copy(k_hbm.at[r], k_buf.at[r], sems.at[0, r]),
                pltpu.make_async_copy(v_hbm.at[r], v_buf.at[r], sems.at[1, r]),
            )
        )
    rank = lax.axis_index("tp")
    held = [(rank == 0) | (len_ref[0, r] > rank * positions) for r in range(residents)]
    for r in range(residents):

        @pl.when(held[r])
        def _():
            for copy in copies[r]:
                copy.start()

    heads = q_ref.shape[0]
    kv_heads = width // 128
    group = heads // kv_heads
    pair_rows = 2 * group
    heads_mine = heads // ranks
    top_half = iota((pair_rows, 128), 0) < group
    position = rank * positions + iota((pair_rows, positions), 1)
    scale = F32(1.0) / jnp.sqrt(F32(128.0))
    diagonal = iota((heads, 128), 0) % heads_mine == iota((heads, 128), 1)

    def to_rows(column):
        spread = jnp.where(diagonal, column, 0.0)
        return jnp.sum(spread.reshape(ranks, heads_mine, 128), axis=1)

    q_wide[...] = q_ref[...].astype(F32)
    for r in range(residents):
        q_all[r] = q_wide[:, r, :].astype(BF16)
    def attend(r):
        valid = position < len_ref[0, r]
        copies[r][0].wait()
        weights = []
        for p in range(kv_heads // 2):
            rows = slice(p * pair_rows, (p + 1) * pair_rows)
            q = q_all[r, rows, :]
            zero = jnp.zeros_like(q)
            lhs = jnp.concatenate(
                [jnp.where(top_half, q, zero), jnp.where(top_half, zero, q)], axis=1
            )
            scores = lax.dot_general(
                lhs,
                k_buf[r, :, p * 256 : (p + 1) * 256],
                (((1,), (1,)), ((), ())),
                preferred_element_type=F32,
            )
            scores = jnp.where(valid, scores * scale, ABSENT)
            peak = jnp.max(scores, axis=1, keepdims=True).astype(BF16).astype(F32)
            weight = jnp.where(valid, jnp.exp(scores - peak), 0.0)
            m_all[r, rows, :] = peak
            l_all[r, rows, :] = jnp.sum(weight, axis=1, keepdims=True)
            weights.append(weight.astype(BF16))
        copies[r][1].wait()
        for p in range(kv_heads // 2):
            both = jnp.dot(
                weights[p], v_buf[r, :, p * 256 : (p + 1) * 256], preferred_element_type=F32
            )
            o_all[r, p * pair_rows : (p + 1) * pair_rows, :] = jnp.where(
                top_half, both[:, :128], both[:, 128:]
            )

    for r in range(residents):
        pl.when(held[r])(functools.partial(attend, r))

        @pl.when(jnp.logical_not(held[r]))
        def _():
            o_all[r] = jnp.zeros((heads, 128), F32)
            m_all[r] = jnp.full((heads, 1), ABSENT, F32)
            l_all[r] = jnp.zeros((heads, 1), F32)

    for r in range(residents):
        s_all[r, 0] = to_rows(m_all[r])
        high, low = split_bf16(to_rows(l_all[r]))
        s_all[r, 1] = high.astype(F32)
        s_all[r, 2] = low.astype(F32)
    filled = residents * (heads_mine + 3)
    for j in range(ranks):
        target = rank ^ j
        first = pl.multiple_of(target * heads_mine, heads_mine)
        parts = [o_all[r, pl.ds(first, heads_mine), :] for r in range(residents)]
        parts += [s_all[r, i, pl.ds(target, 1), :] for i in range(3) for r in range(residents)]
        if outs[j].shape[0] > filled:
            parts.append(jnp.zeros((outs[j].shape[0] - filled, 128), F32))
        outs[j][...] = jnp.concatenate(parts, axis=0).astype(BF16)


def attend_resident(lengths, queries, k_cache, v_cache, ranks):
    residents, positions, width = k_cache.shape
    heads = queries.shape[0]
    heads_mine = heads // ranks
    rows = -(-(residents * (heads_mine + 3)) // 16) * 16
    return pl.pallas_call(
        functools.partial(resident_kernel, ranks),
        in_specs=[SMEM, VMEM, HBM, HBM],
        out_specs=[VMEM] * ranks,
        out_shape=[jax.ShapeDtypeStruct((rows, 128), BF16)] * ranks,
        scratch_shapes=[
            pltpu.VMEM(queries.shape, F32),
            pltpu.VMEM((residents, heads, 128), BF16),
            pltpu.VMEM((residents, positions, width), BF16),
            pltpu.VMEM((residents, positions, width), BF16),
            pltpu.VMEM((residents, heads, 128), F32),
            pltpu.VMEM((residents, heads, 1), F32),
            pltpu.VMEM((residents, heads, 1), F32),
            pltpu.VMEM((residents, 3, ranks, 128), F32),
            pltpu.SemaphoreType.DMA((2, residents)),
        ],
        compiler_params=pltpu.CompilerParams(vmem_limit_bytes=56 * MIB),
        cost_estimate=pl.CostEstimate(
            flops=4 * residents * heads * positions * 128,
            bytes_accessed=4 * residents * positions * width,
            transcendentals=residents * heads * positions,
        ),
        name="attend_resident",
    )(lengths, queries, k_cache, v_cache)


def expand(own, rows):
    which = iota((rows, 128), 0) // (rows // own.shape[0])
    out = jnp.broadcast_to(own[0:1], (rows, 128))
    for h in range(1, own.shape[0]):
        out = jnp.where(which == h, own[h : h + 1], out)
    return out


def heads_of(line, heads_mine, kv_mine):
    per = heads_mine // kv_mine
    blocks = [line[:, c : c + 128] for c in range(0, line.shape[1], 128)]
    q = jnp.concatenate(blocks[:heads_mine], axis=0)
    k = blocks[heads_mine : heads_mine + kv_mine]
    v = blocks[heads_mine + kv_mine :]
    return (
        q,
        expand(jnp.concatenate(k, axis=0), heads_mine),
        expand(jnp.concatenate(v, axis=0), heads_mine),
    )


def moved_kernel(
    insts, ranks, residents, features, dest_ref, count_ref, gain_ref, cos_ref, sin_ref, *rest
):
    asks, rest = rest[: insts - 1], rest[insts - 1 :]
    pieces, rest = rest[:ranks], rest[ranks:]
    out_ref, place_out, ask_ref, q_ref, own_ref, line_ref = rest
    requests = out_ref.shape[0]
    tokens = cos_ref.shape[0]
    piece = pieces[0].shape[1] // 2
    kv_mine = piece // 128
    rows = q_ref.shape[0]
    heads_mine = rows // requests
    scale = F32(1.0) / jnp.sqrt(F32(128.0))
    here = lax.axis_index("inst")

    ask_row = iota(asks[0].shape, 0)
    row_request = iota((rows, tokens), 0) // heads_mine
    limit = jnp.zeros((rows, tokens), jnp.int32)
    for r in range(requests):
        dest = dest_ref[r, here]
        limit = jnp.where(row_request == r, count_ref[r, here], limit)
        place = jnp.int32(residents)
        for s in range(insts):
            for c in range(requests):
                place += jnp.where((dest_ref[c, s] == dest) & (here > s), 1, 0).astype(jnp.int32)
        for b in range(1, insts):

            @pl.when(here ^ b == dest)
            def _():
                ask = asks[b - 1][...].astype(F32)
                ask_ref[r : r + 1, :] = jnp.sum(
                    jnp.where(ask_row == place, ask, 0.0), axis=0, keepdims=True
                )

        at = slice(r * heads_mine, (r + 1) * heads_mine)
        q_ref[at, :], own_ref[0, at, :], own_ref[1, at, :] = heads_of(
            ask_ref[r : r + 1, :], heads_mine, kv_mine
        )
    places = jnp.full(place_out.shape, -1, jnp.int32)
    row = iota(place_out.shape, 0)
    place = jnp.int32(residents)
    for s in range(insts):
        for c in range(requests):
            mine = dest_ref[c, s] == here
            places = jnp.where((row == (here ^ s) * requests + c) & mine, place, places)
            place += jnp.where(mine, 1, 0).astype(jnp.int32)
    place_out[...] = places

    blocks = tokens // 128
    last = tokens + 2 * blocks
    tail = pieces[0][tokens:last, :128].astype(F32)
    for t in range(1, ranks):
        tail = tail + pieces[t][tokens:last, :128].astype(F32)
    squares = tail[:blocks] + tail[blocks:]
    squares = jnp.concatenate(
        [row_to_column(squares[b : b + 1], 128) for b in range(blocks)], axis=0
    )
    token_scale = lax.rsqrt(squares / features + EPS)

    def column_block(c):
        total = pieces[0][:tokens, c : c + 128].astype(F32)
        for t in range(1, ranks):
            total = total + pieces[t][:tokens, c : c + 128].astype(F32)
        return total * token_scale

    gain = gain_ref[...].astype(F32)
    q = q_ref[...]
    q16 = q.astype(BF16)
    which = iota((rows, tokens), 0) % heads_mine // (heads_mine // kv_mine)
    scores = None
    for h in range(kv_mine):
        key = column_block(h * 128)
        key = key * lax.rsqrt(jnp.mean(key * key, axis=1, keepdims=True) + EPS) * gain
        key = key * cos_ref[...] + pltpu.roll(key, 64, 1) * sin_ref[...]
        part = lax.dot_general(
            q16, key.astype(BF16), (((1,), (1,)), ((), ())), preferred_element_type=F32
        )
        scores = part if scores is None else jnp.where(which == h, part, scores)
    token = iota((rows, tokens), 1)
    valid = (token % requests == row_request) & (token // requests < limit)
    scores = jnp.where(valid, scores * scale, ABSENT)
    own_score = jnp.sum(q * own_ref[0], axis=1, keepdims=True) * scale
    top = jnp.maximum(jnp.max(scores, axis=1, keepdims=True), own_score)
    weights = jnp.where(valid, jnp.exp(scores - top), 0.0)
    own_weight = jnp.exp(own_score - top)
    total = jnp.sum(weights, axis=1, keepdims=True) + own_weight
    weights = weights.astype(BF16)
    summed = None
    for h in range(kv_mine):
        value = column_block(piece + h * 128).astype(BF16)
        part = jnp.dot(weights, value, preferred_element_type=F32)
        summed = part if summed is None else jnp.where(which[:, :128] == h, part, summed)
    summed = summed + own_weight.astype(BF16).astype(F32) * own_ref[1]
    result = summed / total
    for r in range(requests):
        for h in range(heads_mine):
            at = r * heads_mine + h
            line_ref[r : r + 1, h * 128 : (h + 1) * 128] = result[at : at + 1, :]
    out_ref[...] = line_ref[...].astype(BF16)


def attend_moved(dest, count, k_gain, cos, sin, asks, pieces, residents, heads_mine, features):
    requests, insts = dest.shape
    rows = requests * heads_mine
    return pl.pallas_call(
        functools.partial(moved_kernel, insts, len(pieces), residents, features),
        in_specs=[SMEM] * 2 + [VMEM] * (3 + len(asks) + len(pieces)),
        out_specs=[VMEM] * 2,
        out_shape=[
            jax.ShapeDtypeStruct((requests, heads_mine * 128), BF16),
            jax.ShapeDtypeStruct((insts * requests, 128), jnp.int32),
        ],
        scratch_shapes=[
            pltpu.VMEM((requests, asks[0].shape[1]), F32),
            pltpu.VMEM((rows, 128), F32),
            pltpu.VMEM((2, rows, 128), F32),
            pltpu.VMEM((requests, heads_mine * 128), F32),
        ],
        compiler_params=pltpu.CompilerParams(vmem_limit_bytes=16 * MIB),
        name="attend_moved",
    )(dest, count, k_gain, cos, sin, *asks, *pieces)


def combine_kernel(residents, kv_mine, ask_ref, *rest):
    refs, out_ref = rest[:-1], rest[-1]
    heads_mine = out_ref.shape[1] // 128
    scale = F32(1.0) / jnp.sqrt(F32(128.0))
    payloads = [ref[...].astype(F32) for ref in refs]
    at = residents * heads_mine
    ask = ask_ref[...].astype(F32)
    for r in range(residents):
        q, own_k, own_v = heads_of(ask[r : r + 1], heads_mine, kv_mine)
        own_score = jnp.sum(q * own_k, axis=1, keepdims=True) * scale
        peaks, totals = [], []
        for payload in payloads:
            stat = payload[at : at + 3 * residents]
            peaks.append(row_to_column(stat[r : r + 1], heads_mine))
            total = stat[residents + r : residents + r + 1]
            total = total + stat[2 * residents + r : 2 * residents + r + 1]
            totals.append(row_to_column(total, heads_mine))
        top = own_score
        for peak in peaks:
            top = jnp.maximum(top, peak)
        own_weight = jnp.exp(own_score - top)
        denom = own_weight
        numer = own_weight.astype(BF16).astype(F32) * own_v
        for peak, total, payload in zip(peaks, totals, payloads):
            keep = jnp.exp(peak - top)
            denom = denom + keep * total
            numer = numer + keep * payload[r * heads_mine : (r + 1) * heads_mine]
        result = numer / denom
        for h in range(heads_mine):
            out_ref[r : r + 1, h * 128 : (h + 1) * 128] = result[h : h + 1, :]


def combine_resident(ask, payloads, residents, heads_mine, kv_mine):
    return pl.pallas_call(
        functools.partial(combine_kernel, residents, kv_mine),
        in_specs=[VMEM] * (1 + len(payloads)),
        out_specs=VMEM,
        out_shape=jax.ShapeDtypeStruct((residents, heads_mine * 128), F32),
        compiler_params=pltpu.CompilerParams(vmem_limit_bytes=8 * MIB),
        name="combine_resident",
    )(ask, *payloads)


def finish_kernel(kept_ref, place_ref, *rest):
    moved, out_ref = rest[:-1], rest[-1]
    residents = kept_ref.shape[0]
    decoded, width = out_ref.shape
    requests = decoded - residents
    row = iota((decoded, 128), 0)
    arrived = [ref[...].astype(F32) for ref in moved]
    for c in range(0, width, 128):
        kept = kept_ref[:, c : c + 128]
        line = jnp.concatenate([kept, jnp.zeros((requests, 128), F32)], axis=0)
        for b in range(len(moved)):
            for i in range(requests):
                at = (b + 1) * requests + i
                line = jnp.where(
                    place_ref[at : at + 1, :] == row, arrived[b][i : i + 1, c : c + 128], line
                )
        out_ref[:, c : c + 128] = line.astype(BF16)


def finish(kept, places, moved, requests):
    residents, width = kept.shape
    return pl.pallas_call(
        finish_kernel,
        in_specs=[VMEM] * (2 + len(moved)),
        out_specs=VMEM,
        out_shape=jax.ShapeDtypeStruct((residents + requests, width), BF16),
        compiler_params=pltpu.CompilerParams(vmem_limit_bytes=8 * MIB),
        name="finish",
    )(kept, places, *moved)


def swapped(x, axis, j, n):
    return lax.ppermute(x, axis, [(i, i ^ j) for i in range(n)])


def rotation(slots, requests, head_size):
    half = head_size // 2
    freq = THETA ** (-np.arange(half) * 2.0 / head_size)
    angle = np.repeat(np.arange(slots), requests)[:, None] * freq[None, :]
    cos, sin = np.cos(angle), np.sin(angle)
    return (
        np.concatenate([cos, cos], axis=1).astype(np.float32),
        np.concatenate([-sin, sin], axis=1).astype(np.float32),
    )


def per_device(
    mig_hidden,
    mig_dest,
    mig_count,
    attn_gain,
    kv_weight,
    k_gain,
    query,
    new_kv,
    k_cache,
    v_cache,
    lengths,
):
    insts = lax.axis_size("inst")
    ranks = lax.axis_size("tp")
    head_size = k_gain.shape[0]
    slots, requests, feats = mig_hidden.shape[1:]
    residents = k_cache.shape[1]
    heads = query.shape[2] // head_size
    kv_heads = kv_weight.shape[1] // 2 // head_size
    heads_mine = heads // ranks
    group = heads // kv_heads
    kv_mine = max(1, heads_mine // group)

    pieces, ask = project(
        mig_hidden[0], attn_gain, kv_weight, query[0], new_kv[0], ranks, group, kv_mine
    )
    order = sorted(range(2, ranks), key=lambda j: (abs(j - ranks // 2), j))
    asks = [swapped(ask, "inst", b, insts) for b in range(1, insts)]
    sent = [swapped(pieces[j], "tp", j, ranks) for j in order]
    asks[0], near = lax.optimization_barrier((asks[0], pieces[1]))
    pieces = [pieces[0]] + sent + [swapped(near, "tp", 1, ranks)]
    queries = jnp.transpose(query[0].reshape(query.shape[1], heads, head_size), (1, 0, 2))
    payloads = attend_resident(lengths, queries, k_cache[0], v_cache[0], ranks)
    asks, payloads = lax.optimization_barrier((asks, payloads))
    order = sorted(range(1, ranks), key=lambda j: (j > 1, -j))
    received = [payloads[0]] + [swapped(payloads[j], "tp", j, ranks) for j in order]
    cos, sin = rotation(slots, requests, head_size)
    moved, places = attend_moved(
        mig_dest.T,
        mig_count.T,
        k_gain.reshape(1, head_size),
        cos,
        sin,
        asks,
        pieces,
        residents,
        heads_mine,
        feats * ranks,
    )
    kept = combine_resident(ask, received, residents, heads_mine, kv_mine)
    moved = [swapped(moved, "inst", b, insts) for b in reversed(range(1, insts))][::-1]
    return finish(kept, places, moved, requests)[None]


def solution(mesh):
    placed = (
        P(("group", "inst"), None, None, "tp"),
        P("group", None),
        P("group", None),
        P("tp"),
        P("tp", None),
        P(),
        P(("group", "inst"), None, None),
        P(("group", "inst"), None, None),
        P(("group", "inst"), None, "tp", None),
        P(("group", "inst"), None, "tp", None),
        P(("group", "inst"), None),
    )
    return jax.shard_map(
        per_device,
        mesh=mesh,
        in_specs=placed,
        out_specs=P(("group", "inst"), None, "tp"),
        check_vma=False,
    )
```

```python
import functools

import jax
import jax.numpy as jnp
import numpy as np
from jax import lax
from jax.experimental import pallas as pl
from jax.experimental.pallas import tpu as pltpu
from jax.sharding import PartitionSpec as P

EPS = 1e-06
THETA = 1000000.0
ABSENT = -1e30
F32 = jnp.float32
BF16 = jnp.bfloat16
MIB = 1024 * 1024
CHUNK = 512

VMEM = pl.BlockSpec(memory_space=pltpu.VMEM)
SMEM = pl.BlockSpec(memory_space=pltpu.SMEM)
HBM = pl.BlockSpec(memory_space=pltpu.HBM)


def iota(shape, dim):
    return lax.broadcasted_iota(jnp.int32, shape, dim)


def column_to_row(column, period):
    n = column.shape[0]
    spread = jnp.where(iota((n, 128), 0) % period == iota((n, 128), 1), column, 0.0)
    return jnp.sum(spread.reshape(n // period, period, 128), axis=1)


def row_to_column(row, n):
    return jnp.sum(
        jnp.where(iota((n, 128), 0) == iota((n, 128), 1), row, 0.0), axis=1, keepdims=True
    )


def split_bf16(x):
    high = x.astype(BF16)
    return high, (x - high.astype(F32)).astype(BF16)


def project_kernel(ranks, group, gain_hbm, x_hbm, w_hbm, q_hbm, own_hbm, *rest):
    outs, ask_ref = rest[:ranks], rest[ranks]
    gain_ref, x_ref, w_ref, acc_ref, in_sems, w_sems = rest[ranks + 1 :]
    slots, requests, feats = x_ref.shape
    rows = slots * requests
    piece = outs[0].shape[1] // 2
    kv_width = w_hbm.shape[1] // 2
    heads_mine = kv_width // 128 * group // ranks
    rank = lax.axis_index("tp")

    def first_column(target):
        return pl.multiple_of(target * heads_mine // group * 128, 128)

    gain_copy = pltpu.make_async_copy(gain_hbm, gain_ref, in_sems.at[0])
    gain_copy.start()
    x_copy = pltpu.make_async_copy(x_hbm, x_ref, in_sems.at[1])
    x_copy.start()
    mine = heads_mine * 128
    q_first = pl.multiple_of(rank * mine, 128)
    asking = [
        pltpu.make_async_copy(
            q_hbm.at[:, pl.ds(q_first, mine)], ask_ref.at[:, :mine], in_sems.at[2]
        )
    ]
    for i in range(2):
        asking.append(
            pltpu.make_async_copy(
                own_hbm.at[:, pl.ds(i * kv_width + first_column(rank), piece)],
                ask_ref.at[:, mine + i * piece : mine + (i + 1) * piece],
                in_sems.at[3 + i],
            )
        )
    for copy in asking:
        copy.start()
    cuts = list(range(0, feats, CHUNK)) + [feats]
    chunks = list(zip(cuts[:-1], cuts[1:]))
    copies = []
    for i, (low, high) in enumerate(chunks):
        copies.append(
            pltpu.make_async_copy(w_hbm.at[low:high, :], w_ref.at[low:high, :], w_sems.at[i])
        )
        copies[-1].start()
    gain_copy.wait()
    x_copy.wait()
    squares = jnp.zeros((rows, 128), F32)
    for i, (low, high) in enumerate(chunks):
        parts = []
        for c in range(low, high, 128):
            width = min(128, high - c)
            x = x_ref[:, :, c : c + width].astype(F32).reshape(rows, width)
            gain = gain_ref[c : c + width].astype(F32).reshape(1, width)
            parts.append((x * gain).astype(BF16))
            x = x * x
            if width < 128:
                x = jnp.concatenate([x, jnp.zeros((rows, 128 - width), F32)], axis=1)
            squares = squares + x
        xg = parts[0] if len(parts) == 1 else jnp.concatenate(parts, axis=1)
        copies[i].wait()
        for j in range(ranks):
            for half in range(2):
                first = pl.multiple_of(half * kv_width + first_column(rank ^ j), 128)
                part = jnp.dot(
                    xg, w_ref[low:high, pl.ds(first, piece)], preferred_element_type=F32
                )
                at = slice(half * piece, (half + 1) * piece)
                if i > 0:
                    part = part + acc_ref[j, :, at]
                if i + 1 < len(chunks):
                    acc_ref[j, :, at] = part
                else:
                    outs[j][:rows, at] = part.astype(BF16)
    sq = column_to_row(jnp.sum(squares, axis=1, keepdims=True), 128)
    high, low = split_bf16(sq)
    tail = jnp.concatenate([high.astype(F32), low.astype(F32)], axis=0)
    fill = outs[1].shape[0] - rows - tail.shape[0]
    if fill:
        tail = jnp.concatenate([tail, jnp.zeros((fill, 128), F32)], axis=0)
    extra = jnp.concatenate([tail.astype(BF16)] * (2 * piece // 128), axis=1)
    for j in range(ranks):
        outs[j][rows:, :] = extra
    for copy in asking:
        copy.wait()


def project(x, gain, weight, query, own, ranks, group, kv_mine):
    slots, requests, feats = x.shape
    rows = slots * requests
    piece = kv_mine * 128
    extra = -(-2 * (rows // 128) // 8) * 8
    decoded, q_width = query.shape
    outs = pl.pallas_call(
        functools.partial(project_kernel, ranks, group),
        in_specs=[HBM] * 5,
        out_specs=[VMEM] * (ranks + 1),
        out_shape=[jax.ShapeDtypeStruct((rows + extra, 2 * piece), BF16)] * ranks
        + [jax.ShapeDtypeStruct((decoded, q_width // ranks + 2 * piece), BF16)],
        scratch_shapes=[
            pltpu.VMEM((feats,), BF16),
            pltpu.VMEM((slots, requests, feats), BF16),
            pltpu.VMEM(weight.shape, BF16),
            pltpu.VMEM((ranks, rows, 2 * piece), F32),
            pltpu.SemaphoreType.DMA((5,)),
            pltpu.SemaphoreType.DMA((-(-feats // CHUNK),)),
        ],
        compiler_params=pltpu.CompilerParams(vmem_limit_bytes=56 * MIB),
        cost_estimate=pl.CostEstimate(
            flops=2 * rows * feats * weight.shape[1],
            bytes_accessed=2 * feats * weight.shape[1],
            transcendentals=0,
        ),
        name="project",
    )(gain, x, weight, query, own)
    return outs[:ranks], outs[ranks]


def resident_kernel(ranks, len_ref, q_ref, k_hbm, v_hbm, *rest):
    outs, rest = rest[:ranks], rest[ranks:]
    q_wide, q_all, k_buf, v_buf, o_all, m_all, l_all, s_all, sems = rest
    residents, positions, width = k_buf.shape
    copies = []
    for r in range(residents):
        copies.append(
            (
                pltpu.make_async_copy(k_hbm.at[r], k_buf.at[r], sems.at[0, r]),
                pltpu.make_async_copy(v_hbm.at[r], v_buf.at[r], sems.at[1, r]),
            )
        )
    rank = lax.axis_index("tp")
    held = [(rank == 0) | (len_ref[0, r] > rank * positions) for r in range(residents)]
    for r in range(residents):

        @pl.when(held[r])
        def _():
            for copy in copies[r]:
                copy.start()

    heads = q_ref.shape[0]
    kv_heads = width // 128
    group = heads // kv_heads
    pair_rows = 2 * group
    heads_mine = heads // ranks
    top_half = iota((pair_rows, 128), 0) < group
    position = rank * positions + iota((pair_rows, positions), 1)
    scale = F32(1.0) / jnp.sqrt(F32(128.0))
    diagonal = iota((heads, 128), 0) % heads_mine == iota((heads, 128), 1)

    def to_rows(column):
        spread = jnp.where(diagonal, column, 0.0)
        return jnp.sum(spread.reshape(ranks, heads_mine, 128), axis=1)

    q_wide[...] = q_ref[...].astype(F32)
    for r in range(residents):
        q_all[r] = q_wide[:, r, :].astype(BF16)
    def attend(r):
        valid = position < len_ref[0, r]
        copies[r][0].wait()
        weights = []
        for p in range(kv_heads // 2):
            rows = slice(p * pair_rows, (p + 1) * pair_rows)
            q = q_all[r, rows, :]
            zero = jnp.zeros_like(q)
            lhs = jnp.concatenate(
                [jnp.where(top_half, q, zero), jnp.where(top_half, zero, q)], axis=1
            )
            scores = lax.dot_general(
                lhs,
                k_buf[r, :, p * 256 : (p + 1) * 256],
                (((1,), (1,)), ((), ())),
                preferred_element_type=F32,
            )
            scores = jnp.where(valid, scores * scale, ABSENT)
            peak = jnp.max(scores, axis=1, keepdims=True).astype(BF16).astype(F32)
            weight = jnp.where(valid, jnp.exp(scores - peak), 0.0)
            m_all[r, rows, :] = peak
            l_all[r, rows, :] = jnp.sum(weight, axis=1, keepdims=True)
            weights.append(weight.astype(BF16))
        copies[r][1].wait()
        for p in range(kv_heads // 2):
            both = jnp.dot(
                weights[p], v_buf[r, :, p * 256 : (p + 1) * 256], preferred_element_type=F32
            )
            o_all[r, p * pair_rows : (p + 1) * pair_rows, :] = jnp.where(
                top_half, both[:, :128], both[:, 128:]
            )

    for r in range(residents):
        pl.when(held[r])(functools.partial(attend, r))

        @pl.when(jnp.logical_not(held[r]))
        def _():
            o_all[r] = jnp.zeros((heads, 128), F32)
            m_all[r] = jnp.full((heads, 1), ABSENT, F32)
            l_all[r] = jnp.zeros((heads, 1), F32)

    for r in range(residents):
        s_all[r, 0] = to_rows(m_all[r])
        high, low = split_bf16(to_rows(l_all[r]))
        s_all[r, 1] = high.astype(F32)
        s_all[r, 2] = low.astype(F32)
    filled = residents * (heads_mine + 3)
    for j in range(ranks):
        target = rank ^ j
        first = pl.multiple_of(target * heads_mine, heads_mine)
        parts = [o_all[r, pl.ds(first, heads_mine), :] for r in range(residents)]
        parts += [s_all[r, i, pl.ds(target, 1), :] for i in range(3) for r in range(residents)]
        if outs[j].shape[0] > filled:
            parts.append(jnp.zeros((outs[j].shape[0] - filled, 128), F32))
        outs[j][...] = jnp.concatenate(parts, axis=0).astype(BF16)


def attend_resident(lengths, queries, k_cache, v_cache, ranks):
    residents, positions, width = k_cache.shape
    heads = queries.shape[0]
    heads_mine = heads // ranks
    rows = -(-(residents * (heads_mine + 3)) // 16) * 16
    return pl.pallas_call(
        functools.partial(resident_kernel, ranks),
        in_specs=[SMEM, VMEM, HBM, HBM],
        out_specs=[VMEM] * ranks,
        out_shape=[jax.ShapeDtypeStruct((rows, 128), BF16)] * ranks,
        scratch_shapes=[
            pltpu.VMEM(queries.shape, F32),
            pltpu.VMEM((residents, heads, 128), BF16),
            pltpu.VMEM((residents, positions, width), BF16),
            pltpu.VMEM((residents, positions, width), BF16),
            pltpu.VMEM((residents, heads, 128), F32),
            pltpu.VMEM((residents, heads, 1), F32),
            pltpu.VMEM((residents, heads, 1), F32),
            pltpu.VMEM((residents, 3, ranks, 128), F32),
            pltpu.SemaphoreType.DMA((2, residents)),
        ],
        compiler_params=pltpu.CompilerParams(vmem_limit_bytes=56 * MIB),
        cost_estimate=pl.CostEstimate(
            flops=4 * residents * heads * positions * 128,
            bytes_accessed=4 * residents * positions * width,
            transcendentals=residents * heads * positions,
        ),
        name="attend_resident",
    )(lengths, queries, k_cache, v_cache)


def expand(own, rows):
    which = iota((rows, 128), 0) // (rows // own.shape[0])
    out = jnp.broadcast_to(own[0:1], (rows, 128))
    for h in range(1, own.shape[0]):
        out = jnp.where(which == h, own[h : h + 1], out)
    return out


def heads_of(line, heads_mine, kv_mine):
    per = heads_mine // kv_mine
    blocks = [line[:, c : c + 128] for c in range(0, line.shape[1], 128)]
    q = jnp.concatenate(blocks[:heads_mine], axis=0)
    k = blocks[heads_mine : heads_mine + kv_mine]
    v = blocks[heads_mine + kv_mine :]
    return (
        q,
        expand(jnp.concatenate(k, axis=0), heads_mine),
        expand(jnp.concatenate(v, axis=0), heads_mine),
    )


def moved_kernel(
    insts, ranks, residents, features, dest_ref, count_ref, gain_ref, cos_ref, sin_ref, *rest
):
    asks, rest = rest[: insts - 1], rest[insts - 1 :]
    pieces, rest = rest[:ranks], rest[ranks:]
    out_ref, place_out, ask_ref, q_ref, own_ref, line_ref = rest
    requests = out_ref.shape[0]
    tokens = cos_ref.shape[0]
    piece = pieces[0].shape[1] // 2
    kv_mine = piece // 128
    rows = q_ref.shape[0]
    heads_mine = rows // requests
    scale = F32(1.0) / jnp.sqrt(F32(128.0))
    here = lax.axis_index("inst")

    ask_row = iota(asks[0].shape, 0)
    row_request = iota((rows, tokens), 0) // heads_mine
    limit = jnp.zeros((rows, tokens), jnp.int32)
    for r in range(requests):
        dest = dest_ref[r, here]
        limit = jnp.where(row_request == r, count_ref[r, here], limit)
        place = jnp.int32(residents)
        for s in range(insts):
            for c in range(requests):
                place += jnp.where((dest_ref[c, s] == dest) & (here > s), 1, 0).astype(jnp.int32)
        for b in range(1, insts):

            @pl.when(here ^ b == dest)
            def _():
                ask = asks[b - 1][...].astype(F32)
                ask_ref[r : r + 1, :] = jnp.sum(
                    jnp.where(ask_row == place, ask, 0.0), axis=0, keepdims=True
                )

        at = slice(r * heads_mine, (r + 1) * heads_mine)
        q_ref[at, :], own_ref[0, at, :], own_ref[1, at, :] = heads_of(
            ask_ref[r : r + 1, :], heads_mine, kv_mine
        )
    places = jnp.full(place_out.shape, -1, jnp.int32)
    row = iota(place_out.shape, 0)
    place = jnp.int32(residents)
    for s in range(insts):
        for c in range(requests):
            mine = dest_ref[c, s] == here
            places = jnp.where((row == (here ^ s) * requests + c) & mine, place, places)
            place += jnp.where(mine, 1, 0).astype(jnp.int32)
    place_out[...] = places

    blocks = tokens // 128
    last = tokens + 2 * blocks
    tail = pieces[0][tokens:last, :128].astype(F32)
    for t in range(1, ranks):
        tail = tail + pieces[t][tokens:last, :128].astype(F32)
    squares = tail[:blocks] + tail[blocks:]
    squares = jnp.concatenate(
        [row_to_column(squares[b : b + 1], 128) for b in range(blocks)], axis=0
    )
    token_scale = lax.rsqrt(squares / features + EPS)

    def column_block(c):
        total = pieces[0][:tokens, c : c + 128].astype(F32)
        for t in range(1, ranks):
            total = total + pieces[t][:tokens, c : c + 128].astype(F32)
        return total * token_scale

    gain = gain_ref[...].astype(F32)
    q = q_ref[...]
    q16 = q.astype(BF16)
    which = iota((rows, tokens), 0) % heads_mine // (heads_mine // kv_mine)
    scores = None
    for h in range(kv_mine):
        key = column_block(h * 128)
        key = key * lax.rsqrt(jnp.mean(key * key, axis=1, keepdims=True) + EPS) * gain
        key = key * cos_ref[...] + pltpu.roll(key, 64, 1) * sin_ref[...]
        part = lax.dot_general(
            q16, key.astype(BF16), (((1,), (1,)), ((), ())), preferred_element_type=F32
        )
        scores = part if scores is None else jnp.where(which == h, part, scores)
    token = iota((rows, tokens), 1)
    valid = (token % requests == row_request) & (token // requests < limit)
    scores = jnp.where(valid, scores * scale, ABSENT)
    own_score = jnp.sum(q * own_ref[0], axis=1, keepdims=True) * scale
    top = jnp.maximum(jnp.max(scores, axis=1, keepdims=True), own_score)
    weights = jnp.where(valid, jnp.exp(scores - top), 0.0)
    own_weight = jnp.exp(own_score - top)
    total = jnp.sum(weights, axis=1, keepdims=True) + own_weight
    weights = weights.astype(BF16)
    summed = None
    for h in range(kv_mine):
        value = column_block(piece + h * 128).astype(BF16)
        part = jnp.dot(weights, value, preferred_element_type=F32)
        summed = part if summed is None else jnp.where(which[:, :128] == h, part, summed)
    summed = summed + own_weight.astype(BF16).astype(F32) * own_ref[1]
    result = summed / total
    for r in range(requests):
        for h in range(heads_mine):
            at = r * heads_mine + h
            line_ref[r : r + 1, h * 128 : (h + 1) * 128] = result[at : at + 1, :]
    out_ref[...] = line_ref[...].astype(BF16)


def attend_moved(dest, count, k_gain, cos, sin, asks, pieces, residents, heads_mine, features):
    requests, insts = dest.shape
    rows = requests * heads_mine
    return pl.pallas_call(
        functools.partial(moved_kernel, insts, len(pieces), residents, features),
        in_specs=[SMEM] * 2 + [VMEM] * (3 + len(asks) + len(pieces)),
        out_specs=[VMEM] * 2,
        out_shape=[
            jax.ShapeDtypeStruct((requests, heads_mine * 128), BF16),
            jax.ShapeDtypeStruct((insts * requests, 128), jnp.int32),
        ],
        scratch_shapes=[
            pltpu.VMEM((requests, asks[0].shape[1]), F32),
            pltpu.VMEM((rows, 128), F32),
            pltpu.VMEM((2, rows, 128), F32),
            pltpu.VMEM((requests, heads_mine * 128), F32),
        ],
        compiler_params=pltpu.CompilerParams(vmem_limit_bytes=16 * MIB),
        name="attend_moved",
    )(dest, count, k_gain, cos, sin, *asks, *pieces)


def combine_kernel(residents, kv_mine, ask_ref, *rest):
    refs, out_ref = rest[:-1], rest[-1]
    heads_mine = out_ref.shape[1] // 128
    scale = F32(1.0) / jnp.sqrt(F32(128.0))
    payloads = [ref[...].astype(F32) for ref in refs]
    at = residents * heads_mine
    ask = ask_ref[...].astype(F32)
    for r in range(residents):
        q, own_k, own_v = heads_of(ask[r : r + 1], heads_mine, kv_mine)
        own_score = jnp.sum(q * own_k, axis=1, keepdims=True) * scale
        peaks, totals = [], []
        for payload in payloads:
            stat = payload[at : at + 3 * residents]
            peaks.append(row_to_column(stat[r : r + 1], heads_mine))
            total = stat[residents + r : residents + r + 1]
            total = total + stat[2 * residents + r : 2 * residents + r + 1]
            totals.append(row_to_column(total, heads_mine))
        top = own_score
        for peak in peaks:
            top = jnp.maximum(top, peak)
        own_weight = jnp.exp(own_score - top)
        denom = own_weight
        numer = own_weight.astype(BF16).astype(F32) * own_v
        for peak, total, payload in zip(peaks, totals, payloads):
            keep = jnp.exp(peak - top)
            denom = denom + keep * total
            numer = numer + keep * payload[r * heads_mine : (r + 1) * heads_mine]
        result = numer / denom
        for h in range(heads_mine):
            out_ref[r : r + 1, h * 128 : (h + 1) * 128] = result[h : h + 1, :]


def combine_resident(ask, payloads, residents, heads_mine, kv_mine):
    return pl.pallas_call(
        functools.partial(combine_kernel, residents, kv_mine),
        in_specs=[VMEM] * (1 + len(payloads)),
        out_specs=VMEM,
        out_shape=jax.ShapeDtypeStruct((residents, heads_mine * 128), F32),
        compiler_params=pltpu.CompilerParams(vmem_limit_bytes=8 * MIB),
        name="combine_resident",
    )(ask, *payloads)


def finish_kernel(kept_ref, place_ref, *rest):
    moved, out_ref = rest[:-1], rest[-1]
    residents = kept_ref.shape[0]
    decoded, width = out_ref.shape
    requests = decoded - residents
    row = iota((decoded, 128), 0)
    arrived = [ref[...].astype(F32) for ref in moved]
    for c in range(0, width, 128):
        kept = kept_ref[:, c : c + 128]
        line = jnp.concatenate([kept, jnp.zeros((requests, 128), F32)], axis=0)
        for b in range(len(moved)):
            for i in range(requests):
                at = (b + 1) * requests + i
                line = jnp.where(
                    place_ref[at : at + 1, :] == row, arrived[b][i : i + 1, c : c + 128], line
                )
        out_ref[:, c : c + 128] = line.astype(BF16)


def finish(kept, places, moved, requests):
    residents, width = kept.shape
    return pl.pallas_call(
        finish_kernel,
        in_specs=[VMEM] * (2 + len(moved)),
        out_specs=VMEM,
        out_shape=jax.ShapeDtypeStruct((residents + requests, width), BF16),
        compiler_params=pltpu.CompilerParams(vmem_limit_bytes=8 * MIB),
        name="finish",
    )(kept, places, *moved)


def swapped(x, axis, j, n):
    return lax.ppermute(x, axis, [(i, i ^ j) for i in range(n)])


def rotation(slots, requests, head_size):
    half = head_size // 2
    freq = THETA ** (-np.arange(half) * 2.0 / head_size)
    angle = np.repeat(np.arange(slots), requests)[:, None] * freq[None, :]
    cos, sin = np.cos(angle), np.sin(angle)
    return (
        np.concatenate([cos, cos], axis=1).astype(np.float32),
        np.concatenate([-sin, sin], axis=1).astype(np.float32),
    )


def per_device(
    mig_hidden,
    mig_dest,
    mig_count,
    attn_gain,
    kv_weight,
    k_gain,
    query,
    new_kv,
    k_cache,
    v_cache,
    lengths,
):
    insts = lax.axis_size("inst")
    ranks = lax.axis_size("tp")
    head_size = k_gain.shape[0]
    slots, requests, feats = mig_hidden.shape[1:]
    residents = k_cache.shape[1]
    heads = query.shape[2] // head_size
    kv_heads = kv_weight.shape[1] // 2 // head_size
    heads_mine = heads // ranks
    group = heads // kv_heads
    kv_mine = max(1, heads_mine // group)

    pieces, ask = project(
        mig_hidden[0], attn_gain, kv_weight, query[0], new_kv[0], ranks, group, kv_mine
    )
    order = sorted(range(2, ranks), key=lambda j: (abs(j - ranks // 2), j))
    asks = [swapped(ask, "inst", b, insts) for b in range(1, insts)]
    sent = [swapped(pieces[j], "tp", j, ranks) for j in order]
    asks[0], near = lax.optimization_barrier((asks[0], pieces[1]))
    pieces = [pieces[0]] + sent + [swapped(near, "tp", 1, ranks)]
    queries = jnp.transpose(query[0].reshape(query.shape[1], heads, head_size), (1, 0, 2))
    payloads = attend_resident(lengths, queries, k_cache[0], v_cache[0], ranks)
    asks, payloads = lax.optimization_barrier((asks, payloads))
    order = sorted(range(1, ranks), key=lambda j: (j > 1, -j))
    received = [payloads[0]] + [swapped(payloads[j], "tp", j, ranks) for j in order]
    cos, sin = rotation(slots, requests, head_size)
    moved, places = attend_moved(
        mig_dest.T,
        mig_count.T,
        k_gain.reshape(1, head_size),
        cos,
        sin,
        asks,
        pieces,
        residents,
        heads_mine,
        feats * ranks,
    )
    kept = combine_resident(ask, received, residents, heads_mine, kv_mine)
    moved = [swapped(moved, "inst", b, insts) for b in reversed(range(1, insts))][::-1]
    return finish(kept, places, moved, requests)[None]


def solution(mesh):
    placed = (
        P(("group", "inst"), None, None, "tp"),
        P("group", None),
        P("group", None),
        P("tp"),
        P("tp", None),
        P(),
        P(("group", "inst"), None, None),
        P(("group", "inst"), None, None),
        P(("group", "inst"), None, "tp", None),
        P(("group", "inst"), None, "tp", None),
        P(("group", "inst"), None),
    )
    return jax.shard_map(
        per_device,
        mesh=mesh,
        in_specs=placed,
        out_specs=P(("group", "inst"), None, "tp"),
        check_vma=False,
    )
```

```python
import functools

import jax
import jax.numpy as jnp
import numpy as np
from jax import lax
from jax.experimental import pallas as pl
from jax.experimental.pallas import tpu as pltpu
from jax.sharding import PartitionSpec as P

EPS = 1e-06
THETA = 1000000.0
ABSENT = -1e30
F32 = jnp.float32
BF16 = jnp.bfloat16
MIB = 1024 * 1024
CHUNK = 512

VMEM = pl.BlockSpec(memory_space=pltpu.VMEM)
SMEM = pl.BlockSpec(memory_space=pltpu.SMEM)
HBM = pl.BlockSpec(memory_space=pltpu.HBM)


def iota(shape, dim):
    return lax.broadcasted_iota(jnp.int32, shape, dim)


def column_to_row(column, period):
    n = column.shape[0]
    spread = jnp.where(iota((n, 128), 0) % period == iota((n, 128), 1), column, 0.0)
    return jnp.sum(spread.reshape(n // period, period, 128), axis=1)


def row_to_column(row, n):
    return jnp.sum(
        jnp.where(iota((n, 128), 0) == iota((n, 128), 1), row, 0.0), axis=1, keepdims=True
    )


def split_bf16(x):
    high = x.astype(BF16)
    return high, (x - high.astype(F32)).astype(BF16)


def project_kernel(ranks, group, gain_hbm, x_hbm, w_hbm, q_hbm, own_hbm, *rest):
    outs, ask_ref = rest[:ranks], rest[ranks]
    gain_ref, x_ref, rows_ref, w_ref, acc_ref, in_sems, w_sems = rest[ranks + 1 :]
    slots, requests, feats = x_ref.shape
    rows = slots * requests
    piece = outs[0].shape[1] // 2
    kv_width = w_hbm.shape[1] // 2
    heads_mine = kv_width // 128 * group // ranks
    rank = lax.axis_index("tp")

    def first_column(target):
        return pl.multiple_of(target * heads_mine // group * 128, 128)

    gain_copy = pltpu.make_async_copy(gain_hbm, gain_ref, in_sems.at[0])
    gain_copy.start()
    x_copy = pltpu.make_async_copy(x_hbm, x_ref, in_sems.at[1])
    x_copy.start()
    cuts = list(range(0, feats, CHUNK)) + [feats]
    chunks = list(zip(cuts[:-1], cuts[1:]))
    copies = []
    for i, (low, high) in enumerate(chunks):
        copies.append(
            pltpu.make_async_copy(w_hbm.at[low:high, :], w_ref.at[low:high, :], w_sems.at[i])
        )
        copies[-1].start()
    mine = heads_mine * 128
    q_first = pl.multiple_of(rank * mine, 128)
    asking = [
        pltpu.make_async_copy(
            q_hbm.at[:, pl.ds(q_first, mine)], ask_ref.at[:, :mine], in_sems.at[2]
        )
    ]
    for i in range(2):
        asking.append(
            pltpu.make_async_copy(
                own_hbm.at[:, pl.ds(i * kv_width + first_column(rank), piece)],
                ask_ref.at[:, mine + i * piece : mine + (i + 1) * piece],
                in_sems.at[3 + i],
            )
        )
    for copy in asking:
        copy.start()
    gain_copy.wait()
    x_copy.wait()
    for slot in range(slots):
        rows_ref[slot * requests : (slot + 1) * requests, :] = x_ref[slot].astype(F32)
    squares = jnp.zeros((rows, 128), F32)
    for i, (low, high) in enumerate(chunks):
        parts = []
        for c in range(low, high, 128):
            width = min(128, high - c)
            x = rows_ref[:, c : c + width]
            gain = gain_ref[c : c + width].astype(F32).reshape(1, width)
            parts.append((x * gain).astype(BF16))
            x = x * x
            if width < 128:
                x = jnp.concatenate([x, jnp.zeros((rows, 128 - width), F32)], axis=1)
            squares = squares + x
        xg = parts[0] if len(parts) == 1 else jnp.concatenate(parts, axis=1)
        copies[i].wait()
        for n in range(0, 2 * kv_width, 512):
            part = jnp.dot(xg, w_ref[low:high, n : n + 512], preferred_element_type=F32)
            if i == 0:
                acc_ref[:, n : n + 512] = part
            else:
                acc_ref[:, n : n + 512] += part
    sq = column_to_row(jnp.sum(squares, axis=1, keepdims=True), 128)
    high, low = split_bf16(sq)
    tail = jnp.concatenate([high.astype(F32), low.astype(F32)], axis=0)
    fill = outs[1].shape[0] - rows - tail.shape[0]
    if fill:
        tail = jnp.concatenate([tail, jnp.zeros((fill, 128), F32)], axis=0)
    extra = jnp.concatenate([tail.astype(BF16)] * (2 * piece // 128), axis=1)
    for j in range(ranks):
        first = first_column(rank ^ j)
        outs[j][:rows, :piece] = acc_ref[:, pl.ds(first, piece)].astype(BF16)
        outs[j][:rows, piece:] = acc_ref[:, pl.ds(kv_width + first, piece)].astype(BF16)
        outs[j][rows:, :] = extra
    for copy in asking:
        copy.wait()


def project(x, gain, weight, query, own, ranks, group, kv_mine):
    slots, requests, feats = x.shape
    rows = slots * requests
    piece = kv_mine * 128
    extra = -(-2 * (rows // 128) // 8) * 8
    decoded, q_width = query.shape
    outs = pl.pallas_call(
        functools.partial(project_kernel, ranks, group),
        in_specs=[HBM] * 5,
        out_specs=[VMEM] * (ranks + 1),
        out_shape=[jax.ShapeDtypeStruct((rows + extra, 2 * piece), BF16)] * ranks
        + [jax.ShapeDtypeStruct((decoded, q_width // ranks + 2 * piece), BF16)],
        scratch_shapes=[
            pltpu.VMEM((feats,), BF16),
            pltpu.VMEM((slots, requests, feats), BF16),
            pltpu.VMEM((rows, feats), F32),
            pltpu.VMEM(weight.shape, BF16),
            pltpu.VMEM((rows, weight.shape[1]), F32),
            pltpu.SemaphoreType.DMA((5,)),
            pltpu.SemaphoreType.DMA((-(-feats // CHUNK),)),
        ],
        compiler_params=pltpu.CompilerParams(vmem_limit_bytes=56 * MIB),
        cost_estimate=pl.CostEstimate(
            flops=2 * rows * feats * weight.shape[1],
            bytes_accessed=2 * feats * weight.shape[1],
            transcendentals=0,
        ),
        name="project",
    )(gain, x, weight, query, own)
    return outs[:ranks], outs[ranks]


def resident_kernel(ranks, len_ref, q_ref, k_hbm, v_hbm, *rest):
    outs, rest = rest[:ranks], rest[ranks:]
    q_wide, q_all, k_buf, v_buf, o_all, m_all, l_all, s_all, sems = rest
    residents, positions, width = k_buf.shape
    copies = []
    for r in range(residents):
        copies.append(
            (
                pltpu.make_async_copy(k_hbm.at[r], k_buf.at[r], sems.at[0, r]),
                pltpu.make_async_copy(v_hbm.at[r], v_buf.at[r], sems.at[1, r]),
            )
        )
    rank = lax.axis_index("tp")
    held = [(rank == 0) | (len_ref[0, r] > rank * positions) for r in range(residents)]
    for r in range(residents):

        @pl.when(held[r])
        def _():
            for copy in copies[r]:
                copy.start()

    heads = q_ref.shape[0]
    kv_heads = width // 128
    group = heads // kv_heads
    pair_rows = 2 * group
    heads_mine = heads // ranks
    top_half = iota((pair_rows, 128), 0) < group
    position = rank * positions + iota((pair_rows, positions), 1)
    scale = F32(1.0) / jnp.sqrt(F32(128.0))
    diagonal = iota((heads, 128), 0) % heads_mine == iota((heads, 128), 1)

    def to_rows(column):
        spread = jnp.where(diagonal, column, 0.0)
        return jnp.sum(spread.reshape(ranks, heads_mine, 128), axis=1)

    q_wide[...] = q_ref[...].astype(F32)
    for r in range(residents):
        q_all[r] = q_wide[:, r, :].astype(BF16)
    def attend(r):
        valid = position < len_ref[0, r]
        copies[r][0].wait()
        weights = []
        for p in range(kv_heads // 2):
            rows = slice(p * pair_rows, (p + 1) * pair_rows)
            q = q_all[r, rows, :]
            zero = jnp.zeros_like(q)
            lhs = jnp.concatenate(
                [jnp.where(top_half, q, zero), jnp.where(top_half, zero, q)], axis=1
            )
            scores = lax.dot_general(
                lhs,
                k_buf[r, :, p * 256 : (p + 1) * 256],
                (((1,), (1,)), ((), ())),
                preferred_element_type=F32,
            )
            scores = jnp.where(valid, scores * scale, ABSENT)
            peak = jnp.max(scores, axis=1, keepdims=True).astype(BF16).astype(F32)
            weight = jnp.where(valid, jnp.exp(scores - peak), 0.0)
            m_all[r, rows, :] = peak
            l_all[r, rows, :] = jnp.sum(weight, axis=1, keepdims=True)
            weights.append(weight.astype(BF16))
        copies[r][1].wait()
        for p in range(kv_heads // 2):
            both = jnp.dot(
                weights[p], v_buf[r, :, p * 256 : (p + 1) * 256], preferred_element_type=F32
            )
            o_all[r, p * pair_rows : (p + 1) * pair_rows, :] = jnp.where(
                top_half, both[:, :128], both[:, 128:]
            )

    for r in range(residents):
        pl.when(held[r])(functools.partial(attend, r))

        @pl.when(jnp.logical_not(held[r]))
        def _():
            o_all[r] = jnp.zeros((heads, 128), F32)
            m_all[r] = jnp.full((heads, 1), ABSENT, F32)
            l_all[r] = jnp.zeros((heads, 1), F32)

    for r in range(residents):
        s_all[r, 0] = to_rows(m_all[r])
        high, low = split_bf16(to_rows(l_all[r]))
        s_all[r, 1] = high.astype(F32)
        s_all[r, 2] = low.astype(F32)
    filled = residents * (heads_mine + 3)
    for j in range(ranks):
        target = rank ^ j
        first = pl.multiple_of(target * heads_mine, heads_mine)
        parts = [o_all[r, pl.ds(first, heads_mine), :] for r in range(residents)]
        parts += [s_all[r, i, pl.ds(target, 1), :] for i in range(3) for r in range(residents)]
        if outs[j].shape[0] > filled:
            parts.append(jnp.zeros((outs[j].shape[0] - filled, 128), F32))
        outs[j][...] = jnp.concatenate(parts, axis=0).astype(BF16)


def attend_resident(lengths, queries, k_cache, v_cache, ranks):
    residents, positions, width = k_cache.shape
    heads = queries.shape[0]
    heads_mine = heads // ranks
    rows = -(-(residents * (heads_mine + 3)) // 16) * 16
    return pl.pallas_call(
        functools.partial(resident_kernel, ranks),
        in_specs=[SMEM, VMEM, HBM, HBM],
        out_specs=[VMEM] * ranks,
        out_shape=[jax.ShapeDtypeStruct((rows, 128), BF16)] * ranks,
        scratch_shapes=[
            pltpu.VMEM(queries.shape, F32),
            pltpu.VMEM((residents, heads, 128), BF16),
            pltpu.VMEM((residents, positions, width), BF16),
            pltpu.VMEM((residents, positions, width), BF16),
            pltpu.VMEM((residents, heads, 128), F32),
            pltpu.VMEM((residents, heads, 1), F32),
            pltpu.VMEM((residents, heads, 1), F32),
            pltpu.VMEM((residents, 3, ranks, 128), F32),
            pltpu.SemaphoreType.DMA((2, residents)),
        ],
        compiler_params=pltpu.CompilerParams(vmem_limit_bytes=56 * MIB),
        cost_estimate=pl.CostEstimate(
            flops=4 * residents * heads * positions * 128,
            bytes_accessed=4 * residents * positions * width,
            transcendentals=residents * heads * positions,
        ),
        name="attend_resident",
    )(lengths, queries, k_cache, v_cache)


def expand(own, rows):
    which = iota((rows, 128), 0) // (rows // own.shape[0])
    out = jnp.broadcast_to(own[0:1], (rows, 128))
    for h in range(1, own.shape[0]):
        out = jnp.where(which == h, own[h : h + 1], out)
    return out


def heads_of(line, heads_mine, kv_mine):
    per = heads_mine // kv_mine
    blocks = [line[:, c : c + 128] for c in range(0, line.shape[1], 128)]
    q = jnp.concatenate(blocks[:heads_mine], axis=0)
    k = blocks[heads_mine : heads_mine + kv_mine]
    v = blocks[heads_mine + kv_mine :]
    return (
        q,
        expand(jnp.concatenate(k, axis=0), heads_mine),
        expand(jnp.concatenate(v, axis=0), heads_mine),
    )


def moved_kernel(
    insts, ranks, residents, features, dest_ref, count_ref, gain_ref, cos_ref, sin_ref, *rest
):
    asks, rest = rest[: insts - 1], rest[insts - 1 :]
    pieces, rest = rest[:ranks], rest[ranks:]
    out_ref, place_out, ask_ref, q_ref, own_ref, line_ref = rest
    requests = out_ref.shape[0]
    tokens = cos_ref.shape[0]
    piece = pieces[0].shape[1] // 2
    kv_mine = piece // 128
    rows = q_ref.shape[0]
    heads_mine = rows // requests
    scale = F32(1.0) / jnp.sqrt(F32(128.0))
    here = lax.axis_index("inst")

    ask_row = iota(asks[0].shape, 0)
    row_request = iota((rows, tokens), 0) // heads_mine
    limit = jnp.zeros((rows, tokens), jnp.int32)
    for r in range(requests):
        dest = dest_ref[r, here]
        limit = jnp.where(row_request == r, count_ref[r, here], limit)
        place = jnp.int32(residents)
        for s in range(insts):
            for c in range(requests):
                place += jnp.where((dest_ref[c, s] == dest) & (here > s), 1, 0).astype(jnp.int32)
        for b in range(1, insts):

            @pl.when(here ^ b == dest)
            def _():
                ask = asks[b - 1][...].astype(F32)
                ask_ref[r : r + 1, :] = jnp.sum(
                    jnp.where(ask_row == place, ask, 0.0), axis=0, keepdims=True
                )

        at = slice(r * heads_mine, (r + 1) * heads_mine)
        q_ref[at, :], own_ref[0, at, :], own_ref[1, at, :] = heads_of(
            ask_ref[r : r + 1, :], heads_mine, kv_mine
        )
    places = jnp.full(place_out.shape, -1, jnp.int32)
    row = iota(place_out.shape, 0)
    place = jnp.int32(residents)
    for s in range(insts):
        for c in range(requests):
            mine = dest_ref[c, s] == here
            places = jnp.where((row == (here ^ s) * requests + c) & mine, place, places)
            place += jnp.where(mine, 1, 0).astype(jnp.int32)
    place_out[...] = places

    blocks = tokens // 128
    last = tokens + 2 * blocks
    tail = pieces[0][tokens:last, :128].astype(F32)
    for t in range(1, ranks):
        tail = tail + pieces[t][tokens:last, :128].astype(F32)
    squares = tail[:blocks] + tail[blocks:]
    squares = jnp.concatenate(
        [row_to_column(squares[b : b + 1], 128) for b in range(blocks)], axis=0
    )
    token_scale = lax.rsqrt(squares / features + EPS)

    def column_block(c):
        total = pieces[0][:tokens, c : c + 128].astype(F32)
        for t in range(1, ranks):
            total = total + pieces[t][:tokens, c : c + 128].astype(F32)
        return total * token_scale

    gain = gain_ref[...].astype(F32)
    q = q_ref[...]
    q16 = q.astype(BF16)
    which = iota((rows, tokens), 0) % heads_mine // (heads_mine // kv_mine)
    scores = None
    for h in range(kv_mine):
        key = column_block(h * 128)
        key = key * lax.rsqrt(jnp.mean(key * key, axis=1, keepdims=True) + EPS) * gain
        key = key * cos_ref[...] + pltpu.roll(key, 64, 1) * sin_ref[...]
        part = lax.dot_general(
            q16, key.astype(BF16), (((1,), (1,)), ((), ())), preferred_element_type=F32
        )
        scores = part if scores is None else jnp.where(which == h, part, scores)
    token = iota((rows, tokens), 1)
    valid = (token % requests == row_request) & (token // requests < limit)
    scores = jnp.where(valid, scores * scale, ABSENT)
    own_score = jnp.sum(q * own_ref[0], axis=1, keepdims=True) * scale
    top = jnp.maximum(jnp.max(scores, axis=1, keepdims=True), own_score)
    weights = jnp.where(valid, jnp.exp(scores - top), 0.0)
    own_weight = jnp.exp(own_score - top)
    total = jnp.sum(weights, axis=1, keepdims=True) + own_weight
    weights = weights.astype(BF16)
    summed = None
    for h in range(kv_mine):
        value = column_block(piece + h * 128).astype(BF16)
        part = jnp.dot(weights, value, preferred_element_type=F32)
        summed = part if summed is None else jnp.where(which[:, :128] == h, part, summed)
    summed = summed + own_weight.astype(BF16).astype(F32) * own_ref[1]
    result = summed / total
    for r in range(requests):
        for h in range(heads_mine):
            at = r * heads_mine + h
            line_ref[r : r + 1, h * 128 : (h + 1) * 128] = result[at : at + 1, :]
    out_ref[...] = line_ref[...].astype(BF16)


def attend_moved(dest, count, k_gain, cos, sin, asks, pieces, residents, heads_mine, features):
    requests, insts = dest.shape
    rows = requests * heads_mine
    return pl.pallas_call(
        functools.partial(moved_kernel, insts, len(pieces), residents, features),
        in_specs=[SMEM] * 2 + [VMEM] * (3 + len(asks) + len(pieces)),
        out_specs=[VMEM] * 2,
        out_shape=[
            jax.ShapeDtypeStruct((requests, heads_mine * 128), BF16),
            jax.ShapeDtypeStruct((insts * requests, 128), jnp.int32),
        ],
        scratch_shapes=[
            pltpu.VMEM((requests, asks[0].shape[1]), F32),
            pltpu.VMEM((rows, 128), F32),
            pltpu.VMEM((2, rows, 128), F32),
            pltpu.VMEM((requests, heads_mine * 128), F32),
        ],
        compiler_params=pltpu.CompilerParams(vmem_limit_bytes=16 * MIB),
        name="attend_moved",
    )(dest, count, k_gain, cos, sin, *asks, *pieces)


def combine_kernel(residents, kv_mine, ask_ref, *rest):
    refs, out_ref = rest[:-1], rest[-1]
    heads_mine = out_ref.shape[1] // 128
    scale = F32(1.0) / jnp.sqrt(F32(128.0))
    payloads = [ref[...].astype(F32) for ref in refs]
    at = residents * heads_mine
    ask = ask_ref[...].astype(F32)
    for r in range(residents):
        q, own_k, own_v = heads_of(ask[r : r + 1], heads_mine, kv_mine)
        own_score = jnp.sum(q * own_k, axis=1, keepdims=True) * scale
        peaks, totals = [], []
        for payload in payloads:
            stat = payload[at : at + 3 * residents]
            peaks.append(row_to_column(stat[r : r + 1], heads_mine))
            total = stat[residents + r : residents + r + 1]
            total = total + stat[2 * residents + r : 2 * residents + r + 1]
            totals.append(row_to_column(total, heads_mine))
        top = own_score
        for peak in peaks:
            top = jnp.maximum(top, peak)
        own_weight = jnp.exp(own_score - top)
        denom = own_weight
        numer = own_weight.astype(BF16).astype(F32) * own_v
        for peak, total, payload in zip(peaks, totals, payloads):
            keep = jnp.exp(peak - top)
            denom = denom + keep * total
            numer = numer + keep * payload[r * heads_mine : (r + 1) * heads_mine]
        result = numer / denom
        for h in range(heads_mine):
            out_ref[r : r + 1, h * 128 : (h + 1) * 128] = result[h : h + 1, :]


def combine_resident(ask, payloads, residents, heads_mine, kv_mine):
    return pl.pallas_call(
        functools.partial(combine_kernel, residents, kv_mine),
        in_specs=[VMEM] * (1 + len(payloads)),
        out_specs=VMEM,
        out_shape=jax.ShapeDtypeStruct((residents, heads_mine * 128), F32),
        compiler_params=pltpu.CompilerParams(vmem_limit_bytes=8 * MIB),
        name="combine_resident",
    )(ask, *payloads)


def finish_kernel(kept_ref, place_ref, *rest):
    moved, out_ref = rest[:-1], rest[-1]
    residents = kept_ref.shape[0]
    decoded, width = out_ref.shape
    requests = decoded - residents
    row = iota((decoded, 128), 0)
    arrived = [ref[...].astype(F32) for ref in moved]
    for c in range(0, width, 128):
        kept = kept_ref[:, c : c + 128]
        line = jnp.concatenate([kept, jnp.zeros((requests, 128), F32)], axis=0)
        for b in range(len(moved)):
            for i in range(requests):
                at = (b + 1) * requests + i
                line = jnp.where(
                    place_ref[at : at + 1, :] == row, arrived[b][i : i + 1, c : c + 128], line
                )
        out_ref[:, c : c + 128] = line.astype(BF16)


def finish(kept, places, moved, requests):
    residents, width = kept.shape
    return pl.pallas_call(
        finish_kernel,
        in_specs=[VMEM] * (2 + len(moved)),
        out_specs=VMEM,
        out_shape=jax.ShapeDtypeStruct((residents + requests, width), BF16),
        compiler_params=pltpu.CompilerParams(vmem_limit_bytes=8 * MIB),
        name="finish",
    )(kept, places, *moved)


def swapped(x, axis, j, n):
    return lax.ppermute(x, axis, [(i, i ^ j) for i in range(n)])


def rotation(slots, requests, head_size):
    half = head_size // 2
    freq = THETA ** (-np.arange(half) * 2.0 / head_size)
    angle = np.repeat(np.arange(slots), requests)[:, None] * freq[None, :]
    cos, sin = np.cos(angle), np.sin(angle)
    return (
        np.concatenate([cos, cos], axis=1).astype(np.float32),
        np.concatenate([-sin, sin], axis=1).astype(np.float32),
    )


def per_device(
    mig_hidden,
    mig_dest,
    mig_count,
    attn_gain,
    kv_weight,
    k_gain,
    query,
    new_kv,
    k_cache,
    v_cache,
    lengths,
):
    insts = lax.axis_size("inst")
    ranks = lax.axis_size("tp")
    head_size = k_gain.shape[0]
    slots, requests, feats = mig_hidden.shape[1:]
    residents = k_cache.shape[1]
    heads = query.shape[2] // head_size
    kv_heads = kv_weight.shape[1] // 2 // head_size
    heads_mine = heads // ranks
    group = heads // kv_heads
    kv_mine = max(1, heads_mine // group)

    pieces, ask = project(
        mig_hidden[0], attn_gain, kv_weight, query[0], new_kv[0], ranks, group, kv_mine
    )
    order = sorted(range(2, ranks), key=lambda j: (abs(j - ranks // 2), j))
    asks = [swapped(ask, "inst", b, insts) for b in range(1, insts)]
    sent = [swapped(pieces[j], "tp", j, ranks) for j in order]
    asks[0], near = lax.optimization_barrier((asks[0], pieces[1]))
    pieces = [pieces[0]] + sent + [swapped(near, "tp", 1, ranks)]
    queries = jnp.transpose(query[0].reshape(query.shape[1], heads, head_size), (1, 0, 2))
    payloads = attend_resident(lengths, queries, k_cache[0], v_cache[0], ranks)
    asks, payloads = lax.optimization_barrier((asks, payloads))
    order = sorted(range(1, ranks), key=lambda j: (j > 1, -j))
    received = [payloads[0]] + [swapped(payloads[j], "tp", j, ranks) for j in order]
    cos, sin = rotation(slots, requests, head_size)
    moved, places = attend_moved(
        mig_dest.T,
        mig_count.T,
        k_gain.reshape(1, head_size),
        cos,
        sin,
        asks,
        pieces,
        residents,
        heads_mine,
        feats * ranks,
    )
    kept = combine_resident(ask, received, residents, heads_mine, kv_mine)
    moved = [swapped(moved, "inst", b, insts) for b in reversed(range(1, insts))][::-1]
    return finish(kept, places, moved, requests)[None]


def solution(mesh):
    placed = (
        P(("group", "inst"), None, None, "tp"),
        P("group", None),
        P("group", None),
        P("tp"),
        P("tp", None),
        P(),
        P(("group", "inst"), None, None),
        P(("group", "inst"), None, None),
        P(("group", "inst"), None, "tp", None),
        P(("group", "inst"), None, "tp", None),
        P(("group", "inst"), None),
    )
    return jax.shard_map(
        per_device,
        mesh=mesh,
        in_specs=placed,
        out_specs=P(("group", "inst"), None, "tp"),
        check_vma=False,
    )
```

```python
import functools

import jax
import jax.numpy as jnp
import numpy as np
from jax import lax
from jax.experimental import pallas as pl
from jax.experimental.pallas import tpu as pltpu
from jax.sharding import PartitionSpec as P

EPS = 1e-06
THETA = 1000000.0
ABSENT = -1e30
F32 = jnp.float32
BF16 = jnp.bfloat16
MIB = 1024 * 1024
CHUNK = 256

VMEM = pl.BlockSpec(memory_space=pltpu.VMEM)
SMEM = pl.BlockSpec(memory_space=pltpu.SMEM)
HBM = pl.BlockSpec(memory_space=pltpu.HBM)


def iota(shape, dim):
    return lax.broadcasted_iota(jnp.int32, shape, dim)


def div(x, n):
    return lax.shift_right_logical(x, n.bit_length() - 1) if n & (n - 1) == 0 else x // n


def mod(x, n):
    return x & (n - 1) if n & (n - 1) == 0 else x % n


def column_to_row(column, period):
    n = column.shape[0]
    spread = jnp.where(mod(iota((n, 128), 0), period) == iota((n, 128), 1), column, 0.0)
    return jnp.sum(spread.reshape(n // period, period, 128), axis=1)


def row_to_column(row, n):
    return jnp.sum(
        jnp.where(iota((n, 128), 0) == iota((n, 128), 1), row, 0.0), axis=1, keepdims=True
    )


def split_bf16(x):
    high = x.astype(BF16)
    return high, (x - high.astype(F32)).astype(BF16)


def project_kernel(ranks, group, gain_hbm, x_hbm, w_hbm, q_hbm, own_hbm, *rest):
    outs, ask_ref = rest[:ranks], rest[ranks]
    gain_ref, x_ref, rows_ref, w_ref, acc_ref, in_sems, w_sems = rest[ranks + 1 :]
    slots, requests, feats = x_ref.shape
    rows = slots * requests
    piece = outs[0].shape[1] // 2
    kv_width = w_hbm.shape[1] // 2
    heads_mine = kv_width // 128 * group // ranks
    rank = lax.axis_index("tp")

    def first_column(target):
        return pl.multiple_of(target * heads_mine // group * 128, 128)

    gain_copy = pltpu.make_async_copy(gain_hbm, gain_ref, in_sems.at[0])
    gain_copy.start()
    x_copy = pltpu.make_async_copy(x_hbm, x_ref, in_sems.at[1])
    x_copy.start()
    cuts = list(range(0, feats, CHUNK)) + [feats]
    chunks = list(zip(cuts[:-1], cuts[1:]))
    copies = []
    for i, (low, high) in enumerate(chunks):
        copies.append(
            pltpu.make_async_copy(w_hbm.at[low:high, :], w_ref.at[low:high, :], w_sems.at[i])
        )
        copies[-1].start()
    mine = heads_mine * 128
    q_first = pl.multiple_of(rank * mine, 128)
    asking = [
        pltpu.make_async_copy(
            q_hbm.at[:, pl.ds(q_first, mine)], ask_ref.at[:, :mine], in_sems.at[2]
        )
    ]
    for i in range(2):
        asking.append(
            pltpu.make_async_copy(
                own_hbm.at[:, pl.ds(i * kv_width + first_column(rank), piece)],
                ask_ref.at[:, mine + i * piece : mine + (i + 1) * piece],
                in_sems.at[3 + i],
            )
        )
    for copy in asking:
        copy.start()
    gain_copy.wait()
    x_copy.wait()
    for slot in range(slots):
        rows_ref[slot * requests : (slot + 1) * requests, :] = x_ref[slot].astype(F32)
    squares = jnp.zeros((rows, 128), F32)
    for i, (low, high) in enumerate(chunks):
        parts = []
        for c in range(low, high, 128):
            width = min(128, high - c)
            x = rows_ref[:, c : c + width]
            gain = gain_ref[c : c + width].astype(F32).reshape(1, width)
            parts.append((x * gain).astype(BF16))
            x = x * x
            if width < 128:
                x = jnp.concatenate([x, jnp.zeros((rows, 128 - width), F32)], axis=1)
            squares = squares + x
        xg = parts[0] if len(parts) == 1 else jnp.concatenate(parts, axis=1)
        copies[i].wait()
        for n in range(0, 2 * kv_width, 512):
            part = jnp.dot(xg, w_ref[low:high, n : n + 512], preferred_element_type=F32)
            if i == 0:
                acc_ref[:, n : n + 512] = part
            else:
                acc_ref[:, n : n + 512] += part
    sq = column_to_row(jnp.sum(squares, axis=1, keepdims=True), 128)
    high, low = split_bf16(sq)
    tail = jnp.concatenate([high.astype(F32), low.astype(F32)], axis=0)
    fill = outs[1].shape[0] - rows - tail.shape[0]
    if fill:
        tail = jnp.concatenate([tail, jnp.zeros((fill, 128), F32)], axis=0)
    extra = jnp.concatenate([tail.astype(BF16)] * (2 * piece // 128), axis=1)
    for j in range(ranks):
        first = first_column(rank ^ j)
        outs[j][:rows, :piece] = acc_ref[:, pl.ds(first, piece)].astype(BF16)
        outs[j][:rows, piece:] = acc_ref[:, pl.ds(kv_width + first, piece)].astype(BF16)
        outs[j][rows:, :] = extra
    for copy in asking:
        copy.wait()


def project(x, gain, weight, query, own, ranks, group, kv_mine):
    slots, requests, feats = x.shape
    rows = slots * requests
    piece = kv_mine * 128
    extra = -(-2 * (rows // 128) // 8) * 8
    decoded, q_width = query.shape
    outs = pl.pallas_call(
        functools.partial(project_kernel, ranks, group),
        in_specs=[HBM] * 5,
        out_specs=[VMEM] * (ranks + 1),
        out_shape=[jax.ShapeDtypeStruct((rows + extra, 2 * piece), BF16)] * ranks
        + [jax.ShapeDtypeStruct((decoded, q_width // ranks + 2 * piece), BF16)],
        scratch_shapes=[
            pltpu.VMEM((feats,), BF16),
            pltpu.VMEM((slots, requests, feats), BF16),
            pltpu.VMEM((rows, feats), F32),
            pltpu.VMEM(weight.shape, BF16),
            pltpu.VMEM((rows, weight.shape[1]), F32),
            pltpu.SemaphoreType.DMA((5,)),
            pltpu.SemaphoreType.DMA((-(-feats // CHUNK),)),
        ],
        compiler_params=pltpu.CompilerParams(vmem_limit_bytes=56 * MIB),
        cost_estimate=pl.CostEstimate(
            flops=2 * rows * feats * weight.shape[1],
            bytes_accessed=2 * feats * weight.shape[1],
            transcendentals=0,
        ),
        name="project",
    )(gain, x, weight, query, own)
    return outs[:ranks], outs[ranks]


def resident_kernel(ranks, len_ref, q_ref, k_hbm, v_hbm, *rest):
    outs, rest = rest[:ranks], rest[ranks:]
    q_wide, q_all, k_buf, v_buf, o_all, m_all, l_all, s_all, sems = rest
    residents, positions, width = k_buf.shape
    copies = []
    for r in range(residents):
        copies.append(
            (
                pltpu.make_async_copy(k_hbm.at[r], k_buf.at[r], sems.at[0, r]),
                pltpu.make_async_copy(v_hbm.at[r], v_buf.at[r], sems.at[1, r]),
            )
        )
    rank = lax.axis_index("tp")
    held = [(rank == 0) | (len_ref[0, r] > rank * positions) for r in range(residents)]
    for r in range(residents):

        @pl.when(held[r])
        def _():
            for copy in copies[r]:
                copy.start()

    heads = q_ref.shape[0]
    kv_heads = width // 128
    group = heads // kv_heads
    pair_rows = 2 * group
    heads_mine = heads // ranks
    top_half = iota((pair_rows, 128), 0) < group
    position = rank * positions + iota((pair_rows, positions), 1)
    scale = F32(1.0) / jnp.sqrt(F32(128.0))
    diagonal = mod(iota((heads, 128), 0), heads_mine) == iota((heads, 128), 1)

    def to_rows(column):
        spread = jnp.where(diagonal, column, 0.0)
        return jnp.sum(spread.reshape(ranks, heads_mine, 128), axis=1)

    q_wide[...] = q_ref[...].astype(F32)
    for r in range(residents):
        q_all[r] = q_wide[:, r, :].astype(BF16)
    def attend(r):
        valid = position < len_ref[0, r]
        copies[r][0].wait()
        weights = []
        for p in range(kv_heads // 2):
            rows = slice(p * pair_rows, (p + 1) * pair_rows)
            q = q_all[r, rows, :]
            zero = jnp.zeros_like(q)
            lhs = jnp.concatenate(
                [jnp.where(top_half, q, zero), jnp.where(top_half, zero, q)], axis=1
            )
            scores = lax.dot_general(
                lhs,
                k_buf[r, :, p * 256 : (p + 1) * 256],
                (((1,), (1,)), ((), ())),
                preferred_element_type=F32,
            )
            scores = jnp.where(valid, scores * scale, ABSENT)
            peak = jnp.max(scores, axis=1, keepdims=True).astype(BF16).astype(F32)
            weight = jnp.where(valid, jnp.exp(scores - peak), 0.0)
            m_all[r, rows, :] = peak
            l_all[r, rows, :] = jnp.sum(weight, axis=1, keepdims=True)
            weights.append(weight.astype(BF16))
        copies[r][1].wait()
        for p in range(kv_heads // 2):
            both = jnp.dot(
                weights[p], v_buf[r, :, p * 256 : (p + 1) * 256], preferred_element_type=F32
            )
            o_all[r, p * pair_rows : (p + 1) * pair_rows, :] = jnp.where(
                top_half, both[:, :128], both[:, 128:]
            )

    for r in range(residents):
        pl.when(held[r])(functools.partial(attend, r))

        @pl.when(jnp.logical_not(held[r]))
        def _():
            o_all[r] = jnp.zeros((heads, 128), F32)
            m_all[r] = jnp.full((heads, 1), ABSENT, F32)
            l_all[r] = jnp.zeros((heads, 1), F32)

    for r in range(residents):
        s_all[r, 0] = to_rows(m_all[r])
        high, low = split_bf16(to_rows(l_all[r]))
        s_all[r, 1] = high.astype(F32)
        s_all[r, 2] = low.astype(F32)
    filled = residents * (heads_mine + 3)
    for j in range(ranks):
        target = rank ^ j
        first = pl.multiple_of(target * heads_mine, heads_mine)
        parts = [o_all[r, pl.ds(first, heads_mine), :] for r in range(residents)]
        parts += [s_all[r, i, pl.ds(target, 1), :] for i in range(3) for r in range(residents)]
        if outs[j].shape[0] > filled:
            parts.append(jnp.zeros((outs[j].shape[0] - filled, 128), F32))
        outs[j][...] = jnp.concatenate(parts, axis=0).astype(BF16)


def attend_resident(lengths, queries, k_cache, v_cache, ranks):
    residents, positions, width = k_cache.shape
    heads = queries.shape[0]
    heads_mine = heads // ranks
    rows = -(-(residents * (heads_mine + 3)) // 16) * 16
    return pl.pallas_call(
        functools.partial(resident_kernel, ranks),
        in_specs=[SMEM, VMEM, HBM, HBM],
        out_specs=[VMEM] * ranks,
        out_shape=[jax.ShapeDtypeStruct((rows, 128), BF16)] * ranks,
        scratch_shapes=[
            pltpu.VMEM(queries.shape, F32),
            pltpu.VMEM((residents, heads, 128), BF16),
            pltpu.VMEM((residents, positions, width), BF16),
            pltpu.VMEM((residents, positions, width), BF16),
            pltpu.VMEM((residents, heads, 128), F32),
            pltpu.VMEM((residents, heads, 1), F32),
            pltpu.VMEM((residents, heads, 1), F32),
            pltpu.VMEM((residents, 3, ranks, 128), F32),
            pltpu.SemaphoreType.DMA((2, residents)),
        ],
        compiler_params=pltpu.CompilerParams(vmem_limit_bytes=56 * MIB),
        cost_estimate=pl.CostEstimate(
            flops=4 * residents * heads * positions * 128,
            bytes_accessed=4 * residents * positions * width,
            transcendentals=residents * heads * positions,
        ),
        name="attend_resident",
    )(lengths, queries, k_cache, v_cache)


def expand(own, rows):
    which = div(iota((rows, 128), 0), rows // own.shape[0])
    out = jnp.broadcast_to(own[0:1], (rows, 128))
    for h in range(1, own.shape[0]):
        out = jnp.where(which == h, own[h : h + 1], out)
    return out


def heads_of(line, heads_mine, kv_mine):
    per = heads_mine // kv_mine
    blocks = [line[:, c : c + 128] for c in range(0, line.shape[1], 128)]
    q = jnp.concatenate(blocks[:heads_mine], axis=0)
    k = blocks[heads_mine : heads_mine + kv_mine]
    v = blocks[heads_mine + kv_mine :]
    return (
        q,
        expand(jnp.concatenate(k, axis=0), heads_mine),
        expand(jnp.concatenate(v, axis=0), heads_mine),
    )


def moved_kernel(
    insts, ranks, residents, features, dest_ref, count_ref, gain_ref, cos_ref, sin_ref, *rest
):
    asks, rest = rest[: insts - 1], rest[insts - 1 :]
    pieces, rest = rest[:ranks], rest[ranks:]
    out_ref, place_out, q_ref, own_ref, line_ref = rest
    requests = out_ref.shape[0]
    tokens = cos_ref.shape[0]
    piece = pieces[0].shape[1] // 2
    kv_mine = piece // 128
    rows = q_ref.shape[0]
    heads_mine = rows // requests
    scale = F32(1.0) / jnp.sqrt(F32(128.0))
    here = lax.axis_index("inst")

    arrived = [ask[...].astype(F32) for ask in asks]
    ask_row = iota(asks[0].shape, 0)
    row_request = div(iota((rows, tokens), 0), heads_mine)
    limit = jnp.zeros((rows, tokens), jnp.int32)
    for r in range(requests):
        dest = dest_ref[r, here]
        limit = jnp.where(row_request == r, count_ref[r, here], limit)
        place = jnp.int32(residents)
        for s in range(insts):
            for c in range(requests):
                place += jnp.where((dest_ref[c, s] == dest) & (here > s), 1, 0).astype(jnp.int32)
        line = None
        for b in range(1, insts):
            wanted = jnp.where(here ^ b == dest, place, -1)
            part = jnp.sum(jnp.where(ask_row == wanted, arrived[b - 1], 0.0), axis=0, keepdims=True)
            line = part if line is None else line + part
        at = slice(r * heads_mine, (r + 1) * heads_mine)
        q_ref[at, :], own_ref[0, at, :], own_ref[1, at, :] = heads_of(line, heads_mine, kv_mine)
    places = jnp.full(place_out.shape, -1, jnp.int32)
    row = iota(place_out.shape, 0)
    place = jnp.int32(residents)
    for s in range(insts):
        for c in range(requests):
            mine = dest_ref[c, s] == here
            places = jnp.where((row == (here ^ s) * requests + c) & mine, place, places)
            place += jnp.where(mine, 1, 0).astype(jnp.int32)
    place_out[...] = places

    blocks = tokens // 128
    last = tokens + 2 * blocks
    tail = pieces[0][tokens:last, :128].astype(F32)
    for t in range(1, ranks):
        tail = tail + pieces[t][tokens:last, :128].astype(F32)
    squares = tail[:blocks] + tail[blocks:]
    squares = jnp.concatenate(
        [row_to_column(squares[b : b + 1], 128) for b in range(blocks)], axis=0
    )
    token_scale = lax.rsqrt(squares / features + EPS)

    def column_block(c):
        total = pieces[0][:tokens, c : c + 128].astype(F32)
        for t in range(1, ranks):
            total = total + pieces[t][:tokens, c : c + 128].astype(F32)
        return total * token_scale

    gain = gain_ref[...].astype(F32)
    q = q_ref[...]
    q16 = q.astype(BF16)
    which = div(mod(iota((rows, tokens), 0), heads_mine), heads_mine // kv_mine)
    scores = None
    for h in range(kv_mine):
        key = column_block(h * 128)
        key = key * lax.rsqrt(jnp.mean(key * key, axis=1, keepdims=True) + EPS) * gain
        key = key * cos_ref[...] + pltpu.roll(key, 64, 1) * sin_ref[...]
        part = lax.dot_general(
            q16, key.astype(BF16), (((1,), (1,)), ((), ())), preferred_element_type=F32
        )
        scores = part if scores is None else jnp.where(which == h, part, scores)
    token = iota((rows, tokens), 1)
    valid = (mod(token, requests) == row_request) & (div(token, requests) < limit)
    scores = jnp.where(valid, scores * scale, ABSENT)
    own_score = jnp.sum(q * own_ref[0], axis=1, keepdims=True) * scale
    top = jnp.maximum(jnp.max(scores, axis=1, keepdims=True), own_score)
    weights = jnp.where(valid, jnp.exp(scores - top), 0.0)
    own_weight = jnp.exp(own_score - top)
    total = jnp.sum(weights, axis=1, keepdims=True) + own_weight
    weights = weights.astype(BF16)
    summed = None
    for h in range(kv_mine):
        value = column_block(piece + h * 128).astype(BF16)
        part = jnp.dot(weights, value, preferred_element_type=F32)
        summed = part if summed is None else jnp.where(which[:, :128] == h, part, summed)
    summed = summed + own_weight.astype(BF16).astype(F32) * own_ref[1]
    result = summed / total
    for r in range(requests):
        for h in range(heads_mine):
            at = r * heads_mine + h
            line_ref[r : r + 1, h * 128 : (h + 1) * 128] = result[at : at + 1, :]
    out_ref[...] = line_ref[...].astype(BF16)


def attend_moved(dest, count, k_gain, cos, sin, asks, pieces, residents, heads_mine, features):
    requests, insts = dest.shape
    rows = requests * heads_mine
    return pl.pallas_call(
        functools.partial(moved_kernel, insts, len(pieces), residents, features),
        in_specs=[SMEM] * 2 + [VMEM] * (3 + len(asks) + len(pieces)),
        out_specs=[VMEM] * 2,
        out_shape=[
            jax.ShapeDtypeStruct((requests, heads_mine * 128), BF16),
            jax.ShapeDtypeStruct((insts * requests, 128), jnp.int32),
        ],
        scratch_shapes=[
            pltpu.VMEM((rows, 128), F32),
            pltpu.VMEM((2, rows, 128), F32),
            pltpu.VMEM((requests, heads_mine * 128), F32),
        ],
        compiler_params=pltpu.CompilerParams(vmem_limit_bytes=16 * MIB),
        name="attend_moved",
    )(dest, count, k_gain, cos, sin, *asks, *pieces)


def combine_kernel(residents, kv_mine, ask_ref, *rest):
    refs, out_ref = rest[:-1], rest[-1]
    heads_mine = out_ref.shape[1] // 128
    scale = F32(1.0) / jnp.sqrt(F32(128.0))
    payloads = [ref[...].astype(F32) for ref in refs]
    at = residents * heads_mine
    ask = ask_ref[...].astype(F32)
    for r in range(residents):
        q, own_k, own_v = heads_of(ask[r : r + 1], heads_mine, kv_mine)
        own_score = jnp.sum(q * own_k, axis=1, keepdims=True) * scale
        peaks, totals = [], []
        for payload in payloads:
            stat = payload[at : at + 3 * residents]
            peaks.append(row_to_column(stat[r : r + 1], heads_mine))
            total = stat[residents + r : residents + r + 1]
            total = total + stat[2 * residents + r : 2 * residents + r + 1]
            totals.append(row_to_column(total, heads_mine))
        top = own_score
        for peak in peaks:
            top = jnp.maximum(top, peak)
        own_weight = jnp.exp(own_score - top)
        denom = own_weight
        numer = own_weight.astype(BF16).astype(F32) * own_v
        for peak, total, payload in zip(peaks, totals, payloads):
            keep = jnp.exp(peak - top)
            denom = denom + keep * total
            numer = numer + keep * payload[r * heads_mine : (r + 1) * heads_mine]
        result = numer / denom
        for h in range(heads_mine):
            out_ref[r : r + 1, h * 128 : (h + 1) * 128] = result[h : h + 1, :]


def combine_resident(ask, payloads, residents, heads_mine, kv_mine):
    return pl.pallas_call(
        functools.partial(combine_kernel, residents, kv_mine),
        in_specs=[VMEM] * (1 + len(payloads)),
        out_specs=VMEM,
        out_shape=jax.ShapeDtypeStruct((residents, heads_mine * 128), F32),
        compiler_params=pltpu.CompilerParams(vmem_limit_bytes=8 * MIB),
        name="combine_resident",
    )(ask, *payloads)


def finish_kernel(kept_ref, place_ref, *rest):
    moved, out_ref = rest[:-1], rest[-1]
    residents = kept_ref.shape[0]
    decoded, width = out_ref.shape
    requests = decoded - residents
    row = iota((decoded, 128), 0)
    arrived = [ref[...].astype(F32) for ref in moved]
    for c in range(0, width, 128):
        kept = kept_ref[:, c : c + 128]
        line = jnp.concatenate([kept, jnp.zeros((requests, 128), F32)], axis=0)
        for b in range(len(moved)):
            for i in range(requests):
                at = (b + 1) * requests + i
                line = jnp.where(
                    place_ref[at : at + 1, :] == row, arrived[b][i : i + 1, c : c + 128], line
                )
        out_ref[:, c : c + 128] = line.astype(BF16)


def finish(kept, places, moved, requests):
    residents, width = kept.shape
    return pl.pallas_call(
        finish_kernel,
        in_specs=[VMEM] * (2 + len(moved)),
        out_specs=VMEM,
        out_shape=jax.ShapeDtypeStruct((residents + requests, width), BF16),
        compiler_params=pltpu.CompilerParams(vmem_limit_bytes=8 * MIB),
        name="finish",
    )(kept, places, *moved)


def swapped(x, axis, j, n):
    return lax.ppermute(x, axis, [(i, i ^ j) for i in range(n)])


def rotation(slots, requests, head_size):
    half = head_size // 2
    freq = THETA ** (-np.arange(half) * 2.0 / head_size)
    angle = np.repeat(np.arange(slots), requests)[:, None] * freq[None, :]
    cos, sin = np.cos(angle), np.sin(angle)
    return (
        np.concatenate([cos, cos], axis=1).astype(np.float32),
        np.concatenate([-sin, sin], axis=1).astype(np.float32),
    )


def per_device(
    mig_hidden,
    mig_dest,
    mig_count,
    attn_gain,
    kv_weight,
    k_gain,
    query,
    new_kv,
    k_cache,
    v_cache,
    lengths,
):
    insts = lax.axis_size("inst")
    ranks = lax.axis_size("tp")
    head_size = k_gain.shape[0]
    slots, requests, feats = mig_hidden.shape[1:]
    residents = k_cache.shape[1]
    heads = query.shape[2] // head_size
    kv_heads = kv_weight.shape[1] // 2 // head_size
    heads_mine = heads // ranks
    group = heads // kv_heads
    kv_mine = max(1, heads_mine // group)

    pieces, ask = project(
        mig_hidden[0], attn_gain, kv_weight, query[0], new_kv[0], ranks, group, kv_mine
    )
    order = sorted(range(2, ranks), key=lambda j: (abs(j - ranks // 2), j))
    asks = [swapped(ask, "inst", b, insts) for b in range(1, insts)]
    sent = [swapped(pieces[j], "tp", j, ranks) for j in order]
    asks[0], near = lax.optimization_barrier((asks[0], pieces[1]))
    pieces = [pieces[0]] + sent + [swapped(near, "tp", 1, ranks)]
    queries = jnp.transpose(query[0].reshape(query.shape[1], heads, head_size), (1, 0, 2))
    payloads = attend_resident(lengths, queries, k_cache[0], v_cache[0], ranks)
    asks, payloads = lax.optimization_barrier((asks, payloads))
    order = sorted(range(1, ranks), key=lambda j: (j > 1, -j))
    received = [payloads[0]] + [swapped(payloads[j], "tp", j, ranks) for j in order]
    cos, sin = rotation(slots, requests, head_size)
    moved, places = attend_moved(
        mig_dest.T,
        mig_count.T,
        k_gain.reshape(1, head_size),
        cos,
        sin,
        asks,
        pieces,
        residents,
        heads_mine,
        feats * ranks,
    )
    kept = combine_resident(ask, received, residents, heads_mine, kv_mine)
    moved = [swapped(moved, "inst", b, insts) for b in reversed(range(1, insts))][::-1]
    return finish(kept, places, moved, requests)[None]


def solution(mesh):
    placed = (
        P(("group", "inst"), None, None, "tp"),
        P("group", None),
        P("group", None),
        P("tp"),
        P("tp", None),
        P(),
        P(("group", "inst"), None, None),
        P(("group", "inst"), None, None),
        P(("group", "inst"), None, "tp", None),
        P(("group", "inst"), None, "tp", None),
        P(("group", "inst"), None),
    )
    return jax.shard_map(
        per_device,
        mesh=mesh,
        in_specs=placed,
        out_specs=P(("group", "inst"), None, "tp"),
        check_vma=False,
    )
```

```python
import functools

import jax
import jax.numpy as jnp
import numpy as np
from jax import lax
from jax.experimental import pallas as pl
from jax.experimental.pallas import tpu as pltpu
from jax.sharding import PartitionSpec as P

EPS = 1e-06
THETA = 1000000.0
ABSENT = -1e30
F32 = jnp.float32
BF16 = jnp.bfloat16
MIB = 1024 * 1024
CHUNK = 512

VMEM = pl.BlockSpec(memory_space=pltpu.VMEM)
SMEM = pl.BlockSpec(memory_space=pltpu.SMEM)
HBM = pl.BlockSpec(memory_space=pltpu.HBM)


def iota(shape, dim):
    return lax.broadcasted_iota(jnp.int32, shape, dim)


def column_to_row(column, period):
    n = column.shape[0]
    spread = jnp.where(iota((n, 128), 0) % period == iota((n, 128), 1), column, 0.0)
    return jnp.sum(spread.reshape(n // period, period, 128), axis=1)


def row_to_column(row, n):
    return jnp.sum(
        jnp.where(iota((n, 128), 0) == iota((n, 128), 1), row, 0.0), axis=1, keepdims=True
    )


def split_bf16(x):
    high = x.astype(BF16)
    return high, (x - high.astype(F32)).astype(BF16)


def project_kernel(ranks, group, gain_hbm, x_hbm, w_hbm, q_hbm, own_hbm, *rest):
    outs, ask_ref = rest[:ranks], rest[ranks]
    gain_ref, x_ref, rows_ref, w_ref, acc_ref, in_sems, w_sems = rest[ranks + 1 :]
    slots, requests, feats = x_ref.shape
    rows = slots * requests
    piece = outs[0].shape[1] // 2
    kv_width = w_hbm.shape[1] // 2
    heads_mine = kv_width // 128 * group // ranks
    rank = lax.axis_index("tp")

    def first_column(target):
        return pl.multiple_of(target * heads_mine // group * 128, 128)

    gain_copy = pltpu.make_async_copy(gain_hbm, gain_ref, in_sems.at[0])
    gain_copy.start()
    x_copy = pltpu.make_async_copy(x_hbm, x_ref, in_sems.at[1])
    x_copy.start()
    cuts = list(range(0, feats, CHUNK)) + [feats]
    chunks = list(zip(cuts[:-1], cuts[1:]))
    copies = []
    for i, (low, high) in enumerate(chunks):
        copies.append(
            pltpu.make_async_copy(w_hbm.at[low:high, :], w_ref.at[low:high, :], w_sems.at[i])
        )
        copies[-1].start()
    mine = heads_mine * 128
    q_first = pl.multiple_of(rank * mine, 128)
    asking = [
        pltpu.make_async_copy(
            q_hbm.at[:, pl.ds(q_first, mine)], ask_ref.at[:, :mine], in_sems.at[2]
        )
    ]
    for i in range(2):
        asking.append(
            pltpu.make_async_copy(
                own_hbm.at[:, pl.ds(i * kv_width + first_column(rank), piece)],
                ask_ref.at[:, mine + i * piece : mine + (i + 1) * piece],
                in_sems.at[3 + i],
            )
        )
    for copy in asking:
        copy.start()
    gain_copy.wait()
    x_copy.wait()
    for slot in range(slots):
        rows_ref[slot * requests : (slot + 1) * requests, :] = x_ref[slot].astype(F32)
    squares = jnp.zeros((rows, 128), F32)
    for i, (low, high) in enumerate(chunks):
        parts = []
        for c in range(low, high, 128):
            width = min(128, high - c)
            x = rows_ref[:, c : c + width]
            gain = gain_ref[c : c + width].astype(F32).reshape(1, width)
            parts.append((x * gain).astype(BF16))
            x = x * x
            if width < 128:
                x = jnp.concatenate([x, jnp.zeros((rows, 128 - width), F32)], axis=1)
            squares = squares + x
        xg = parts[0] if len(parts) == 1 else jnp.concatenate(parts, axis=1)
        copies[i].wait()
        for n in range(0, 2 * kv_width, 512):
            part = jnp.dot(xg, w_ref[low:high, n : n + 512], preferred_element_type=F32)
            if i == 0:
                acc_ref[:, n : n + 512] = part
            else:
                acc_ref[:, n : n + 512] += part
    sq = column_to_row(jnp.sum(squares, axis=1, keepdims=True), 128)
    high, low = split_bf16(sq)
    tail = jnp.concatenate([high.astype(F32), low.astype(F32)], axis=0)
    fill = outs[1].shape[0] - rows - tail.shape[0]
    if fill:
        tail = jnp.concatenate([tail, jnp.zeros((fill, 128), F32)], axis=0)
    extra = jnp.concatenate([tail.astype(BF16)] * (2 * piece // 128), axis=1)
    for j in range(ranks):
        first = first_column(rank ^ j)
        outs[j][:rows, :piece] = acc_ref[:, pl.ds(first, piece)].astype(BF16)
        outs[j][:rows, piece:] = acc_ref[:, pl.ds(kv_width + first, piece)].astype(BF16)
        outs[j][rows:, :] = extra
    for copy in asking:
        copy.wait()


def project(x, gain, weight, query, own, ranks, group, kv_mine):
    slots, requests, feats = x.shape
    rows = slots * requests
    piece = kv_mine * 128
    extra = -(-2 * (rows // 128) // 8) * 8
    decoded, q_width = query.shape
    outs = pl.pallas_call(
        functools.partial(project_kernel, ranks, group),
        in_specs=[HBM] * 5,
        out_specs=[VMEM] * (ranks + 1),
        out_shape=[jax.ShapeDtypeStruct((rows + extra, 2 * piece), BF16)] * ranks
        + [jax.ShapeDtypeStruct((decoded, q_width // ranks + 2 * piece), BF16)],
        scratch_shapes=[
            pltpu.VMEM((feats,), BF16),
            pltpu.VMEM((slots, requests, feats), BF16),
            pltpu.VMEM((rows, feats), F32),
            pltpu.VMEM(weight.shape, BF16),
            pltpu.VMEM((rows, weight.shape[1]), F32),
            pltpu.SemaphoreType.DMA((5,)),
            pltpu.SemaphoreType.DMA((-(-feats // CHUNK),)),
        ],
        compiler_params=pltpu.CompilerParams(vmem_limit_bytes=56 * MIB),
        cost_estimate=pl.CostEstimate(
            flops=2 * rows * feats * weight.shape[1],
            bytes_accessed=2 * feats * weight.shape[1],
            transcendentals=0,
        ),
        name="project",
    )(gain, x, weight, query, own)
    return outs[:ranks], outs[ranks]


def resident_kernel(ranks, len_ref, q_hbm, k_hbm, v_hbm, *rest):
    outs, rest = rest[:ranks], rest[ranks:]
    q_ref, q_wide, q_all, k_buf, v_buf, o_all, m_all, l_all, s_all, q_sem, sems = rest
    residents, positions, width = k_buf.shape
    copies = []
    for r in range(residents):
        copies.append(
            (
                pltpu.make_async_copy(k_hbm.at[r], k_buf.at[r], sems.at[0, r]),
                pltpu.make_async_copy(v_hbm.at[r], v_buf.at[r], sems.at[1, r]),
            )
        )
    rank = lax.axis_index("tp")
    held = [(rank == 0) | (len_ref[0, r] > rank * positions) for r in range(residents)]
    for r in range(residents):

        @pl.when(held[r])
        def _():
            for copy in copies[r]:
                copy.start()

        if r == 0:
            q_copy = pltpu.make_async_copy(q_hbm, q_ref, q_sem)
            q_copy.start()

    heads = q_ref.shape[0]
    kv_heads = width // 128
    group = heads // kv_heads
    pair_rows = 2 * group
    heads_mine = heads // ranks
    top_half = iota((pair_rows, 128), 0) < group
    position = rank * positions + iota((pair_rows, positions), 1)
    scale = F32(1.0) / jnp.sqrt(F32(128.0))
    diagonal = iota((heads, 128), 0) % heads_mine == iota((heads, 128), 1)

    def to_rows(column):
        spread = jnp.where(diagonal, column, 0.0)
        return jnp.sum(spread.reshape(ranks, heads_mine, 128), axis=1)

    q_copy.wait()
    q_wide[...] = q_ref[...].astype(F32)
    for r in range(residents):
        q_all[r] = q_wide[:, r, :].astype(BF16)
    def attend(r):
        valid = position < len_ref[0, r]
        copies[r][0].wait()
        weights = []
        for p in range(kv_heads // 2):
            rows = slice(p * pair_rows, (p + 1) * pair_rows)
            q = q_all[r, rows, :]
            zero = jnp.zeros_like(q)
            lhs = jnp.concatenate(
                [jnp.where(top_half, q, zero), jnp.where(top_half, zero, q)], axis=1
            )
            scores = lax.dot_general(
                lhs,
                k_buf[r, :, p * 256 : (p + 1) * 256],
                (((1,), (1,)), ((), ())),
                preferred_element_type=F32,
            )
            scores = jnp.where(valid, scores * scale, ABSENT)
            peak = jnp.max(scores, axis=1, keepdims=True).astype(BF16).astype(F32)
            weight = jnp.where(valid, jnp.exp(scores - peak), 0.0)
            m_all[r, rows, :] = peak
            l_all[r, rows, :] = jnp.sum(weight, axis=1, keepdims=True)
            weights.append(weight.astype(BF16))
        copies[r][1].wait()
        for p in range(kv_heads // 2):
            both = jnp.dot(
                weights[p], v_buf[r, :, p * 256 : (p + 1) * 256], preferred_element_type=F32
            )
            o_all[r, p * pair_rows : (p + 1) * pair_rows, :] = jnp.where(
                top_half, both[:, :128], both[:, 128:]
            )

    for r in range(residents):
        pl.when(held[r])(functools.partial(attend, r))

        @pl.when(jnp.logical_not(held[r]))
        def _():
            o_all[r] = jnp.zeros((heads, 128), F32)
            m_all[r] = jnp.full((heads, 1), ABSENT, F32)
            l_all[r] = jnp.zeros((heads, 1), F32)

    for r in range(residents):
        s_all[r, 0] = to_rows(m_all[r])
        high, low = split_bf16(to_rows(l_all[r]))
        s_all[r, 1] = high.astype(F32)
        s_all[r, 2] = low.astype(F32)
    filled = residents * (heads_mine + 3)
    for j in range(ranks):
        target = rank ^ j
        first = pl.multiple_of(target * heads_mine, heads_mine)
        parts = [o_all[r, pl.ds(first, heads_mine), :] for r in range(residents)]
        parts += [s_all[r, i, pl.ds(target, 1), :] for i in range(3) for r in range(residents)]
        if outs[j].shape[0] > filled:
            parts.append(jnp.zeros((outs[j].shape[0] - filled, 128), F32))
        outs[j][...] = jnp.concatenate(parts, axis=0).astype(BF16)


def attend_resident(lengths, queries, k_cache, v_cache, ranks):
    residents, positions, width = k_cache.shape
    heads = queries.shape[0]
    heads_mine = heads // ranks
    rows = -(-(residents * (heads_mine + 3)) // 16) * 16
    return pl.pallas_call(
        functools.partial(resident_kernel, ranks),
        in_specs=[SMEM, HBM, HBM, HBM],
        out_specs=[VMEM] * ranks,
        out_shape=[jax.ShapeDtypeStruct((rows, 128), BF16)] * ranks,
        scratch_shapes=[
            pltpu.VMEM(queries.shape, BF16),
            pltpu.VMEM(queries.shape, F32),
            pltpu.VMEM((residents, heads, 128), BF16),
            pltpu.VMEM((residents, positions, width), BF16),
            pltpu.VMEM((residents, positions, width), BF16),
            pltpu.VMEM((residents, heads, 128), F32),
            pltpu.VMEM((residents, heads, 1), F32),
            pltpu.VMEM((residents, heads, 1), F32),
            pltpu.VMEM((residents, 3, ranks, 128), F32),
            pltpu.SemaphoreType.DMA,
            pltpu.SemaphoreType.DMA((2, residents)),
        ],
        compiler_params=pltpu.CompilerParams(vmem_limit_bytes=56 * MIB),
        cost_estimate=pl.CostEstimate(
            flops=4 * residents * heads * positions * 128,
            bytes_accessed=4 * residents * positions * width,
            transcendentals=residents * heads * positions,
        ),
        name="attend_resident",
    )(lengths, queries, k_cache, v_cache)


def expand(own, rows):
    which = iota((rows, 128), 0) // (rows // own.shape[0])
    out = jnp.broadcast_to(own[0:1], (rows, 128))
    for h in range(1, own.shape[0]):
        out = jnp.where(which == h, own[h : h + 1], out)
    return out


def heads_of(line, heads_mine, kv_mine):
    per = heads_mine // kv_mine
    blocks = [line[:, c : c + 128] for c in range(0, line.shape[1], 128)]
    q = jnp.concatenate(blocks[:heads_mine], axis=0)
    k = blocks[heads_mine : heads_mine + kv_mine]
    v = blocks[heads_mine + kv_mine :]
    return (
        q,
        expand(jnp.concatenate(k, axis=0), heads_mine),
        expand(jnp.concatenate(v, axis=0), heads_mine),
    )


def moved_kernel(
    insts, ranks, residents, features, dest_ref, count_ref, gain_ref, cos_ref, sin_ref, *rest
):
    asks, rest = rest[: insts - 1], rest[insts - 1 :]
    pieces, rest = rest[:ranks], rest[ranks:]
    out_ref, place_out, ask_ref, q_ref, own_ref, line_ref = rest
    requests = out_ref.shape[0]
    tokens = cos_ref.shape[0]
    piece = pieces[0].shape[1] // 2
    kv_mine = piece // 128
    rows = q_ref.shape[0]
    heads_mine = rows // requests
    scale = F32(1.0) / jnp.sqrt(F32(128.0))
    here = lax.axis_index("inst")

    ask_row = iota(asks[0].shape, 0)
    row_request = iota((rows, tokens), 0) // heads_mine
    limit = jnp.zeros((rows, tokens), jnp.int32)
    for r in range(requests):
        dest = dest_ref[r, here]
        limit = jnp.where(row_request == r, count_ref[r, here], limit)
        place = jnp.int32(residents)
        for s in range(insts):
            for c in range(requests):
                place += jnp.where((dest_ref[c, s] == dest) & (here > s), 1, 0).astype(jnp.int32)
        for b in range(1, insts):

            @pl.when(here ^ b == dest)
            def _():
                ask = asks[b - 1][...].astype(F32)
                ask_ref[r : r + 1, :] = jnp.sum(
                    jnp.where(ask_row == place, ask, 0.0), axis=0, keepdims=True
                )

        at = slice(r * heads_mine, (r + 1) * heads_mine)
        q_ref[at, :], own_ref[0, at, :], own_ref[1, at, :] = heads_of(
            ask_ref[r : r + 1, :], heads_mine, kv_mine
        )
    places = jnp.full(place_out.shape, -1, jnp.int32)
    row = iota(place_out.shape, 0)
    place = jnp.int32(residents)
    for s in range(insts):
        for c in range(requests):
            mine = dest_ref[c, s] == here
            places = jnp.where((row == (here ^ s) * requests + c) & mine, place, places)
            place += jnp.where(mine, 1, 0).astype(jnp.int32)
    place_out[...] = places

    blocks = tokens // 128
    last = tokens + 2 * blocks
    tail = pieces[0][tokens:last, :128].astype(F32)
    for t in range(1, ranks):
        tail = tail + pieces[t][tokens:last, :128].astype(F32)
    squares = tail[:blocks] + tail[blocks:]
    squares = jnp.concatenate(
        [row_to_column(squares[b : b + 1], 128) for b in range(blocks)], axis=0
    )
    token_scale = lax.rsqrt(squares / features + EPS)

    def column_block(c):
        total = pieces[0][:tokens, c : c + 128].astype(F32)
        for t in range(1, ranks):
            total = total + pieces[t][:tokens, c : c + 128].astype(F32)
        return total * token_scale

    gain = gain_ref[...].astype(F32)
    q = q_ref[...]
    q16 = q.astype(BF16)
    which = iota((rows, tokens), 0) % heads_mine // (heads_mine // kv_mine)
    scores = None
    for h in range(kv_mine):
        key = column_block(h * 128)
        key = key * lax.rsqrt(jnp.mean(key * key, axis=1, keepdims=True) + EPS) * gain
        key = key * cos_ref[...] + pltpu.roll(key, 64, 1) * sin_ref[...]
        part = lax.dot_general(
            q16, key.astype(BF16), (((1,), (1,)), ((), ())), preferred_element_type=F32
        )
        scores = part if scores is None else jnp.where(which == h, part, scores)
    token = iota((rows, tokens), 1)
    valid = (token % requests == row_request) & (token // requests < limit)
    scores = jnp.where(valid, scores * scale, ABSENT)
    own_score = jnp.sum(q * own_ref[0], axis=1, keepdims=True) * scale
    top = jnp.maximum(jnp.max(scores, axis=1, keepdims=True), own_score)
    weights = jnp.where(valid, jnp.exp(scores - top), 0.0)
    own_weight = jnp.exp(own_score - top)
    total = jnp.sum(weights, axis=1, keepdims=True) + own_weight
    weights = weights.astype(BF16)
    summed = None
    for h in range(kv_mine):
        value = column_block(piece + h * 128).astype(BF16)
        part = jnp.dot(weights, value, preferred_element_type=F32)
        summed = part if summed is None else jnp.where(which[:, :128] == h, part, summed)
    summed = summed + own_weight.astype(BF16).astype(F32) * own_ref[1]
    result = summed / total
    for r in range(requests):
        for h in range(heads_mine):
            at = r * heads_mine + h
            line_ref[r : r + 1, h * 128 : (h + 1) * 128] = result[at : at + 1, :]
    out_ref[...] = line_ref[...].astype(BF16)


def attend_moved(dest, count, k_gain, cos, sin, asks, pieces, residents, heads_mine, features):
    requests, insts = dest.shape
    rows = requests * heads_mine
    return pl.pallas_call(
        functools.partial(moved_kernel, insts, len(pieces), residents, features),
        in_specs=[SMEM] * 2 + [VMEM] * (3 + len(asks) + len(pieces)),
        out_specs=[VMEM] * 2,
        out_shape=[
            jax.ShapeDtypeStruct((requests, heads_mine * 128), BF16),
            jax.ShapeDtypeStruct((insts * requests, 128), jnp.int32),
        ],
        scratch_shapes=[
            pltpu.VMEM((requests, asks[0].shape[1]), F32),
            pltpu.VMEM((rows, 128), F32),
            pltpu.VMEM((2, rows, 128), F32),
            pltpu.VMEM((requests, heads_mine * 128), F32),
        ],
        compiler_params=pltpu.CompilerParams(vmem_limit_bytes=16 * MIB),
        name="attend_moved",
    )(dest, count, k_gain, cos, sin, *asks, *pieces)


def combine_kernel(residents, kv_mine, ask_ref, *rest):
    refs, out_ref = rest[:-1], rest[-1]
    heads_mine = out_ref.shape[1] // 128
    scale = F32(1.0) / jnp.sqrt(F32(128.0))
    payloads = [ref[...].astype(F32) for ref in refs]
    at = residents * heads_mine
    ask = ask_ref[...].astype(F32)
    for r in range(residents):
        q, own_k, own_v = heads_of(ask[r : r + 1], heads_mine, kv_mine)
        own_score = jnp.sum(q * own_k, axis=1, keepdims=True) * scale
        peaks, totals = [], []
        for payload in payloads:
            stat = payload[at : at + 3 * residents]
            peaks.append(row_to_column(stat[r : r + 1], heads_mine))
            total = stat[residents + r : residents + r + 1]
            total = total + stat[2 * residents + r : 2 * residents + r + 1]
            totals.append(row_to_column(total, heads_mine))
        top = own_score
        for peak in peaks:
            top = jnp.maximum(top, peak)
        own_weight = jnp.exp(own_score - top)
        denom = own_weight
        numer = own_weight.astype(BF16).astype(F32) * own_v
        for peak, total, payload in zip(peaks, totals, payloads):
            keep = jnp.exp(peak - top)
            denom = denom + keep * total
            numer = numer + keep * payload[r * heads_mine : (r + 1) * heads_mine]
        result = numer / denom
        for h in range(heads_mine):
            out_ref[r : r + 1, h * 128 : (h + 1) * 128] = result[h : h + 1, :]


def combine_resident(ask, payloads, residents, heads_mine, kv_mine):
    return pl.pallas_call(
        functools.partial(combine_kernel, residents, kv_mine),
        in_specs=[VMEM] * (1 + len(payloads)),
        out_specs=VMEM,
        out_shape=jax.ShapeDtypeStruct((residents, heads_mine * 128), F32),
        compiler_params=pltpu.CompilerParams(vmem_limit_bytes=8 * MIB),
        name="combine_resident",
    )(ask, *payloads)


def finish_kernel(kept_ref, place_ref, *rest):
    moved, out_ref = rest[:-1], rest[-1]
    residents = kept_ref.shape[0]
    decoded, width = out_ref.shape
    requests = decoded - residents
    row = iota((decoded, 128), 0)
    arrived = [ref[...].astype(F32) for ref in moved]
    for c in range(0, width, 128):
        kept = kept_ref[:, c : c + 128]
        line = jnp.concatenate([kept, jnp.zeros((requests, 128), F32)], axis=0)
        for b in range(len(moved)):
            for i in range(requests):
                at = (b + 1) * requests + i
                line = jnp.where(
                    place_ref[at : at + 1, :] == row, arrived[b][i : i + 1, c : c + 128], line
                )
        out_ref[:, c : c + 128] = line.astype(BF16)


def finish(kept, places, moved, requests):
    residents, width = kept.shape
    return pl.pallas_call(
        finish_kernel,
        in_specs=[VMEM] * (2 + len(moved)),
        out_specs=VMEM,
        out_shape=jax.ShapeDtypeStruct((residents + requests, width), BF16),
        compiler_params=pltpu.CompilerParams(vmem_limit_bytes=8 * MIB),
        name="finish",
    )(kept, places, *moved)


def swapped(x, axis, j, n):
    return lax.ppermute(x, axis, [(i, i ^ j) for i in range(n)])


def rotation(slots, requests, head_size):
    half = head_size // 2
    freq = THETA ** (-np.arange(half) * 2.0 / head_size)
    angle = np.repeat(np.arange(slots), requests)[:, None] * freq[None, :]
    cos, sin = np.cos(angle), np.sin(angle)
    return (
        np.concatenate([cos, cos], axis=1).astype(np.float32),
        np.concatenate([-sin, sin], axis=1).astype(np.float32),
    )


def per_device(
    mig_hidden,
    mig_dest,
    mig_count,
    attn_gain,
    kv_weight,
    k_gain,
    query,
    new_kv,
    k_cache,
    v_cache,
    lengths,
):
    insts = lax.axis_size("inst")
    ranks = lax.axis_size("tp")
    head_size = k_gain.shape[0]
    slots, requests, feats = mig_hidden.shape[1:]
    residents = k_cache.shape[1]
    heads = query.shape[2] // head_size
    kv_heads = kv_weight.shape[1] // 2 // head_size
    heads_mine = heads // ranks
    group = heads // kv_heads
    kv_mine = max(1, heads_mine // group)

    pieces, ask = project(
        mig_hidden[0], attn_gain, kv_weight, query[0], new_kv[0], ranks, group, kv_mine
    )
    order = sorted(range(2, ranks), key=lambda j: (abs(j - ranks // 2), j))
    asks = [swapped(ask, "inst", b, insts) for b in range(1, insts)]
    sent = [swapped(pieces[j], "tp", j, ranks) for j in order]
    asks[0], near = lax.optimization_barrier((asks[0], pieces[1]))
    pieces = [pieces[0]] + sent + [swapped(near, "tp", 1, ranks)]
    queries = jnp.transpose(query[0].reshape(query.shape[1], heads, head_size), (1, 0, 2))
    payloads = attend_resident(lengths, queries, k_cache[0], v_cache[0], ranks)
    asks, payloads = lax.optimization_barrier((asks, payloads))
    order = sorted(range(1, ranks), key=lambda j: (j > 1, -j))
    received = [payloads[0]] + [swapped(payloads[j], "tp", j, ranks) for j in order]
    cos, sin = rotation(slots, requests, head_size)
    moved, places = attend_moved(
        mig_dest.T,
        mig_count.T,
        k_gain.reshape(1, head_size),
        cos,
        sin,
        asks,
        pieces,
        residents,
        heads_mine,
        feats * ranks,
    )
    kept = combine_resident(ask, received, residents, heads_mine, kv_mine)
    moved = [swapped(moved, "inst", b, insts) for b in reversed(range(1, insts))][::-1]
    return finish(kept, places, moved, requests)[None]


def solution(mesh):
    placed = (
        P(("group", "inst"), None, None, "tp"),
        P("group", None),
        P("group", None),
        P("tp"),
        P("tp", None),
        P(),
        P(("group", "inst"), None, None),
        P(("group", "inst"), None, None),
        P(("group", "inst"), None, "tp", None),
        P(("group", "inst"), None, "tp", None),
        P(("group", "inst"), None),
    )
    return jax.shard_map(
        per_device,
        mesh=mesh,
        in_specs=placed,
        out_specs=P(("group", "inst"), None, "tp"),
        check_vma=False,
    )
```

```python
import functools

import jax
import jax.numpy as jnp
import numpy as np
from jax import lax
from jax.experimental import pallas as pl
from jax.experimental.pallas import tpu as pltpu
from jax.sharding import PartitionSpec as P

EPS = 1e-06
THETA = 1000000.0
ABSENT = -1e30
F32 = jnp.float32
BF16 = jnp.bfloat16
MIB = 1024 * 1024
CHUNK = 512

VMEM = pl.BlockSpec(memory_space=pltpu.VMEM)
SMEM = pl.BlockSpec(memory_space=pltpu.SMEM)
HBM = pl.BlockSpec(memory_space=pltpu.HBM)


def iota(shape, dim):
    return lax.broadcasted_iota(jnp.int32, shape, dim)


def column_to_row(column, period):
    n = column.shape[0]
    spread = jnp.where(iota((n, 128), 0) % period == iota((n, 128), 1), column, 0.0)
    return jnp.sum(spread.reshape(n // period, period, 128), axis=1)


def row_to_column(row, n):
    return jnp.sum(
        jnp.where(iota((n, 128), 0) == iota((n, 128), 1), row, 0.0), axis=1, keepdims=True
    )


def split_bf16(x):
    high = x.astype(BF16)
    return high, (x - high.astype(F32)).astype(BF16)


def project_kernel(ranks, group, gain_hbm, x_hbm, w_hbm, q_hbm, own_hbm, *rest):
    outs, ask_ref = rest[:ranks], rest[ranks]
    gain_ref, x_ref, rows_ref, w_ref, acc_ref, in_sems, w_sems = rest[ranks + 1 :]
    slots, requests, feats = x_ref.shape
    rows = slots * requests
    piece = outs[0].shape[1] // 2
    kv_width = w_hbm.shape[1] // 2
    heads_mine = kv_width // 128 * group // ranks
    rank = lax.axis_index("tp")

    def first_column(target):
        return pl.multiple_of(target * heads_mine // group * 128, 128)

    gain_copy = pltpu.make_async_copy(gain_hbm, gain_ref, in_sems.at[0])
    gain_copy.start()
    x_copy = pltpu.make_async_copy(x_hbm, x_ref, in_sems.at[1])
    x_copy.start()
    cuts = list(range(0, feats, CHUNK)) + [feats]
    chunks = list(zip(cuts[:-1], cuts[1:]))
    copies = []
    for i, (low, high) in enumerate(chunks):
        copies.append(
            pltpu.make_async_copy(w_hbm.at[low:high, :], w_ref.at[low:high, :], w_sems.at[i])
        )
        copies[-1].start()
    mine = heads_mine * 128
    q_first = pl.multiple_of(rank * mine, 128)
    asking = [
        pltpu.make_async_copy(
            q_hbm.at[:, pl.ds(q_first, mine)], ask_ref.at[:, :mine], in_sems.at[2]
        )
    ]
    for i in range(2):
        asking.append(
            pltpu.make_async_copy(
                own_hbm.at[:, pl.ds(i * kv_width + first_column(rank), piece)],
                ask_ref.at[:, mine + i * piece : mine + (i + 1) * piece],
                in_sems.at[3 + i],
            )
        )
    for copy in asking:
        copy.start()
    gain_copy.wait()
    x_copy.wait()
    for slot in range(slots):
        rows_ref[slot * requests : (slot + 1) * requests, :] = x_ref[slot].astype(F32)
    squares = jnp.zeros((rows, 128), F32)
    for i, (low, high) in enumerate(chunks):
        parts = []
        for c in range(low, high, 128):
            width = min(128, high - c)
            x = rows_ref[:, c : c + width]
            gain = gain_ref[c : c + width].astype(F32).reshape(1, width)
            parts.append((x * gain).astype(BF16))
            x = x * x
            if width < 128:
                x = jnp.concatenate([x, jnp.zeros((rows, 128 - width), F32)], axis=1)
            squares = squares + x
        xg = parts[0] if len(parts) == 1 else jnp.concatenate(parts, axis=1)
        copies[i].wait()
        for n in range(0, 2 * kv_width, 512):
            part = jnp.dot(xg, w_ref[low:high, n : n + 512], preferred_element_type=F32)
            if i == 0:
                acc_ref[:, n : n + 512] = part
            else:
                acc_ref[:, n : n + 512] += part
    sq = column_to_row(jnp.sum(squares, axis=1, keepdims=True), 128)
    high, low = split_bf16(sq)
    tail = jnp.concatenate([high.astype(F32), low.astype(F32)], axis=0)
    fill = outs[1].shape[0] - rows - tail.shape[0]
    if fill:
        tail = jnp.concatenate([tail, jnp.zeros((fill, 128), F32)], axis=0)
    extra = jnp.concatenate([tail.astype(BF16)] * (2 * piece // 128), axis=1)
    for j in range(ranks):
        first = first_column(rank ^ j)
        outs[j][:rows, :piece] = acc_ref[:, pl.ds(first, piece)].astype(BF16)
        outs[j][:rows, piece:] = acc_ref[:, pl.ds(kv_width + first, piece)].astype(BF16)
        outs[j][rows:, :] = extra
    for copy in asking:
        copy.wait()


def project(x, gain, weight, query, own, ranks, group, kv_mine):
    slots, requests, feats = x.shape
    rows = slots * requests
    piece = kv_mine * 128
    extra = -(-2 * (rows // 128) // 8) * 8
    decoded, q_width = query.shape
    outs = pl.pallas_call(
        functools.partial(project_kernel, ranks, group),
        in_specs=[HBM] * 5,
        out_specs=[VMEM] * (ranks + 1),
        out_shape=[jax.ShapeDtypeStruct((rows + extra, 2 * piece), BF16)] * ranks
        + [jax.ShapeDtypeStruct((decoded, q_width // ranks + 2 * piece), BF16)],
        scratch_shapes=[
            pltpu.VMEM((feats,), BF16),
            pltpu.VMEM((slots, requests, feats), BF16),
            pltpu.VMEM((rows, feats), F32),
            pltpu.VMEM(weight.shape, BF16),
            pltpu.VMEM((rows, weight.shape[1]), F32),
            pltpu.SemaphoreType.DMA((5,)),
            pltpu.SemaphoreType.DMA((-(-feats // CHUNK),)),
        ],
        compiler_params=pltpu.CompilerParams(vmem_limit_bytes=56 * MIB),
        cost_estimate=pl.CostEstimate(
            flops=2 * rows * feats * weight.shape[1],
            bytes_accessed=2 * feats * weight.shape[1],
            transcendentals=0,
        ),
        name="project",
    )(gain, x, weight, query, own)
    return outs[:ranks], outs[ranks]


def resident_kernel(ranks, len_ref, q_ref, k_hbm, v_hbm, *rest):
    outs, rest = rest[:ranks], rest[ranks:]
    q_wide, q_all, k_buf, v_buf, o_all, m_all, l_all, s_all, sems = rest
    residents, positions, width = k_buf.shape
    copies = []
    for r in range(residents):
        copies.append(
            (
                pltpu.make_async_copy(k_hbm.at[r], k_buf.at[r], sems.at[0, r]),
                pltpu.make_async_copy(
                    v_hbm.at[r, : positions // 2, :], v_buf.at[r, : positions // 2, :], sems.at[1, r]
                ),
                pltpu.make_async_copy(
                    v_hbm.at[r, positions // 2 :, :], v_buf.at[r, positions // 2 :, :], sems.at[2, r]
                ),
            )
        )
    rank = lax.axis_index("tp")
    held = [(rank == 0) | (len_ref[0, r] > rank * positions) for r in range(residents)]
    for r in range(residents):

        @pl.when(held[r])
        def _():
            for copy in copies[r]:
                copy.start()

    heads = q_ref.shape[0]
    kv_heads = width // 128
    group = heads // kv_heads
    pair_rows = 2 * group
    heads_mine = heads // ranks
    top_half = iota((pair_rows, 128), 0) < group
    position = rank * positions + iota((pair_rows, positions), 1)
    scale = F32(1.0) / jnp.sqrt(F32(128.0))
    diagonal = iota((heads, 128), 0) % heads_mine == iota((heads, 128), 1)

    def to_rows(column):
        spread = jnp.where(diagonal, column, 0.0)
        return jnp.sum(spread.reshape(ranks, heads_mine, 128), axis=1)

    q_wide[...] = q_ref[...].astype(F32)
    for r in range(residents):
        q_all[r] = q_wide[:, r, :].astype(BF16)
    def attend(r):
        valid = position < len_ref[0, r]
        copies[r][0].wait()
        weights = []
        for p in range(kv_heads // 2):
            rows = slice(p * pair_rows, (p + 1) * pair_rows)
            q = q_all[r, rows, :]
            zero = jnp.zeros_like(q)
            lhs = jnp.concatenate(
                [jnp.where(top_half, q, zero), jnp.where(top_half, zero, q)], axis=1
            )
            scores = lax.dot_general(
                lhs,
                k_buf[r, :, p * 256 : (p + 1) * 256],
                (((1,), (1,)), ((), ())),
                preferred_element_type=F32,
            )
            scores = jnp.where(valid, scores * scale, ABSENT)
            peak = jnp.max(scores, axis=1, keepdims=True).astype(BF16).astype(F32)
            weight = jnp.where(valid, jnp.exp(scores - peak), 0.0)
            m_all[r, rows, :] = peak
            l_all[r, rows, :] = jnp.sum(weight, axis=1, keepdims=True)
            weights.append(weight.astype(BF16))
        for i in range(2):
            at = slice(i * positions // 2, (i + 1) * positions // 2)
            copies[r][1 + i].wait()
            for p in range(kv_heads // 2):
                both = jnp.dot(
                    weights[p][:, at],
                    v_buf[r, at, p * 256 : (p + 1) * 256],
                    preferred_element_type=F32,
                )
                rows = slice(p * pair_rows, (p + 1) * pair_rows)
                part = jnp.where(top_half, both[:, :128], both[:, 128:])
                if i == 0:
                    o_all[r, rows, :] = part
                else:
                    o_all[r, rows, :] += part

    for r in range(residents):
        pl.when(held[r])(functools.partial(attend, r))

        @pl.when(jnp.logical_not(held[r]))
        def _():
            o_all[r] = jnp.zeros((heads, 128), F32)
            m_all[r] = jnp.full((heads, 1), ABSENT, F32)
            l_all[r] = jnp.zeros((heads, 1), F32)

    for r in range(residents):
        s_all[r, 0] = to_rows(m_all[r])
        high, low = split_bf16(to_rows(l_all[r]))
        s_all[r, 1] = high.astype(F32)
        s_all[r, 2] = low.astype(F32)
    filled = residents * (heads_mine + 3)
    for j in range(ranks):
        target = rank ^ j
        first = pl.multiple_of(target * heads_mine, heads_mine)
        parts = [o_all[r, pl.ds(first, heads_mine), :] for r in range(residents)]
        parts += [s_all[r, i, pl.ds(target, 1), :] for i in range(3) for r in range(residents)]
        if outs[j].shape[0] > filled:
            parts.append(jnp.zeros((outs[j].shape[0] - filled, 128), F32))
        outs[j][...] = jnp.concatenate(parts, axis=0).astype(BF16)


def attend_resident(lengths, queries, k_cache, v_cache, ranks):
    residents, positions, width = k_cache.shape
    heads = queries.shape[0]
    heads_mine = heads // ranks
    rows = -(-(residents * (heads_mine + 3)) // 16) * 16
    return pl.pallas_call(
        functools.partial(resident_kernel, ranks),
        in_specs=[SMEM, VMEM, HBM, HBM],
        out_specs=[VMEM] * ranks,
        out_shape=[jax.ShapeDtypeStruct((rows, 128), BF16)] * ranks,
        scratch_shapes=[
            pltpu.VMEM(queries.shape, F32),
            pltpu.VMEM((residents, heads, 128), BF16),
            pltpu.VMEM((residents, positions, width), BF16),
            pltpu.VMEM((residents, positions, width), BF16),
            pltpu.VMEM((residents, heads, 128), F32),
            pltpu.VMEM((residents, heads, 1), F32),
            pltpu.VMEM((residents, heads, 1), F32),
            pltpu.VMEM((residents, 3, ranks, 128), F32),
            pltpu.SemaphoreType.DMA((3, residents)),
        ],
        compiler_params=pltpu.CompilerParams(vmem_limit_bytes=56 * MIB),
        cost_estimate=pl.CostEstimate(
            flops=4 * residents * heads * positions * 128,
            bytes_accessed=4 * residents * positions * width,
            transcendentals=residents * heads * positions,
        ),
        name="attend_resident",
    )(lengths, queries, k_cache, v_cache)


def expand(own, rows):
    which = iota((rows, 128), 0) // (rows // own.shape[0])
    out = jnp.broadcast_to(own[0:1], (rows, 128))
    for h in range(1, own.shape[0]):
        out = jnp.where(which == h, own[h : h + 1], out)
    return out


def heads_of(line, heads_mine, kv_mine):
    per = heads_mine // kv_mine
    blocks = [line[:, c : c + 128] for c in range(0, line.shape[1], 128)]
    q = jnp.concatenate(blocks[:heads_mine], axis=0)
    k = blocks[heads_mine : heads_mine + kv_mine]
    v = blocks[heads_mine + kv_mine :]
    return (
        q,
        expand(jnp.concatenate(k, axis=0), heads_mine),
        expand(jnp.concatenate(v, axis=0), heads_mine),
    )


def moved_kernel(
    insts, ranks, residents, features, dest_ref, count_ref, gain_ref, cos_ref, sin_ref, *rest
):
    asks, rest = rest[: insts - 1], rest[insts - 1 :]
    pieces, rest = rest[:ranks], rest[ranks:]
    out_ref, place_out, ask_ref, q_ref, own_ref, line_ref = rest
    requests = out_ref.shape[0]
    tokens = cos_ref.shape[0]
    piece = pieces[0].shape[1] // 2
    kv_mine = piece // 128
    rows = q_ref.shape[0]
    heads_mine = rows // requests
    scale = F32(1.0) / jnp.sqrt(F32(128.0))
    here = lax.axis_index("inst")

    ask_row = iota(asks[0].shape, 0)
    row_request = iota((rows, tokens), 0) // heads_mine
    limit = jnp.zeros((rows, tokens), jnp.int32)
    for r in range(requests):
        dest = dest_ref[r, here]
        limit = jnp.where(row_request == r, count_ref[r, here], limit)
        place = jnp.int32(residents)
        for s in range(insts):
            for c in range(requests):
                place += jnp.where((dest_ref[c, s] == dest) & (here > s), 1, 0).astype(jnp.int32)
        for b in range(1, insts):

            @pl.when(here ^ b == dest)
            def _():
                ask = asks[b - 1][...].astype(F32)
                ask_ref[r : r + 1, :] = jnp.sum(
                    jnp.where(ask_row == place, ask, 0.0), axis=0, keepdims=True
                )

        at = slice(r * heads_mine, (r + 1) * heads_mine)
        q_ref[at, :], own_ref[0, at, :], own_ref[1, at, :] = heads_of(
            ask_ref[r : r + 1, :], heads_mine, kv_mine
        )
    places = jnp.full(place_out.shape, -1, jnp.int32)
    row = iota(place_out.shape, 0)
    place = jnp.int32(residents)
    for s in range(insts):
        for c in range(requests):
            mine = dest_ref[c, s] == here
            places = jnp.where((row == (here ^ s) * requests + c) & mine, place, places)
            place += jnp.where(mine, 1, 0).astype(jnp.int32)
    place_out[...] = places

    blocks = tokens // 128
    last = tokens + 2 * blocks
    tail = pieces[0][tokens:last, :128].astype(F32)
    for t in range(1, ranks):
        tail = tail + pieces[t][tokens:last, :128].astype(F32)
    squares = tail[:blocks] + tail[blocks:]
    squares = jnp.concatenate(
        [row_to_column(squares[b : b + 1], 128) for b in range(blocks)], axis=0
    )
    token_scale = lax.rsqrt(squares / features + EPS)

    def column_block(c):
        total = pieces[0][:tokens, c : c + 128].astype(F32)
        for t in range(1, ranks):
            total = total + pieces[t][:tokens, c : c + 128].astype(F32)
        return total * token_scale

    gain = gain_ref[...].astype(F32)
    q = q_ref[...]
    q16 = q.astype(BF16)
    which = iota((rows, tokens), 0) % heads_mine // (heads_mine // kv_mine)
    scores = None
    for h in range(kv_mine):
        key = column_block(h * 128)
        key = key * lax.rsqrt(jnp.mean(key * key, axis=1, keepdims=True) + EPS) * gain
        key = key * cos_ref[...] + pltpu.roll(key, 64, 1) * sin_ref[...]
        part = lax.dot_general(
            q16, key.astype(BF16), (((1,), (1,)), ((), ())), preferred_element_type=F32
        )
        scores = part if scores is None else jnp.where(which == h, part, scores)
    token = iota((rows, tokens), 1)
    valid = (token % requests == row_request) & (token // requests < limit)
    scores = jnp.where(valid, scores * scale, ABSENT)
    own_score = jnp.sum(q * own_ref[0], axis=1, keepdims=True) * scale
    top = jnp.maximum(jnp.max(scores, axis=1, keepdims=True), own_score)
    weights = jnp.where(valid, jnp.exp(scores - top), 0.0)
    own_weight = jnp.exp(own_score - top)
    total = jnp.sum(weights, axis=1, keepdims=True) + own_weight
    weights = weights.astype(BF16)
    summed = None
    for h in range(kv_mine):
        value = column_block(piece + h * 128).astype(BF16)
        part = jnp.dot(weights, value, preferred_element_type=F32)
        summed = part if summed is None else jnp.where(which[:, :128] == h, part, summed)
    summed = summed + own_weight.astype(BF16).astype(F32) * own_ref[1]
    result = summed / total
    for r in range(requests):
        for h in range(heads_mine):
            at = r * heads_mine + h
            line_ref[r : r + 1, h * 128 : (h + 1) * 128] = result[at : at + 1, :]
    out_ref[...] = line_ref[...].astype(BF16)


def attend_moved(dest, count, k_gain, cos, sin, asks, pieces, residents, heads_mine, features):
    requests, insts = dest.shape
    rows = requests * heads_mine
    return pl.pallas_call(
        functools.partial(moved_kernel, insts, len(pieces), residents, features),
        in_specs=[SMEM] * 2 + [VMEM] * (3 + len(asks) + len(pieces)),
        out_specs=[VMEM] * 2,
        out_shape=[
            jax.ShapeDtypeStruct((requests, heads_mine * 128), BF16),
            jax.ShapeDtypeStruct((insts * requests, 128), jnp.int32),
        ],
        scratch_shapes=[
            pltpu.VMEM((requests, asks[0].shape[1]), F32),
            pltpu.VMEM((rows, 128), F32),
            pltpu.VMEM((2, rows, 128), F32),
            pltpu.VMEM((requests, heads_mine * 128), F32),
        ],
        compiler_params=pltpu.CompilerParams(vmem_limit_bytes=16 * MIB),
        name="attend_moved",
    )(dest, count, k_gain, cos, sin, *asks, *pieces)


def combine_kernel(residents, kv_mine, ask_ref, *rest):
    refs, out_ref = rest[:-1], rest[-1]
    heads_mine = out_ref.shape[1] // 128
    scale = F32(1.0) / jnp.sqrt(F32(128.0))
    payloads = [ref[...].astype(F32) for ref in refs]
    at = residents * heads_mine
    ask = ask_ref[...].astype(F32)
    for r in range(residents):
        q, own_k, own_v = heads_of(ask[r : r + 1], heads_mine, kv_mine)
        own_score = jnp.sum(q * own_k, axis=1, keepdims=True) * scale
        peaks, totals = [], []
        for payload in payloads:
            stat = payload[at : at + 3 * residents]
            peaks.append(row_to_column(stat[r : r + 1], heads_mine))
            total = stat[residents + r : residents + r + 1]
            total = total + stat[2 * residents + r : 2 * residents + r + 1]
            totals.append(row_to_column(total, heads_mine))
        top = own_score
        for peak in peaks:
            top = jnp.maximum(top, peak)
        own_weight = jnp.exp(own_score - top)
        denom = own_weight
        numer = own_weight.astype(BF16).astype(F32) * own_v
        for peak, total, payload in zip(peaks, totals, payloads):
            keep = jnp.exp(peak - top)
            denom = denom + keep * total
            numer = numer + keep * payload[r * heads_mine : (r + 1) * heads_mine]
        result = numer / denom
        for h in range(heads_mine):
            out_ref[r : r + 1, h * 128 : (h + 1) * 128] = result[h : h + 1, :]


def combine_resident(ask, payloads, residents, heads_mine, kv_mine):
    return pl.pallas_call(
        functools.partial(combine_kernel, residents, kv_mine),
        in_specs=[VMEM] * (1 + len(payloads)),
        out_specs=VMEM,
        out_shape=jax.ShapeDtypeStruct((residents, heads_mine * 128), F32),
        compiler_params=pltpu.CompilerParams(vmem_limit_bytes=8 * MIB),
        name="combine_resident",
    )(ask, *payloads)


def finish_kernel(kept_ref, place_ref, *rest):
    moved, out_ref = rest[:-1], rest[-1]
    residents = kept_ref.shape[0]
    decoded, width = out_ref.shape
    requests = decoded - residents
    row = iota((decoded, 128), 0)
    arrived = [ref[...].astype(F32) for ref in moved]
    for c in range(0, width, 128):
        kept = kept_ref[:, c : c + 128]
        line = jnp.concatenate([kept, jnp.zeros((requests, 128), F32)], axis=0)
        for b in range(len(moved)):
            for i in range(requests):
                at = (b + 1) * requests + i
                line = jnp.where(
                    place_ref[at : at + 1, :] == row, arrived[b][i : i + 1, c : c + 128], line
                )
        out_ref[:, c : c + 128] = line.astype(BF16)


def finish(kept, places, moved, requests):
    residents, width = kept.shape
    return pl.pallas_call(
        finish_kernel,
        in_specs=[VMEM] * (2 + len(moved)),
        out_specs=VMEM,
        out_shape=jax.ShapeDtypeStruct((residents + requests, width), BF16),
        compiler_params=pltpu.CompilerParams(vmem_limit_bytes=8 * MIB),
        name="finish",
    )(kept, places, *moved)


def swapped(x, axis, j, n):
    return lax.ppermute(x, axis, [(i, i ^ j) for i in range(n)])


def rotation(slots, requests, head_size):
    half = head_size // 2
    freq = THETA ** (-np.arange(half) * 2.0 / head_size)
    angle = np.repeat(np.arange(slots), requests)[:, None] * freq[None, :]
    cos, sin = np.cos(angle), np.sin(angle)
    return (
        np.concatenate([cos, cos], axis=1).astype(np.float32),
        np.concatenate([-sin, sin], axis=1).astype(np.float32),
    )


def per_device(
    mig_hidden,
    mig_dest,
    mig_count,
    attn_gain,
    kv_weight,
    k_gain,
    query,
    new_kv,
    k_cache,
    v_cache,
    lengths,
):
    insts = lax.axis_size("inst")
    ranks = lax.axis_size("tp")
    head_size = k_gain.shape[0]
    slots, requests, feats = mig_hidden.shape[1:]
    residents = k_cache.shape[1]
    heads = query.shape[2] // head_size
    kv_heads = kv_weight.shape[1] // 2 // head_size
    heads_mine = heads // ranks
    group = heads // kv_heads
    kv_mine = max(1, heads_mine // group)

    pieces, ask = project(
        mig_hidden[0], attn_gain, kv_weight, query[0], new_kv[0], ranks, group, kv_mine
    )
    order = sorted(range(2, ranks), key=lambda j: (abs(j - ranks // 2), j))
    asks = [swapped(ask, "inst", b, insts) for b in range(1, insts)]
    sent = [swapped(pieces[j], "tp", j, ranks) for j in order]
    asks[0], near = lax.optimization_barrier((asks[0], pieces[1]))
    pieces = [pieces[0]] + sent + [swapped(near, "tp", 1, ranks)]
    queries = jnp.transpose(query[0].reshape(query.shape[1], heads, head_size), (1, 0, 2))
    payloads = attend_resident(lengths, queries, k_cache[0], v_cache[0], ranks)
    asks, payloads = lax.optimization_barrier((asks, payloads))
    order = sorted(range(1, ranks), key=lambda j: (j > 1, -j))
    received = [payloads[0]] + [swapped(payloads[j], "tp", j, ranks) for j in order]
    cos, sin = rotation(slots, requests, head_size)
    moved, places = attend_moved(
        mig_dest.T,
        mig_count.T,
        k_gain.reshape(1, head_size),
        cos,
        sin,
        asks,
        pieces,
        residents,
        heads_mine,
        feats * ranks,
    )
    kept = combine_resident(ask, received, residents, heads_mine, kv_mine)
    moved = [swapped(moved, "inst", b, insts) for b in reversed(range(1, insts))][::-1]
    return finish(kept, places, moved, requests)[None]


def solution(mesh):
    placed = (
        P(("group", "inst"), None, None, "tp"),
        P("group", None),
        P("group", None),
        P("tp"),
        P("tp", None),
        P(),
        P(("group", "inst"), None, None),
        P(("group", "inst"), None, None),
        P(("group", "inst"), None, "tp", None),
        P(("group", "inst"), None, "tp", None),
        P(("group", "inst"), None),
    )
    return jax.shard_map(
        per_device,
        mesh=mesh,
        in_specs=placed,
        out_specs=P(("group", "inst"), None, "tp"),
        check_vma=False,
    )
```

```python
import functools

import jax
import jax.numpy as jnp
import numpy as np
from jax import lax
from jax.experimental import pallas as pl
from jax.experimental.pallas import tpu as pltpu
from jax.sharding import PartitionSpec as P

EPS = 1e-06
THETA = 1000000.0
ABSENT = -1e30
F32 = jnp.float32
BF16 = jnp.bfloat16
MIB = 1024 * 1024
CHUNK = 512

VMEM = pl.BlockSpec(memory_space=pltpu.VMEM)
SMEM = pl.BlockSpec(memory_space=pltpu.SMEM)
HBM = pl.BlockSpec(memory_space=pltpu.HBM)


def iota(shape, dim):
    return lax.broadcasted_iota(jnp.int32, shape, dim)


def column_to_row(column, period):
    n = column.shape[0]
    spread = jnp.where(iota((n, 128), 0) % period == iota((n, 128), 1), column, 0.0)
    return jnp.sum(spread.reshape(n // period, period, 128), axis=1)


def row_to_column(row, n):
    return jnp.sum(
        jnp.where(iota((n, 128), 0) == iota((n, 128), 1), row, 0.0), axis=1, keepdims=True
    )


def split_bf16(x):
    high = x.astype(BF16)
    return high, (x - high.astype(F32)).astype(BF16)


def project_kernel(ranks, group, gain_hbm, x_hbm, w_hbm, q_hbm, own_hbm, *rest):
    outs, ask_ref = rest[:ranks], rest[ranks]
    gain_ref, x_ref, rows_ref, w_ref, acc_ref, in_sems, w_sems = rest[ranks + 1 :]
    slots, requests, feats = x_ref.shape
    rows = slots * requests
    piece = outs[0].shape[1] // 2
    kv_width = w_hbm.shape[1] // 2
    heads_mine = kv_width // 128 * group // ranks
    rank = lax.axis_index("tp")

    def first_column(target):
        return pl.multiple_of(target * heads_mine // group * 128, 128)

    gain_copy = pltpu.make_async_copy(gain_hbm, gain_ref, in_sems.at[0])
    gain_copy.start()
    x_copy = pltpu.make_async_copy(x_hbm, x_ref, in_sems.at[1])
    x_copy.start()
    cuts = list(range(0, feats, CHUNK)) + [feats]
    chunks = list(zip(cuts[:-1], cuts[1:]))
    copies = []
    for i, (low, high) in enumerate(chunks):
        copies.append(
            pltpu.make_async_copy(w_hbm.at[low:high, :], w_ref.at[low:high, :], w_sems.at[i])
        )
        copies[-1].start()
    mine = heads_mine * 128
    q_first = pl.multiple_of(rank * mine, 128)
    asking = [
        pltpu.make_async_copy(
            q_hbm.at[:, pl.ds(q_first, mine)], ask_ref.at[:, :mine], in_sems.at[2]
        )
    ]
    for i in range(2):
        asking.append(
            pltpu.make_async_copy(
                own_hbm.at[:, pl.ds(i * kv_width + first_column(rank), piece)],
                ask_ref.at[:, mine + i * piece : mine + (i + 1) * piece],
                in_sems.at[3 + i],
            )
        )
    for copy in asking:
        copy.start()
    gain_copy.wait()
    x_copy.wait()
    for slot in range(slots):
        rows_ref[slot * requests : (slot + 1) * requests, :] = x_ref[slot].astype(F32)
    squares = jnp.zeros((rows, 128), F32)
    for i, (low, high) in enumerate(chunks):
        parts = []
        for c in range(low, high, 128):
            width = min(128, high - c)
            x = rows_ref[:, c : c + width]
            gain = gain_ref[c : c + width].astype(F32).reshape(1, width)
            parts.append((x * gain).astype(BF16))
            x = x * x
            if width < 128:
                x = jnp.concatenate([x, jnp.zeros((rows, 128 - width), F32)], axis=1)
            squares = squares + x
        xg = parts[0] if len(parts) == 1 else jnp.concatenate(parts, axis=1)
        copies[i].wait()
        for n in range(0, 2 * kv_width, 512):
            part = jnp.dot(xg, w_ref[low:high, n : n + 512], preferred_element_type=F32)
            if i == 0:
                acc_ref[:, n : n + 512] = part
            else:
                acc_ref[:, n : n + 512] += part
    sq = column_to_row(jnp.sum(squares, axis=1, keepdims=True), 128)
    high, low = split_bf16(sq)
    tail = jnp.concatenate([high.astype(F32), low.astype(F32)], axis=0)
    fill = outs[1].shape[0] - rows - tail.shape[0]
    if fill:
        tail = jnp.concatenate([tail, jnp.zeros((fill, 128), F32)], axis=0)
    extra = jnp.concatenate([tail.astype(BF16)] * (2 * piece // 128), axis=1)
    for j in range(ranks):
        first = first_column(rank ^ j)
        outs[j][:rows, :piece] = acc_ref[:, pl.ds(first, piece)].astype(BF16)
        outs[j][:rows, piece:] = acc_ref[:, pl.ds(kv_width + first, piece)].astype(BF16)
        outs[j][rows:, :] = extra
    for copy in asking:
        copy.wait()


def project(x, gain, weight, query, own, ranks, group, kv_mine):
    slots, requests, feats = x.shape
    rows = slots * requests
    piece = kv_mine * 128
    extra = -(-2 * (rows // 128) // 8) * 8
    decoded, q_width = query.shape
    outs = pl.pallas_call(
        functools.partial(project_kernel, ranks, group),
        in_specs=[HBM] * 5,
        out_specs=[VMEM] * (ranks + 1),
        out_shape=[jax.ShapeDtypeStruct((rows + extra, 2 * piece), BF16)] * ranks
        + [jax.ShapeDtypeStruct((decoded, q_width // ranks + 2 * piece), BF16)],
        scratch_shapes=[
            pltpu.VMEM((feats,), BF16),
            pltpu.VMEM((slots, requests, feats), BF16),
            pltpu.VMEM((rows, feats), F32),
            pltpu.VMEM(weight.shape, BF16),
            pltpu.VMEM((rows, weight.shape[1]), F32),
            pltpu.SemaphoreType.DMA((5,)),
            pltpu.SemaphoreType.DMA((-(-feats // CHUNK),)),
        ],
        compiler_params=pltpu.CompilerParams(vmem_limit_bytes=56 * MIB),
        cost_estimate=pl.CostEstimate(
            flops=2 * rows * feats * weight.shape[1],
            bytes_accessed=2 * feats * weight.shape[1],
            transcendentals=0,
        ),
        name="project",
    )(gain, x, weight, query, own)
    return outs[:ranks], outs[ranks]


def resident_kernel(ranks, len_ref, q_ref, k_hbm, v_hbm, *rest):
    outs, rest = rest[:ranks], rest[ranks:]
    q_wide, q_all, k_buf, v_buf, o_all, m_all, l_all, s_all, sems = rest
    residents, positions, width = k_buf.shape
    copies = []
    for r in range(residents):
        copies.append(
            (
                pltpu.make_async_copy(k_hbm.at[r], k_buf.at[r], sems.at[0, r]),
                pltpu.make_async_copy(v_hbm.at[r], v_buf.at[r], sems.at[1, r]),
            )
        )
    rank = lax.axis_index("tp")
    held = [(rank == 0) | (len_ref[0, r] > rank * positions) for r in range(residents)]
    for r in range(residents):

        @pl.when(held[r])
        def _():
            for copy in copies[r]:
                copy.start()

    heads = q_ref.shape[0]
    kv_heads = width // 128
    group = heads // kv_heads
    pair_rows = 2 * group
    heads_mine = heads // ranks
    top_half = iota((pair_rows, 128), 0) < group
    position = rank * positions + iota((pair_rows, positions), 1)
    scale = F32(1.0) / jnp.sqrt(F32(128.0))
    diagonal = iota((heads, 128), 0) % heads_mine == iota((heads, 128), 1)

    def to_rows(column):
        spread = jnp.where(diagonal, column, 0.0)
        return jnp.sum(spread.reshape(ranks, heads_mine, 128), axis=1)

    q_wide[...] = q_ref[...].astype(F32)
    for r in range(residents):
        q_all[r] = q_wide[:, r, :].astype(BF16)
    def attend(r):
        valid = position < len_ref[0, r]
        copies[r][0].wait()
        weights = []
        for p in range(kv_heads // 2):
            rows = slice(p * pair_rows, (p + 1) * pair_rows)
            q = q_all[r, rows, :]
            zero = jnp.zeros_like(q)
            lhs = jnp.concatenate(
                [jnp.where(top_half, q, zero), jnp.where(top_half, zero, q)], axis=1
            )
            scores = lax.dot_general(
                lhs,
                k_buf[r, :, p * 256 : (p + 1) * 256],
                (((1,), (1,)), ((), ())),
                preferred_element_type=F32,
            )
            scores = jnp.where(valid, scores * scale, ABSENT)
            peak = jnp.max(scores, axis=1, keepdims=True).astype(BF16).astype(F32)
            weight = jnp.where(valid, jnp.exp(scores - peak), 0.0)
            m_all[r, rows, :] = peak
            l_all[r, rows, :] = jnp.sum(weight, axis=1, keepdims=True)
            weights.append(weight.astype(BF16))
        copies[r][1].wait()
        for p in range(kv_heads // 2):
            both = jnp.dot(
                weights[p], v_buf[r, :, p * 256 : (p + 1) * 256], preferred_element_type=F32
            )
            o_all[r, p * pair_rows : (p + 1) * pair_rows, :] = jnp.where(
                top_half, both[:, :128], both[:, 128:]
            )

    for r in range(residents):
        pl.when(held[r])(functools.partial(attend, r))

        @pl.when(jnp.logical_not(held[r]))
        def _():
            o_all[r] = jnp.zeros((heads, 128), F32)
            m_all[r] = jnp.full((heads, 1), ABSENT, F32)
            l_all[r] = jnp.zeros((heads, 1), F32)

    for r in range(residents):
        s_all[r, 0] = to_rows(m_all[r])
        high, low = split_bf16(to_rows(l_all[r]))
        s_all[r, 1] = high.astype(F32)
        s_all[r, 2] = low.astype(F32)
    filled = residents * (heads_mine + 3)
    for j in range(ranks):
        target = rank ^ j
        first = pl.multiple_of(target * heads_mine, heads_mine)
        parts = [o_all[r, pl.ds(first, heads_mine), :] for r in range(residents)]
        parts += [s_all[r, i, pl.ds(target, 1), :] for i in range(3) for r in range(residents)]
        if outs[j].shape[0] > filled:
            parts.append(jnp.zeros((outs[j].shape[0] - filled, 128), F32))
        outs[j][...] = jnp.concatenate(parts, axis=0).astype(BF16)


def attend_resident(lengths, queries, k_cache, v_cache, ranks):
    residents, positions, width = k_cache.shape
    heads = queries.shape[0]
    heads_mine = heads // ranks
    rows = -(-(residents * (heads_mine + 3)) // 16) * 16
    return pl.pallas_call(
        functools.partial(resident_kernel, ranks),
        in_specs=[SMEM, VMEM, HBM, HBM],
        out_specs=[VMEM] * ranks,
        out_shape=[jax.ShapeDtypeStruct((rows, 128), BF16)] * ranks,
        scratch_shapes=[
            pltpu.VMEM(queries.shape, F32),
            pltpu.VMEM((residents, heads, 128), BF16),
            pltpu.VMEM((residents, positions, width), BF16),
            pltpu.VMEM((residents, positions, width), BF16),
            pltpu.VMEM((residents, heads, 128), F32),
            pltpu.VMEM((residents, heads, 1), F32),
            pltpu.VMEM((residents, heads, 1), F32),
            pltpu.VMEM((residents, 3, ranks, 128), F32),
            pltpu.SemaphoreType.DMA((2, residents)),
        ],
        compiler_params=pltpu.CompilerParams(vmem_limit_bytes=56 * MIB),
        cost_estimate=pl.CostEstimate(
            flops=4 * residents * heads * positions * 128,
            bytes_accessed=4 * residents * positions * width,
            transcendentals=residents * heads * positions,
        ),
        name="attend_resident",
    )(lengths, queries, k_cache, v_cache)


def expand(own, rows):
    which = iota((rows, 128), 0) // (rows // own.shape[0])
    out = jnp.broadcast_to(own[0:1], (rows, 128))
    for h in range(1, own.shape[0]):
        out = jnp.where(which == h, own[h : h + 1], out)
    return out


def heads_of(line, heads_mine, kv_mine):
    per = heads_mine // kv_mine
    blocks = [line[:, c : c + 128] for c in range(0, line.shape[1], 128)]
    q = jnp.concatenate(blocks[:heads_mine], axis=0)
    k = blocks[heads_mine : heads_mine + kv_mine]
    v = blocks[heads_mine + kv_mine :]
    return (
        q,
        expand(jnp.concatenate(k, axis=0), heads_mine),
        expand(jnp.concatenate(v, axis=0), heads_mine),
    )


def moved_kernel(
    insts, ranks, residents, features, dest_ref, count_ref, gain_ref, cos_ref, sin_ref, *rest
):
    asks, rest = rest[: insts - 1], rest[insts - 1 :]
    pieces, rest = rest[:ranks], rest[ranks:]
    out_ref, place_out, ask_ref, q_ref, own_ref, line_ref = rest
    requests = out_ref.shape[0]
    tokens = cos_ref.shape[0]
    piece = pieces[0].shape[1] // 2
    kv_mine = piece // 128
    rows = q_ref.shape[0]
    heads_mine = rows // requests
    scale = F32(1.0) / jnp.sqrt(F32(128.0))
    here = lax.axis_index("inst")

    ask_row = iota(asks[0].shape, 0)
    row_request = iota((rows, tokens), 0) // heads_mine
    limit = jnp.zeros((rows, tokens), jnp.int32)
    for r in range(requests):
        dest = dest_ref[r, here]
        limit = jnp.where(row_request == r, count_ref[r, here], limit)
        place = jnp.int32(residents)
        for s in range(insts):
            for c in range(requests):
                place += jnp.where((dest_ref[c, s] == dest) & (here > s), 1, 0).astype(jnp.int32)
        for b in range(1, insts):

            @pl.when(here ^ b == dest)
            def _():
                ask = asks[b - 1][...].astype(F32)
                ask_ref[r : r + 1, :] = jnp.sum(
                    jnp.where(ask_row == place, ask, 0.0), axis=0, keepdims=True
                )

        at = slice(r * heads_mine, (r + 1) * heads_mine)
        q_ref[at, :], own_ref[0, at, :], own_ref[1, at, :] = heads_of(
            ask_ref[r : r + 1, :], heads_mine, kv_mine
        )
    places = jnp.full(place_out.shape, -1, jnp.int32)
    row = iota(place_out.shape, 0)
    place = jnp.int32(residents)
    for s in range(insts):
        for c in range(requests):
            mine = dest_ref[c, s] == here
            places = jnp.where((row == (here ^ s) * requests + c) & mine, place, places)
            place += jnp.where(mine, 1, 0).astype(jnp.int32)
    place_out[...] = places

    blocks = tokens // 128
    last = tokens + 2 * blocks
    tail = pieces[0][tokens:last, :128].astype(F32)
    for t in range(1, ranks):
        tail = tail + pieces[t][tokens:last, :128].astype(F32)
    squares = tail[:blocks] + tail[blocks:]
    squares = jnp.concatenate(
        [row_to_column(squares[b : b + 1], 128) for b in range(blocks)], axis=0
    )
    token_scale = lax.rsqrt(squares / features + EPS)

    def column_block(c):
        total = pieces[0][:tokens, c : c + 128].astype(F32)
        for t in range(1, ranks):
            total = total + pieces[t][:tokens, c : c + 128].astype(F32)
        return total * token_scale

    gain = gain_ref[...].astype(F32)
    q = q_ref[...]
    q16 = q.astype(BF16)
    which = iota((rows, tokens), 0) % heads_mine // (heads_mine // kv_mine)
    scores = None
    for h in range(kv_mine):
        key = column_block(h * 128)
        key = key * lax.rsqrt(jnp.mean(key * key, axis=1, keepdims=True) + EPS) * gain
        key = key * cos_ref[...] + pltpu.roll(key, 64, 1) * sin_ref[...]
        part = lax.dot_general(
            q16, key.astype(BF16), (((1,), (1,)), ((), ())), preferred_element_type=F32
        )
        scores = part if scores is None else jnp.where(which == h, part, scores)
    token = iota((rows, tokens), 1)
    valid = (token % requests == row_request) & (token // requests < limit)
    scores = jnp.where(valid, scores * scale, ABSENT)
    own_score = jnp.sum(q * own_ref[0], axis=1, keepdims=True) * scale
    top = jnp.maximum(jnp.max(scores, axis=1, keepdims=True), own_score)
    weights = jnp.where(valid, jnp.exp(scores - top), 0.0)
    own_weight = jnp.exp(own_score - top)
    total = jnp.sum(weights, axis=1, keepdims=True) + own_weight
    weights = weights.astype(BF16)
    summed = None
    for h in range(kv_mine):
        value = column_block(piece + h * 128).astype(BF16)
        part = jnp.dot(weights, value, preferred_element_type=F32)
        summed = part if summed is None else jnp.where(which[:, :128] == h, part, summed)
    summed = summed + own_weight.astype(BF16).astype(F32) * own_ref[1]
    result = summed / total
    for r in range(requests):
        for h in range(heads_mine):
            at = r * heads_mine + h
            line_ref[r : r + 1, h * 128 : (h + 1) * 128] = result[at : at + 1, :]
    out_ref[...] = line_ref[...].astype(BF16)


def attend_moved(dest, count, k_gain, cos, sin, asks, pieces, residents, heads_mine, features):
    requests, insts = dest.shape
    rows = requests * heads_mine
    return pl.pallas_call(
        functools.partial(moved_kernel, insts, len(pieces), residents, features),
        in_specs=[SMEM] * 2 + [VMEM] * (3 + len(asks) + len(pieces)),
        out_specs=[VMEM] * 2,
        out_shape=[
            jax.ShapeDtypeStruct((requests, heads_mine * 128), BF16),
            jax.ShapeDtypeStruct((insts * requests, 128), jnp.int32),
        ],
        scratch_shapes=[
            pltpu.VMEM((requests, asks[0].shape[1]), F32),
            pltpu.VMEM((rows, 128), F32),
            pltpu.VMEM((2, rows, 128), F32),
            pltpu.VMEM((requests, heads_mine * 128), F32),
        ],
        compiler_params=pltpu.CompilerParams(vmem_limit_bytes=16 * MIB),
        name="attend_moved",
    )(dest, count, k_gain, cos, sin, *asks, *pieces)


def combine_kernel(residents, kv_mine, ask_ref, *rest):
    refs, out_ref = rest[:-1], rest[-1]
    heads_mine = out_ref.shape[1] // 128
    scale = F32(1.0) / jnp.sqrt(F32(128.0))
    payloads = [ref[...].astype(F32) for ref in refs]
    at = residents * heads_mine
    ask = ask_ref[...].astype(F32)
    for r in range(residents):
        q, own_k, own_v = heads_of(ask[r : r + 1], heads_mine, kv_mine)
        own_score = jnp.sum(q * own_k, axis=1, keepdims=True) * scale
        peaks, totals = [], []
        for payload in payloads:
            stat = payload[at : at + 3 * residents]
            peaks.append(row_to_column(stat[r : r + 1], heads_mine))
            total = stat[residents + r : residents + r + 1]
            total = total + stat[2 * residents + r : 2 * residents + r + 1]
            totals.append(row_to_column(total, heads_mine))
        top = own_score
        for peak in peaks:
            top = jnp.maximum(top, peak)
        own_weight = jnp.exp(own_score - top)
        denom = own_weight
        numer = own_weight.astype(BF16).astype(F32) * own_v
        for peak, total, payload in zip(peaks, totals, payloads):
            keep = jnp.exp(peak - top)
            denom = denom + keep * total
            numer = numer + keep * payload[r * heads_mine : (r + 1) * heads_mine]
        result = numer / denom
        for h in range(heads_mine):
            out_ref[r : r + 1, h * 128 : (h + 1) * 128] = result[h : h + 1, :]


def combine_resident(ask, payloads, residents, heads_mine, kv_mine):
    return pl.pallas_call(
        functools.partial(combine_kernel, residents, kv_mine),
        in_specs=[VMEM] * (1 + len(payloads)),
        out_specs=VMEM,
        out_shape=jax.ShapeDtypeStruct((residents, heads_mine * 128), F32),
        compiler_params=pltpu.CompilerParams(vmem_limit_bytes=8 * MIB),
        name="combine_resident",
    )(ask, *payloads)


def finish_kernel(kept_ref, place_ref, *rest):
    moved, out_ref = rest[:-1], rest[-1]
    residents = kept_ref.shape[0]
    decoded, width = out_ref.shape
    requests = decoded - residents
    row = iota((decoded, 128), 0)
    arrived = [ref[...].astype(F32) for ref in moved]
    for c in range(0, width, 128):
        kept = kept_ref[:, c : c + 128]
        line = jnp.concatenate([kept, jnp.zeros((requests, 128), F32)], axis=0)
        for b in range(len(moved)):
            for i in range(requests):
                at = (b + 1) * requests + i
                line = jnp.where(
                    place_ref[at : at + 1, :] == row, arrived[b][i : i + 1, c : c + 128], line
                )
        out_ref[:, c : c + 128] = line.astype(BF16)


def finish(kept, places, moved, requests):
    residents, width = kept.shape
    return pl.pallas_call(
        finish_kernel,
        in_specs=[VMEM] * (2 + len(moved)),
        out_specs=VMEM,
        out_shape=jax.ShapeDtypeStruct((residents + requests, width), BF16),
        compiler_params=pltpu.CompilerParams(vmem_limit_bytes=8 * MIB),
        name="finish",
    )(kept, places, *moved)


def swapped(x, axis, j, n):
    return lax.ppermute(x, axis, [(i, i ^ j) for i in range(n)])


def rotation(slots, requests, head_size):
    half = head_size // 2
    freq = THETA ** (-np.arange(half) * 2.0 / head_size)
    angle = np.repeat(np.arange(slots), requests)[:, None] * freq[None, :]
    cos, sin = np.cos(angle), np.sin(angle)
    return (
        np.concatenate([cos, cos], axis=1).astype(np.float32),
        np.concatenate([-sin, sin], axis=1).astype(np.float32),
    )


def per_device(
    mig_hidden,
    mig_dest,
    mig_count,
    attn_gain,
    kv_weight,
    k_gain,
    query,
    new_kv,
    k_cache,
    v_cache,
    lengths,
):
    insts = lax.axis_size("inst")
    ranks = lax.axis_size("tp")
    head_size = k_gain.shape[0]
    slots, requests, feats = mig_hidden.shape[1:]
    residents = k_cache.shape[1]
    heads = query.shape[2] // head_size
    kv_heads = kv_weight.shape[1] // 2 // head_size
    heads_mine = heads // ranks
    group = heads // kv_heads
    kv_mine = max(1, heads_mine // group)

    pieces, ask = project(
        mig_hidden[0], attn_gain, kv_weight, query[0], new_kv[0], ranks, group, kv_mine
    )
    order = sorted(range(2, ranks), key=lambda j: (abs(j - ranks // 2), j))
    asks = [swapped(ask, "inst", b, insts) for b in range(1, insts)]
    sent = [swapped(pieces[j], "tp", j, ranks) for j in order]
    asks[0], near = lax.optimization_barrier((asks[0], pieces[1]))
    pieces = [pieces[0]] + sent + [swapped(near, "tp", 1, ranks)]
    queries = jnp.transpose(query[0].reshape(query.shape[1], heads, head_size), (1, 0, 2))
    payloads = attend_resident(lengths, queries, k_cache[0], v_cache[0], ranks)
    asks, payloads = lax.optimization_barrier((asks, payloads))
    order = sorted(range(1, ranks), key=lambda j: (j > 1, -j))
    received = [payloads[0]] + [swapped(payloads[j], "tp", j, ranks) for j in order]
    cos, sin = rotation(slots, requests, head_size)
    moved, places = attend_moved(
        mig_dest.T,
        mig_count.T,
        k_gain.reshape(1, head_size),
        cos,
        sin,
        asks,
        pieces,
        residents,
        heads_mine,
        feats * ranks,
    )
    kept = combine_resident(ask, received, residents, heads_mine, kv_mine)
    order = sorted(range(1, insts), key=lambda b: (b == 1, b % 2, b))
    results = {b: swapped(moved, "inst", b, insts) for b in order}
    moved = [results[b] for b in range(1, insts)]
    return finish(kept, places, moved, requests)[None]


def solution(mesh):
    placed = (
        P(("group", "inst"), None, None, "tp"),
        P("group", None),
        P("group", None),
        P("tp"),
        P("tp", None),
        P(),
        P(("group", "inst"), None, None),
        P(("group", "inst"), None, None),
        P(("group", "inst"), None, "tp", None),
        P(("group", "inst"), None, "tp", None),
        P(("group", "inst"), None),
    )
    return jax.shard_map(
        per_device,
        mesh=mesh,
        in_specs=placed,
        out_specs=P(("group", "inst"), None, "tp"),
        check_vma=False,
    )
```
